32 devices in a mesh: dp: 2 (over y), expert: 16 (over z, x, core).
Axes of the slice: x: 2, y: 2, z: 4, core: 2. Of those that a mesh axis runs over, the one named last changes fastest.
Arguments:
- tokens: bfloat16 [32768, 768], P(('dp', 'expert')), may hold values from -6 to 6
- seq_ids: int32 [32768], P(('dp', 'expert')), may hold values from 0 to 3, as said below
- routes: int32 [32768, 1], P(('dp', 'expert')), may hold values from 0 to 15; in each aligned block of 1024 rows (0 to 1023, 1024 to 2047, ...) at most 128 rows name the same one
- cotangent: bfloat16 [32768, 768], P(('dp', 'expert')), may hold values from -6 to 6
- w_query: bfloat16 [768, 768], P(('dp', 'expert')), may hold values from -0.02734375 to 0.02734375
- w_key: bfloat16 [768, 768], P(('dp', 'expert')), may hold values from -0.21875 to 0.21875
- w_value: bfloat16 [768, 768], P(('dp', 'expert')), may hold values from -0.21875 to 0.21875
- w_out: bfloat16 [768, 768], P(('dp', 'expert')), may hold values from -3.5 to 3.5
- rel_table: bfloat16 [32, 12], P('dp'), may hold values from -6 to 6
- gain_attn: bfloat16 [768], P(('dp', 'expert')), may hold values from 0.099609375 to 1.8984375
- gain_ffn: bfloat16 [768], P(('dp', 'expert')), may hold values from 0.099609375 to 1.8984375
- router: bfloat16 [768, 16], P(('dp', 'expert')), may hold values from -0.109375 to 0.109375
- expert_in: bfloat16 [16, 768, 3072], P('expert', 'dp'), may hold values from -0.21875 to 0.21875
- expert_out: bfloat16 [16, 3072, 768], P('expert', 'dp'), may hold values from -10 to 10
Outputs:
- mixed: float32 [32768, 768], P(('dp', 'expert'))
- grad_tokens: float32 [32768, 768], P(('dp', 'expert'))
- grad_w_query: float32 [768, 768], P(('dp', 'expert'))
- grad_w_key: float32 [768, 768], P(('dp', 'expert'))
- grad_w_value: float32 [768, 768], P(('dp', 'expert'))
- grad_w_out: float32 [768, 768], P(('dp', 'expert'))
- grad_rel_table: float32 [32, 12], P('dp')
- grad_gain_attn: float32 [768], P(('dp', 'expert'))
- grad_gain_ffn: float32 [768], P(('dp', 'expert'))
- grad_router: float32 [768, 16], P(('dp', 'expert'))
- grad_expert_in: float32 [16, 768, 3072], P('expert', 'dp')
- grad_expert_out: float32 [16, 3072, 768], P('expert', 'dp')
The draws below stay inside these ranges and needn't reach their ends.
Inputs may be any that keep to these rules, and one draw needn't show every extreme that they name: `seq_ids`: within each device's 1024 tokens the ids never fall; tokens with equal ids on one device form one sequence; some device holds a single sequence of all its 1024 tokens. `routes`: no expert is named by more than 128 of one device's tokens.
All inputs are finite; a program needn't handle non-finite values.
Results may differ from the reference program's by a relative error of at most 0.015.
Values may be sent and summed in bfloat16 or wider, within the bound.
No kernel may reach another device: no remote copies, remote signals or barrier semaphores. Data moves between devices by JAX's collectives and lax.ppermute only.
A program may use at most 320 MiB of HBM per device.

```python
import math
from functools import partial
import jax
import jax.numpy as jnp
import numpy as np
from jax import lax

D = 768
HEADS = 12
HEAD_DIM = 64
FF = 3072
BUCKETS = 32
TOK_DEV = 1024
SEQS = 4
EXPERTS = 16
CAP = 128
TOKENS = 32768
N_DP = 2
N_EXPERT = 16


def draw_seq_ids(key, part):
    device_count = TOKENS // TOK_DEV
    boundaries = jax.random.randint(key, (device_count, SEQS - 1), 1, TOK_DEV + 1)
    single = jax.random.randint(jax.random.fold_in(key, 7), (), 0, device_count)
    unsplit = jnp.arange(device_count)[:, None] == single
    boundaries = jnp.where(unsplit, TOK_DEV, boundaries)
    places = jnp.arange(TOK_DEV)
    sequence_ids = jnp.sum((places[None, :, None] >= boundaries[:, None, :]).astype(jnp.int32), axis=2)
    return sequence_ids.reshape(TOKENS).astype(jnp.int32)


def level_of(rng, shape, pieces, least, top_value):
    loudness, own = 1.0, jax.random.fold_in(rng, 6)
    for position, parts in pieces:
        draws = jnp.exp(jax.random.uniform(jax.random.fold_in(own, position), (parts,), jnp.float32, least / len(pieces), top_value / len(pieces)))
        loudness = loudness * jnp.repeat(draws, shape[position] // parts).reshape([-1 if axis == position else 1 for axis in range(len(shape))])
    return loudness


def routed_block(rng, own, number, rows, number_of, top, reach, skew):
    ranking = jax.random.permutation(rng, number_of)
    heavy_load, common = portions_of(number_of, rows * top, reach, skew, True), portions_of(number_of, rows * top, reach, skew, False)
    places = jnp.arange(number_of)

    def named(tallies, offset_by):
        used = int((tallies > 0).sum())
        fixed = max(1, used // 4)
        moved = fixed + (places - fixed + offset_by * (used - fixed)) % max(1, number_of - fixed)
        return jnp.zeros((number_of,), jnp.int32).at[ranking[jnp.where(places < fixed, places, moved)]].set(jnp.asarray(tallies, jnp.int32))

    tallies = jnp.where(number % 4 == 0, named(heavy_load, number // 4), named(common, number - number // 4 - 1))
    mixed = jax.random.permutation(jax.random.fold_in(own, 3), number_of)
    donor, sink = mixed[0:number_of // 2 * 2:2], mixed[1:number_of // 2 * 2:2]
    slack = jnp.minimum(tallies[donor] - 1, reach - tallies[sink]) // 2
    slack = jnp.where((donor == ranking[0]) | (sink == ranking[0]) | (tallies[sink] == 0), 0, jnp.maximum(slack, 0))
    moved = jax.random.randint(jax.random.fold_in(own, 4), (number_of // 2,), 0, 1 << 20) % (slack + 1)
    tallies = tallies.at[donor].add(-moved).at[sink].add(moved)
    items = jnp.searchsorted(jnp.cumsum(tallies), jnp.arange(rows * top), side="right").astype(jnp.int32)
    listing = items.reshape(top, rows).T
    listing = listing[jax.random.permutation(jax.random.fold_in(own, 1), rows)]
    offset_by = jax.random.randint(jax.random.fold_in(own, 2), (rows, 1), 0, top)
    return jnp.take_along_axis(listing, (jnp.arange(top)[None, :] + offset_by) % top, axis=1)


def portions_of(amount, total, most, skew, full):
    portions = [(1 << 20) // math.isqrt(grade ** skew) + 1 for grade in range(1, amount + 1)]
    largest = most if full else min(most, max(-(-total // amount), total * portions[0] // sum(portions)))
    least = 1 if total - largest >= amount - 1 else 0
    counts, rest = [largest] + [least] * (amount - 1), total - largest - least * (amount - 1)
    while rest > 0:
        free = [i for i in range(1, amount) if counts[i] < largest] or [i for i in range(1, amount) if counts[i] < most]
        pool, left = sum([portions[i] for i in free]), rest
        for i in free:
            more = min(most - counts[i], max(1, left * portions[i] // pool), rest)
            counts[i] = counts[i] + more
            rest = rest - more
    return np.array(counts)


def normal_values(own_key, extent, scale, bound, cuts=(), held_as=jnp.bfloat16):
    loudness = level_of(own_key, extent, cuts, -0.22, 0.18) if cuts else 1.0
    entries = jax.random.normal(own_key, extent, jnp.float32) * scale * loudness
    return jnp.minimum(jnp.maximum(entries, -bound), bound).astype(held_as)


def setup_inputs(seed: int = 0) -> dict:
    streams_of = jax.random.split(jax.random.key(seed), 15)
    tokens = normal_values(streams_of[0], (TOKENS, D), 1.0, 6.0, ((0, 32),))
    seq_ids = draw_seq_ids(jax.random.fold_in(streams_of[14], 71), 0)
    routes_keys = jax.random.split(jax.random.fold_in(streams_of[2], 1), TOKENS // TOK_DEV)
    routes_turns = jax.random.permutation(jax.random.fold_in(streams_of[2], 3), TOKENS // TOK_DEV)
    routes = jax.vmap(lambda own, number: routed_block(jax.random.fold_in(streams_of[2], 2), own, number, TOK_DEV, EXPERTS, 1, CAP, 2))(routes_keys, routes_turns).reshape((TOKENS, 1))
    cotangent = normal_values(streams_of[3], (TOKENS, D), 1.0, 6.0, ((0, 32),))
    w_query = normal_values(streams_of[4], (D, D), (D * HEAD_DIM) ** -0.5, 0.02734375, ((0, 32),))
    w_key = normal_values(streams_of[5], (D, D), D ** -0.5, 0.21875, ((0, 32),))
    w_value = normal_values(streams_of[6], (D, D), D ** -0.5, 0.21875, ((0, 32),))
    w_out = normal_values(streams_of[7], (D, D), (D // 256) ** -0.5, 3.5, ((0, 32),))
    rel_table = normal_values(streams_of[8], (BUCKETS, HEADS), 1.0, 6.0, ((0, 2),))
    gain_attn = jnp.clip(1.0 + 0.18 * jax.random.normal(streams_of[9], (D,), jnp.float32), 0.099609375, 1.8984375).astype(jnp.bfloat16)
    gain_ffn = jnp.clip(1.0 + 0.18 * jax.random.normal(streams_of[10], (D,), jnp.float32), 0.099609375, 1.8984375).astype(jnp.bfloat16)
    router = normal_values(streams_of[11], (D, EXPERTS), (4 * D) ** -0.5, 0.109375, ((0, 32),))
    expert_in = normal_values(streams_of[12], (EXPERTS, D, FF), D ** -0.5, 0.21875, ((0, 16), (1, 2)))
    expert_out = normal_values(streams_of[13], (EXPERTS, FF, D), (0.04 * EXPERTS), 10.0, ((0, 16), (1, 2)))
    return dict(tokens=tokens, seq_ids=seq_ids, routes=routes, cotangent=cotangent, w_query=w_query, w_key=w_key, w_value=w_value, w_out=w_out, rel_table=rel_table, gain_attn=gain_attn, gain_ffn=gain_ffn, router=router, expert_in=expert_in, expert_out=expert_out)


EPSILON = 1e-06
DISTANCE_EDGES = (12, 16, 23, 32, 46, 64, 91)
MASKED = -1e+30
PRECISE = lax.Precision.HIGHEST

@jax.custom_vjp
def low(v):
    return lax.optimization_barrier(v.astype(jnp.bfloat16)).astype(jnp.float32)

@jax.custom_vjp
def low_back(v):
    return v

def low_keep(v):
    return (low(v), None)

def low_pass(kept, grad):
    return (grad,)

def back_keep(v):
    return (v, None)

def back_low(kept, grad):
    return (low(grad),)
low.defvjp(low_keep, low_pass)
low_back.defvjp(back_keep, back_low)

def gelu_exact(values):
    return jax.nn.gelu(values, approximate=False)

def bucket_of(offset):
    distance = jnp.abs(offset).astype(jnp.int32)
    distant = jnp.full(distance.shape, 8, jnp.int32)
    for boundary in DISTANCE_EDGES:
        distant = distant + (distance >= boundary).astype(jnp.int32)
    near = jnp.where(distance < 8, distance, distant).astype(jnp.int32)
    sided = (offset > 0).astype(jnp.int32) * jnp.int32(16)
    return (near + sided).astype(jnp.int32)

def rms_scale(values, factor):
    inverse = lax.rsqrt(lax.optimization_barrier(jnp.mean(values * values, axis=-1, keepdims=True)) + EPSILON)
    return values * inverse * factor

def product(left, right):
    return jnp.dot(left, right, precision=PRECISE, preferred_element_type=jnp.float32)

def attention(query, keys, values_in, seq_ids, rel_table):
    places = jnp.arange(TOK_DEV, dtype=jnp.int32)
    offsets = (places[None, :] - places[:, None]).astype(jnp.int32)
    buckets = bucket_of(offsets)

    def attend_device(inputs):
        query_dev, key_dev, value_dev, ids_dev = inputs
        scores = jnp.einsum('qhd,khd->hqk', query_dev, key_dev, precision=PRECISE)
        biases = jnp.transpose(jnp.take(rel_table, buckets, axis=0), (2, 0, 1))
        scores = low_back(scores + biases)
        paired = ids_dev[:, None] == ids_dev[None, :]
        masked_value = jnp.full(scores.shape, MASKED, scores.dtype)
        weights = jax.nn.softmax(jnp.where(paired[None], scores, masked_value), axis=-1)
        return jnp.einsum('hqk,khd->qhd', low(weights), value_dev, precision=PRECISE)
    return lax.map(jax.checkpoint(attend_device), (query, keys, values_in, seq_ids))

def forward(tokens, w_query, w_key, w_value, w_out, rel_table, gain_attn, gain_ffn, router, expert_in, expert_out, seq_ids, routes):
    devices = N_DP * N_EXPERT
    normed = low(rms_scale(tokens, gain_attn))
    query = low_back(low(product(normed, w_query)))
    keys = low_back(low(product(normed, w_key)))
    values_in = low_back(low(product(normed, w_value)))
    heads_shape = (devices, TOK_DEV, HEADS, HEAD_DIM)
    context = attention(query.reshape(heads_shape), keys.reshape(heads_shape), values_in.reshape(heads_shape), seq_ids.reshape(devices, TOK_DEV), rel_table)
    context = low_back(low(context.reshape(TOKENS, D)))
    middle = tokens + low_back(product(context, w_out))
    normed_ffn = low(rms_scale(middle, gain_ffn))
    logits = low_back(product(normed_ffn, router))
    router_probs = jax.nn.softmax(logits, axis=-1)
    chosen = routes[:, 0].astype(jnp.int32)
    picked = chosen[:, None] == jnp.arange(EXPERTS, dtype=jnp.int32)[None, :]
    gate_prob = lax.optimization_barrier(jnp.sum(jnp.where(picked, router_probs, jnp.zeros_like(router_probs)), axis=-1))
    owned = picked.reshape(devices, TOK_DEV, EXPERTS).astype(jnp.int32)
    ranks = lax.optimization_barrier(jnp.sum(jnp.cumsum(owned, axis=1, dtype=jnp.int32) * owned, axis=2, dtype=jnp.int32)) - jnp.int32(1)
    device_ids = jnp.arange(devices, dtype=jnp.int32)[:, None]
    slots = ((chosen.reshape(devices, TOK_DEV) * jnp.int32(devices) + device_ids) * jnp.int32(CAP) + ranks).reshape(TOKENS).astype(jnp.int32)
    filler = jnp.full((EXPERTS * devices * CAP,), TOKENS, jnp.int32).at[slots].set(jnp.arange(TOKENS, dtype=jnp.int32))
    sending = low_back(normed_ffn)
    padded = jnp.concatenate([sending, jnp.zeros((1, D), sending.dtype)], axis=0)
    buffer = padded[filler].reshape(EXPERTS, devices * CAP, D)

    def expert_run(inputs):
        rows_in, w_first, w_second = inputs
        hidden = low_back(product(rows_in, w_first))
        active = low(gelu_exact(hidden))
        return low_back(low(product(active, w_second)))
    outputs = lax.map(jax.checkpoint(expert_run), (buffer, expert_in, expert_out))
    returned = outputs.reshape(EXPERTS * devices * CAP, D)[slots]
    return middle + gate_prob[:, None] * returned

def reference(tokens, seq_ids, routes, cotangent, w_query, w_key, w_value, w_out, rel_table, gain_attn, gain_ffn, router, expert_in, expert_out):
    floats = [argument.astype(jnp.float32) for argument in (tokens, w_query, w_key, w_value, w_out, rel_table, gain_attn, gain_ffn, router, expert_in, expert_out)]
    mixed, pullback = jax.vjp(partial(forward, seq_ids=seq_ids.astype(jnp.int32), routes=routes.astype(jnp.int32)), floats[0], floats[1], floats[2], floats[3], floats[4], floats[5], floats[6], floats[7], floats[8], floats[9], floats[10])
    gradients = pullback(cotangent.astype(jnp.float32))
    return (mixed, gradients[0], gradients[1], gradients[2], gradients[3], gradients[4], gradients[5], gradients[6], gradients[7], gradients[8], gradients[9], gradients[10])
```

```python
import functools

import jax
import jax.numpy as jnp
from jax import lax
from jax.experimental import pallas as pl
from jax.experimental.pallas import tpu as pltpu
from jax.sharding import PartitionSpec as P

D = 768
HEADS = 12
HEAD_DIM = 64
BUCKETS = 32
TOK = 1024
TILE = 128
TILES = TOK // TILE
QBLK = 256
FF_TILE = 512
HALVES = 2
SPLIT = 3 * D // 2
LANES = 128

EPSILON = 1e-06
DISTANCE_EDGES = (12, 16, 23, 32, 46, 64, 91)
FAR_BEFORE = 15
FAR_AFTER = 31
UNPAIRED = -1e30
BF = jnp.bfloat16
F32 = jnp.float32
VMEM_LIMIT = 56 * 1024 * 1024


def dot(left, right, left_dim=1, right_dim=0):
    return lax.dot_general(
        left, right, (((left_dim,), (right_dim,)), ((), ())), preferred_element_type=F32
    )


def params(semantics=None):
    return pltpu.CompilerParams(vmem_limit_bytes=VMEM_LIMIT, dimension_semantics=semantics)


def cost(flops, bytes_accessed, transcendentals=0):
    return pl.CostEstimate(
        flops=int(flops), bytes_accessed=int(bytes_accessed), transcendentals=int(transcendentals)
    )


def whole(shape):
    return pl.BlockSpec(shape, lambda *_: (0,) * len(shape))


def inverse_rms(values):
    return lax.rsqrt(jnp.mean(values * values, axis=-1, keepdims=True) + EPSILON)


def bucket_of(offset):
    distance = jnp.abs(offset)
    distant = 8 + sum(((distance >= boundary).astype(jnp.int32) for boundary in DISTANCE_EDGES))
    return jnp.where(distance < 8, distance, distant) + jnp.where(offset > 0, 16, 0)


def place_in_buffers(route, rank, experts, capacity):
    share = capacity // HALVES
    part = (rank >= share).astype(jnp.int32)
    return part * (experts * share) + route * share + (rank - part * share)


def slots_kernel(experts, capacity, route_col, route_row, cot, slot_col, slot_row, sending):
    padded = -(-experts // LANES) * LANES
    picked = (
        lax.broadcasted_iota(jnp.int32, (TOK, padded), 1) == route_col[...]
    ).astype(BF)
    picked_t = (
        lax.broadcasted_iota(jnp.int32, (padded, TOK), 0) == route_row[...]
    ).astype(BF)
    upto = (
        lax.broadcasted_iota(jnp.int32, (TOK, TOK), 0)
        <= lax.broadcasted_iota(jnp.int32, (TOK, TOK), 1)
    ).astype(BF)
    from_t = (
        lax.broadcasted_iota(jnp.int32, (TOK, TOK), 0)
        >= lax.broadcasted_iota(jnp.int32, (TOK, TOK), 1)
    ).astype(BF)
    counts = dot(from_t, picked) * picked.astype(F32)
    rank = jnp.sum(counts, axis=1, keepdims=True).astype(jnp.int32) - 1
    slot_col[...] = place_in_buffers(route_col[...], rank, experts, capacity)
    counts_t = dot(picked_t, upto) * picked_t.astype(F32)
    rank_row = jnp.sum(counts_t, axis=0, keepdims=True).astype(jnp.int32) - 1
    slot_row[...] = place_in_buffers(route_row[...], rank_row, experts, capacity)
    dispatch(route_row[...] * capacity + rank_row, cot[...], [sending])


def dispatch(row, rows, parts):
    step = 512
    offset = 0
    for sending in parts:
        for first in range(0, sending.shape[0], step):
            chosen = (
                lax.broadcasted_iota(jnp.int32, (step, TOK), 0) + (first + offset) == row
            ).astype(BF)
            sending[first : first + step, :] = dot(chosen, rows).astype(BF)
        offset += sending.shape[0]


def make_slots(routes, cotangent, experts, capacity):
    total = experts * capacity
    return pl.pallas_call(
        functools.partial(slots_kernel, experts, capacity),
        out_shape=(
            jax.ShapeDtypeStruct((TOK, 1), jnp.int32),
            jax.ShapeDtypeStruct((1, TOK), jnp.int32),
            jax.ShapeDtypeStruct((total, D), BF),
        ),
        compiler_params=params(),
        cost_estimate=cost(2 * total * TOK * D, 6 * total * D),
        name="slots",
    )(routes, routes.reshape(1, TOK), cotangent)


def project_kernel(tokens, gain, left, right, normed, qkv):
    x = tokens[...].astype(F32)
    low = (x * inverse_rms(x) * gain[...]).astype(BF)
    normed[...] = low
    qkv[:, :SPLIT] = dot(low, left[...]).astype(BF)
    qkv[:, SPLIT:] = dot(low, right[:, :SPLIT]).astype(BF)


def project(tokens, gain, left, right):
    block = 256
    rows = pl.BlockSpec((block, D), lambda r: (r, 0))
    return pl.pallas_call(
        project_kernel,
        grid=(TOK // block,),
        in_specs=[rows, whole((1, D)), whole(left.shape), whole(right.shape)],
        out_specs=[rows, pl.BlockSpec((block, 3 * D), lambda r: (r, 0))],
        out_shape=[
            jax.ShapeDtypeStruct((TOK, D), BF),
            jax.ShapeDtypeStruct((TOK, 3 * D), BF),
        ],
        compiler_params=params(("arbitrary",)),
        cost_estimate=cost(6 * TOK * D * D, 12 * TOK * D),
        name="project",
    )(tokens, gain, left, right)


def lane_features(seq_col, rel_table):
    lane = jnp.arange(LANES, dtype=jnp.int32)[None, :]
    feature = lane % HEAD_DIM
    tile = jnp.arange(TOK, dtype=jnp.int32)[:, None] // TILE
    on_tile = feature - 4
    query_features = jnp.where(
        feature < 4,
        jnp.where(feature == seq_col, 0.0, UNPAIRED),
        jnp.where(on_tile == tile, 1.0, 0.0),
    ).astype(BF)
    wide = jnp.arange(D, dtype=jnp.int32)[None, :]
    feature = wide % HEAD_DIM
    on_tile = feature - 4
    swapped = jnp.arange(HEADS, dtype=jnp.int32) ^ 1
    before = jnp.repeat(rel_table[FAR_BEFORE][swapped], HEAD_DIM)[None, :]
    after = jnp.repeat(rel_table[FAR_AFTER][swapped], HEAD_DIM)[None, :]
    apart = tile - on_tile
    far = jnp.where(apart >= 2, after, jnp.where(apart <= -2, before, 0.0))
    key_features = jnp.where(
        feature < 4,
        jnp.where(feature == seq_col, 1.0, 0.0),
        jnp.where(on_tile < TILES, far, 0.0),
    ).astype(BF)
    return query_features, key_features


def band_offsets():
    place = jnp.arange(4 * LANES, dtype=jnp.int32)
    return 255 - (place + 383) % 512


def band_onehot():
    return (
        bucket_of(band_offsets())[:, None] == jnp.arange(BUCKETS, dtype=jnp.int32)[None, :]
    ).astype(F32)


def near_rows(tile):
    first = max(tile - 1, 0)
    last = min(tile + 2, TILES)
    return first, last


def spread_band(values):
    wide = jnp.broadcast_to(values, (3 * TILE, 4 * LANES))
    return pltpu.roll(wide, 0, 1, stride=1, stride_axis=0)[:, :TILE]


def attend_kernel(q_ref, k_ref, v_ref, qx_ref, kx_ref, band_ref, out_ref, lse_ref, st, pb, ot):
    low = lax.broadcasted_iota(jnp.int32, (TOK, LANES), 1) < HEAD_DIM
    v_t = v_ref[...].astype(F32).T.astype(BF)
    for side in range(2):
        own = low if side == 0 else ~low
        queries = jnp.where(own, q_ref[...], qx_ref[...])
        keys = jnp.where(own, k_ref[...], kx_ref[...])
        band = spread_band(band_ref[side])
        for block in range(TOK // QBLK):
            rows = slice(block * QBLK, (block + 1) * QBLK)
            slot = block % 2
            st[slot] = dot(keys, queries[rows], 1, 1)
            for part in range(QBLK // TILE):
                tile = block * (QBLK // TILE) + part
                first, last = near_rows(tile)
                at = (slot, slice(first * TILE, last * TILE), slice(part * TILE, (part + 1) * TILE))
                st[at] += band[(first - tile + 1) * TILE : (last - tile + 1) * TILE]
            top = jnp.max(st[slot, 0:TILE], axis=0, keepdims=True)
            for chunk in range(1, TILES):
                top = jnp.maximum(
                    top,
                    jnp.max(
                        st[slot, chunk * TILE : (chunk + 1) * TILE], axis=0, keepdims=True
                    ),
                )
            total = jnp.zeros((1, QBLK), F32)
            for chunk in range(TILES):
                at = slice(chunk * TILE, (chunk + 1) * TILE)
                raised = jnp.exp(st[slot, at] - top)
                total = total + jnp.sum(raised, axis=0, keepdims=True)
                pb[slot, at] = raised.astype(BF)
            half = slice(side * HEAD_DIM, (side + 1) * HEAD_DIM)
            ot[half, rows] = dot(v_t[half], pb[slot]) * (1.0 / total)
            lse_ref[side, :, rows] = top + jnp.log(total)
    out_ref[...] = ot[...].T.astype(BF)


def attend(qkv, query_features, key_features, band):
    pairs = HEADS // 2
    return pl.pallas_call(
        attend_kernel,
        grid=(pairs,),
        in_specs=[
            pl.BlockSpec((TOK, LANES), lambda p: (0, p)),
            pl.BlockSpec((TOK, LANES), lambda p: (0, p + pairs)),
            pl.BlockSpec((TOK, LANES), lambda p: (0, p + 2 * pairs)),
            whole((TOK, LANES)),
            pl.BlockSpec((TOK, LANES), lambda p: (0, p)),
            pl.BlockSpec((2, 1, 4 * LANES), lambda p: (p, 0, 0)),
        ],
        out_specs=[
            pl.BlockSpec((TOK, LANES), lambda p: (0, p)),
            pl.BlockSpec((2, 1, TOK), lambda p: (p, 0, 0)),
        ],
        out_shape=[
            jax.ShapeDtypeStruct((TOK, D), BF),
            jax.ShapeDtypeStruct((HEADS, 1, TOK), F32),
        ],
        scratch_shapes=[
            pltpu.VMEM((2, TOK, QBLK), F32),
            pltpu.VMEM((2, TOK, QBLK), BF),
            pltpu.VMEM((LANES, TOK), F32),
        ],
        compiler_params=params(("arbitrary",)),
        cost_estimate=cost(2 * 3 * HEADS * TOK * TOK * 256, 10 * TOK * D, HEADS * TOK * TOK),
        name="attend",
    )(qkv, qkv, qkv, query_features, key_features, band)


def attend_back_kernel(
    q_ref, k_ref, v_ref, do_ref, qx_ref, kx_ref, lse_ref, band_ref,
    dq_ref, dk_ref, dv_ref, tiles_ref, diag_ref,
    st, dp, pb, sb, dqt, dkt, dvt, near,
):
    low = lax.broadcasted_iota(jnp.int32, (TOK, LANES), 1) < HEAD_DIM
    k_t = k_ref[...].astype(F32).T.astype(BF)
    for side in range(2):
        own = low if side == 0 else ~low
        queries = jnp.where(own, q_ref[...], qx_ref[...])
        keys = jnp.where(own, k_ref[...], kx_ref[...])
        values = jnp.where(own, v_ref[...], jnp.zeros((), BF))
        band = spread_band(band_ref[side])
        near[...] = jnp.zeros_like(near)
        half = slice(side * HEAD_DIM, (side + 1) * HEAD_DIM)
        for block in range(TOK // QBLK):
            rows = slice(block * QBLK, (block + 1) * QBLK)
            slot = block % 2
            st[slot] = dot(keys, queries[rows], 1, 1)
            dp[slot] = dot(values, do_ref[rows, :], 1, 1)
            for part in range(QBLK // TILE):
                tile = block * (QBLK // TILE) + part
                first, last = near_rows(tile)
                at = (slot, slice(first * TILE, last * TILE), slice(part * TILE, (part + 1) * TILE))
                st[at] += band[(first - tile + 1) * TILE : (last - tile + 1) * TILE]
            lse = lse_ref[side, :, rows]
            spread = jnp.zeros((1, QBLK), F32)
            for chunk in range(TILES):
                at = slice(chunk * TILE, (chunk + 1) * TILE)
                weights = jnp.exp(st[slot, at] - lse)
                st[slot, at] = weights
                pb[slot, at] = weights.astype(BF)
                spread = spread + jnp.sum(weights * dp[slot, at], axis=0, keepdims=True)
            for chunk in range(TILES):
                at = slice(chunk * TILE, (chunk + 1) * TILE)
                sb[slot, at] = (st[slot, at] * (dp[slot, at] - spread)).astype(BF)
            for part in range(QBLK // TILE):
                tile = block * (QBLK // TILE) + part
                first, last = near_rows(tile)
                at = (slot, slice(first * TILE, last * TILE), slice(part * TILE, (part + 1) * TILE))
                near[(first - tile + 1) * TILE : (last - tile + 1) * TILE, :TILE] += sb[at].astype(F32)
            dv = dot(pb[slot], do_ref[rows, :])
            dk = dot(sb[slot], queries[rows])
            if block == 0:
                dvt[side] = dv
                dkt[side] = dk
            else:
                dvt[side] += dv
                dkt[side] += dk
            dqt[half, rows] = dot(k_t[half], sb[slot])
        for tile in range(TILES):
            tiles_ref[side, tile : tile + 1, :] = jnp.sum(
                dkt[side, tile * TILE : (tile + 1) * TILE], axis=0, keepdims=True
            )
        folded = near[0:8, :]
        for first in range(8, 3 * TILE, 8):
            folded = folded + pltpu.roll(near[first : first + 8, :], 4 * LANES - first, 1)
        diagonal = folded[0:1]
        for row in range(1, 8):
            diagonal = diagonal + pltpu.roll(folded[row : row + 1], 4 * LANES - row, 1)
        diag_ref[side] = diagonal
    dq_ref[...] = dqt[...].T.astype(BF)
    dk_ref[...] = jnp.where(low, dkt[0], dkt[1]).astype(BF)
    dv_ref[...] = jnp.where(low, dvt[0], dvt[1]).astype(BF)


def attend_back(qkv, grad_context, query_features, key_features, lse, band):
    pairs = HEADS // 2
    column = pl.BlockSpec((TOK, LANES), lambda p: (0, p))
    return pl.pallas_call(
        attend_back_kernel,
        grid=(pairs,),
        in_specs=[
            column,
            pl.BlockSpec((TOK, LANES), lambda p: (0, p + pairs)),
            pl.BlockSpec((TOK, LANES), lambda p: (0, p + 2 * pairs)),
            column,
            whole((TOK, LANES)),
            column,
            pl.BlockSpec((2, 1, TOK), lambda p: (p, 0, 0)),
            pl.BlockSpec((2, 1, 4 * LANES), lambda p: (p, 0, 0)),
        ],
        out_specs=[
            column,
            column,
            column,
            pl.BlockSpec((2, TILES, LANES), lambda p: (p, 0, 0)),
            pl.BlockSpec((2, 1, 4 * LANES), lambda p: (p, 0, 0)),
        ],
        out_shape=[
            jax.ShapeDtypeStruct((TOK, D), BF),
            jax.ShapeDtypeStruct((TOK, D), BF),
            jax.ShapeDtypeStruct((TOK, D), BF),
            jax.ShapeDtypeStruct((HEADS, TILES, LANES), F32),
            jax.ShapeDtypeStruct((HEADS, 1, 4 * LANES), F32),
        ],
        scratch_shapes=[
            pltpu.VMEM((2, TOK, QBLK), F32),
            pltpu.VMEM((2, TOK, QBLK), F32),
            pltpu.VMEM((2, TOK, QBLK), BF),
            pltpu.VMEM((2, TOK, QBLK), BF),
            pltpu.VMEM((LANES, TOK), F32),
            pltpu.VMEM((2, TOK, LANES), F32),
            pltpu.VMEM((2, TOK, LANES), F32),
            pltpu.VMEM((3 * TILE, 4 * LANES), F32),
        ],
        compiler_params=params(("arbitrary",)),
        cost_estimate=cost(2 * 5 * HEADS * TOK * TOK * 256, 16 * TOK * D, HEADS * TOK * TOK),
        name="attend_back",
    )(qkv, qkv, qkv, grad_context, query_features, key_features, lse, band)


def table_gradient(tiles, diagonals):
    near = jnp.einsum(
        "hl,lb->bh", diagonals[:, 0, :], band_onehot(), precision=lax.Precision.HIGHEST
    )
    sums = jnp.concatenate(
        [tiles[h : h + 1, :, (HEAD_DIM if h % 2 == 0 else 0) + 4 :][:, :, :TILES] for h in range(HEADS)],
        axis=0,
    )
    apart = (
        jnp.arange(TILES, dtype=jnp.int32)[:, None] - jnp.arange(TILES, dtype=jnp.int32)[None, :]
    )[None]
    before = jnp.sum(jnp.where(apart <= -2, sums, 0.0), axis=(1, 2))
    after = jnp.sum(jnp.where(apart >= 2, sums, 0.0), axis=(1, 2))
    place = jnp.arange(BUCKETS, dtype=jnp.int32)[:, None]
    return (
        near
        + jnp.where(place == FAR_BEFORE, before[None, :], 0.0)
        + jnp.where(place == FAR_AFTER, after[None, :], 0.0)
    )


def middle_kernel(context, tokens, w_out, gain, router, route_col, slot_row, experts,
                  middle, sending_low, sending_high, gate, normed):
    for first in range(0, TOK, 256):
        at = slice(first, first + 256)
        mid = tokens[at, :].astype(F32) + dot(context[at, :], w_out[...])
        middle[at, :] = mid
        low = (mid * inverse_rms(mid) * gain[...]).astype(BF)
        normed[at, :] = low
        probs = router_softmax(low, router[...], experts)
        lane = lax.broadcasted_iota(jnp.int32, probs.shape, 1)
        gate[at, :] = jnp.sum(
            jnp.where(lane == route_col[at, :], probs, 0.0), axis=1, keepdims=True
        )
    dispatch(slot_row[...], normed[...], [sending_low, sending_high])


def router_softmax(rows, router, experts):
    logits = dot(rows, router)
    lane = lax.broadcasted_iota(jnp.int32, logits.shape, 1)
    logits = jnp.where(lane < experts, logits, UNPAIRED)
    raised = jnp.exp(logits - jnp.max(logits, axis=1, keepdims=True))
    return raised / jnp.sum(raised, axis=1, keepdims=True)


def make_middle(context, tokens, w_out, gain, router, routes, slot_row, experts, capacity):
    total = experts * capacity

    def kernel(*refs):
        middle_kernel(*refs[:7], experts, *refs[7:])

    return pl.pallas_call(
        kernel,
        out_shape=(
            jax.ShapeDtypeStruct((TOK, D), F32),
            jax.ShapeDtypeStruct((total // 2, D), BF),
            jax.ShapeDtypeStruct((total // 2, D), BF),
            jax.ShapeDtypeStruct((TOK, 1), F32),
        ),
        scratch_shapes=[pltpu.VMEM((TOK, D), BF)],
        compiler_params=params(),
        cost_estimate=cost(2 * total * TOK * D + 2 * TOK * D * D, 12 * TOK * D + 2 * total * D),
        name="middle",
    )(context, tokens, w_out, gain, router, routes, slot_row)


def gelu_parts(v):
    size = jnp.abs(v)
    t = 1.0 / (1.0 + (0.3275911 * 0.7071067811865476) * size)
    bell = jnp.exp(-0.5 * (v * v))
    series = t * (
        0.5 * 0.254829592
        + t * (0.5 * -0.284496736 + t * (0.5 * 1.421413741 + t * (0.5 * -1.453152027 + t * (0.5 * 1.061405429))))
    )
    tail = series * bell
    phi = jnp.where(v < 0, tail, 1.0 - tail)
    return v * phi, phi + v * (bell * 0.3989422804014327)


def expert_kernel(experts, x, c3, w_first, w_second, router, router_t, mine,
                  act_ref, dh_ref, result, grad_x, gate_ref, grad_router, acc_r, acc_x):
    step = pl.program_id(0)
    rows = x.shape[0]
    chunk = 256
    per = chunk // c3.shape[1]
    for first in range(0, rows, chunk):
        at = slice(first, first + chunk)
        hidden = dot(x[at, :], w_first[...])
        cot = c3[first // chunk * per : (first // chunk + 1) * per].reshape(chunk, D)
        grad_act = dot(cot, w_second[...], 1, 1)
        act, slope = gelu_parts(hidden)
        act = act.astype(BF)
        grad_hidden = (grad_act * slope).astype(BF)
        act_ref[at, :] = act
        dh_ref[at, :] = grad_hidden
        part_r = dot(act, w_second[...])
        part_x = dot(grad_hidden, w_first[...], 1, 1)

        @pl.when(step == 0)
        def _():
            acc_r[at, :] = part_r
            acc_x[at, :] = part_x

        @pl.when(step > 0)
        def _():
            acc_r[at, :] += part_r
            acc_x[at, :] += part_x

    @pl.when(step == pl.num_programs(0) - 1)
    def _():
        total_router = jnp.zeros(grad_router.shape, F32)
        for first in range(0, rows, chunk):
            at = slice(first, first + chunk)
            rounded = acc_r[at, :].astype(BF)
            result[at, :] = rounded
            probs = router_softmax(x[at, :], router[...], experts)
            lane = lax.broadcasted_iota(jnp.int32, probs.shape, 1)
            here = lane == mine[0, 0]
            gate = jnp.sum(jnp.where(here, probs, 0.0), axis=1, keepdims=True)
            grad_gate = jnp.sum(
                c3[first // chunk * per : (first // chunk + 1) * per].reshape(chunk, D).astype(F32) * rounded.astype(F32), axis=1, keepdims=True
            )
            grad_logits = (
                probs * (jnp.where(here, grad_gate, 0.0) - gate * grad_gate)
            ).astype(BF)
            gate_ref[at, :] = gate
            grad_x[at, :] = (acc_x[at, :] * gate + dot(grad_logits, router_t[...])).astype(BF)
            total_router = total_router + dot(x[at, :], grad_logits, 0, 0)
        grad_router[...] = total_router


def run_expert(part, x, c, w_first, w_second, router, router_t, mine, experts):
    rows = x.shape[0]
    hidden_size = w_first.shape[1]
    lanes = router.shape[1]
    return pl.pallas_call(
        functools.partial(expert_kernel, experts),
        grid=(hidden_size // FF_TILE,),
        in_specs=[
            whole((rows, D)),
            pl.BlockSpec((c.shape[0], c.shape[1] // HALVES, D), lambda f: (0, part, 0)),
            pl.BlockSpec((D, FF_TILE), lambda f: (0, f)),
            pl.BlockSpec((FF_TILE, D), lambda f: (f, 0)),
            whole((D, lanes)),
            whole((lanes, D)),
            pl.BlockSpec(memory_space=pltpu.SMEM),
        ],
        out_specs=[
            pl.BlockSpec((rows, FF_TILE), lambda f: (0, f)),
            pl.BlockSpec((rows, FF_TILE), lambda f: (0, f)),
            whole((rows, D)),
            whole((rows, D)),
            whole((rows, 1)),
            whole((D, lanes)),
        ],
        out_shape=[
            jax.ShapeDtypeStruct((rows, hidden_size), BF),
            jax.ShapeDtypeStruct((rows, hidden_size), BF),
            jax.ShapeDtypeStruct((rows, D), BF),
            jax.ShapeDtypeStruct((rows, D), BF),
            jax.ShapeDtypeStruct((rows, 1), F32),
            jax.ShapeDtypeStruct((D, lanes), F32),
        ],
        scratch_shapes=[pltpu.VMEM((rows, D), F32), pltpu.VMEM((rows, D), F32)],
        compiler_params=params(("arbitrary",)),
        cost_estimate=cost(
            8 * rows * D * hidden_size, 4 * rows * hidden_size + 4 * D * hidden_size
        ),
        name="expert",
    )(x, c, w_first, w_second, router, router_t, mine)


def expert_weights_kernel(parts, *refs):
    xs, gates = refs[:parts], refs[parts : 2 * parts]
    acts, dhs = refs[2 * parts : 3 * parts], refs[3 * parts : 4 * parts]
    cots, grad_first, grad_second, x_t, c_t = refs[4 * parts :]
    rows = xs[0].shape[0]
    share = cots.shape[1] // parts
    chunk = 256
    per = chunk // share

    @pl.when(pl.program_id(0) == 0)
    def _():
        for part in range(parts):
            for first in range(0, rows, chunk):
                at = slice(first, first + chunk)
                to = slice(part * rows + first, part * rows + first + chunk)
                gate = gates[part][at, :]
                x_t[:, to] = (xs[part][at, :].astype(F32) * gate).T.astype(BF)
                cot = cots[
                    first // chunk * per : (first // chunk + 1) * per,
                    part * share : (part + 1) * share,
                ].reshape(chunk, D)
                c_t[:, to] = (cot.astype(F32) * gate).T.astype(BF)

    first_sum, second_sum = None, None
    for part in range(parts):
        at = slice(part * rows, (part + 1) * rows)
        one = dot(x_t[:, at], dhs[part][...])
        two = dot(c_t[:, at], acts[part][...])
        first_sum = one if first_sum is None else first_sum + one
        second_sum = two if second_sum is None else second_sum + two
    grad_first[...] = first_sum.astype(BF)
    grad_second[...] = second_sum.T.astype(BF)


def expert_weights(xs, cots, gates, acts, dhs):
    parts = len(xs)
    rows = xs[0].shape[0]
    hidden_size = acts[0].shape[1]
    tile = pl.BlockSpec((rows, FF_TILE), lambda f: (0, f))
    return pl.pallas_call(
        functools.partial(expert_weights_kernel, parts),
        grid=(hidden_size // FF_TILE,),
        in_specs=[whole((rows, D))] * parts
        + [whole((rows, 1))] * parts
        + [tile] * (2 * parts)
        + [whole(cots.shape)],
        out_specs=[
            pl.BlockSpec((D, FF_TILE), lambda f: (0, f)),
            pl.BlockSpec((FF_TILE, D), lambda f: (f, 0)),
        ],
        out_shape=[
            jax.ShapeDtypeStruct((D, hidden_size), BF),
            jax.ShapeDtypeStruct((hidden_size, D), BF),
        ],
        scratch_shapes=[
            pltpu.VMEM((D, parts * rows), BF),
            pltpu.VMEM((D, parts * rows), BF),
        ],
        compiler_params=params(("arbitrary",)),
        cost_estimate=cost(
            4 * parts * rows * D * hidden_size, 4 * (parts * rows + D) * hidden_size
        ),
        name="expert_weights",
    )(*xs, *gates, *acts, *dhs, cots)


def rms_back(values, factor, grad):
    inverse = inverse_rms(values)
    scaled = grad * factor
    mean = jnp.mean(scaled * values, axis=-1, keepdims=True)
    return (
        inverse * scaled - values * (inverse * inverse * inverse * mean),
        jnp.sum(grad * values * inverse, axis=0, keepdims=True),
    )


def undispatch(slot_col, parts):
    out = None
    offset = 0
    for part in parts:
        total = part.shape[0]
        place = lax.broadcasted_iota(jnp.int32, (slot_col.shape[0], total), 1) + offset
        found = dot((place == slot_col).astype(BF), part[...])
        out = found if out is None else out + found
        offset += total
    return out


def middle_back_kernel(parts, *refs):
    backs = refs[:parts]
    slot_col, middle, cot, gain, w_out, grad_middle, grad_attn, grad_context, grad_gain = refs[parts:]
    grad_normed = undispatch(slot_col[...], backs)
    part, gain_part = rms_back(middle[...], gain[...], grad_normed)
    grad = cot[...].astype(F32) + part
    grad_middle[...] = grad
    low = grad.astype(BF)
    grad_attn[...] = low
    grad_context[...] = dot(low, w_out[...], 1, 1).astype(BF)

    @pl.when(pl.program_id(0) == 0)
    def _():
        grad_gain[...] = gain_part

    @pl.when(pl.program_id(0) > 0)
    def _():
        grad_gain[...] += gain_part


def middle_back(backs, slot_col, middle, cot, gain, w_out):
    parts = len(backs)
    block = 256
    rows = pl.BlockSpec((block, D), lambda r: (r, 0))
    return pl.pallas_call(
        functools.partial(middle_back_kernel, parts),
        grid=(TOK // block,),
        in_specs=[whole(back.shape) for back in backs]
        + [
            pl.BlockSpec((block, 1), lambda r: (r, 0)),
            rows,
            rows,
            whole((1, D)),
            whole((D, D)),
        ],
        out_specs=[rows, rows, rows, whole((1, D))],
        out_shape=[
            jax.ShapeDtypeStruct((TOK, D), F32),
            jax.ShapeDtypeStruct((TOK, D), BF),
            jax.ShapeDtypeStruct((TOK, D), BF),
            jax.ShapeDtypeStruct((1, D), F32),
        ],
        compiler_params=params(("arbitrary",)),
        cost_estimate=cost(2 * 2 * TOK * TOK * D + 2 * TOK * D * D, 16 * TOK * D),
        name="middle_back",
    )(*backs, slot_col, middle, cot, gain, w_out)


def mix_kernel(parts, *refs):
    backs = refs[:parts]
    slot_col, middle, gate, mixed = refs[parts:]
    mixed[...] = middle[...] + gate[...] * undispatch(slot_col[...], backs)


def mix(backs, slot_col, middle, gate):
    parts = len(backs)
    block = 256
    rows = pl.BlockSpec((block, D), lambda r: (r, 0))
    column = pl.BlockSpec((block, 1), lambda r: (r, 0))
    return pl.pallas_call(
        functools.partial(mix_kernel, parts),
        grid=(TOK // block,),
        in_specs=[whole(back.shape) for back in backs] + [column, rows, column],
        out_specs=rows,
        out_shape=jax.ShapeDtypeStruct((TOK, D), F32),
        compiler_params=params(("arbitrary",)),
        cost_estimate=cost(2 * 2 * TOK * TOK * D, 12 * TOK * D),
        name="mix",
    )(*backs, slot_col, middle, gate)


def tokens_back_kernel(gq, gk, gv, left, right, tokens, gain, grad_middle, grad_tokens, grad_gain):
    cut = SPLIT - D
    grad_normed = (
        dot(gq[...], left[:, :D], 1, 1)
        + dot(gk[:, :cut], left[:, D:], 1, 1)
        + dot(gk[:, cut:], right[:, : D - cut], 1, 1)
        + dot(gv[...], right[:, D - cut : SPLIT], 1, 1)
    )
    part, gain_part = rms_back(tokens[...].astype(F32), gain[...], grad_normed)
    grad_tokens[...] = grad_middle[...] + part

    @pl.when(pl.program_id(0) == 0)
    def _():
        grad_gain[...] = gain_part

    @pl.when(pl.program_id(0) > 0)
    def _():
        grad_gain[...] += gain_part


def tokens_back(gq, gk, gv, left, right, tokens, gain, grad_middle):
    block = 256
    rows = pl.BlockSpec((block, D), lambda r: (r, 0))
    return pl.pallas_call(
        tokens_back_kernel,
        grid=(TOK // block,),
        in_specs=[rows, rows, rows, whole(left.shape), whole(right.shape), rows, whole((1, D)), rows],
        out_specs=[rows, whole((1, D))],
        out_shape=[
            jax.ShapeDtypeStruct((TOK, D), F32),
            jax.ShapeDtypeStruct((1, D), F32),
        ],
        compiler_params=params(("arbitrary",)),
        cost_estimate=cost(6 * TOK * D * D, 16 * TOK * D),
        name="tokens_back",
    )(gq, gk, gv, left, right, tokens, gain, grad_middle)


def weights_back_kernel(normed, gq, gk, gv, left, right):
    cut = SPLIT - D
    turned = normed[...].astype(F32).T.astype(BF)
    left[:, :D] = dot(turned, gq[...])
    left[:, D:] = dot(turned, gk[:, :cut])
    right[:, : D - cut] = dot(turned, gk[:, cut:])
    right[:, D - cut :] = dot(turned, gv[...])


def weights_back(normed, gq, gk, gv):
    return pl.pallas_call(
        weights_back_kernel,
        out_shape=(
            jax.ShapeDtypeStruct((D, SPLIT), F32),
            jax.ShapeDtypeStruct((D, SPLIT), F32),
        ),
        compiler_params=params(),
        cost_estimate=cost(6 * TOK * D * D, 8 * TOK * D + 12 * D * D),
        name="weights_back",
    )(normed, gq, gk, gv)


def swap(block, axis, bit):
    size = lax.axis_size(axis)
    return lax.ppermute(block, axis, [(place, place ^ bit) for place in range(size)])


def on_upper(axis, bit):
    return (lax.axis_index(axis) // bit) % 2 == 1


def axis_bits(*axes):
    found = []
    for axis in axes:
        bit = lax.axis_size(axis) // 2
        while bit >= 1:
            found.append((axis, bit))
            bit //= 2
    return found


def orders():
    bits = axis_bits("dp", "expert")
    dp = [at for at, (axis, _) in enumerate(bits) if axis == "dp"]
    core = len(bits) - 1
    along = [at for at, (axis, bit) in enumerate(bits) if axis == "expert" and bit == 2]
    rest = [at for at in range(core) if at not in dp and at not in along]
    return (rest + along + dp + [core], rest + dp + along + [core])


def gather_rows(shard, order):
    bits = axis_bits("dp", "expert")
    block = shard.reshape((1,) * len(bits) + shard.shape)
    for place in order:
        axis, bit = bits[place]
        other = swap(block, axis, bit)
        upper = on_upper(axis, bit)
        block = jnp.concatenate(
            [jnp.where(upper, other, block), jnp.where(upper, block, other)], axis=place
        )
    return block.reshape((-1,) + shard.shape[1:])


def scatter_sum(total, order):
    bits = axis_bits("dp", "expert")
    rows = total.shape[0] >> len(bits)
    block = total.reshape((2,) * len(bits) + (rows,) + total.shape[1:])
    for place in reversed(order):
        axis, bit = bits[place]
        lower = lax.slice_in_dim(block, 0, 1, axis=place)
        higher = lax.slice_in_dim(block, 1, 2, axis=place)
        upper = on_upper(axis, bit)
        sent = jnp.where(upper, lower, higher).astype(BF)
        block = jnp.where(upper, higher, lower) + swap(sent, axis, bit).astype(F32)
    return block.reshape(block.shape[len(bits) :])


def sum_all(total):
    for axis, bit in axis_bits("dp", "expert"):
        total = total + swap(total, axis, bit)
    return total


def gather_dp(block, axis):
    if lax.axis_size("dp") != 2:
        return lax.all_gather(block, "dp", axis=axis, tiled=True)
    other = swap(block, "dp", 1)
    upper = on_upper("dp", 1)
    return jnp.concatenate(
        [jnp.where(upper, other, block), jnp.where(upper, block, other)], axis=axis
    )


def scatter_dp(total):
    if lax.axis_size("dp") != 2:
        return lax.psum_scatter(
            total[None], "dp", scatter_dimension=1, tiled=True
        ).astype(F32)
    half = total.shape[0] // 2
    upper = on_upper("dp", 1)
    sent = jnp.where(upper, total[:half], total[half:])
    kept = jnp.where(upper, total[half:], total[:half])
    return (kept.astype(F32) + swap(sent, "dp", 1).astype(F32))[None]


def after(value, *others):
    return lax.optimization_barrier((value, *others))[0]


def body(
    tokens, seq_ids, routes, cotangent, w_query, w_key, w_value, w_out,
    rel_table, gain_attn, gain_ffn, router, expert_in, expert_out,
):
    experts = lax.axis_size("expert")
    capacity = 2 * TOK // experts
    shard = w_query.shape[0]
    lanes = -(-(experts + 2) // LANES) * LANES
    everyone = ("dp", "expert")

    small = jnp.concatenate(
        [
            router,
            gain_attn[:, None],
            gain_ffn[:, None],
            jnp.zeros((shard, lanes - experts - 2), BF),
        ],
        axis=1,
    )
    cut = SPLIT - D
    first, second = orders()
    left = gather_rows(jnp.concatenate([w_query, w_key[:, :cut]], axis=1), first)
    right = gather_rows(jnp.concatenate([w_key[:, cut:], w_value, small], axis=1), second)
    full_out = lax.all_gather(w_out, everyone, axis=0, tiled=True)
    table = gather_dp(rel_table, 0).astype(F32)
    w_first = gather_dp(after(expert_in, left, right), 1)[0]
    w_second = lax.all_gather(after(expert_out, full_out), "dp", axis=1, tiled=True)[0]

    slot_col, slot_row, sending_cot = make_slots(routes, cotangent, experts, capacity)

    def exchange(rows):
        return lax.all_to_all(
            rows.reshape(experts, -1, D), "expert", split_axis=0, concat_axis=0, tiled=True
        )

    cots = exchange(after(sending_cot, left, right))

    extra = right[:, SPLIT:]
    full_router = jnp.where(jnp.arange(lanes)[None, :] < experts, extra, jnp.zeros((), BF))
    router_t = full_router.T
    attn_gain = extra[:, experts].astype(F32).reshape(1, D)
    ffn_gain = extra[:, experts + 1].astype(F32).reshape(1, D)

    normed, qkv = project(tokens, attn_gain, left, right)
    query_features, key_features = lane_features(seq_ids.reshape(TOK, 1), table)
    band = jnp.sum(band_onehot()[None, :, :] * table.T[:, None, :], axis=2)[:, None, :]
    context, lse = attend(qkv, query_features, key_features, band)

    middle, *sending, gate = make_middle(
        context, tokens, full_out, ffn_gain, full_router, routes, slot_row, experts, capacity
    )
    rows_in = [exchange(part).reshape(-1, D) for part in sending]
    mine = lax.axis_index("expert").astype(jnp.int32).reshape(1, 1)
    acts, dhs, results, grads, gates, router_parts = zip(
        *(
            run_expert(
                part, rows, cots, w_first, w_second, full_router, router_t, mine, experts
            )
            for part, rows in enumerate(rows_in)
        )
    )
    grads_home = [exchange(part).reshape(-1, D) for part in grads]
    grad_first, grad_second = expert_weights(rows_in, cots, gates, acts, dhs)
    results_home = [
        exchange(after(part, *grads_home)).reshape(-1, D) for part in results
    ]
    grads_home[0] = after(grads_home[0], grad_first, grad_second)
    grad_expert_in = scatter_dp(grad_first)
    grad_expert_out = scatter_dp(grad_second)

    grad_middle, grad_attn, grad_context, grad_gain_f = middle_back(
        grads_home, slot_col, middle, cotangent, ffn_gain, full_out
    )
    grad_w_out = lax.psum_scatter(
        dot(context, grad_attn, 0, 0), everyone, scatter_dimension=0, tiled=True
    )
    gq, gk, gv, tiles, diagonals = attend_back(
        qkv, grad_context, query_features, key_features, lse, band
    )
    grad_left, grad_right = weights_back(normed, gq, gk, gv)
    grad_tokens, grad_gain_a = tokens_back(
        after(gq, grad_left, grad_right), gk, gv, left, right, tokens, attn_gain, grad_middle
    )
    grad_left = scatter_sum(grad_left, first)
    grad_right = scatter_sum(grad_right, second)
    mixed = mix(results_home, slot_col, middle, gate)
    grad_router = sum(router_parts)[:, :experts]
    grad_table = table_gradient(tiles, diagonals)

    sizes = (D * experts, D, D, BUCKETS * HEADS)
    sums = sum_all(
        jnp.concatenate(
            [
                part.reshape(-1, LANES)
                for part in (grad_router, grad_gain_a, grad_gain_f, grad_table)
            ],
            axis=0,
        )
    ).reshape(-1)
    ends = [sum(sizes[: at + 1]) for at in range(len(sizes))]
    grad_router, grad_gain_a, grad_gain_f, grad_table = (
        sums[end - size : end] for end, size in zip(ends, sizes)
    )
    number = lax.axis_index("dp") * experts + lax.axis_index("expert")
    table_height = BUCKETS // lax.axis_size("dp")

    def own(rows, height, place):
        return lax.dynamic_slice_in_dim(rows, place * height, height, 0)

    return (
        mixed,
        grad_tokens,
        grad_left[:, :D],
        jnp.concatenate([grad_left[:, D:], grad_right[:, : D - cut]], axis=1),
        grad_right[:, D - cut :],
        grad_w_out,
        own(grad_table.reshape(BUCKETS, HEADS), table_height, lax.axis_index("dp")),
        own(grad_gain_a, shard, number),
        own(grad_gain_f, shard, number),
        own(grad_router.reshape(D, experts), shard, number),
        grad_expert_in,
        grad_expert_out,
    )


def solution(mesh):
    rows = P(("dp", "expert"), None)
    flat = P(("dp", "expert"))
    expert = P("expert", "dp", None)
    return jax.shard_map(
        body,
        mesh=mesh,
        in_specs=(
            rows, flat, rows, rows, rows, rows, rows, rows,
            P("dp", None), flat, flat, rows, expert, expert,
        ),
        out_specs=(
            rows, rows, rows, rows, rows, rows,
            P("dp", None), flat, flat, rows, expert, expert,
        ),
        check_vma=False,
    )
```

```python
import functools

import jax
import jax.numpy as jnp
from jax import lax
from jax.experimental import pallas as pl
from jax.experimental.pallas import tpu as pltpu
from jax.sharding import PartitionSpec as P

D = 768
HEADS = 12
HEAD_DIM = 64
BUCKETS = 32
TOK = 1024
TILE = 128
TILES = TOK // TILE
QBLK = 256
FF_TILE = 512
HALVES = 2
SIDE = D // 2
SPLIT = 3 * SIDE
PAIRS = HEADS // 2
SIDE_PAIRS = PAIRS // 2
COST_SHARE = 0.05
LANES = 128

EPSILON = 1e-06
DISTANCE_EDGES = (12, 16, 23, 32, 46, 64, 91)
FAR_BEFORE = 15
FAR_AFTER = 31
UNPAIRED = -1e30
BF = jnp.bfloat16
F32 = jnp.float32
VMEM_LIMIT = 56 * 1024 * 1024


def dot(left, right, left_dim=1, right_dim=0):
    return lax.dot_general(
        left, right, (((left_dim,), (right_dim,)), ((), ())), preferred_element_type=F32
    )


def params(semantics=None):
    return pltpu.CompilerParams(vmem_limit_bytes=VMEM_LIMIT, dimension_semantics=semantics)


def cost(flops, bytes_accessed, transcendentals=0, share=COST_SHARE):
    return pl.CostEstimate(
        flops=int(flops * share),
        bytes_accessed=int(bytes_accessed * share),
        transcendentals=int(transcendentals * share),
    )


def whole(shape):
    return pl.BlockSpec(shape, lambda *_: (0,) * len(shape))


def inverse_rms(values):
    return lax.rsqrt(jnp.mean(values * values, axis=-1, keepdims=True) + EPSILON)


def bucket_of(offset):
    distance = jnp.abs(offset)
    distant = 8 + sum(((distance >= boundary).astype(jnp.int32) for boundary in DISTANCE_EDGES))
    return jnp.where(distance < 8, distance, distant) + jnp.where(offset > 0, 16, 0)


def place_in_buffers(route, rank, experts, capacity):
    share = capacity // HALVES
    part = (rank >= share).astype(jnp.int32)
    return part * (experts * share) + route * share + (rank - part * share)


def slots_kernel(experts, capacity, route_col, route_row, cot, slot_col, slot_row, sending):
    padded = -(-experts // LANES) * LANES
    picked = (
        lax.broadcasted_iota(jnp.int32, (TOK, padded), 1) == route_col[...]
    ).astype(BF)
    picked_t = (
        lax.broadcasted_iota(jnp.int32, (padded, TOK), 0) == route_row[...]
    ).astype(BF)
    upto = (
        lax.broadcasted_iota(jnp.int32, (TOK, TOK), 0)
        <= lax.broadcasted_iota(jnp.int32, (TOK, TOK), 1)
    ).astype(BF)
    from_t = (
        lax.broadcasted_iota(jnp.int32, (TOK, TOK), 0)
        >= lax.broadcasted_iota(jnp.int32, (TOK, TOK), 1)
    ).astype(BF)
    counts = dot(from_t, picked) * picked.astype(F32)
    rank = jnp.sum(counts, axis=1, keepdims=True).astype(jnp.int32) - 1
    slot_col[...] = place_in_buffers(route_col[...], rank, experts, capacity)
    counts_t = dot(picked_t, upto) * picked_t.astype(F32)
    rank_row = jnp.sum(counts_t, axis=0, keepdims=True).astype(jnp.int32) - 1
    slot_row[...] = place_in_buffers(route_row[...], rank_row, experts, capacity)
    dispatch(route_row[...] * capacity + rank_row, cot[...], [sending])


def dispatch(row, rows, parts):
    step = 512
    offset = 0
    for sending in parts:
        for first in range(0, sending.shape[0], step):
            chosen = (
                lax.broadcasted_iota(jnp.int32, (step, TOK), 0) + (first + offset) == row
            ).astype(BF)
            sending[first : first + step, :] = dot(chosen, rows).astype(BF)
        offset += sending.shape[0]


def make_slots(routes, cotangent, experts, capacity):
    total = experts * capacity
    return pl.pallas_call(
        functools.partial(slots_kernel, experts, capacity),
        out_shape=(
            jax.ShapeDtypeStruct((TOK, 1), jnp.int32),
            jax.ShapeDtypeStruct((1, TOK), jnp.int32),
            jax.ShapeDtypeStruct((total, D), BF),
        ),
        compiler_params=params(),
        cost_estimate=cost(2 * total * TOK * D, 6 * total * D),
        name="slots",
    )(routes, routes.reshape(1, TOK), cotangent)


def project_kernel(tokens, gain, left, right, turned, qkv):
    x = tokens[...].astype(F32)
    wide = x * inverse_rms(x) * gain[...]
    low = wide.astype(BF)
    turned[...] = wide.T.astype(BF)
    qkv[:, :SPLIT] = dot(low, left[...]).astype(BF)
    qkv[:, SPLIT:] = dot(low, right[:, :SPLIT]).astype(BF)


def project(tokens, gain, left, right):
    block = 256
    rows = pl.BlockSpec((block, D), lambda r: (r, 0))
    return pl.pallas_call(
        project_kernel,
        grid=(TOK // block,),
        in_specs=[rows, whole((1, D)), whole(left.shape), whole(right.shape)],
        out_specs=[
            pl.BlockSpec((D, block), lambda r: (0, r)),
            pl.BlockSpec((block, 3 * D), lambda r: (r, 0)),
        ],
        out_shape=[
            jax.ShapeDtypeStruct((D, TOK), BF),
            jax.ShapeDtypeStruct((TOK, 3 * D), BF),
        ],
        compiler_params=params(("arbitrary",)),
        cost_estimate=cost(6 * TOK * D * D, 12 * TOK * D),
        name="project",
    )(tokens, gain, left, right)


def lane_features(seq_col, rel_table):
    lane = jnp.arange(LANES, dtype=jnp.int32)[None, :]
    feature = lane % HEAD_DIM
    tile = jnp.arange(TOK, dtype=jnp.int32)[:, None] // TILE
    on_tile = feature - 4
    query_features = jnp.where(
        feature < 4,
        jnp.where(feature == seq_col, 0.0, UNPAIRED),
        jnp.where(on_tile == tile, 1.0, 0.0),
    ).astype(BF)
    wide = jnp.arange(D, dtype=jnp.int32)[None, :]
    feature = wide % HEAD_DIM
    on_tile = feature - 4
    swapped = jnp.arange(HEADS, dtype=jnp.int32) ^ 1
    before = jnp.repeat(rel_table[FAR_BEFORE][swapped], HEAD_DIM)[None, :]
    after = jnp.repeat(rel_table[FAR_AFTER][swapped], HEAD_DIM)[None, :]
    apart = tile - on_tile
    far = jnp.where(apart >= 2, after, jnp.where(apart <= -2, before, 0.0))
    key_features = jnp.where(
        feature < 4,
        jnp.where(feature == seq_col, 1.0, 0.0),
        jnp.where(on_tile < TILES, far, 0.0),
    ).astype(BF)
    return query_features, key_features


def band_offsets():
    place = jnp.arange(4 * LANES, dtype=jnp.int32)
    return 255 - (place + 383) % 512


def band_onehot():
    return (
        bucket_of(band_offsets())[:, None] == jnp.arange(BUCKETS, dtype=jnp.int32)[None, :]
    ).astype(F32)


def near_rows(tile):
    first = max(tile - 1, 0)
    last = min(tile + 2, TILES)
    return first, last


def spread_band(values):
    wide = jnp.broadcast_to(values, (3 * TILE, 4 * LANES))
    return pltpu.roll(wide, 0, 1, stride=1, stride_axis=0)[:, :TILE]


def attend_kernel(q_ref, k_ref, v_ref, qx_ref, kx_ref, band_ref, out_ref, lse_ref, st, pb, ot):
    low = lax.broadcasted_iota(jnp.int32, (TOK, LANES), 1) < HEAD_DIM
    v_t = v_ref[...].astype(F32).T.astype(BF)
    for side in range(2):
        own = low if side == 0 else ~low
        queries = jnp.where(own, q_ref[...], qx_ref[...])
        keys = jnp.where(own, k_ref[...], kx_ref[...])
        band = spread_band(band_ref[side])
        for block in range(TOK // QBLK):
            rows = slice(block * QBLK, (block + 1) * QBLK)
            slot = block % 2
            st[slot] = dot(keys, queries[rows], 1, 1)
            for part in range(QBLK // TILE):
                tile = block * (QBLK // TILE) + part
                first, last = near_rows(tile)
                at = (slot, slice(first * TILE, last * TILE), slice(part * TILE, (part + 1) * TILE))
                st[at] += band[(first - tile + 1) * TILE : (last - tile + 1) * TILE]
            top = jnp.max(st[slot, 0:TILE], axis=0, keepdims=True)
            for chunk in range(1, TILES):
                top = jnp.maximum(
                    top,
                    jnp.max(
                        st[slot, chunk * TILE : (chunk + 1) * TILE], axis=0, keepdims=True
                    ),
                )
            total = jnp.zeros((1, QBLK), F32)
            for chunk in range(TILES):
                at = slice(chunk * TILE, (chunk + 1) * TILE)
                raised = jnp.exp(st[slot, at] - top)
                total = total + jnp.sum(raised, axis=0, keepdims=True)
                pb[slot, at] = raised.astype(BF)
            half = slice(side * HEAD_DIM, (side + 1) * HEAD_DIM)
            ot[half, rows] = dot(v_t[half], pb[slot]) * (1.0 / total)
            lse_ref[side, :, rows] = top + jnp.log(total)
    out_ref[...] = ot[...].T.astype(BF)


def attend(qkv, query_features, key_features, band):
    return pl.pallas_call(
        attend_kernel,
        grid=(PAIRS,),
        in_specs=[
            *(
                pl.BlockSpec(
                    (TOK, LANES),
                    lambda p, kind=kind: (
                        0,
                        p // SIDE_PAIRS * (3 * SIDE_PAIRS) + kind * SIDE_PAIRS + p % SIDE_PAIRS,
                    ),
                )
                for kind in range(3)
            ),
            whole((TOK, LANES)),
            pl.BlockSpec((TOK, LANES), lambda p: (0, p)),
            pl.BlockSpec((2, 1, 4 * LANES), lambda p: (p, 0, 0)),
        ],
        out_specs=[
            pl.BlockSpec((TOK, LANES), lambda p: (0, p)),
            pl.BlockSpec((2, 1, TOK), lambda p: (p, 0, 0)),
        ],
        out_shape=[
            jax.ShapeDtypeStruct((TOK, D), BF),
            jax.ShapeDtypeStruct((HEADS, 1, TOK), F32),
        ],
        scratch_shapes=[
            pltpu.VMEM((2, TOK, QBLK), F32),
            pltpu.VMEM((2, TOK, QBLK), BF),
            pltpu.VMEM((LANES, TOK), F32),
        ],
        compiler_params=params(("arbitrary",)),
        cost_estimate=cost(2 * 3 * HEADS * TOK * TOK * 256, 10 * TOK * D, HEADS * TOK * TOK),
        name="attend",
    )(qkv, qkv, qkv, query_features, key_features, band)


def attend_back_kernel(
    q_ref, k_ref, v_ref, do_ref, qx_ref, kx_ref, lse_ref, band_ref,
    grad_ref, tiles_ref, diag_ref,
    st, dp, pb, sb, dqt, dkt, dvt, near,
):
    low = lax.broadcasted_iota(jnp.int32, (TOK, LANES), 1) < HEAD_DIM
    k_t = k_ref[...].astype(F32).T.astype(BF)
    for side in range(2):
        own = low if side == 0 else ~low
        queries = jnp.where(own, q_ref[...], qx_ref[...])
        keys = jnp.where(own, k_ref[...], kx_ref[...])
        values = jnp.where(own, v_ref[...], jnp.zeros((), BF))
        band = spread_band(band_ref[side])
        near[...] = jnp.zeros_like(near)
        half = slice(side * HEAD_DIM, (side + 1) * HEAD_DIM)
        for block in range(TOK // QBLK):
            rows = slice(block * QBLK, (block + 1) * QBLK)
            slot = block % 2
            st[slot] = dot(keys, queries[rows], 1, 1)
            dp[slot] = dot(values, do_ref[rows, :], 1, 1)
            for part in range(QBLK // TILE):
                tile = block * (QBLK // TILE) + part
                first, last = near_rows(tile)
                at = (slot, slice(first * TILE, last * TILE), slice(part * TILE, (part + 1) * TILE))
                st[at] += band[(first - tile + 1) * TILE : (last - tile + 1) * TILE]
            lse = lse_ref[side, :, rows]
            spread = jnp.zeros((1, QBLK), F32)
            for chunk in range(TILES):
                at = slice(chunk * TILE, (chunk + 1) * TILE)
                weights = jnp.exp(st[slot, at] - lse)
                st[slot, at] = weights
                pb[slot, at] = weights.astype(BF)
                spread = spread + jnp.sum(weights * dp[slot, at], axis=0, keepdims=True)
            for chunk in range(TILES):
                at = slice(chunk * TILE, (chunk + 1) * TILE)
                sb[slot, at] = (st[slot, at] * (dp[slot, at] - spread)).astype(BF)
            for part in range(QBLK // TILE):
                tile = block * (QBLK // TILE) + part
                first, last = near_rows(tile)
                at = (slot, slice(first * TILE, last * TILE), slice(part * TILE, (part + 1) * TILE))
                near[(first - tile + 1) * TILE : (last - tile + 1) * TILE, :TILE] += sb[at].astype(F32)
            dv = dot(pb[slot], do_ref[rows, :])
            dk = dot(sb[slot], queries[rows])
            if block == 0:
                dvt[side] = dv
                dkt[side] = dk
            else:
                dvt[side] += dv
                dkt[side] += dk
            dqt[half, rows] = dot(k_t[half], sb[slot])
        for tile in range(TILES):
            tiles_ref[side, tile : tile + 1, :] = jnp.sum(
                dkt[side, tile * TILE : (tile + 1) * TILE], axis=0, keepdims=True
            )
        folded = near[0:8, :]
        for first in range(8, 3 * TILE, 8):
            folded = folded + pltpu.roll(near[first : first + 8, :], 4 * LANES - first, 1)
        diagonal = folded[0:1]
        for row in range(1, 8):
            diagonal = diagonal + pltpu.roll(folded[row : row + 1], 4 * LANES - row, 1)
        diag_ref[side] = diagonal
    found = (
        dqt[...].T.astype(BF),
        jnp.where(low, dkt[0], dkt[1]).astype(BF),
        jnp.where(low, dvt[0], dvt[1]).astype(BF),
    )
    for pair in range(SIDE_PAIRS):

        @pl.when(pl.program_id(0) == pair)
        def _():
            for kind in range(3):
                first = kind * SIDE + pair * LANES
                grad_ref[:, first : first + LANES] = found[kind]


def attend_back(half, qkv, grad_context, query_features, key_features, lse, band):
    first = half * SIDE_PAIRS
    column = pl.BlockSpec((TOK, LANES), lambda p: (0, first + p))
    return pl.pallas_call(
        attend_back_kernel,
        grid=(SIDE_PAIRS,),
        in_specs=[
            *(
                pl.BlockSpec(
                    (TOK, LANES), lambda p, kind=kind: (0, (3 * half + kind) * SIDE_PAIRS + p)
                )
                for kind in range(3)
            ),
            column,
            whole((TOK, LANES)),
            column,
            pl.BlockSpec((2, 1, TOK), lambda p: (first + p, 0, 0)),
            pl.BlockSpec((2, 1, 4 * LANES), lambda p: (first + p, 0, 0)),
        ],
        out_specs=[
            whole((TOK, SPLIT)),
            pl.BlockSpec((2, TILES, LANES), lambda p: (p, 0, 0)),
            pl.BlockSpec((2, 1, 4 * LANES), lambda p: (p, 0, 0)),
        ],
        out_shape=[
            jax.ShapeDtypeStruct((TOK, SPLIT), BF),
            jax.ShapeDtypeStruct((HEADS // 2, TILES, LANES), F32),
            jax.ShapeDtypeStruct((HEADS // 2, 1, 4 * LANES), F32),
        ],
        scratch_shapes=[
            pltpu.VMEM((2, TOK, QBLK), F32),
            pltpu.VMEM((2, TOK, QBLK), F32),
            pltpu.VMEM((2, TOK, QBLK), BF),
            pltpu.VMEM((2, TOK, QBLK), BF),
            pltpu.VMEM((LANES, TOK), F32),
            pltpu.VMEM((2, TOK, LANES), F32),
            pltpu.VMEM((2, TOK, LANES), F32),
            pltpu.VMEM((3 * TILE, 4 * LANES), F32),
        ],
        compiler_params=params(("arbitrary",)),
        cost_estimate=cost(5 * HEADS * TOK * TOK * 256, 8 * TOK * D, HEADS * TOK * TOK // 2, share=1),
        name="attend_back",
    )(qkv, qkv, qkv, grad_context, query_features, key_features, lse, band)


def table_gradient(tiles, diagonals):
    near = jnp.einsum(
        "hl,lb->bh", diagonals[:, 0, :], band_onehot(), precision=lax.Precision.HIGHEST
    )
    sums = jnp.concatenate(
        [tiles[h : h + 1, :, (HEAD_DIM if h % 2 == 0 else 0) + 4 :][:, :, :TILES] for h in range(HEADS)],
        axis=0,
    )
    apart = (
        jnp.arange(TILES, dtype=jnp.int32)[:, None] - jnp.arange(TILES, dtype=jnp.int32)[None, :]
    )[None]
    before = jnp.sum(jnp.where(apart <= -2, sums, 0.0), axis=(1, 2))
    after = jnp.sum(jnp.where(apart >= 2, sums, 0.0), axis=(1, 2))
    place = jnp.arange(BUCKETS, dtype=jnp.int32)[:, None]
    return (
        near
        + jnp.where(place == FAR_BEFORE, before[None, :], 0.0)
        + jnp.where(place == FAR_AFTER, after[None, :], 0.0)
    )


def middle_kernel(context, tokens, w_out, gain, router, route_col, slot_row, experts,
                  middle, sending_low, sending_high, gate, normed):
    for first in range(0, TOK, 256):
        at = slice(first, first + 256)
        mid = tokens[at, :].astype(F32) + dot(context[at, :], w_out[...])
        middle[at, :] = mid
        low = (mid * inverse_rms(mid) * gain[...]).astype(BF)
        normed[at, :] = low
        probs = router_softmax(low, router[...], experts)
        lane = lax.broadcasted_iota(jnp.int32, probs.shape, 1)
        gate[at, :] = jnp.sum(
            jnp.where(lane == route_col[at, :], probs, 0.0), axis=1, keepdims=True
        )
    dispatch(slot_row[...], normed[...], [sending_low, sending_high])


def router_softmax(rows, router, experts):
    logits = dot(rows, router)
    lane = lax.broadcasted_iota(jnp.int32, logits.shape, 1)
    logits = jnp.where(lane < experts, logits, UNPAIRED)
    raised = jnp.exp(logits - jnp.max(logits, axis=1, keepdims=True))
    return raised / jnp.sum(raised, axis=1, keepdims=True)


def make_middle(context, tokens, w_out, gain, router, routes, slot_row, experts, capacity):
    total = experts * capacity

    def kernel(*refs):
        middle_kernel(*refs[:7], experts, *refs[7:])

    return pl.pallas_call(
        kernel,
        out_shape=(
            jax.ShapeDtypeStruct((TOK, D), F32),
            jax.ShapeDtypeStruct((total // 2, D), BF),
            jax.ShapeDtypeStruct((total // 2, D), BF),
            jax.ShapeDtypeStruct((TOK, 1), F32),
        ),
        scratch_shapes=[pltpu.VMEM((TOK, D), BF)],
        compiler_params=params(),
        cost_estimate=cost(2 * total * TOK * D + 2 * TOK * D * D, 12 * TOK * D + 2 * total * D),
        name="middle",
    )(context, tokens, w_out, gain, router, routes, slot_row)


def gelu_parts(v):
    size = jnp.abs(v)
    t = 1.0 / (1.0 + (0.3275911 * 0.7071067811865476) * size)
    bell = jnp.exp(-0.5 * (v * v))
    series = t * (
        0.5 * 0.254829592
        + t * (0.5 * -0.284496736 + t * (0.5 * 1.421413741 + t * (0.5 * -1.453152027 + t * (0.5 * 1.061405429))))
    )
    tail = series * bell
    phi = jnp.where(v < 0, tail, 1.0 - tail)
    return v * phi, phi + v * (bell * 0.3989422804014327)


def expert_kernel(experts, x, c3, w_first, w_second, router, router_t, mine,
                  act_ref, dh_ref, result, grad_x, gate_ref, grad_router, acc_r, acc_x):
    step = pl.program_id(0)
    rows = x.shape[0]
    chunk = 256
    per = chunk // c3.shape[1]
    for first in range(0, rows, chunk):
        at = slice(first, first + chunk)
        hidden = dot(x[at, :], w_first[...])
        cot = c3[first // chunk * per : (first // chunk + 1) * per].reshape(chunk, D)
        grad_act = dot(cot, w_second[...], 1, 1)
        act, slope = gelu_parts(hidden)
        act = act.astype(BF)
        grad_hidden = (grad_act * slope).astype(BF)
        act_ref[at, :] = act
        dh_ref[at, :] = grad_hidden
        part_r = dot(act, w_second[...])
        part_x = dot(grad_hidden, w_first[...], 1, 1)

        @pl.when(step == 0)
        def _():
            acc_r[at, :] = part_r
            acc_x[at, :] = part_x

        @pl.when(step > 0)
        def _():
            acc_r[at, :] += part_r
            acc_x[at, :] += part_x

    @pl.when(step == pl.num_programs(0) - 1)
    def _():
        total_router = jnp.zeros(grad_router.shape, F32)
        for first in range(0, rows, chunk):
            at = slice(first, first + chunk)
            rounded = acc_r[at, :].astype(BF)
            result[at, :] = rounded
            probs = router_softmax(x[at, :], router[...], experts)
            lane = lax.broadcasted_iota(jnp.int32, probs.shape, 1)
            here = lane == mine[0, 0]
            gate = jnp.sum(jnp.where(here, probs, 0.0), axis=1, keepdims=True)
            grad_gate = jnp.sum(
                c3[first // chunk * per : (first // chunk + 1) * per].reshape(chunk, D).astype(F32) * rounded.astype(F32), axis=1, keepdims=True
            )
            grad_logits = (
                probs * (jnp.where(here, grad_gate, 0.0) - gate * grad_gate)
            ).astype(BF)
            gate_ref[at, :] = gate
            grad_x[at, :] = (acc_x[at, :] * gate + dot(grad_logits, router_t[...])).astype(BF)
            total_router = total_router + dot(x[at, :], grad_logits, 0, 0)
        grad_router[...] = total_router


def run_expert(part, x, c, w_first, w_second, router, router_t, mine, experts):
    rows = x.shape[0]
    hidden_size = w_first.shape[1]
    lanes = router.shape[1]
    return pl.pallas_call(
        functools.partial(expert_kernel, experts),
        grid=(hidden_size // FF_TILE,),
        in_specs=[
            whole((rows, D)),
            pl.BlockSpec((c.shape[0], c.shape[1] // HALVES, D), lambda f: (0, part, 0)),
            pl.BlockSpec((D, FF_TILE), lambda f: (0, f)),
            pl.BlockSpec((FF_TILE, D), lambda f: (f, 0)),
            whole((D, lanes)),
            whole((lanes, D)),
            pl.BlockSpec(memory_space=pltpu.SMEM),
        ],
        out_specs=[
            pl.BlockSpec((rows, FF_TILE), lambda f: (0, f)),
            pl.BlockSpec((rows, FF_TILE), lambda f: (0, f)),
            whole((rows, D)),
            whole((rows, D)),
            whole((rows, 1)),
            whole((D, lanes)),
        ],
        out_shape=[
            jax.ShapeDtypeStruct((rows, hidden_size), BF),
            jax.ShapeDtypeStruct((rows, hidden_size), BF),
            jax.ShapeDtypeStruct((rows, D), BF),
            jax.ShapeDtypeStruct((rows, D), BF),
            jax.ShapeDtypeStruct((rows, 1), F32),
            jax.ShapeDtypeStruct((D, lanes), F32),
        ],
        scratch_shapes=[pltpu.VMEM((rows, D), F32), pltpu.VMEM((rows, D), F32)],
        compiler_params=params(("arbitrary",)),
        cost_estimate=cost(
            8 * rows * D * hidden_size, 4 * rows * hidden_size + 4 * D * hidden_size
        ),
        name="expert",
    )(x, c, w_first, w_second, router, router_t, mine)


def expert_weights_kernel(parts, *refs):
    xs, gates = refs[:parts], refs[parts : 2 * parts]
    acts, dhs = refs[2 * parts : 3 * parts], refs[3 * parts : 4 * parts]
    cots, grad_first, grad_second, x_t, c_t = refs[4 * parts :]
    rows = xs[0].shape[0]
    share = cots.shape[1] // parts
    chunk = 256
    per = chunk // share

    @pl.when(pl.program_id(0) == 0)
    def _():
        for part in range(parts):
            for first in range(0, rows, chunk):
                at = slice(first, first + chunk)
                to = slice(part * rows + first, part * rows + first + chunk)
                gate = gates[part][at, :]
                x_t[:, to] = (xs[part][at, :].astype(F32) * gate).T.astype(BF)
                cot = cots[
                    first // chunk * per : (first // chunk + 1) * per,
                    part * share : (part + 1) * share,
                ].reshape(chunk, D)
                c_t[:, to] = (cot.astype(F32) * gate).T.astype(BF)

    first_sum, second_sum = None, None
    for part in range(parts):
        at = slice(part * rows, (part + 1) * rows)
        one = dot(x_t[:, at], dhs[part][...])
        two = dot(c_t[:, at], acts[part][...])
        first_sum = one if first_sum is None else first_sum + one
        second_sum = two if second_sum is None else second_sum + two
    grad_first[...] = first_sum.astype(BF)
    grad_second[...] = second_sum.T.astype(BF)


def expert_weights(xs, cots, gates, acts, dhs):
    parts = len(xs)
    rows = xs[0].shape[0]
    hidden_size = acts[0].shape[1]
    tile = pl.BlockSpec((rows, FF_TILE), lambda f: (0, f))
    return pl.pallas_call(
        functools.partial(expert_weights_kernel, parts),
        grid=(hidden_size // FF_TILE,),
        in_specs=[whole((rows, D))] * parts
        + [whole((rows, 1))] * parts
        + [tile] * (2 * parts)
        + [whole(cots.shape)],
        out_specs=[
            pl.BlockSpec((D, FF_TILE), lambda f: (0, f)),
            pl.BlockSpec((FF_TILE, D), lambda f: (f, 0)),
        ],
        out_shape=[
            jax.ShapeDtypeStruct((D, hidden_size), BF),
            jax.ShapeDtypeStruct((hidden_size, D), BF),
        ],
        scratch_shapes=[
            pltpu.VMEM((D, parts * rows), BF),
            pltpu.VMEM((D, parts * rows), BF),
        ],
        compiler_params=params(("arbitrary",)),
        cost_estimate=cost(
            4 * parts * rows * D * hidden_size, 4 * (parts * rows + D) * hidden_size, share=1
        ),
        name="expert_weights",
    )(*xs, *gates, *acts, *dhs, cots)


def rms_back(values, factor, grad):
    inverse = inverse_rms(values)
    scaled = grad * factor
    mean = jnp.mean(scaled * values, axis=-1, keepdims=True)
    return (
        inverse * scaled - values * (inverse * inverse * inverse * mean),
        jnp.sum(grad * values * inverse, axis=0, keepdims=True),
    )


def undispatch(slot_col, parts):
    out = None
    offset = 0
    for part in parts:
        total = part.shape[0]
        place = lax.broadcasted_iota(jnp.int32, (slot_col.shape[0], total), 1) + offset
        found = dot((place == slot_col).astype(BF), part[...])
        out = found if out is None else out + found
        offset += total
    return out


def middle_back_kernel(parts, *refs):
    backs = refs[:parts]
    slot_col, middle, cot, gain, w_out, grad_middle, grad_attn, grad_context, grad_gain = refs[parts:]
    grad_normed = undispatch(slot_col[...], backs)
    part, gain_part = rms_back(middle[...], gain[...], grad_normed)
    grad = cot[...].astype(F32) + part
    grad_middle[...] = grad
    low = grad.astype(BF)
    grad_attn[...] = low
    grad_context[...] = dot(low, w_out[...], 1, 1).astype(BF)

    @pl.when(pl.program_id(0) == 0)
    def _():
        grad_gain[...] = gain_part

    @pl.when(pl.program_id(0) > 0)
    def _():
        grad_gain[...] += gain_part


def middle_back(backs, slot_col, middle, cot, gain, w_out):
    parts = len(backs)
    block = 256
    rows = pl.BlockSpec((block, D), lambda r: (r, 0))
    return pl.pallas_call(
        functools.partial(middle_back_kernel, parts),
        grid=(TOK // block,),
        in_specs=[whole(back.shape) for back in backs]
        + [
            pl.BlockSpec((block, 1), lambda r: (r, 0)),
            rows,
            rows,
            whole((1, D)),
            whole((D, D)),
        ],
        out_specs=[rows, rows, rows, whole((1, D))],
        out_shape=[
            jax.ShapeDtypeStruct((TOK, D), F32),
            jax.ShapeDtypeStruct((TOK, D), BF),
            jax.ShapeDtypeStruct((TOK, D), BF),
            jax.ShapeDtypeStruct((1, D), F32),
        ],
        compiler_params=params(("arbitrary",)),
        cost_estimate=cost(2 * 2 * TOK * TOK * D + 2 * TOK * D * D, 16 * TOK * D, share=1),
        name="middle_back",
    )(*backs, slot_col, middle, cot, gain, w_out)


def mix_kernel(parts, *refs):
    backs = refs[:parts]
    slot_col, middle, gate, mixed = refs[parts:]
    mixed[...] = middle[...] + gate[...] * undispatch(slot_col[...], backs)


def mix(backs, slot_col, middle, gate):
    parts = len(backs)
    block = 256
    rows = pl.BlockSpec((block, D), lambda r: (r, 0))
    column = pl.BlockSpec((block, 1), lambda r: (r, 0))
    return pl.pallas_call(
        functools.partial(mix_kernel, parts),
        grid=(TOK // block,),
        in_specs=[whole(back.shape) for back in backs] + [column, rows, column],
        out_specs=rows,
        out_shape=jax.ShapeDtypeStruct((TOK, D), F32),
        compiler_params=params(("arbitrary",)),
        cost_estimate=cost(2 * 2 * TOK * TOK * D, 12 * TOK * D, share=1),
        name="mix",
    )(*backs, slot_col, middle, gate)


def tokens_back_kernel(g_left, g_right, left, right, tokens, gain, grad_middle, grad_tokens, grad_gain):
    grad_normed = dot(g_left[...], left[...], 1, 1) + dot(g_right[...], right[:, :SPLIT], 1, 1)
    part, gain_part = rms_back(tokens[...].astype(F32), gain[...], grad_normed)
    grad_tokens[...] = grad_middle[...] + part

    @pl.when(pl.program_id(0) == 0)
    def _():
        grad_gain[...] = gain_part

    @pl.when(pl.program_id(0) > 0)
    def _():
        grad_gain[...] += gain_part


def tokens_back(g_left, g_right, left, right, tokens, gain, grad_middle):
    block = 256
    rows = pl.BlockSpec((block, D), lambda r: (r, 0))
    return pl.pallas_call(
        tokens_back_kernel,
        grid=(TOK // block,),
        in_specs=[
            pl.BlockSpec((block, SPLIT), lambda r: (r, 0)),
            pl.BlockSpec((block, SPLIT), lambda r: (r, 0)),
            whole(left.shape),
            whole(right.shape),
            rows,
            whole((1, D)),
            rows,
        ],
        out_specs=[rows, whole((1, D))],
        out_shape=[
            jax.ShapeDtypeStruct((TOK, D), F32),
            jax.ShapeDtypeStruct((1, D), F32),
        ],
        compiler_params=params(("arbitrary",)),
        cost_estimate=cost(6 * TOK * D * D, 16 * TOK * D, share=1),
        name="tokens_back",
    )(g_left, g_right, left, right, tokens, gain, grad_middle)


def weights_back_kernel(turned, grads, out):
    out[...] = dot(turned[...], grads[...])


def weights_back(turned, grads):
    block = 384
    columns = grads.shape[1]
    return pl.pallas_call(
        weights_back_kernel,
        grid=(columns // block,),
        in_specs=[whole(turned.shape), pl.BlockSpec((TOK, block), lambda c: (0, c))],
        out_specs=pl.BlockSpec((D, block), lambda c: (0, c)),
        out_shape=jax.ShapeDtypeStruct((D, columns), F32),
        compiler_params=params(("arbitrary",)),
        cost_estimate=cost(2 * TOK * D * columns, 2 * TOK * (D + columns) + 4 * D * columns, share=1),
        name="weights_back",
    )(turned, grads)


def swap(block, axis, bit):
    size = lax.axis_size(axis)
    return lax.ppermute(block, axis, [(place, place ^ bit) for place in range(size)])


def on_upper(axis, bit):
    return (lax.axis_index(axis) // bit) % 2 == 1


def axis_bits(*axes):
    found = []
    for axis in axes:
        bit = lax.axis_size(axis) // 2
        while bit >= 1:
            found.append((axis, bit))
            bit //= 2
    return found


def orders():
    bits = axis_bits("dp", "expert")
    dp = [at for at, (axis, _) in enumerate(bits) if axis == "dp"]
    core = len(bits) - 1
    along = [at for at, (axis, bit) in enumerate(bits) if axis == "expert" and bit == 2]
    rest = [at for at in range(core) if at not in dp and at not in along]
    return (rest + along + dp + [core], rest + dp + along + [core])


def gather_rows(shard, order):
    bits = axis_bits("dp", "expert")
    block = shard.reshape((1,) * len(bits) + shard.shape)
    for place in order:
        axis, bit = bits[place]
        other = swap(block, axis, bit)
        upper = on_upper(axis, bit)
        block = jnp.concatenate(
            [jnp.where(upper, other, block), jnp.where(upper, block, other)], axis=place
        )
    return block.reshape((-1,) + shard.shape[1:])


def scatter_start(total):
    bits = axis_bits("dp", "expert")
    rows = total.shape[0] >> len(bits)
    return total.reshape((2,) * len(bits) + (rows,) + total.shape[1:])


def scatter_step(block, place, *others):
    axis, bit = axis_bits("dp", "expert")[place]
    lower = lax.slice_in_dim(block, 0, 1, axis=place)
    higher = lax.slice_in_dim(block, 1, 2, axis=place)
    upper = on_upper(axis, bit)
    sent = jnp.where(upper, lower, higher).astype(BF)
    kept = after(jnp.where(upper, higher, lower), *others)
    return kept + swap(sent, axis, bit).astype(F32)


def scatter_rest(block, order):
    for place in order:
        block = scatter_step(block, place)
    return block.reshape(block.shape[len(axis_bits("dp", "expert")) :])


def sum_all(total):
    for axis, bit in axis_bits("dp", "expert"):
        total = total + swap(total, axis, bit)
    return total


def gather_dp(block, axis):
    if lax.axis_size("dp") != 2:
        return lax.all_gather(block, "dp", axis=axis, tiled=True)
    other = swap(block, "dp", 1)
    upper = on_upper("dp", 1)
    return jnp.concatenate(
        [jnp.where(upper, other, block), jnp.where(upper, block, other)], axis=axis
    )


def scatter_dp(total, *others):
    if lax.axis_size("dp") != 2:
        return lax.psum_scatter(
            total[None], "dp", scatter_dimension=1, tiled=True
        ).astype(F32)
    half = total.shape[0] // 2
    upper = on_upper("dp", 1)
    sent = jnp.where(upper, total[:half], total[half:])
    kept = jnp.where(upper, total[half:], total[:half])
    return (after(kept, *others).astype(F32) + swap(sent, "dp", 1).astype(F32))[None]


def after(value, *others):
    return lax.optimization_barrier((value, *others))[0]


def body(
    tokens, seq_ids, routes, cotangent, w_query, w_key, w_value, w_out,
    rel_table, gain_attn, gain_ffn, router, expert_in, expert_out,
):
    experts = lax.axis_size("expert")
    capacity = 2 * TOK // experts
    shard = w_query.shape[0]
    lanes = -(-(experts + 2) // LANES) * LANES
    everyone = ("dp", "expert")

    small = jnp.concatenate(
        [
            router,
            gain_attn[:, None],
            gain_ffn[:, None],
            jnp.zeros((shard, lanes - experts - 2), BF),
        ],
        axis=1,
    )
    first, second = orders()
    kinds = (w_query, w_key, w_value)
    left = gather_rows(jnp.concatenate([w[:, :SIDE] for w in kinds], axis=1), first)
    right = gather_rows(
        jnp.concatenate([w[:, SIDE:] for w in kinds] + [small], axis=1), second
    )
    full_out = lax.all_gather(w_out, everyone, axis=0, tiled=True)
    table = gather_dp(rel_table, 0).astype(F32)

    slot_col, slot_row, sending_cot = make_slots(routes, cotangent, experts, capacity)

    def exchange(rows):
        return lax.all_to_all(
            rows.reshape(experts, -1, D), "expert", split_axis=0, concat_axis=0, tiled=True
        )

    w_first = gather_dp(after(expert_in, slot_row), 1)[0]
    w_second = gather_dp(after(expert_out, slot_row), 1)[0]
    cots = exchange(sending_cot)

    extra = right[:, SPLIT:]
    full_router = jnp.where(jnp.arange(lanes)[None, :] < experts, extra, jnp.zeros((), BF))
    router_t = full_router.T
    attn_gain = extra[:, experts].astype(F32).reshape(1, D)
    ffn_gain = extra[:, experts + 1].astype(F32).reshape(1, D)

    turned, qkv = project(tokens, attn_gain, left, right)
    query_features, key_features = lane_features(seq_ids.reshape(TOK, 1), table)
    band = jnp.sum(band_onehot()[None, :, :] * table.T[:, None, :], axis=2)[:, None, :]
    context, lse = attend(qkv, query_features, key_features, band)

    middle, *sending, gate = make_middle(
        after(context, cots, w_first), tokens, full_out, ffn_gain, full_router, routes, slot_row, experts, capacity
    )
    sending[0] = after(sending[0], w_second)
    rows_in = [exchange(part).reshape(-1, D) for part in sending]
    mine = lax.axis_index("expert").astype(jnp.int32).reshape(1, 1)
    acts, dhs, results, grads, gates, router_parts = zip(
        *(
            run_expert(
                part, rows, cots, w_first, w_second, full_router, router_t, mine, experts
            )
            for part, rows in enumerate(rows_in)
        )
    )
    grads_home = [exchange(part).reshape(-1, D) for part in grads]
    grad_first, grad_second = expert_weights(
        rows_in, cots, (after(gates[0], grads_home[0]), *gates[1:]), acts, dhs
    )
    results_home = [
        exchange(after(part, *grads_home)).reshape(-1, D) for part in results
    ]
    grads_home[0] = after(grads_home[0], grad_first, grad_second)
    grad_middle, grad_attn, grad_context, grad_gain_f = middle_back(
        grads_home, slot_col, middle, cotangent, ffn_gain, full_out
    )
    down, down_other = first[::-1], second[::-1]
    out_block = scatter_step(scatter_start(dot(context, grad_attn, 0, 0)), down_other[0])

    def back(half, *others):
        return attend_back(
            half, qkv, after(grad_context, *others), query_features, key_features, lse, band
        )

    g_left, tiles_left, diagonals_left = back(0)
    left_block = scatter_start(weights_back(turned, after(g_left, out_block)))
    g_right, tiles_right, diagonals_right = back(1, left_block, out_block, results_home[0])
    out_block = scatter_step(out_block, down_other[1], g_right)
    left_block = scatter_step(left_block, down[0], g_right)
    grad_expert_out = scatter_dp(grad_second, g_right)
    grad_right = weights_back(
        turned, after(g_right, results_home[1], out_block, left_block, grad_expert_out)
    )
    grad_tokens, grad_gain_a = tokens_back(
        g_left, after(g_right, grad_right), left, right, tokens, attn_gain, grad_middle
    )
    mixed = mix(results_home, slot_col, middle, after(gate, grad_tokens))
    right_block = scatter_step(scatter_start(grad_right), down_other[0], grad_tokens)
    left_block = scatter_step(left_block, down[1], grad_tokens)
    out_block = scatter_step(out_block, down_other[2], grad_tokens)
    near = 2 + len(axis_bits("dp"))
    for place in down_other[1:near]:
        right_block = scatter_step(right_block, place)
    for place in down[2:near]:
        left_block = scatter_step(left_block, place)
    for place in down_other[3:near]:
        out_block = scatter_step(out_block, place)
    joined = jnp.concatenate([left_block, right_block, out_block], axis=-1)
    grad_expert_in = scatter_dp(grad_first, joined)
    dense = scatter_rest(joined, down[near:])
    grad_left, grad_right = dense[:, :SPLIT], dense[:, SPLIT : 2 * SPLIT]
    grad_w_out = dense[:, 2 * SPLIT :]
    tiles = jnp.concatenate([tiles_left, tiles_right], axis=0)
    diagonals = jnp.concatenate([diagonals_left, diagonals_right], axis=0)
    grad_router = sum(router_parts)[:, :experts]
    grad_table = table_gradient(tiles, diagonals)

    sizes = (D * experts, D, D, BUCKETS * HEADS)
    sums = sum_all(
        jnp.concatenate(
            [
                part.reshape(-1, LANES)
                for part in (grad_router, grad_gain_a, grad_gain_f, grad_table)
            ],
            axis=0,
        )
    ).reshape(-1)
    ends = [sum(sizes[: at + 1]) for at in range(len(sizes))]
    grad_router, grad_gain_a, grad_gain_f, grad_table = (
        sums[end - size : end] for end, size in zip(ends, sizes)
    )
    number = lax.axis_index("dp") * experts + lax.axis_index("expert")
    table_height = BUCKETS // lax.axis_size("dp")

    def own(rows, height, place):
        return lax.dynamic_slice_in_dim(rows, place * height, height, 0)

    return (
        mixed,
        grad_tokens,
        *(
            jnp.concatenate(
                [side[:, kind * SIDE : (kind + 1) * SIDE] for side in (grad_left, grad_right)],
                axis=1,
            )
            for kind in range(3)
        ),
        grad_w_out,
        own(grad_table.reshape(BUCKETS, HEADS), table_height, lax.axis_index("dp")),
        own(grad_gain_a, shard, number),
        own(grad_gain_f, shard, number),
        own(grad_router.reshape(D, experts), shard, number),
        grad_expert_in,
        grad_expert_out,
    )


def solution(mesh):
    rows = P(("dp", "expert"), None)
    flat = P(("dp", "expert"))
    expert = P("expert", "dp", None)
    return jax.shard_map(
        body,
        mesh=mesh,
        in_specs=(
            rows, flat, rows, rows, rows, rows, rows, rows,
            P("dp", None), flat, flat, rows, expert, expert,
        ),
        out_specs=(
            rows, rows, rows, rows, rows, rows,
            P("dp", None), flat, flat, rows, expert, expert,
        ),
        check_vma=False,
    )
```

```python
import functools

import jax
import jax.numpy as jnp
from jax import lax
from jax.experimental import pallas as pl
from jax.experimental.pallas import tpu as pltpu
from jax.sharding import PartitionSpec as P

D = 768
HEADS = 12
HEAD_DIM = 64
BUCKETS = 32
TOK = 1024
TILE = 128
TILES = TOK // TILE
QBLK = 256
FF_TILE = 512
HALVES = 2
SIDE = D // 2
SPLIT = 3 * SIDE
PAIRS = HEADS // 2
SIDE_PAIRS = PAIRS // 2
COST_SHARE = 0.05
LANES = 128

EPSILON = 1e-06
DISTANCE_EDGES = (12, 16, 23, 32, 46, 64, 91)
FAR_BEFORE = 15
FAR_AFTER = 31
UNPAIRED = -1e30
BF = jnp.bfloat16
F32 = jnp.float32
VMEM_LIMIT = 56 * 1024 * 1024


def dot(left, right, left_dim=1, right_dim=0):
    return lax.dot_general(
        left, right, (((left_dim,), (right_dim,)), ((), ())), preferred_element_type=F32
    )


def params(semantics=None):
    return pltpu.CompilerParams(vmem_limit_bytes=VMEM_LIMIT, dimension_semantics=semantics)


def cost(flops, bytes_accessed, transcendentals=0, share=COST_SHARE):
    return pl.CostEstimate(
        flops=int(flops * share),
        bytes_accessed=int(bytes_accessed * share),
        transcendentals=int(transcendentals * share),
    )


def whole(shape):
    return pl.BlockSpec(shape, lambda *_: (0,) * len(shape))


def inverse_rms(values):
    return lax.rsqrt(jnp.mean(values * values, axis=-1, keepdims=True) + EPSILON)


def bucket_of(offset):
    distance = jnp.abs(offset)
    distant = 8 + sum(((distance >= boundary).astype(jnp.int32) for boundary in DISTANCE_EDGES))
    return jnp.where(distance < 8, distance, distant) + jnp.where(offset > 0, 16, 0)


def place_in_buffers(route, rank, experts, capacity):
    share = capacity // HALVES
    part = (rank >= share).astype(jnp.int32)
    return part * (experts * share) + route * share + (rank - part * share)


def slots_kernel(experts, capacity, route_col, route_row, cot, slot_col, slot_row, sending):
    padded = -(-experts // LANES) * LANES
    picked = (
        lax.broadcasted_iota(jnp.int32, (TOK, padded), 1) == route_col[...]
    ).astype(BF)
    picked_t = (
        lax.broadcasted_iota(jnp.int32, (padded, TOK), 0) == route_row[...]
    ).astype(BF)
    upto = (
        lax.broadcasted_iota(jnp.int32, (TOK, TOK), 0)
        <= lax.broadcasted_iota(jnp.int32, (TOK, TOK), 1)
    ).astype(BF)
    from_t = (
        lax.broadcasted_iota(jnp.int32, (TOK, TOK), 0)
        >= lax.broadcasted_iota(jnp.int32, (TOK, TOK), 1)
    ).astype(BF)
    counts = dot(from_t, picked) * picked.astype(F32)
    rank = jnp.sum(counts, axis=1, keepdims=True).astype(jnp.int32) - 1
    slot_col[...] = place_in_buffers(route_col[...], rank, experts, capacity)
    counts_t = dot(picked_t, upto) * picked_t.astype(F32)
    rank_row = jnp.sum(counts_t, axis=0, keepdims=True).astype(jnp.int32) - 1
    slot_row[...] = place_in_buffers(route_row[...], rank_row, experts, capacity)
    dispatch(route_row[...] * capacity + rank_row, cot[...], [sending])


def dispatch(row, rows, parts):
    step = 512
    offset = 0
    for sending in parts:
        for first in range(0, sending.shape[0], step):
            chosen = (
                lax.broadcasted_iota(jnp.int32, (step, TOK), 0) + (first + offset) == row
            ).astype(BF)
            sending[first : first + step, :] = dot(chosen, rows).astype(BF)
        offset += sending.shape[0]


def make_slots(routes, cotangent, experts, capacity):
    total = experts * capacity
    return pl.pallas_call(
        functools.partial(slots_kernel, experts, capacity),
        out_shape=(
            jax.ShapeDtypeStruct((TOK, 1), jnp.int32),
            jax.ShapeDtypeStruct((1, TOK), jnp.int32),
            jax.ShapeDtypeStruct((total, D), BF),
        ),
        compiler_params=params(),
        cost_estimate=cost(2 * total * TOK * D, 6 * total * D),
        name="slots",
    )(routes, routes.reshape(1, TOK), cotangent)


def project_kernel(tokens, gain, left, right, turned, qkv):
    x = tokens[...].astype(F32)
    wide = x * inverse_rms(x) * gain[...]
    low = wide.astype(BF)
    turned[...] = wide.T.astype(BF)
    qkv[:, :SPLIT] = dot(low, left[...]).astype(BF)
    qkv[:, SPLIT:] = dot(low, right[...]).astype(BF)


def project(tokens, gain, left, right):
    block = 256
    rows = pl.BlockSpec((block, D), lambda r: (r, 0))
    return pl.pallas_call(
        project_kernel,
        grid=(TOK // block,),
        in_specs=[rows, whole((1, D)), whole((D, SPLIT)), whole((D, SPLIT))],
        out_specs=[
            pl.BlockSpec((D, block), lambda r: (0, r)),
            pl.BlockSpec((block, 3 * D), lambda r: (r, 0)),
        ],
        out_shape=[
            jax.ShapeDtypeStruct((D, TOK), BF),
            jax.ShapeDtypeStruct((TOK, 3 * D), BF),
        ],
        compiler_params=params(("arbitrary",)),
        cost_estimate=cost(6 * TOK * D * D, 12 * TOK * D),
        name="project",
    )(tokens, gain, left, right)


def lane_features(seq_col, rel_table):
    lane = jnp.arange(LANES, dtype=jnp.int32)[None, :]
    feature = lane % HEAD_DIM
    tile = jnp.arange(TOK, dtype=jnp.int32)[:, None] // TILE
    on_tile = feature - 4
    query_features = jnp.where(
        feature < 4,
        jnp.where(feature == seq_col, 0.0, UNPAIRED),
        jnp.where(on_tile == tile, 1.0, 0.0),
    ).astype(BF)
    wide = jnp.arange(D, dtype=jnp.int32)[None, :]
    feature = wide % HEAD_DIM
    on_tile = feature - 4
    swapped = jnp.arange(HEADS, dtype=jnp.int32) ^ 1
    before = jnp.repeat(rel_table[FAR_BEFORE][swapped], HEAD_DIM)[None, :]
    after = jnp.repeat(rel_table[FAR_AFTER][swapped], HEAD_DIM)[None, :]
    apart = tile - on_tile
    far = jnp.where(apart >= 2, after, jnp.where(apart <= -2, before, 0.0))
    key_features = jnp.where(
        feature < 4,
        jnp.where(feature == seq_col, 1.0, 0.0),
        jnp.where(on_tile < TILES, far, 0.0),
    ).astype(BF)
    return query_features, key_features


def band_offsets():
    place = jnp.arange(4 * LANES, dtype=jnp.int32)
    return 255 - (place + 383) % 512


def band_onehot():
    return (
        bucket_of(band_offsets())[:, None] == jnp.arange(BUCKETS, dtype=jnp.int32)[None, :]
    ).astype(F32)


def near_rows(tile):
    first = max(tile - 1, 0)
    last = min(tile + 2, TILES)
    return first, last


def spread_band(values):
    wide = jnp.broadcast_to(values, (3 * TILE, 4 * LANES))
    return pltpu.roll(wide, 0, 1, stride=1, stride_axis=0)[:, :TILE]


def attend_kernel(q_ref, k_ref, v_ref, qx_ref, kx_ref, band_ref, out_ref, lse_ref, st, pb, ot):
    low = lax.broadcasted_iota(jnp.int32, (TOK, LANES), 1) < HEAD_DIM
    v_t = v_ref[...].astype(F32).T.astype(BF)
    for side in range(2):
        own = low if side == 0 else ~low
        queries = jnp.where(own, q_ref[...], qx_ref[...])
        keys = jnp.where(own, k_ref[...], kx_ref[...])
        band = spread_band(band_ref[side])
        for block in range(TOK // QBLK):
            rows = slice(block * QBLK, (block + 1) * QBLK)
            slot = block % 2
            st[slot] = dot(keys, queries[rows], 1, 1)
            for part in range(QBLK // TILE):
                tile = block * (QBLK // TILE) + part
                first, last = near_rows(tile)
                at = (slot, slice(first * TILE, last * TILE), slice(part * TILE, (part + 1) * TILE))
                st[at] += band[(first - tile + 1) * TILE : (last - tile + 1) * TILE]
            top = jnp.max(st[slot, 0:TILE], axis=0, keepdims=True)
            for chunk in range(1, TILES):
                top = jnp.maximum(
                    top,
                    jnp.max(
                        st[slot, chunk * TILE : (chunk + 1) * TILE], axis=0, keepdims=True
                    ),
                )
            total = jnp.zeros((1, QBLK), F32)
            for chunk in range(TILES):
                at = slice(chunk * TILE, (chunk + 1) * TILE)
                raised = jnp.exp(st[slot, at] - top)
                total = total + jnp.sum(raised, axis=0, keepdims=True)
                pb[slot, at] = raised.astype(BF)
            half = slice(side * HEAD_DIM, (side + 1) * HEAD_DIM)
            ot[half, rows] = dot(v_t[half], pb[slot]) * (1.0 / total)
            lse_ref[side, :, rows] = top + jnp.log(total)
    out_ref[...] = ot[...].T.astype(BF)


def attend(qkv, query_features, key_features, band):
    return pl.pallas_call(
        attend_kernel,
        grid=(PAIRS,),
        in_specs=[
            *(
                pl.BlockSpec(
                    (TOK, LANES),
                    lambda p, kind=kind: (
                        0,
                        p // SIDE_PAIRS * (3 * SIDE_PAIRS) + kind * SIDE_PAIRS + p % SIDE_PAIRS,
                    ),
                )
                for kind in range(3)
            ),
            whole((TOK, LANES)),
            pl.BlockSpec((TOK, LANES), lambda p: (0, p)),
            pl.BlockSpec((2, 1, 4 * LANES), lambda p: (p, 0, 0)),
        ],
        out_specs=[
            pl.BlockSpec((TOK, LANES), lambda p: (0, p)),
            pl.BlockSpec((2, 1, TOK), lambda p: (p, 0, 0)),
        ],
        out_shape=[
            jax.ShapeDtypeStruct((TOK, D), BF),
            jax.ShapeDtypeStruct((HEADS, 1, TOK), F32),
        ],
        scratch_shapes=[
            pltpu.VMEM((2, TOK, QBLK), F32),
            pltpu.VMEM((2, TOK, QBLK), BF),
            pltpu.VMEM((LANES, TOK), F32),
        ],
        compiler_params=params(("arbitrary",)),
        cost_estimate=cost(2 * 3 * HEADS * TOK * TOK * 256, 10 * TOK * D, HEADS * TOK * TOK),
        name="attend",
    )(qkv, qkv, qkv, query_features, key_features, band)


def attend_back_kernel(
    q_ref, k_ref, v_ref, do_ref, qx_ref, kx_ref, lse_ref, band_ref,
    grad_ref, tiles_ref, diag_ref,
    st, dp, pb, sb, dqt, dkt, dvt, near,
):
    low = lax.broadcasted_iota(jnp.int32, (TOK, LANES), 1) < HEAD_DIM
    k_t = k_ref[...].astype(F32).T.astype(BF)
    for side in range(2):
        own = low if side == 0 else ~low
        queries = jnp.where(own, q_ref[...], qx_ref[...])
        keys = jnp.where(own, k_ref[...], kx_ref[...])
        values = jnp.where(own, v_ref[...], jnp.zeros((), BF))
        band = spread_band(band_ref[side])
        near[...] = jnp.zeros_like(near)
        half = slice(side * HEAD_DIM, (side + 1) * HEAD_DIM)
        for block in range(TOK // QBLK):
            rows = slice(block * QBLK, (block + 1) * QBLK)
            slot = block % 2
            st[slot] = dot(keys, queries[rows], 1, 1)
            dp[slot] = dot(values, do_ref[rows, :], 1, 1)
            for part in range(QBLK // TILE):
                tile = block * (QBLK // TILE) + part
                first, last = near_rows(tile)
                at = (slot, slice(first * TILE, last * TILE), slice(part * TILE, (part + 1) * TILE))
                st[at] += band[(first - tile + 1) * TILE : (last - tile + 1) * TILE]
            lse = lse_ref[side, :, rows]
            spread = jnp.zeros((1, QBLK), F32)
            for chunk in range(TILES):
                at = slice(chunk * TILE, (chunk + 1) * TILE)
                weights = jnp.exp(st[slot, at] - lse)
                st[slot, at] = weights
                pb[slot, at] = weights.astype(BF)
                spread = spread + jnp.sum(weights * dp[slot, at], axis=0, keepdims=True)
            for chunk in range(TILES):
                at = slice(chunk * TILE, (chunk + 1) * TILE)
                sb[slot, at] = (st[slot, at] * (dp[slot, at] - spread)).astype(BF)
            for part in range(QBLK // TILE):
                tile = block * (QBLK // TILE) + part
                first, last = near_rows(tile)
                at = (slot, slice(first * TILE, last * TILE), slice(part * TILE, (part + 1) * TILE))
                near[(first - tile + 1) * TILE : (last - tile + 1) * TILE, :TILE] += sb[at].astype(F32)
            dv = dot(pb[slot], do_ref[rows, :])
            dk = dot(sb[slot], queries[rows])
            if block == 0:
                dvt[side] = dv
                dkt[side] = dk
            else:
                dvt[side] += dv
                dkt[side] += dk
            dqt[half, rows] = dot(k_t[half], sb[slot])
        for tile in range(TILES):
            tiles_ref[side, tile : tile + 1, :] = jnp.sum(
                dkt[side, tile * TILE : (tile + 1) * TILE], axis=0, keepdims=True
            )
        folded = near[0:8, :]
        for first in range(8, 3 * TILE, 8):
            folded = folded + pltpu.roll(near[first : first + 8, :], 4 * LANES - first, 1)
        diagonal = folded[0:1]
        for row in range(1, 8):
            diagonal = diagonal + pltpu.roll(folded[row : row + 1], 4 * LANES - row, 1)
        diag_ref[side] = diagonal
    found = (
        dqt[...].T.astype(BF),
        jnp.where(low, dkt[0], dkt[1]).astype(BF),
        jnp.where(low, dvt[0], dvt[1]).astype(BF),
    )
    for pair in range(SIDE_PAIRS):

        @pl.when(pl.program_id(0) == pair)
        def _():
            for kind in range(3):
                first = kind * SIDE + pair * LANES
                grad_ref[:, first : first + LANES] = found[kind]


def attend_back(half, qkv, grad_context, query_features, key_features, lse, band):
    first = half * SIDE_PAIRS
    column = pl.BlockSpec((TOK, LANES), lambda p: (0, first + p))
    return pl.pallas_call(
        attend_back_kernel,
        grid=(SIDE_PAIRS,),
        in_specs=[
            *(
                pl.BlockSpec(
                    (TOK, LANES), lambda p, kind=kind: (0, (3 * half + kind) * SIDE_PAIRS + p)
                )
                for kind in range(3)
            ),
            column,
            whole((TOK, LANES)),
            column,
            pl.BlockSpec((2, 1, TOK), lambda p: (first + p, 0, 0)),
            pl.BlockSpec((2, 1, 4 * LANES), lambda p: (first + p, 0, 0)),
        ],
        out_specs=[
            whole((TOK, SPLIT)),
            pl.BlockSpec((2, TILES, LANES), lambda p: (p, 0, 0)),
            pl.BlockSpec((2, 1, 4 * LANES), lambda p: (p, 0, 0)),
        ],
        out_shape=[
            jax.ShapeDtypeStruct((TOK, SPLIT), BF),
            jax.ShapeDtypeStruct((HEADS // 2, TILES, LANES), F32),
            jax.ShapeDtypeStruct((HEADS // 2, 1, 4 * LANES), F32),
        ],
        scratch_shapes=[
            pltpu.VMEM((2, TOK, QBLK), F32),
            pltpu.VMEM((2, TOK, QBLK), F32),
            pltpu.VMEM((2, TOK, QBLK), BF),
            pltpu.VMEM((2, TOK, QBLK), BF),
            pltpu.VMEM((LANES, TOK), F32),
            pltpu.VMEM((2, TOK, LANES), F32),
            pltpu.VMEM((2, TOK, LANES), F32),
            pltpu.VMEM((3 * TILE, 4 * LANES), F32),
        ],
        compiler_params=params(("arbitrary",)),
        cost_estimate=cost(5 * HEADS * TOK * TOK * 256, 8 * TOK * D, HEADS * TOK * TOK // 2, share=1),
        name="attend_back",
    )(qkv, qkv, qkv, grad_context, query_features, key_features, lse, band)


def table_gradient(tiles, diagonals):
    near = jnp.einsum(
        "hl,lb->bh", diagonals[:, 0, :], band_onehot(), precision=lax.Precision.HIGHEST
    )
    sums = jnp.concatenate(
        [tiles[h : h + 1, :, (HEAD_DIM if h % 2 == 0 else 0) + 4 :][:, :, :TILES] for h in range(HEADS)],
        axis=0,
    )
    apart = (
        jnp.arange(TILES, dtype=jnp.int32)[:, None] - jnp.arange(TILES, dtype=jnp.int32)[None, :]
    )[None]
    before = jnp.sum(jnp.where(apart <= -2, sums, 0.0), axis=(1, 2))
    after = jnp.sum(jnp.where(apart >= 2, sums, 0.0), axis=(1, 2))
    place = jnp.arange(BUCKETS, dtype=jnp.int32)[:, None]
    return (
        near
        + jnp.where(place == FAR_BEFORE, before[None, :], 0.0)
        + jnp.where(place == FAR_AFTER, after[None, :], 0.0)
    )


def middle_kernel(context, tokens, out_left, out_right, gain, router, route_col, slot_row, experts,
                  middle, sending_low, sending_high, gate, normed, w_out):
    w_out[:, :SIDE] = out_left[...]
    w_out[:, SIDE:] = out_right[...]
    for first in range(0, TOK, 256):
        at = slice(first, first + 256)
        mid = tokens[at, :].astype(F32) + dot(context[at, :], w_out[...])
        middle[at, :] = mid
        low = (mid * inverse_rms(mid) * gain[...]).astype(BF)
        normed[at, :] = low
        probs = router_softmax(low, router[...], experts)
        lane = lax.broadcasted_iota(jnp.int32, probs.shape, 1)
        gate[at, :] = jnp.sum(
            jnp.where(lane == route_col[at, :], probs, 0.0), axis=1, keepdims=True
        )
    dispatch(slot_row[...], normed[...], [sending_low, sending_high])


def router_softmax(rows, router, experts):
    logits = dot(rows, router)
    lane = lax.broadcasted_iota(jnp.int32, logits.shape, 1)
    logits = jnp.where(lane < experts, logits, UNPAIRED)
    raised = jnp.exp(logits - jnp.max(logits, axis=1, keepdims=True))
    return raised / jnp.sum(raised, axis=1, keepdims=True)


def make_middle(context, tokens, left, right, gain, router, routes, slot_row, experts, capacity):
    total = experts * capacity

    def kernel(*refs):
        middle_kernel(*refs[:8], experts, *refs[8:])

    out_half = pl.BlockSpec((D, SIDE), lambda r: (0, 3))
    return pl.pallas_call(
        kernel,
        grid=(1,),
        in_specs=[
            whole((TOK, D)),
            whole((TOK, D)),
            out_half,
            out_half,
            whole((1, D)),
            whole(router.shape),
            whole((TOK, 1)),
            whole((1, TOK)),
        ],
        out_specs=(
            whole((TOK, D)),
            whole((total // 2, D)),
            whole((total // 2, D)),
            whole((TOK, 1)),
        ),
        out_shape=(
            jax.ShapeDtypeStruct((TOK, D), F32),
            jax.ShapeDtypeStruct((total // 2, D), BF),
            jax.ShapeDtypeStruct((total // 2, D), BF),
            jax.ShapeDtypeStruct((TOK, 1), F32),
        ),
        scratch_shapes=[pltpu.VMEM((TOK, D), BF), pltpu.VMEM((D, D), BF)],
        compiler_params=params(),
        cost_estimate=cost(2 * total * TOK * D + 2 * TOK * D * D, 12 * TOK * D + 2 * total * D),
        name="middle",
    )(context, tokens, left, right, gain, router, routes, slot_row)


def gelu_parts(v):
    size = jnp.abs(v)
    t = 1.0 / (1.0 + (0.3275911 * 0.7071067811865476) * size)
    bell = jnp.exp(-0.5 * (v * v))
    series = t * (
        0.5 * 0.254829592
        + t * (0.5 * -0.284496736 + t * (0.5 * 1.421413741 + t * (0.5 * -1.453152027 + t * (0.5 * 1.061405429))))
    )
    tail = series * bell
    phi = jnp.where(v < 0, tail, 1.0 - tail)
    return v * phi, phi + v * (bell * 0.3989422804014327)


def expert_kernel(experts, x, c3, w_first, w_second, router, router_t, mine,
                  act_ref, dh_ref, result, grad_x, gate_ref, grad_router, acc_r, acc_x):
    step = pl.program_id(0)
    rows = x.shape[0]
    chunk = 256
    per = chunk // c3.shape[1]
    for first in range(0, rows, chunk):
        at = slice(first, first + chunk)
        hidden = dot(x[at, :], w_first[...])
        cot = c3[first // chunk * per : (first // chunk + 1) * per].reshape(chunk, D)
        grad_act = dot(cot, w_second[...], 1, 1)
        act, slope = gelu_parts(hidden)
        act = act.astype(BF)
        grad_hidden = (grad_act * slope).astype(BF)
        act_ref[at, :] = act
        dh_ref[at, :] = grad_hidden
        part_r = dot(act, w_second[...])
        part_x = dot(grad_hidden, w_first[...], 1, 1)

        @pl.when(step == 0)
        def _():
            acc_r[at, :] = part_r
            acc_x[at, :] = part_x

        @pl.when(step > 0)
        def _():
            acc_r[at, :] += part_r
            acc_x[at, :] += part_x

    @pl.when(step == pl.num_programs(0) - 1)
    def _():
        total_router = jnp.zeros(grad_router.shape, F32)
        for first in range(0, rows, chunk):
            at = slice(first, first + chunk)
            rounded = acc_r[at, :].astype(BF)
            result[at, :] = rounded
            probs = router_softmax(x[at, :], router[...], experts)
            lane = lax.broadcasted_iota(jnp.int32, probs.shape, 1)
            here = lane == mine[0, 0]
            gate = jnp.sum(jnp.where(here, probs, 0.0), axis=1, keepdims=True)
            grad_gate = jnp.sum(
                c3[first // chunk * per : (first // chunk + 1) * per].reshape(chunk, D).astype(F32) * rounded.astype(F32), axis=1, keepdims=True
            )
            grad_logits = (
                probs * (jnp.where(here, grad_gate, 0.0) - gate * grad_gate)
            ).astype(BF)
            gate_ref[at, :] = gate
            grad_x[at, :] = (acc_x[at, :] * gate + dot(grad_logits, router_t[...])).astype(BF)
            total_router = total_router + dot(x[at, :], grad_logits, 0, 0)
        grad_router[...] = total_router


def run_expert(part, x, c, w_first, w_second, router, router_t, mine, experts):
    rows = x.shape[0]
    hidden_size = w_first.shape[1]
    lanes = router.shape[1]
    return pl.pallas_call(
        functools.partial(expert_kernel, experts),
        grid=(hidden_size // FF_TILE,),
        in_specs=[
            whole((rows, D)),
            pl.BlockSpec((c.shape[0], c.shape[1] // HALVES, D), lambda f: (0, part, 0)),
            pl.BlockSpec((D, FF_TILE), lambda f: (0, f)),
            pl.BlockSpec((FF_TILE, D), lambda f: (f, 0)),
            whole((D, lanes)),
            whole((lanes, D)),
            pl.BlockSpec(memory_space=pltpu.SMEM),
        ],
        out_specs=[
            pl.BlockSpec((rows, FF_TILE), lambda f: (0, f)),
            pl.BlockSpec((rows, FF_TILE), lambda f: (0, f)),
            whole((rows, D)),
            whole((rows, D)),
            whole((rows, 1)),
            whole((D, lanes)),
        ],
        out_shape=[
            jax.ShapeDtypeStruct((rows, hidden_size), BF),
            jax.ShapeDtypeStruct((rows, hidden_size), BF),
            jax.ShapeDtypeStruct((rows, D), BF),
            jax.ShapeDtypeStruct((rows, D), BF),
            jax.ShapeDtypeStruct((rows, 1), F32),
            jax.ShapeDtypeStruct((D, lanes), F32),
        ],
        scratch_shapes=[pltpu.VMEM((rows, D), F32), pltpu.VMEM((rows, D), F32)],
        compiler_params=params(("arbitrary",)),
        cost_estimate=cost(
            8 * rows * D * hidden_size, 4 * rows * hidden_size + 4 * D * hidden_size
        ),
        name="expert",
    )(x, c, w_first, w_second, router, router_t, mine)


def expert_weights_kernel(parts, side, *refs):
    if side is not None:
        side, refs = refs[0], refs[1:]
    xs, gates = refs[:parts], refs[parts : 2 * parts]
    acts, dhs = refs[2 * parts : 3 * parts], refs[3 * parts : 4 * parts]
    cots = refs[4 * parts]
    if side is None:
        grad_first, grad_second, x_t, c_t = refs[4 * parts + 1 :]
    else:
        kept_first, sent_first, kept_second, sent_second, x_t, c_t, whole_first = refs[4 * parts + 1 :]
    rows = xs[0].shape[0]
    share = cots.shape[1] // parts
    chunk = 256
    per = chunk // share

    @pl.when(pl.program_id(0) == 0)
    def _():
        for part in range(parts):
            for first in range(0, rows, chunk):
                at = slice(first, first + chunk)
                to = slice(part * rows + first, part * rows + first + chunk)
                gate = gates[part][at, :]
                x_t[:, to] = (xs[part][at, :].astype(F32) * gate).T.astype(BF)
                cot = cots[
                    first // chunk * per : (first // chunk + 1) * per,
                    part * share : (part + 1) * share,
                ].reshape(chunk, D)
                c_t[:, to] = (cot.astype(F32) * gate).T.astype(BF)

    first_sum, second_sum = None, None
    for part in range(parts):
        at = slice(part * rows, (part + 1) * rows)
        one = dot(x_t[:, at], dhs[part][...])
        two = dot(c_t[:, at], acts[part][...])
        first_sum = one if first_sum is None else first_sum + one
        second_sum = two if second_sum is None else second_sum + two
    if side is None:
        grad_first[...] = first_sum.astype(BF)
        grad_second[...] = second_sum.T.astype(BF)
        return
    mine = side[0]
    half = D // 2
    whole_first[...] = first_sum.astype(BF)
    kept_first[...] = whole_first[pl.ds(pl.multiple_of(mine * half, half), half), :]
    sent_first[...] = whole_first[pl.ds(pl.multiple_of((1 - mine) * half, half), half), :]
    here = pl.program_id(0) // (pl.num_programs(0) // 2) == mine

    @pl.when(here)
    def _():
        kept_second[...] = second_sum.T.astype(BF)

    @pl.when(jnp.logical_not(here))
    def _():
        sent_second[...] = second_sum.T.astype(BF)


def expert_weights(xs, cots, gates, acts, dhs, side):
    parts = len(xs)
    rows = xs[0].shape[0]
    hidden_size = acts[0].shape[1]
    steps = hidden_size // FF_TILE
    in_specs = (
        [whole((rows, D))] * parts
        + [whole((rows, 1))] * parts
        + [pl.BlockSpec((rows, FF_TILE), lambda f, *_: (0, f))] * (2 * parts)
        + [whole(cots.shape)]
    )
    scratch = [pltpu.VMEM((D, parts * rows), BF), pltpu.VMEM((D, parts * rows), BF)]
    if side is None:
        out_specs = [
            pl.BlockSpec((D, FF_TILE), lambda f: (0, f)),
            pl.BlockSpec((FF_TILE, D), lambda f: (f, 0)),
        ]
        shapes = [(D, hidden_size), (hidden_size, D)]
    else:
        columns = pl.BlockSpec((D // 2, FF_TILE), lambda f, s: (0, f))

        def rows_of(place):
            def index(f, s):
                start = jnp.where(s[0] == 1, place, 1 - place) * (steps // 2)
                return (jnp.clip(f - start, 0, steps // 2 - 1), 0)

            return pl.BlockSpec((FF_TILE, D), index)

        out_specs = [columns, columns, rows_of(1), rows_of(0)]
        shapes = [(D // 2, hidden_size)] * 2 + [(hidden_size // 2, D)] * 2
        scratch = scratch + [pltpu.VMEM((D, FF_TILE), BF)]
    prefetched = () if side is None else (side,)
    return pl.pallas_call(
        functools.partial(expert_weights_kernel, parts, side is not None or None),
        grid_spec=pltpu.PrefetchScalarGridSpec(
            num_scalar_prefetch=len(prefetched),
            grid=(steps,),
            in_specs=in_specs,
            out_specs=out_specs,
            scratch_shapes=scratch,
        ),
        out_shape=[jax.ShapeDtypeStruct(shape, BF) for shape in shapes],
        compiler_params=params(("arbitrary",)),
        cost_estimate=cost(
            4 * parts * rows * D * hidden_size, 4 * (parts * rows + D) * hidden_size, share=1
        ),
        name="expert_weights",
    )(*prefetched, *xs, *gates, *acts, *dhs, cots)


def rms_back(values, factor, grad):
    inverse = inverse_rms(values)
    scaled = grad * factor
    mean = jnp.mean(scaled * values, axis=-1, keepdims=True)
    return (
        inverse * scaled - values * (inverse * inverse * inverse * mean),
        jnp.sum(grad * values * inverse, axis=0, keepdims=True),
    )


def undispatch(slot_col, parts):
    out = None
    offset = 0
    for part in parts:
        total = part.shape[0]
        place = lax.broadcasted_iota(jnp.int32, (slot_col.shape[0], total), 1) + offset
        found = dot((place == slot_col).astype(BF), part[...])
        out = found if out is None else out + found
        offset += total
    return out


def middle_back_kernel(parts, *refs):
    backs = refs[:parts]
    (
        slot_col, middle, cot, gain, out_left, out_right,
        grad_middle, grad_attn, grad_context, grad_gain, w_out,
    ) = refs[parts:]

    @pl.when(pl.program_id(0) == 0)
    def _():
        w_out[:, :SIDE] = out_left[...]
        w_out[:, SIDE:] = out_right[...]

    grad_normed = undispatch(slot_col[...], backs)
    part, gain_part = rms_back(middle[...], gain[...], grad_normed)
    grad = cot[...].astype(F32) + part
    grad_middle[...] = grad
    low = grad.astype(BF)
    grad_attn[...] = low
    grad_context[...] = dot(low, w_out[...], 1, 1).astype(BF)

    @pl.when(pl.program_id(0) == 0)
    def _():
        grad_gain[...] = gain_part

    @pl.when(pl.program_id(0) > 0)
    def _():
        grad_gain[...] += gain_part


def middle_back(backs, slot_col, middle, cot, gain, left, right):
    parts = len(backs)
    block = 256
    rows = pl.BlockSpec((block, D), lambda r: (r, 0))
    return pl.pallas_call(
        functools.partial(middle_back_kernel, parts),
        grid=(TOK // block,),
        in_specs=[whole(back.shape) for back in backs]
        + [
            pl.BlockSpec((block, 1), lambda r: (r, 0)),
            rows,
            rows,
            whole((1, D)),
            pl.BlockSpec((D, SIDE), lambda r: (0, 3)),
            pl.BlockSpec((D, SIDE), lambda r: (0, 3)),
        ],
        out_specs=[rows, rows, rows, whole((1, D))],
        scratch_shapes=[pltpu.VMEM((D, D), BF)],
        out_shape=[
            jax.ShapeDtypeStruct((TOK, D), F32),
            jax.ShapeDtypeStruct((TOK, D), BF),
            jax.ShapeDtypeStruct((TOK, D), BF),
            jax.ShapeDtypeStruct((1, D), F32),
        ],
        compiler_params=params(("arbitrary",)),
        cost_estimate=cost(2 * 2 * TOK * TOK * D + 2 * TOK * D * D, 16 * TOK * D, share=1),
        name="middle_back",
    )(*backs, slot_col, middle, cot, gain, left, right)


def mix_kernel(parts, *refs):
    backs = refs[:parts]
    slot_col, middle, gate, mixed = refs[parts:]
    mixed[...] = middle[...] + gate[...] * undispatch(slot_col[...], backs)


def mix(backs, slot_col, middle, gate):
    parts = len(backs)
    block = 256
    rows = pl.BlockSpec((block, D), lambda r: (r, 0))
    column = pl.BlockSpec((block, 1), lambda r: (r, 0))
    return pl.pallas_call(
        functools.partial(mix_kernel, parts),
        grid=(TOK // block,),
        in_specs=[whole(back.shape) for back in backs] + [column, rows, column],
        out_specs=rows,
        out_shape=jax.ShapeDtypeStruct((TOK, D), F32),
        compiler_params=params(("arbitrary",)),
        cost_estimate=cost(2 * 2 * TOK * TOK * D, 12 * TOK * D, share=1),
        name="mix",
    )(*backs, slot_col, middle, gate)


def tokens_back_kernel(g_left, g_right, left, right, tokens, gain, grad_middle, grad_tokens, grad_gain):
    grad_normed = dot(g_left[...], left[...], 1, 1) + dot(g_right[...], right[...], 1, 1)
    part, gain_part = rms_back(tokens[...].astype(F32), gain[...], grad_normed)
    grad_tokens[...] = grad_middle[...] + part

    @pl.when(pl.program_id(0) == 0)
    def _():
        grad_gain[...] = gain_part

    @pl.when(pl.program_id(0) > 0)
    def _():
        grad_gain[...] += gain_part


def tokens_back(g_left, g_right, left, right, tokens, gain, grad_middle):
    block = 256
    rows = pl.BlockSpec((block, D), lambda r: (r, 0))
    return pl.pallas_call(
        tokens_back_kernel,
        grid=(TOK // block,),
        in_specs=[
            pl.BlockSpec((block, SPLIT), lambda r: (r, 0)),
            pl.BlockSpec((block, SPLIT), lambda r: (r, 0)),
            whole((D, SPLIT)),
            whole((D, SPLIT)),
            rows,
            whole((1, D)),
            rows,
        ],
        out_specs=[rows, whole((1, D))],
        out_shape=[
            jax.ShapeDtypeStruct((TOK, D), F32),
            jax.ShapeDtypeStruct((1, D), F32),
        ],
        compiler_params=params(("arbitrary",)),
        cost_estimate=cost(6 * TOK * D * D, 16 * TOK * D, share=1),
        name="tokens_back",
    )(g_left, g_right, left, right, tokens, gain, grad_middle)


def weights_back_kernel(turned, grads, out):
    out[...] = dot(turned[...], grads[...])


def weights_back(turned, grads):
    block = 384
    columns = grads.shape[1]
    return pl.pallas_call(
        weights_back_kernel,
        grid=(columns // block,),
        in_specs=[whole(turned.shape), pl.BlockSpec((TOK, block), lambda c: (0, c))],
        out_specs=pl.BlockSpec((D, block), lambda c: (0, c)),
        out_shape=jax.ShapeDtypeStruct((D, columns), F32),
        compiler_params=params(("arbitrary",)),
        cost_estimate=cost(2 * TOK * D * columns, 2 * TOK * (D + columns) + 4 * D * columns, share=1),
        name="weights_back",
    )(turned, grads)


def swap(block, axis, bit):
    size = lax.axis_size(axis)
    return lax.ppermute(block, axis, [(place, place ^ bit) for place in range(size)])


def on_upper(axis, bit):
    return (lax.axis_index(axis) // bit) % 2 == 1


def axis_bits(*axes):
    found = []
    for axis in axes:
        bit = lax.axis_size(axis) // 2
        while bit >= 1:
            found.append((axis, bit))
            bit //= 2
    return found


def orders():
    bits = axis_bits("dp", "expert")
    dp = [at for at, (axis, _) in enumerate(bits) if axis == "dp"]
    core = len(bits) - 1
    along = [at for at, (axis, bit) in enumerate(bits) if axis == "expert" and bit == 2]
    rest = [at for at in range(core) if at not in dp and at not in along]
    return (rest + along + dp + [core], rest + dp + along + [core])


def gather_rows(shard, order, *before_dp):
    bits = axis_bits("dp", "expert")
    block = shard.reshape((1,) * len(bits) + shard.shape)
    for place in order:
        axis, bit = bits[place]
        if axis == "dp" and before_dp:
            block = after(block, *before_dp)
        other = swap(block, axis, bit)
        upper = on_upper(axis, bit)
        block = jnp.concatenate(
            [jnp.where(upper, other, block), jnp.where(upper, block, other)], axis=place
        )
    return block.reshape((-1,) + shard.shape[1:])


def scatter_start(total):
    bits = axis_bits("dp", "expert")
    rows = total.shape[0] >> len(bits)
    return total.reshape((2,) * len(bits) + (rows,) + total.shape[1:])


def scatter_step(block, place, *others):
    axis, bit = axis_bits("dp", "expert")[place]
    lower = lax.slice_in_dim(block, 0, 1, axis=place)
    higher = lax.slice_in_dim(block, 1, 2, axis=place)
    upper = on_upper(axis, bit)
    sent = jnp.where(upper, lower, higher).astype(BF)
    kept = after(jnp.where(upper, higher, lower), *others)
    return kept + swap(sent, axis, bit).astype(F32)


def scatter_rest(block, order):
    for place in order:
        block = scatter_step(block, place)
    return block.reshape(block.shape[len(axis_bits("dp", "expert")) :])


def sum_all(total):
    for axis, bit in axis_bits("dp", "expert"):
        total = total + swap(total, axis, bit)
    return total


def gather_dp(block, axis, other=None):
    if lax.axis_size("dp") != 2:
        return lax.all_gather(block, "dp", axis=axis, tiled=True)
    if other is None:
        other = swap(block, "dp", 1)
    upper = on_upper("dp", 1)
    return jnp.concatenate(
        [jnp.where(upper, other, block), jnp.where(upper, block, other)], axis=axis
    )


def scatter_dp(halves, *others):
    if len(halves) == 1:
        return lax.psum_scatter(
            halves[0][None], "dp", scatter_dimension=1, tiled=True
        ).astype(F32)
    kept, sent = halves
    return (after(kept, *others).astype(F32) + swap(sent, "dp", 1).astype(F32))[None]


def after(value, *others):
    return lax.optimization_barrier((value, *others))[0]


def body(
    tokens, seq_ids, routes, cotangent, w_query, w_key, w_value, w_out,
    rel_table, gain_attn, gain_ffn, router, expert_in, expert_out,
):
    experts = lax.axis_size("expert")
    capacity = 2 * TOK // experts
    shard = w_query.shape[0]
    lanes = -(-(experts + 2) // LANES) * LANES

    small = jnp.concatenate(
        [
            router,
            gain_attn[:, None],
            gain_ffn[:, None],
            jnp.zeros((shard, lanes - experts - 2), BF),
        ],
        axis=1,
    )
    first, second = orders()
    kinds = (w_query, w_key, w_value, w_out)
    paired = lax.axis_size("dp") == 2
    own_first, own_second = expert_in[0], expert_out[0]
    first_cut, second_cut = own_first.shape[1] // 2, own_second.shape[0] // 2
    early = [swap(own_first[:, :first_cut], "dp", 1)] if paired else []
    table = gather_dp(rel_table, 0)
    left = gather_rows(
        jnp.concatenate([w[:, :SIDE] for w in kinds], axis=1), first, table, *early
    )
    right = gather_rows(
        jnp.concatenate([w[:, SIDE:] for w in kinds] + [small], axis=1), second, table, *early
    )

    slot_col, slot_row, sending_cot = make_slots(routes, cotangent, experts, capacity)

    def exchange(rows):
        return lax.all_to_all(
            rows.reshape(experts, -1, D), "expert", split_axis=0, concat_axis=0, tiled=True
        )

    cots = exchange(after(sending_cot, left, right))
    if paired:
        early.append(swap(after(own_first[:, first_cut:], left, right), "dp", 1))
        early.append(swap(after(own_second[:second_cut], left, right), "dp", 1))
        late = swap(after(own_second[second_cut:], *early), "dp", 1)
        other_first = jnp.concatenate(early[:2], axis=1)
        other_second = jnp.concatenate([early[2], late], axis=0)
    else:
        other_first = other_second = None
    w_first = gather_dp(own_first, 0, other_first)
    w_second = gather_dp(own_second, 0, other_second)

    extra = right[:, SPLIT + SIDE :]
    full_router = jnp.where(jnp.arange(lanes)[None, :] < experts, extra, jnp.zeros((), BF))
    router_t = full_router.T
    attn_gain = extra[:, experts].astype(F32).reshape(1, D)
    ffn_gain = extra[:, experts + 1].astype(F32).reshape(1, D)

    turned, qkv = project(tokens, attn_gain, left, right)
    table = table.astype(F32)
    query_features, key_features = lane_features(seq_ids.reshape(TOK, 1), table)
    band = jnp.sum(band_onehot()[None, :, :] * table.T[:, None, :], axis=2)[:, None, :]
    context, lse = attend(qkv, query_features, key_features, band)

    middle, *sending, gate = make_middle(
        context, tokens, left, right, ffn_gain, full_router, routes, slot_row, experts, capacity
    )
    sending[0] = after(sending[0], cots, *early)
    rows_in = [exchange(part).reshape(-1, D) for part in sending]
    mine = lax.axis_index("expert").astype(jnp.int32).reshape(1, 1)
    acts, dhs, results, grads, gates, router_parts = zip(
        *(
            run_expert(
                part, rows, cots, w_first, w_second, full_router, router_t, mine, experts
            )
            for part, rows in enumerate(rows_in)
        )
    )
    grads_home = [exchange(part).reshape(-1, D) for part in grads]
    weight_parts = expert_weights(
        rows_in,
        cots,
        (after(gates[0], grads_home[0]), *gates[1:]),
        acts,
        dhs,
        lax.axis_index("dp").astype(jnp.int32).reshape(1) if paired else None,
    )
    half = len(weight_parts) // 2
    grad_first, grad_second = weight_parts[:half], weight_parts[half:]
    results_home = [
        exchange(after(part, *grads_home)).reshape(-1, D) for part in results
    ]
    grads_home[0] = after(grads_home[0], *weight_parts)
    grad_middle, grad_attn, grad_context, grad_gain_f = middle_back(
        grads_home, slot_col, middle, cotangent, ffn_gain, left, right
    )
    down, down_other = first[::-1], second[::-1]
    out_block = scatter_step(scatter_start(dot(context, grad_attn, 0, 0)), down_other[0])

    def back(half, *others):
        return attend_back(
            half, qkv, after(grad_context, *others), query_features, key_features, lse, band
        )

    g_left, tiles_left, diagonals_left = back(0)
    left_block = scatter_start(weights_back(turned, after(g_left, out_block)))
    g_right, tiles_right, diagonals_right = back(1, left_block, out_block, results_home[0])
    out_block = scatter_step(out_block, down_other[1], g_right)
    left_block = scatter_step(left_block, down[0], g_right)
    grad_expert_out = scatter_dp(grad_second, g_right)
    grad_right = weights_back(
        turned, after(g_right, results_home[1], out_block, left_block, grad_expert_out)
    )
    grad_tokens, grad_gain_a = tokens_back(
        g_left, after(g_right, grad_right), left, right, tokens, attn_gain, grad_middle
    )
    mixed = mix(results_home, slot_col, middle, after(gate, grad_tokens))
    right_block = scatter_step(scatter_start(grad_right), down_other[0], grad_tokens)
    left_block = scatter_step(left_block, down[1], grad_tokens)
    out_block = scatter_step(out_block, down_other[2], grad_tokens)
    near = 2 + len(axis_bits("dp"))
    for place in down_other[1:near]:
        right_block = scatter_step(right_block, place)
    for place in down[2:near]:
        left_block = scatter_step(left_block, place)
    for place in down_other[3:near]:
        out_block = scatter_step(out_block, place)
    joined = jnp.concatenate([left_block, right_block, out_block], axis=-1)
    grad_expert_in = scatter_dp(grad_first, joined)
    dense = scatter_rest(joined, down[near:])
    grad_left, grad_right = dense[:, :SPLIT], dense[:, SPLIT : 2 * SPLIT]
    grad_w_out = dense[:, 2 * SPLIT :]
    tiles = jnp.concatenate([tiles_left, tiles_right], axis=0)
    diagonals = jnp.concatenate([diagonals_left, diagonals_right], axis=0)
    grad_router = sum(router_parts)[:, :experts]
    grad_table = table_gradient(tiles, diagonals)

    sizes = (D * experts, D, D, BUCKETS * HEADS)
    sums = sum_all(
        jnp.concatenate(
            [
                part.reshape(-1, LANES)
                for part in (grad_router, grad_gain_a, grad_gain_f, grad_table)
            ],
            axis=0,
        )
    ).reshape(-1)
    ends = [sum(sizes[: at + 1]) for at in range(len(sizes))]
    grad_router, grad_gain_a, grad_gain_f, grad_table = (
        sums[end - size : end] for end, size in zip(ends, sizes)
    )
    number = lax.axis_index("dp") * experts + lax.axis_index("expert")
    table_height = BUCKETS // lax.axis_size("dp")

    def own(rows, height, place):
        return lax.dynamic_slice_in_dim(rows, place * height, height, 0)

    return (
        mixed,
        grad_tokens,
        *(
            jnp.concatenate(
                [side[:, kind * SIDE : (kind + 1) * SIDE] for side in (grad_left, grad_right)],
                axis=1,
            )
            for kind in range(3)
        ),
        grad_w_out,
        own(grad_table.reshape(BUCKETS, HEADS), table_height, lax.axis_index("dp")),
        own(grad_gain_a, shard, number),
        own(grad_gain_f, shard, number),
        own(grad_router.reshape(D, experts), shard, number),
        grad_expert_in,
        grad_expert_out,
    )


def solution(mesh):
    rows = P(("dp", "expert"), None)
    flat = P(("dp", "expert"))
    expert = P("expert", "dp", None)
    return jax.shard_map(
        body,
        mesh=mesh,
        in_specs=(
            rows, flat, rows, rows, rows, rows, rows, rows,
            P("dp", None), flat, flat, rows, expert, expert,
        ),
        out_specs=(
            rows, rows, rows, rows, rows, rows,
            P("dp", None), flat, flat, rows, expert, expert,
        ),
        check_vma=False,
    )
```

```python
import functools

import jax
import jax.numpy as jnp
from jax import lax
from jax.experimental import pallas as pl
from jax.experimental.pallas import tpu as pltpu
from jax.sharding import PartitionSpec as P

D = 768
HEADS = 12
HEAD_DIM = 64
BUCKETS = 32
TOK = 1024
TILE = 128
TILES = TOK // TILE
QBLK = 256
FF_TILE = 512
EXPERT_TILE = 512
EXPERT_ROWS = 1024
HALVES = 2
SIDE = D // 2
SPLIT = 3 * SIDE
PAIRS = HEADS // 2
SIDE_PAIRS = PAIRS // 2
COST_SHARE = 0.05
LANES = 128

EPSILON = 1e-06
DISTANCE_EDGES = (12, 16, 23, 32, 46, 64, 91)
FAR_BEFORE = 15
FAR_AFTER = 31
UNPAIRED = -1e30
BF = jnp.bfloat16
F32 = jnp.float32
VMEM_LIMIT = 56 * 1024 * 1024


def dot(left, right, left_dim=1, right_dim=0):
    return lax.dot_general(
        left, right, (((left_dim,), (right_dim,)), ((), ())), preferred_element_type=F32
    )


def params(semantics=None):
    return pltpu.CompilerParams(vmem_limit_bytes=VMEM_LIMIT, dimension_semantics=semantics)


def cost(flops, bytes_accessed, transcendentals=0, share=COST_SHARE):
    return pl.CostEstimate(
        flops=int(flops * share),
        bytes_accessed=int(bytes_accessed * share),
        transcendentals=int(transcendentals * share),
    )


def whole(shape):
    return pl.BlockSpec(shape, lambda *_: (0,) * len(shape))


def inverse_rms(values):
    return lax.rsqrt(jnp.mean(values * values, axis=-1, keepdims=True) + EPSILON)


def bucket_of(offset):
    distance = jnp.abs(offset)
    distant = 8 + sum(((distance >= boundary).astype(jnp.int32) for boundary in DISTANCE_EDGES))
    return jnp.where(distance < 8, distance, distant) + jnp.where(offset > 0, 16, 0)


def place_in_buffers(route, rank, experts, capacity):
    share = capacity // HALVES
    part = (rank >= share).astype(jnp.int32)
    return part * (experts * share) + route * share + (rank - part * share)


def slots_kernel(experts, capacity, route_col, route_row, cot, slot_col, slot_row, sending):
    padded = -(-experts // LANES) * LANES
    picked = (
        lax.broadcasted_iota(jnp.int32, (TOK, padded), 1) == route_col[...]
    ).astype(BF)
    picked_t = (
        lax.broadcasted_iota(jnp.int32, (padded, TOK), 0) == route_row[...]
    ).astype(BF)
    upto = (
        lax.broadcasted_iota(jnp.int32, (TOK, TOK), 0)
        <= lax.broadcasted_iota(jnp.int32, (TOK, TOK), 1)
    ).astype(BF)
    from_t = (
        lax.broadcasted_iota(jnp.int32, (TOK, TOK), 0)
        >= lax.broadcasted_iota(jnp.int32, (TOK, TOK), 1)
    ).astype(BF)
    counts = dot(from_t, picked) * picked.astype(F32)
    rank = jnp.sum(counts, axis=1, keepdims=True).astype(jnp.int32) - 1
    slot_col[...] = place_in_buffers(route_col[...], rank, experts, capacity)
    counts_t = dot(picked_t, upto) * picked_t.astype(F32)
    rank_row = jnp.sum(counts_t, axis=0, keepdims=True).astype(jnp.int32) - 1
    slot_row[...] = place_in_buffers(route_row[...], rank_row, experts, capacity)
    dispatch(route_row[...] * capacity + rank_row, cot[...], [sending])


def dispatch(row, rows, parts):
    step = 512
    offset = 0
    for sending in parts:
        for first in range(0, sending.shape[0], step):
            chosen = (
                lax.broadcasted_iota(jnp.int32, (step, TOK), 0) + (first + offset) == row
            ).astype(BF)
            sending[first : first + step, :] = dot(chosen, rows).astype(BF)
        offset += sending.shape[0]


def make_slots(routes, cotangent, experts, capacity):
    total = experts * capacity
    return pl.pallas_call(
        functools.partial(slots_kernel, experts, capacity),
        out_shape=(
            jax.ShapeDtypeStruct((TOK, 1), jnp.int32),
            jax.ShapeDtypeStruct((1, TOK), jnp.int32),
            jax.ShapeDtypeStruct((total, D), BF),
        ),
        compiler_params=params(),
        cost_estimate=cost(2 * total * TOK * D, 6 * total * D),
        name="slots",
    )(routes, routes.reshape(1, TOK), cotangent)


def project_kernel(tokens, gain, left, right, turned, qkv):
    x = tokens[...].astype(F32)
    wide = x * inverse_rms(x) * gain[...]
    low = wide.astype(BF)
    turned[...] = wide.T.astype(BF)
    qkv[:, :SPLIT] = dot(low, left[...]).astype(BF)
    qkv[:, SPLIT:] = dot(low, right[...]).astype(BF)


def project(tokens, gain, left, right):
    block = 256
    rows = pl.BlockSpec((block, D), lambda r: (r, 0))
    return pl.pallas_call(
        project_kernel,
        grid=(TOK // block,),
        in_specs=[rows, whole((1, D)), whole((D, SPLIT)), whole((D, SPLIT))],
        out_specs=[
            pl.BlockSpec((D, block), lambda r: (0, r)),
            pl.BlockSpec((block, 3 * D), lambda r: (r, 0)),
        ],
        out_shape=[
            jax.ShapeDtypeStruct((D, TOK), BF),
            jax.ShapeDtypeStruct((TOK, 3 * D), BF),
        ],
        compiler_params=params(("arbitrary",)),
        cost_estimate=cost(6 * TOK * D * D, 12 * TOK * D),
        name="project",
    )(tokens, gain, left, right)


def lane_features(seq_col, rel_table):
    lane = jnp.arange(LANES, dtype=jnp.int32)[None, :]
    feature = lane % HEAD_DIM
    tile = jnp.arange(TOK, dtype=jnp.int32)[:, None] // TILE
    on_tile = feature - 4
    query_features = jnp.where(
        feature < 4,
        jnp.where(feature == seq_col, 0.0, UNPAIRED),
        jnp.where(on_tile == tile, 1.0, 0.0),
    ).astype(BF)
    wide = jnp.arange(D, dtype=jnp.int32)[None, :]
    feature = wide % HEAD_DIM
    on_tile = feature - 4
    swapped = jnp.arange(HEADS, dtype=jnp.int32) ^ 1
    before = jnp.repeat(rel_table[FAR_BEFORE][swapped], HEAD_DIM)[None, :]
    after = jnp.repeat(rel_table[FAR_AFTER][swapped], HEAD_DIM)[None, :]
    apart = tile - on_tile
    far = jnp.where(apart >= 2, after, jnp.where(apart <= -2, before, 0.0))
    key_features = jnp.where(
        feature < 4,
        jnp.where(feature == seq_col, 1.0, 0.0),
        jnp.where(on_tile < TILES, far, 0.0),
    ).astype(BF)
    return query_features, key_features


def band_offsets():
    place = jnp.arange(4 * LANES, dtype=jnp.int32)
    return 255 - (place + 383) % 512


def band_onehot():
    return (
        bucket_of(band_offsets())[:, None] == jnp.arange(BUCKETS, dtype=jnp.int32)[None, :]
    ).astype(F32)


def near_rows(tile):
    first = max(tile - 1, 0)
    last = min(tile + 2, TILES)
    return first, last


def spread_band(values):
    wide = jnp.broadcast_to(values, (3 * TILE, 4 * LANES))
    return pltpu.roll(wide, 0, 1, stride=1, stride_axis=0)[:, :TILE]


def attend_kernel(q_ref, k_ref, v_ref, qx_ref, kx_ref, band_ref, out_ref, lse_ref, st, pb, ot):
    low = lax.broadcasted_iota(jnp.int32, (TOK, LANES), 1) < HEAD_DIM
    v_t = v_ref[...].astype(F32).T.astype(BF)
    for side in range(2):
        own = low if side == 0 else ~low
        queries = jnp.where(own, q_ref[...], qx_ref[...])
        keys = jnp.where(own, k_ref[...], kx_ref[...])
        band = spread_band(band_ref[side])
        for block in range(TOK // QBLK):
            rows = slice(block * QBLK, (block + 1) * QBLK)
            slot = block % 2
            st[slot] = dot(keys, queries[rows], 1, 1)
            for part in range(QBLK // TILE):
                tile = block * (QBLK // TILE) + part
                first, last = near_rows(tile)
                at = (slot, slice(first * TILE, last * TILE), slice(part * TILE, (part + 1) * TILE))
                st[at] += band[(first - tile + 1) * TILE : (last - tile + 1) * TILE]
            top = jnp.max(st[slot, 0:TILE], axis=0, keepdims=True)
            for chunk in range(1, TILES):
                top = jnp.maximum(
                    top,
                    jnp.max(
                        st[slot, chunk * TILE : (chunk + 1) * TILE], axis=0, keepdims=True
                    ),
                )
            total = jnp.zeros((1, QBLK), F32)
            for chunk in range(TILES):
                at = slice(chunk * TILE, (chunk + 1) * TILE)
                raised = jnp.exp(st[slot, at] - top)
                total = total + jnp.sum(raised, axis=0, keepdims=True)
                pb[slot, at] = raised.astype(BF)
            half = slice(side * HEAD_DIM, (side + 1) * HEAD_DIM)
            ot[half, rows] = dot(v_t[half], pb[slot]) * (1.0 / total)
            lse_ref[side, :, rows] = top + jnp.log(total)
    out_ref[...] = ot[...].T.astype(BF)


def attend(qkv, query_features, key_features, band):
    return pl.pallas_call(
        attend_kernel,
        grid=(PAIRS,),
        in_specs=[
            *(
                pl.BlockSpec(
                    (TOK, LANES),
                    lambda p, kind=kind: (
                        0,
                        p // SIDE_PAIRS * (3 * SIDE_PAIRS) + kind * SIDE_PAIRS + p % SIDE_PAIRS,
                    ),
                )
                for kind in range(3)
            ),
            whole((TOK, LANES)),
            pl.BlockSpec((TOK, LANES), lambda p: (0, p)),
            pl.BlockSpec((2, 1, 4 * LANES), lambda p: (p, 0, 0)),
        ],
        out_specs=[
            pl.BlockSpec((TOK, LANES), lambda p: (0, p)),
            pl.BlockSpec((2, 1, TOK), lambda p: (p, 0, 0)),
        ],
        out_shape=[
            jax.ShapeDtypeStruct((TOK, D), BF),
            jax.ShapeDtypeStruct((HEADS, 1, TOK), F32),
        ],
        scratch_shapes=[
            pltpu.VMEM((2, TOK, QBLK), F32),
            pltpu.VMEM((2, TOK, QBLK), BF),
            pltpu.VMEM((LANES, TOK), F32),
        ],
        compiler_params=params(("arbitrary",)),
        cost_estimate=cost(2 * 3 * HEADS * TOK * TOK * 256, 10 * TOK * D, HEADS * TOK * TOK),
        name="attend",
    )(qkv, qkv, qkv, query_features, key_features, band)


def attend_back_kernel(
    q_ref, k_ref, v_ref, do_ref, qx_ref, kx_ref, lse_ref, band_ref,
    grad_ref, tiles_ref, diag_ref,
    st, dp, pb, sb, dqt, dkt, dvt, near,
):
    low = lax.broadcasted_iota(jnp.int32, (TOK, LANES), 1) < HEAD_DIM
    k_t = k_ref[...].astype(F32).T.astype(BF)
    for side in range(2):
        own = low if side == 0 else ~low
        queries = jnp.where(own, q_ref[...], qx_ref[...])
        keys = jnp.where(own, k_ref[...], kx_ref[...])
        values = jnp.where(own, v_ref[...], jnp.zeros((), BF))
        band = spread_band(band_ref[side])
        near[...] = jnp.zeros_like(near)
        half = slice(side * HEAD_DIM, (side + 1) * HEAD_DIM)
        for block in range(TOK // QBLK):
            rows = slice(block * QBLK, (block + 1) * QBLK)
            slot = block % 2
            st[slot] = dot(keys, queries[rows], 1, 1)
            dp[slot] = dot(values, do_ref[rows, :], 1, 1)
            for part in range(QBLK // TILE):
                tile = block * (QBLK // TILE) + part
                first, last = near_rows(tile)
                at = (slot, slice(first * TILE, last * TILE), slice(part * TILE, (part + 1) * TILE))
                st[at] += band[(first - tile + 1) * TILE : (last - tile + 1) * TILE]
            lse = lse_ref[side, :, rows]
            spread = jnp.zeros((1, QBLK), F32)
            for chunk in range(TILES):
                at = slice(chunk * TILE, (chunk + 1) * TILE)
                weights = jnp.exp(st[slot, at] - lse)
                st[slot, at] = weights
                pb[slot, at] = weights.astype(BF)
                spread = spread + jnp.sum(weights * dp[slot, at], axis=0, keepdims=True)
            for chunk in range(TILES):
                at = slice(chunk * TILE, (chunk + 1) * TILE)
                sb[slot, at] = (st[slot, at] * (dp[slot, at] - spread)).astype(BF)
            for part in range(QBLK // TILE):
                tile = block * (QBLK // TILE) + part
                first, last = near_rows(tile)
                at = (slot, slice(first * TILE, last * TILE), slice(part * TILE, (part + 1) * TILE))
                near[(first - tile + 1) * TILE : (last - tile + 1) * TILE, :TILE] += sb[at].astype(F32)
            dv = dot(pb[slot], do_ref[rows, :])
            dk = dot(sb[slot], queries[rows])
            if block == 0:
                dvt[side] = dv
                dkt[side] = dk
            else:
                dvt[side] += dv
                dkt[side] += dk
            dqt[half, rows] = dot(k_t[half], sb[slot])
        for tile in range(TILES):
            tiles_ref[side, tile : tile + 1, :] = jnp.sum(
                dkt[side, tile * TILE : (tile + 1) * TILE], axis=0, keepdims=True
            )
        folded = near[0:8, :]
        for first in range(8, 3 * TILE, 8):
            folded = folded + pltpu.roll(near[first : first + 8, :], 4 * LANES - first, 1)
        diagonal = folded[0:1]
        for row in range(1, 8):
            diagonal = diagonal + pltpu.roll(folded[row : row + 1], 4 * LANES - row, 1)
        diag_ref[side] = diagonal
    found = (
        dqt[...].T.astype(BF),
        jnp.where(low, dkt[0], dkt[1]).astype(BF),
        jnp.where(low, dvt[0], dvt[1]).astype(BF),
    )
    for pair in range(SIDE_PAIRS):

        @pl.when(pl.program_id(0) == pair)
        def _():
            for kind in range(3):
                first = kind * SIDE + pair * LANES
                grad_ref[:, first : first + LANES] = found[kind]


def attend_back(half, qkv, grad_context, query_features, key_features, lse, band):
    first = half * SIDE_PAIRS
    column = pl.BlockSpec((TOK, LANES), lambda p: (0, first + p))
    return pl.pallas_call(
        attend_back_kernel,
        grid=(SIDE_PAIRS,),
        in_specs=[
            *(
                pl.BlockSpec(
                    (TOK, LANES), lambda p, kind=kind: (0, (3 * half + kind) * SIDE_PAIRS + p)
                )
                for kind in range(3)
            ),
            column,
            whole((TOK, LANES)),
            column,
            pl.BlockSpec((2, 1, TOK), lambda p: (first + p, 0, 0)),
            pl.BlockSpec((2, 1, 4 * LANES), lambda p: (first + p, 0, 0)),
        ],
        out_specs=[
            whole((TOK, SPLIT)),
            pl.BlockSpec((2, TILES, LANES), lambda p: (p, 0, 0)),
            pl.BlockSpec((2, 1, 4 * LANES), lambda p: (p, 0, 0)),
        ],
        out_shape=[
            jax.ShapeDtypeStruct((TOK, SPLIT), BF),
            jax.ShapeDtypeStruct((HEADS // 2, TILES, LANES), F32),
            jax.ShapeDtypeStruct((HEADS // 2, 1, 4 * LANES), F32),
        ],
        scratch_shapes=[
            pltpu.VMEM((2, TOK, QBLK), F32),
            pltpu.VMEM((2, TOK, QBLK), F32),
            pltpu.VMEM((2, TOK, QBLK), BF),
            pltpu.VMEM((2, TOK, QBLK), BF),
            pltpu.VMEM((LANES, TOK), F32),
            pltpu.VMEM((2, TOK, LANES), F32),
            pltpu.VMEM((2, TOK, LANES), F32),
            pltpu.VMEM((3 * TILE, 4 * LANES), F32),
        ],
        compiler_params=params(("arbitrary",)),
        cost_estimate=cost(5 * HEADS * TOK * TOK * 256, 8 * TOK * D, HEADS * TOK * TOK // 2, share=0.3),
        name="attend_back",
    )(qkv, qkv, qkv, grad_context, query_features, key_features, lse, band)


def table_gradient(tiles, diagonals):
    near = jnp.einsum(
        "hl,lb->bh", diagonals[:, 0, :], band_onehot(), precision=lax.Precision.HIGHEST
    )
    sums = jnp.concatenate(
        [tiles[h : h + 1, :, (HEAD_DIM if h % 2 == 0 else 0) + 4 :][:, :, :TILES] for h in range(HEADS)],
        axis=0,
    )
    apart = (
        jnp.arange(TILES, dtype=jnp.int32)[:, None] - jnp.arange(TILES, dtype=jnp.int32)[None, :]
    )[None]
    before = jnp.sum(jnp.where(apart <= -2, sums, 0.0), axis=(1, 2))
    after = jnp.sum(jnp.where(apart >= 2, sums, 0.0), axis=(1, 2))
    place = jnp.arange(BUCKETS, dtype=jnp.int32)[:, None]
    return (
        near
        + jnp.where(place == FAR_BEFORE, before[None, :], 0.0)
        + jnp.where(place == FAR_AFTER, after[None, :], 0.0)
    )


def middle_kernel(context, tokens, out_left, out_right, gain, router, route_col, slot_row, experts,
                  middle, sending_low, sending_high, gate, normed, w_out):
    w_out[:, :SIDE] = out_left[...]
    w_out[:, SIDE:] = out_right[...]
    for first in range(0, TOK, 256):
        at = slice(first, first + 256)
        mid = tokens[at, :].astype(F32) + dot(context[at, :], w_out[...])
        middle[at, :] = mid
        low = (mid * inverse_rms(mid) * gain[...]).astype(BF)
        normed[at, :] = low
        probs = router_softmax(low, router[...], experts)
        lane = lax.broadcasted_iota(jnp.int32, probs.shape, 1)
        gate[at, :] = jnp.sum(
            jnp.where(lane == route_col[at, :], probs, 0.0), axis=1, keepdims=True
        )
    dispatch(slot_row[...], normed[...], [sending_low, sending_high])


def router_softmax(rows, router, experts):
    logits = dot(rows, router)
    lane = lax.broadcasted_iota(jnp.int32, logits.shape, 1)
    logits = jnp.where(lane < experts, logits, UNPAIRED)
    raised = jnp.exp(logits - jnp.max(logits, axis=1, keepdims=True))
    return raised / jnp.sum(raised, axis=1, keepdims=True)


def make_middle(context, tokens, left, right, gain, router, routes, slot_row, experts, capacity):
    total = experts * capacity

    def kernel(*refs):
        middle_kernel(*refs[:8], experts, *refs[8:])

    out_half = pl.BlockSpec((D, SIDE), lambda r: (0, 3))
    return pl.pallas_call(
        kernel,
        grid=(1,),
        in_specs=[
            whole((TOK, D)),
            whole((TOK, D)),
            out_half,
            out_half,
            whole((1, D)),
            whole(router.shape),
            whole((TOK, 1)),
            whole((1, TOK)),
        ],
        out_specs=(
            whole((TOK, D)),
            whole((total // 2, D)),
            whole((total // 2, D)),
            whole((TOK, 1)),
        ),
        out_shape=(
            jax.ShapeDtypeStruct((TOK, D), F32),
            jax.ShapeDtypeStruct((total // 2, D), BF),
            jax.ShapeDtypeStruct((total // 2, D), BF),
            jax.ShapeDtypeStruct((TOK, 1), F32),
        ),
        scratch_shapes=[pltpu.VMEM((TOK, D), BF), pltpu.VMEM((D, D), BF)],
        compiler_params=params(),
        cost_estimate=cost(2 * total * TOK * D + 2 * TOK * D * D, 12 * TOK * D + 2 * total * D),
        name="middle",
    )(context, tokens, left, right, gain, router, routes, slot_row)


def gelu_parts(v):
    size = jnp.abs(v)
    t = 1.0 / (1.0 + (0.3275911 * 0.7071067811865476) * size)
    bell = jnp.exp(-0.5 * (v * v))
    series = t * (
        0.5 * 0.254829592
        + t * (0.5 * -0.284496736 + t * (0.5 * 1.421413741 + t * (0.5 * -1.453152027 + t * (0.5 * 1.061405429))))
    )
    tail = series * bell
    phi = jnp.where(v < 0, tail, 1.0 - tail)
    return v * phi, phi + v * (bell * 0.3989422804014327)


def expert_kernel(experts, x, c3, w_first, w_second, router, router_t, mine, *refs):
    act_ref, dh_ref, result, grad_x, gate_ref, grad_router, acc_r, acc_x = refs[-8:]
    step = pl.program_id(0)
    rows = x.shape[0]
    chunk = EXPERT_ROWS
    share = c3.shape[1]
    per = chunk // share

    @pl.when(step == 0)
    def _():
        acc_r[...] = jnp.zeros_like(acc_r)
        acc_x[...] = jnp.zeros_like(acc_x)

    for first in range(0, rows, chunk):
        at = slice(first, first + chunk)
        sources = slice(first // share, first // share + per)
        hidden = dot(x[at, :], w_first[...])
        grad_act = dot(c3[sources].reshape(chunk, D), w_second[...], 1, 1)
        act, slope = gelu_parts(hidden)
        act = act.astype(BF)
        grad_hidden = (grad_act * slope).astype(BF)
        act_ref[at, :] = act
        dh_ref[at, :] = grad_hidden
        acc_r[at, :] += dot(act, w_second[...])
        acc_x[at, :] += dot(grad_hidden, w_first[...], 1, 1)

    @pl.when(step == pl.num_programs(0) - 1)
    def _():
        total_router = jnp.zeros(grad_router.shape, F32)
        for first in range(0, rows, chunk):
            at = slice(first, first + chunk)
            sources = slice(first // share, first // share + per)
            rounded = acc_r[at, :].astype(BF)
            result[at, :] = rounded
            probs = router_softmax(x[at, :], router[...], experts)
            lane = lax.broadcasted_iota(jnp.int32, probs.shape, 1)
            here = lane == mine[0, 0]
            gate = jnp.sum(jnp.where(here, probs, 0.0), axis=1, keepdims=True)
            grad_gate = jnp.sum(
                c3[sources].reshape(chunk, D).astype(F32) * rounded.astype(F32), axis=1, keepdims=True
            )
            grad_logits = (
                probs * (jnp.where(here, grad_gate, 0.0) - gate * grad_gate)
            ).astype(BF)
            gate_ref[at, :] = gate
            grad_x[at, :] = (acc_x[at, :] * gate + dot(grad_logits, router_t[...])).astype(BF)
            total_router = total_router + dot(x[at, :], grad_logits, 0, 0)
        grad_router[...] = total_router


def run_expert(part, x, c, w_first, w_second, router, router_t, mine, experts):
    rows = x.shape[0]
    hidden_size = w_first.shape[1]
    lanes = router.shape[1]
    sources, capacity = c.shape[:2]
    half = pl.BlockSpec((sources, capacity // HALVES, D), lambda f: (0, part, 0))
    return pl.pallas_call(
        functools.partial(expert_kernel, experts),
        grid=(hidden_size // EXPERT_TILE,),
        in_specs=[
            whole((rows, D)),
            half,
            pl.BlockSpec((D, EXPERT_TILE), lambda f: (0, f)),
            pl.BlockSpec((EXPERT_TILE, D), lambda f: (f, 0)),
            whole((D, lanes)),
            whole((lanes, D)),
            pl.BlockSpec(memory_space=pltpu.SMEM),
        ],
        out_specs=[
            pl.BlockSpec((rows, EXPERT_TILE), lambda f: (0, f)),
            pl.BlockSpec((rows, EXPERT_TILE), lambda f: (0, f)),
            whole((rows, D)),
            whole((rows, D)),
            whole((rows, 1)),
            whole((D, lanes)),
        ],
        out_shape=[
            jax.ShapeDtypeStruct((rows, hidden_size), BF),
            jax.ShapeDtypeStruct((rows, hidden_size), BF),
            jax.ShapeDtypeStruct((rows, D), BF),
            jax.ShapeDtypeStruct((rows, D), BF),
            jax.ShapeDtypeStruct((rows, 1), F32),
            jax.ShapeDtypeStruct((D, lanes), F32),
        ],
        scratch_shapes=[pltpu.VMEM((rows, D), F32), pltpu.VMEM((rows, D), F32)],
        compiler_params=params(("arbitrary",)),
        cost_estimate=cost(
            8 * rows * D * hidden_size, 4 * rows * hidden_size + 4 * D * hidden_size
        ),
        name="expert",
    )(x, c, w_first, w_second, router, router_t, mine)


def expert_weights_kernel(parts, side, *refs):
    if side is not None:
        side, refs = refs[0], refs[1:]
    xs, gates = refs[:parts], refs[parts : 2 * parts]
    acts, dhs = refs[2 * parts : 3 * parts], refs[3 * parts : 4 * parts]
    cots = refs[4 * parts]
    if side is None:
        grad_first, grad_second, x_t, c_t = refs[4 * parts + 1 :]
    else:
        kept_first, sent_first, kept_second, sent_second, x_t, c_t, whole_first = refs[4 * parts + 1 :]
    rows = xs[0].shape[0]
    share = cots.shape[1] // parts
    chunk = 256
    per = chunk // share

    @pl.when(pl.program_id(0) == 0)
    def _():
        for part in range(parts):
            for first in range(0, rows, chunk):
                at = slice(first, first + chunk)
                to = slice(part * rows + first, part * rows + first + chunk)
                gate = gates[part][at, :]
                x_t[:, to] = (xs[part][at, :].astype(F32) * gate).T.astype(BF)
                cot = cots[
                    first // chunk * per : (first // chunk + 1) * per,
                    part * share : (part + 1) * share,
                ].reshape(chunk, D)
                c_t[:, to] = (cot.astype(F32) * gate).T.astype(BF)

    first_sum, second_sum = None, None
    for part in range(parts):
        at = slice(part * rows, (part + 1) * rows)
        one = dot(x_t[:, at], dhs[part][...])
        two = dot(c_t[:, at], acts[part][...])
        first_sum = one if first_sum is None else first_sum + one
        second_sum = two if second_sum is None else second_sum + two
    if side is None:
        grad_first[...] = first_sum.astype(BF)
        grad_second[...] = second_sum.T.astype(BF)
        return
    mine = side[0]
    half = D // 2
    whole_first[...] = first_sum.astype(BF)
    kept_first[...] = whole_first[pl.ds(pl.multiple_of(mine * half, half), half), :]
    sent_first[...] = whole_first[pl.ds(pl.multiple_of((1 - mine) * half, half), half), :]
    here = pl.program_id(0) // (pl.num_programs(0) // 2) == mine

    @pl.when(here)
    def _():
        kept_second[...] = second_sum.T.astype(BF)

    @pl.when(jnp.logical_not(here))
    def _():
        sent_second[...] = second_sum.T.astype(BF)


def expert_weights(xs, cots, gates, acts, dhs, side):
    parts = len(xs)
    rows = xs[0].shape[0]
    hidden_size = acts[0].shape[1]
    steps = hidden_size // FF_TILE
    in_specs = (
        [whole((rows, D))] * parts
        + [whole((rows, 1))] * parts
        + [pl.BlockSpec((rows, FF_TILE), lambda f, *_: (0, f))] * (2 * parts)
        + [whole(cots.shape)]
    )
    scratch = [pltpu.VMEM((D, parts * rows), BF), pltpu.VMEM((D, parts * rows), BF)]
    if side is None:
        out_specs = [
            pl.BlockSpec((D, FF_TILE), lambda f: (0, f)),
            pl.BlockSpec((FF_TILE, D), lambda f: (f, 0)),
        ]
        shapes = [(D, hidden_size), (hidden_size, D)]
    else:
        columns = pl.BlockSpec((D // 2, FF_TILE), lambda f, s: (0, f))

        def rows_of(place):
            def index(f, s):
                start = jnp.where(s[0] == 1, place, 1 - place) * (steps // 2)
                return (jnp.clip(f - start, 0, steps // 2 - 1), 0)

            return pl.BlockSpec((FF_TILE, D), index)

        out_specs = [columns, columns, rows_of(1), rows_of(0)]
        shapes = [(D // 2, hidden_size)] * 2 + [(hidden_size // 2, D)] * 2
        scratch = scratch + [pltpu.VMEM((D, FF_TILE), BF)]
    prefetched = () if side is None else (side,)
    return pl.pallas_call(
        functools.partial(expert_weights_kernel, parts, side is not None or None),
        grid_spec=pltpu.PrefetchScalarGridSpec(
            num_scalar_prefetch=len(prefetched),
            grid=(steps,),
            in_specs=in_specs,
            out_specs=out_specs,
            scratch_shapes=scratch,
        ),
        out_shape=[jax.ShapeDtypeStruct(shape, BF) for shape in shapes],
        compiler_params=params(("arbitrary",)),
        cost_estimate=cost(
            4 * parts * rows * D * hidden_size, 4 * (parts * rows + D) * hidden_size
        ),
        name="expert_weights",
    )(*prefetched, *xs, *gates, *acts, *dhs, cots)


def rms_back(values, factor, grad):
    inverse = inverse_rms(values)
    scaled = grad * factor
    mean = jnp.mean(scaled * values, axis=-1, keepdims=True)
    return (
        inverse * scaled - values * (inverse * inverse * inverse * mean),
        jnp.sum(grad * values * inverse, axis=0, keepdims=True),
    )


def undispatch(slot_col, parts):
    out = None
    offset = 0
    for part in parts:
        total = part.shape[0]
        place = lax.broadcasted_iota(jnp.int32, (slot_col.shape[0], total), 1) + offset
        found = dot((place == slot_col).astype(BF), part[...])
        out = found if out is None else out + found
        offset += total
    return out


def middle_back_kernel(parts, *refs):
    backs = refs[:parts]
    (
        slot_col, middle, cot, gain, out_left, out_right,
        grad_middle, grad_attn, grad_context, grad_gain, w_out,
    ) = refs[parts:]

    @pl.when(pl.program_id(0) == 0)
    def _():
        w_out[:, :SIDE] = out_left[...]
        w_out[:, SIDE:] = out_right[...]

    grad_normed = undispatch(slot_col[...], backs)
    part, gain_part = rms_back(middle[...], gain[...], grad_normed)
    grad = cot[...].astype(F32) + part
    grad_middle[...] = grad
    low = grad.astype(BF)
    grad_attn[...] = low
    grad_context[...] = dot(low, w_out[...], 1, 1).astype(BF)

    @pl.when(pl.program_id(0) == 0)
    def _():
        grad_gain[...] = gain_part

    @pl.when(pl.program_id(0) > 0)
    def _():
        grad_gain[...] += gain_part


def middle_back(backs, slot_col, middle, cot, gain, left, right):
    parts = len(backs)
    block = 256
    rows = pl.BlockSpec((block, D), lambda r: (r, 0))
    return pl.pallas_call(
        functools.partial(middle_back_kernel, parts),
        grid=(TOK // block,),
        in_specs=[whole(back.shape) for back in backs]
        + [
            pl.BlockSpec((block, 1), lambda r: (r, 0)),
            rows,
            rows,
            whole((1, D)),
            pl.BlockSpec((D, SIDE), lambda r: (0, 3)),
            pl.BlockSpec((D, SIDE), lambda r: (0, 3)),
        ],
        out_specs=[rows, rows, rows, whole((1, D))],
        scratch_shapes=[pltpu.VMEM((D, D), BF)],
        out_shape=[
            jax.ShapeDtypeStruct((TOK, D), F32),
            jax.ShapeDtypeStruct((TOK, D), BF),
            jax.ShapeDtypeStruct((TOK, D), BF),
            jax.ShapeDtypeStruct((1, D), F32),
        ],
        compiler_params=params(("arbitrary",)),
        cost_estimate=cost(2 * 2 * TOK * TOK * D + 2 * TOK * D * D, 16 * TOK * D),
        name="middle_back",
    )(*backs, slot_col, middle, cot, gain, left, right)


def mix_kernel(parts, *refs):
    backs = refs[:parts]
    slot_col, middle, gate, mixed = refs[parts:]
    mixed[...] = middle[...] + gate[...] * undispatch(slot_col[...], backs)


def mix(backs, slot_col, middle, gate):
    parts = len(backs)
    block = 256
    rows = pl.BlockSpec((block, D), lambda r: (r, 0))
    column = pl.BlockSpec((block, 1), lambda r: (r, 0))
    return pl.pallas_call(
        functools.partial(mix_kernel, parts),
        grid=(TOK // block,),
        in_specs=[whole(back.shape) for back in backs] + [column, rows, column],
        out_specs=rows,
        out_shape=jax.ShapeDtypeStruct((TOK, D), F32),
        compiler_params=params(("arbitrary",)),
        cost_estimate=cost(2 * 2 * TOK * TOK * D, 12 * TOK * D),
        name="mix",
    )(*backs, slot_col, middle, gate)


def tokens_back_kernel(g_left, g_right, left, right, tokens, gain, grad_middle, grad_tokens, grad_gain):
    grad_normed = dot(g_left[...], left[...], 1, 1) + dot(g_right[...], right[...], 1, 1)
    part, gain_part = rms_back(tokens[...].astype(F32), gain[...], grad_normed)
    grad_tokens[...] = grad_middle[...] + part

    @pl.when(pl.program_id(0) == 0)
    def _():
        grad_gain[...] = gain_part

    @pl.when(pl.program_id(0) > 0)
    def _():
        grad_gain[...] += gain_part


def tokens_back(g_left, g_right, left, right, tokens, gain, grad_middle):
    block = 256
    rows = pl.BlockSpec((block, D), lambda r: (r, 0))
    return pl.pallas_call(
        tokens_back_kernel,
        grid=(TOK // block,),
        in_specs=[
            pl.BlockSpec((block, SPLIT), lambda r: (r, 0)),
            pl.BlockSpec((block, SPLIT), lambda r: (r, 0)),
            whole((D, SPLIT)),
            whole((D, SPLIT)),
            rows,
            whole((1, D)),
            rows,
        ],
        out_specs=[rows, whole((1, D))],
        out_shape=[
            jax.ShapeDtypeStruct((TOK, D), F32),
            jax.ShapeDtypeStruct((1, D), F32),
        ],
        compiler_params=params(("arbitrary",)),
        cost_estimate=cost(6 * TOK * D * D, 16 * TOK * D),
        name="tokens_back",
    )(g_left, g_right, left, right, tokens, gain, grad_middle)


def weights_back_kernel(turned, grads, context, grad_attn, out):
    last = pl.num_programs(0) - 1

    @pl.when(pl.program_id(0) < last)
    def _():
        out[...] = dot(turned[...], grads[...])

    @pl.when(pl.program_id(0) == last)
    def _():
        out[...] = dot(context[...], grad_attn[...], 0, 0)


def weights_back(half, turned, grads, context, grad_attn):
    steps = grads.shape[1] // SIDE
    columns = (steps + 1) * SIDE
    return pl.pallas_call(
        weights_back_kernel,
        grid=(steps + 1,),
        in_specs=[
            whole(turned.shape),
            pl.BlockSpec((TOK, SIDE), lambda c: (0, jnp.minimum(c, steps - 1))),
            whole((TOK, D)),
            pl.BlockSpec((TOK, SIDE), lambda c: (0, half)),
        ],
        out_specs=pl.BlockSpec((D, SIDE), lambda c: (0, c)),
        out_shape=jax.ShapeDtypeStruct((D, columns), F32),
        compiler_params=params(("arbitrary",)),
        cost_estimate=cost(2 * TOK * D * columns, 2 * TOK * (D + columns) + 4 * D * columns),
        name="weights_back",
    )(turned, grads, context, grad_attn)


def swap(block, axis, bit):
    size = lax.axis_size(axis)
    return lax.ppermute(block, axis, [(place, place ^ bit) for place in range(size)])


def on_upper(axis, bit):
    return (lax.axis_index(axis) // bit) % 2 == 1


def axis_bits(*axes):
    found = []
    for axis in axes:
        bit = lax.axis_size(axis) // 2
        while bit >= 1:
            found.append((axis, bit))
            bit //= 2
    return found


def orders():
    bits = axis_bits("dp", "expert")
    dp = [at for at, (axis, _) in enumerate(bits) if axis == "dp"]
    core = len(bits) - 1
    along = [at for at, (axis, bit) in enumerate(bits) if axis == "expert" and bit == 2]
    rest = [at for at in range(core) if at not in dp and at not in along]
    return (rest + along + dp + [core], rest + dp + along + [core])


def gather_rows(shard, order, *before_dp):
    bits = axis_bits("dp", "expert")
    block = shard.reshape((1,) * len(bits) + shard.shape)
    for place in order:
        axis, bit = bits[place]
        if axis == "dp" and before_dp:
            block = after(block, *before_dp)
        other = swap(block, axis, bit)
        upper = on_upper(axis, bit)
        block = jnp.concatenate(
            [jnp.where(upper, other, block), jnp.where(upper, block, other)], axis=place
        )
    return block.reshape((-1,) + shard.shape[1:])


def scatter_start(total):
    bits = axis_bits("dp", "expert")
    rows = total.shape[0] >> len(bits)
    return total.reshape((2,) * len(bits) + (rows,) + total.shape[1:])


def scatter_step(block, place, *others):
    axis, bit = axis_bits("dp", "expert")[place]
    lower = lax.slice_in_dim(block, 0, 1, axis=place)
    higher = lax.slice_in_dim(block, 1, 2, axis=place)
    upper = on_upper(axis, bit)
    sent = jnp.where(upper, lower, higher).astype(BF)
    kept = after(jnp.where(upper, higher, lower), *others)
    return kept + swap(sent, axis, bit).astype(F32)


def scatter_rest(block, order):
    for place in order:
        block = scatter_step(block, place)
    return block.reshape(block.shape[len(axis_bits("dp", "expert")) :])


def sum_all(total):
    for axis, bit in axis_bits("dp", "expert"):
        total = total + swap(total, axis, bit)
    return total


def gather_dp(block, axis, other=None):
    if lax.axis_size("dp") != 2:
        return lax.all_gather(block, "dp", axis=axis, tiled=True)
    if other is None:
        other = swap(block, "dp", 1)
    upper = on_upper("dp", 1)
    return jnp.concatenate(
        [jnp.where(upper, other, block), jnp.where(upper, block, other)], axis=axis
    )


def receive_dp(halves):
    if len(halves) == 1:
        return (lax.psum_scatter(halves[0], "dp", scatter_dimension=0, tiled=True),)
    kept, sent = halves
    return (kept, swap(sent, "dp", 1))


def add_dp(parts, *others):
    kept, *received = parts
    total = after(kept, *others).astype(F32)
    for part in received:
        total = total + part.astype(F32)
    return total[None]


def after(value, *others):
    return lax.optimization_barrier((value, *others))[0]


def body(
    tokens, seq_ids, routes, cotangent, w_query, w_key, w_value, w_out,
    rel_table, gain_attn, gain_ffn, router, expert_in, expert_out,
):
    experts = lax.axis_size("expert")
    capacity = 2 * TOK // experts
    shard = w_query.shape[0]
    lanes = -(-(experts + 2) // LANES) * LANES

    small = jnp.concatenate(
        [
            router,
            gain_attn[:, None],
            gain_ffn[:, None],
            jnp.zeros((shard, lanes - experts - 2), BF),
        ],
        axis=1,
    )
    first, second = orders()
    kinds = (w_query, w_key, w_value, w_out)
    paired = lax.axis_size("dp") == 2
    own_first, own_second = expert_in[0], expert_out[0]
    first_cut, second_cut = own_first.shape[1] // 3, own_second.shape[0] // 2
    table = gather_dp(rel_table, 0)
    if paired:
        early = [swap(own_first[:, :first_cut], "dp", 1)]
        waiting = [own_first[:, first_cut:], own_second[:second_cut], own_second[second_cut:]]
    else:
        early, waiting = [], []
    slot_col, slot_row, sending_cot = make_slots(routes, cotangent, experts, capacity)
    wide_table = table.astype(F32)
    query_features, key_features = lane_features(seq_ids.reshape(TOK, 1), wide_table)
    band = jnp.sum(band_onehot()[None, :, :] * wide_table.T[:, None, :], axis=2)[:, None, :]
    left = gather_rows(
        jnp.concatenate([w[:, :SIDE] for w in kinds], axis=1),
        first,
        sending_cot, query_features, key_features, band, *early, *waiting,
    )
    right = gather_rows(
        jnp.concatenate([w[:, SIDE:] for w in kinds] + [small], axis=1), second, *early
    )

    def exchange(rows):
        return lax.all_to_all(
            rows.reshape(experts, -1, D), "expert", split_axis=0, concat_axis=0, tiled=True
        )

    cots = exchange(after(sending_cot, left, right))
    if paired:
        early.append(swap(after(waiting[0], left, right), "dp", 1))
        early.append(swap(after(waiting[1], left, right), "dp", 1))
        late = swap(after(waiting[2], *early), "dp", 1)
        other_first = jnp.concatenate(early[:2], axis=1)
        other_second = jnp.concatenate([early[2], late], axis=0)
    else:
        other_first = other_second = None
    w_first = gather_dp(own_first, 0, other_first)
    w_second = gather_dp(own_second, 0, other_second)

    extra = right[:, SPLIT + SIDE :]
    full_router = jnp.where(jnp.arange(lanes)[None, :] < experts, extra, jnp.zeros((), BF))
    router_t = full_router.T
    attn_gain = extra[:, experts].astype(F32).reshape(1, D)
    ffn_gain = extra[:, experts + 1].astype(F32).reshape(1, D)

    turned, qkv = project(tokens, attn_gain, left, right)
    context, lse = attend(qkv, query_features, key_features, band)

    middle, *sending, gate = make_middle(
        context, tokens, left, right, ffn_gain, full_router, routes, slot_row, experts, capacity
    )
    sending[0] = after(sending[0], cots, *early)
    sending[1] = after(sending[1], w_first, w_second)
    rows_in = [exchange(part).reshape(-1, D) for part in sending]
    mine = lax.axis_index("expert").astype(jnp.int32).reshape(1, 1)
    acts, dhs, results, grads, gates, router_parts = zip(
        *(
            run_expert(
                part, rows, cots, w_first, w_second, full_router, router_t, mine, experts
            )
            for part, rows in enumerate(rows_in)
        )
    )
    grads_home = [exchange(part).reshape(-1, D) for part in grads]
    weight_parts = expert_weights(
        rows_in,
        cots,
        (after(gates[0], grads_home[0]), *gates[1:]),
        acts,
        dhs,
        lax.axis_index("dp").astype(jnp.int32).reshape(1) if paired else None,
    )
    half = len(weight_parts) // 2
    grad_first, grad_second = weight_parts[:half], weight_parts[half:]
    results_home = []
    for part in results:
        part = after(part, *grads_home, *weight_parts, *results_home)
        results_home.append(exchange(part).reshape(-1, D))
    grads_home[0] = after(grads_home[0], *weight_parts)
    grad_middle, grad_attn, grad_context, grad_gain_f = middle_back(
        grads_home, slot_col, middle, cotangent, ffn_gain, left, right
    )
    down, down_other = first[::-1], second[::-1]

    def back(half, *others):
        return attend_back(
            half, qkv, after(grad_context, *others), query_features, key_features, lse, band
        )

    g_left, tiles_left, diagonals_left = back(0)
    left_block = scatter_start(weights_back(0, turned, g_left, context, grad_attn))
    g_right, tiles_right, diagonals_right = back(1, left_block, results_home[0])
    left_block = after(left_block, results_home[0])
    first_halves, second_halves = receive_dp(grad_first), receive_dp(grad_second)
    grad_right = weights_back(
        1, turned, after(g_right, results_home[1]), context, grad_attn
    )
    left_block = scatter_step(left_block, down[0], grad_right)
    right_block = scatter_step(scatter_start(grad_right), down_other[0], second_halves[-1])
    left_block = scatter_step(left_block, down[1], grad_right)
    grad_tokens, grad_gain_a = tokens_back(
        g_left, after(g_right, right_block), left, right, tokens, attn_gain, grad_middle
    )
    mixed = mix(results_home, slot_col, middle, after(gate, grad_tokens))
    right_block = scatter_step(right_block, down_other[1], mixed, first_halves[-1])
    near = 2 + len(axis_bits("dp"))
    for place in down[2:near]:
        left_block = scatter_step(left_block, place, mixed)
    along = (left_block, right_block)
    for place in down_other[2:near]:
        right_block = scatter_step(right_block, place)
    joined = jnp.concatenate([left_block, right_block], axis=-1)
    grad_expert_in = add_dp(first_halves, joined)
    grad_expert_out = add_dp(second_halves, joined)
    dense = scatter_rest(joined, down[near:])
    grad_left, grad_right = dense[:, : SPLIT + SIDE], dense[:, SPLIT + SIDE :]
    tiles = jnp.concatenate([tiles_left, tiles_right], axis=0)
    diagonals = jnp.concatenate([diagonals_left, diagonals_right], axis=0)
    grad_router = sum(router_parts)[:, :experts]
    grad_table = table_gradient(tiles, diagonals)

    sizes = (D * experts, D, D, BUCKETS * HEADS)
    sums = sum_all(
        jnp.concatenate(
            [
                part.reshape(-1, LANES)
                for part in (grad_router, after(grad_gain_a, *along), grad_gain_f, grad_table)
            ],
            axis=0,
        )
    ).reshape(-1)
    ends = [sum(sizes[: at + 1]) for at in range(len(sizes))]
    grad_router, grad_gain_a, grad_gain_f, grad_table = (
        sums[end - size : end] for end, size in zip(ends, sizes)
    )
    number = lax.axis_index("dp") * experts + lax.axis_index("expert")
    table_height = BUCKETS // lax.axis_size("dp")

    def own(rows, height, place):
        return lax.dynamic_slice_in_dim(rows, place * height, height, 0)

    return (
        mixed,
        grad_tokens,
        *(
            jnp.concatenate(
                [side[:, kind * SIDE : (kind + 1) * SIDE] for side in (grad_left, grad_right)],
                axis=1,
            )
            for kind in range(4)
        ),
        own(grad_table.reshape(BUCKETS, HEADS), table_height, lax.axis_index("dp")),
        own(grad_gain_a, shard, number),
        own(grad_gain_f, shard, number),
        own(grad_router.reshape(D, experts), shard, number),
        grad_expert_in,
        grad_expert_out,
    )


def solution(mesh):
    rows = P(("dp", "expert"), None)
    flat = P(("dp", "expert"))
    expert = P("expert", "dp", None)
    return jax.shard_map(
        body,
        mesh=mesh,
        in_specs=(
            rows, flat, rows, rows, rows, rows, rows, rows,
            P("dp", None), flat, flat, rows, expert, expert,
        ),
        out_specs=(
            rows, rows, rows, rows, rows, rows,
            P("dp", None), flat, flat, rows, expert, expert,
        ),
        check_vma=False,
    )
```

```python
import functools

import jax
import jax.numpy as jnp
from jax import lax
from jax.experimental import pallas as pl
from jax.experimental.pallas import tpu as pltpu
from jax.sharding import PartitionSpec as P

D = 768
HEADS = 12
HEAD_DIM = 64
BUCKETS = 32
TOK = 1024
TILE = 128
TILES = TOK // TILE
QBLK = 256
FF_TILE = 512
EXPERT_TILE = 512
EXPERT_ROWS = 1024
HALVES = 2
SIDE = D // 2
SPLIT = 3 * SIDE
PAIRS = HEADS // 2
SIDE_PAIRS = PAIRS // 2
COST_SHARE = 0.05
LANES = 128

EPSILON = 1e-06
DISTANCE_EDGES = (12, 16, 23, 32, 46, 64, 91)
FAR_BEFORE = 15
FAR_AFTER = 31
UNPAIRED = -1e30
BF = jnp.bfloat16
F32 = jnp.float32
VMEM_LIMIT = 56 * 1024 * 1024


def dot(left, right, left_dim=1, right_dim=0):
    return lax.dot_general(
        left, right, (((left_dim,), (right_dim,)), ((), ())), preferred_element_type=F32
    )


def params(semantics=None):
    return pltpu.CompilerParams(vmem_limit_bytes=VMEM_LIMIT, dimension_semantics=semantics)


def cost(flops, bytes_accessed, transcendentals=0, share=COST_SHARE):
    return pl.CostEstimate(
        flops=int(flops * share),
        bytes_accessed=int(bytes_accessed * share),
        transcendentals=int(transcendentals * share),
    )


def whole(shape):
    return pl.BlockSpec(shape, lambda *_: (0,) * len(shape))


def inverse_rms(values):
    return lax.rsqrt(jnp.mean(values * values, axis=-1, keepdims=True) + EPSILON)


def bucket_of(offset):
    distance = jnp.abs(offset)
    distant = 8 + sum(((distance >= boundary).astype(jnp.int32) for boundary in DISTANCE_EDGES))
    return jnp.where(distance < 8, distance, distant) + jnp.where(offset > 0, 16, 0)


def place_in_buffers(route, rank, experts, capacity):
    share = capacity // HALVES
    part = (rank >= share).astype(jnp.int32)
    return part * (experts * share) + route * share + (rank - part * share)


def slots_kernel(experts, capacity, route_col, route_row, cot, slot_col, slot_row, sending):
    padded = -(-experts // LANES) * LANES
    picked = (
        lax.broadcasted_iota(jnp.int32, (TOK, padded), 1) == route_col[...]
    ).astype(BF)
    picked_t = (
        lax.broadcasted_iota(jnp.int32, (padded, TOK), 0) == route_row[...]
    ).astype(BF)
    upto = (
        lax.broadcasted_iota(jnp.int32, (TOK, TOK), 0)
        <= lax.broadcasted_iota(jnp.int32, (TOK, TOK), 1)
    ).astype(BF)
    from_t = (
        lax.broadcasted_iota(jnp.int32, (TOK, TOK), 0)
        >= lax.broadcasted_iota(jnp.int32, (TOK, TOK), 1)
    ).astype(BF)
    counts = dot(from_t, picked) * picked.astype(F32)
    rank = jnp.sum(counts, axis=1, keepdims=True).astype(jnp.int32) - 1
    slot_col[...] = place_in_buffers(route_col[...], rank, experts, capacity)
    counts_t = dot(picked_t, upto) * picked_t.astype(F32)
    rank_row = jnp.sum(counts_t, axis=0, keepdims=True).astype(jnp.int32) - 1
    slot_row[...] = place_in_buffers(route_row[...], rank_row, experts, capacity)
    dispatch(route_row[...] * capacity + rank_row, cot[...], [sending])


def dispatch(row, rows, parts):
    step = 512
    offset = 0
    for sending in parts:
        for first in range(0, sending.shape[0], step):
            chosen = (
                lax.broadcasted_iota(jnp.int32, (step, TOK), 0) + (first + offset) == row
            ).astype(BF)
            sending[first : first + step, :] = dot(chosen, rows).astype(BF)
        offset += sending.shape[0]


def make_slots(routes, cotangent, experts, capacity):
    total = experts * capacity
    return pl.pallas_call(
        functools.partial(slots_kernel, experts, capacity),
        out_shape=(
            jax.ShapeDtypeStruct((TOK, 1), jnp.int32),
            jax.ShapeDtypeStruct((1, TOK), jnp.int32),
            jax.ShapeDtypeStruct((total, D), BF),
        ),
        compiler_params=params(),
        cost_estimate=cost(2 * total * TOK * D, 6 * total * D),
        name="slots",
    )(routes, routes.reshape(1, TOK), cotangent)


def project_kernel(tokens, gain, left, right, turned, qkv):
    x = tokens[...].astype(F32)
    wide = x * inverse_rms(x) * gain[...]
    low = wide.astype(BF)
    turned[...] = wide.T.astype(BF)
    qkv[:, :SPLIT] = dot(low, left[...]).astype(BF)
    qkv[:, SPLIT:] = dot(low, right[...]).astype(BF)


def project(tokens, gain, left, right):
    block = 256
    rows = pl.BlockSpec((block, D), lambda r: (r, 0))
    return pl.pallas_call(
        project_kernel,
        grid=(TOK // block,),
        in_specs=[rows, whole((1, D)), whole((D, SPLIT)), whole((D, SPLIT))],
        out_specs=[
            pl.BlockSpec((D, block), lambda r: (0, r)),
            pl.BlockSpec((block, 3 * D), lambda r: (r, 0)),
        ],
        out_shape=[
            jax.ShapeDtypeStruct((D, TOK), BF),
            jax.ShapeDtypeStruct((TOK, 3 * D), BF),
        ],
        compiler_params=params(("arbitrary",)),
        cost_estimate=cost(6 * TOK * D * D, 12 * TOK * D),
        name="project",
    )(tokens, gain, left, right)


def lane_features(seq_col, rel_table):
    lane = jnp.arange(LANES, dtype=jnp.int32)[None, :]
    feature = lane % HEAD_DIM
    tile = jnp.arange(TOK, dtype=jnp.int32)[:, None] // TILE
    on_tile = feature - 4
    query_features = jnp.where(
        feature < 4,
        jnp.where(feature == seq_col, 0.0, UNPAIRED),
        jnp.where(on_tile == tile, 1.0, 0.0),
    ).astype(BF)
    wide = jnp.arange(D, dtype=jnp.int32)[None, :]
    feature = wide % HEAD_DIM
    on_tile = feature - 4
    swapped = jnp.arange(HEADS, dtype=jnp.int32) ^ 1
    before = jnp.repeat(rel_table[FAR_BEFORE][swapped], HEAD_DIM)[None, :]
    after = jnp.repeat(rel_table[FAR_AFTER][swapped], HEAD_DIM)[None, :]
    apart = tile - on_tile
    far = jnp.where(apart >= 2, after, jnp.where(apart <= -2, before, 0.0))
    key_features = jnp.where(
        feature < 4,
        jnp.where(feature == seq_col, 1.0, 0.0),
        jnp.where(on_tile < TILES, far, 0.0),
    ).astype(BF)
    return query_features, key_features


def band_offsets():
    place = jnp.arange(4 * LANES, dtype=jnp.int32)
    return 255 - (place + 383) % 512


def band_onehot():
    return (
        bucket_of(band_offsets())[:, None] == jnp.arange(BUCKETS, dtype=jnp.int32)[None, :]
    ).astype(F32)


def near_rows(tile):
    first = max(tile - 1, 0)
    last = min(tile + 2, TILES)
    return first, last


def spread_band(values):
    wide = jnp.broadcast_to(values, (3 * TILE, 4 * LANES))
    return pltpu.roll(wide, 0, 1, stride=1, stride_axis=0)[:, :TILE]


def attend_kernel(q_ref, k_ref, v_ref, qx_ref, kx_ref, band_ref, out_ref, lse_ref, st, pb, ot):
    low = lax.broadcasted_iota(jnp.int32, (TOK, LANES), 1) < HEAD_DIM
    v_t = v_ref[...].astype(F32).T.astype(BF)
    for side in range(2):
        own = low if side == 0 else ~low
        queries = jnp.where(own, q_ref[...], qx_ref[...])
        keys = jnp.where(own, k_ref[...], kx_ref[...])
        band = spread_band(band_ref[side])
        for block in range(TOK // QBLK):
            rows = slice(block * QBLK, (block + 1) * QBLK)
            slot = block % 2
            st[slot] = dot(keys, queries[rows], 1, 1)
            for part in range(QBLK // TILE):
                tile = block * (QBLK // TILE) + part
                first, last = near_rows(tile)
                at = (slot, slice(first * TILE, last * TILE), slice(part * TILE, (part + 1) * TILE))
                st[at] += band[(first - tile + 1) * TILE : (last - tile + 1) * TILE]
            top = jnp.max(st[slot, 0:TILE], axis=0, keepdims=True)
            for chunk in range(1, TILES):
                top = jnp.maximum(
                    top,
                    jnp.max(
                        st[slot, chunk * TILE : (chunk + 1) * TILE], axis=0, keepdims=True
                    ),
                )
            total = jnp.zeros((1, QBLK), F32)
            for chunk in range(TILES):
                at = slice(chunk * TILE, (chunk + 1) * TILE)
                raised = jnp.exp(st[slot, at] - top)
                total = total + jnp.sum(raised, axis=0, keepdims=True)
                pb[slot, at] = raised.astype(BF)
            half = slice(side * HEAD_DIM, (side + 1) * HEAD_DIM)
            ot[half, rows] = dot(v_t[half], pb[slot]) * (1.0 / total)
            lse_ref[side, :, rows] = top + jnp.log(total)
    out_ref[...] = ot[...].T.astype(BF)


def attend(qkv, query_features, key_features, band):
    return pl.pallas_call(
        attend_kernel,
        grid=(PAIRS,),
        in_specs=[
            *(
                pl.BlockSpec(
                    (TOK, LANES),
                    lambda p, kind=kind: (
                        0,
                        p // SIDE_PAIRS * (3 * SIDE_PAIRS) + kind * SIDE_PAIRS + p % SIDE_PAIRS,
                    ),
                )
                for kind in range(3)
            ),
            whole((TOK, LANES)),
            pl.BlockSpec((TOK, LANES), lambda p: (0, p)),
            pl.BlockSpec((2, 1, 4 * LANES), lambda p: (p, 0, 0)),
        ],
        out_specs=[
            pl.BlockSpec((TOK, LANES), lambda p: (0, p)),
            pl.BlockSpec((2, 1, TOK), lambda p: (p, 0, 0)),
        ],
        out_shape=[
            jax.ShapeDtypeStruct((TOK, D), BF),
            jax.ShapeDtypeStruct((HEADS, 1, TOK), F32),
        ],
        scratch_shapes=[
            pltpu.VMEM((2, TOK, QBLK), F32),
            pltpu.VMEM((2, TOK, QBLK), BF),
            pltpu.VMEM((LANES, TOK), F32),
        ],
        compiler_params=params(("arbitrary",)),
        cost_estimate=cost(2 * 3 * HEADS * TOK * TOK * 256, 10 * TOK * D, HEADS * TOK * TOK),
        name="attend",
    )(qkv, qkv, qkv, query_features, key_features, band)


def attend_back_kernel(
    q_ref, k_ref, v_ref, do_ref, qx_ref, kx_ref, lse_ref, band_ref,
    grad_ref, tiles_ref, diag_ref,
    st, dp, pb, sb, dqt, dkt, dvt, near,
):
    low = lax.broadcasted_iota(jnp.int32, (TOK, LANES), 1) < HEAD_DIM
    k_t = k_ref[...].astype(F32).T.astype(BF)
    for side in range(2):
        own = low if side == 0 else ~low
        queries = jnp.where(own, q_ref[...], qx_ref[...])
        keys = jnp.where(own, k_ref[...], kx_ref[...])
        values = jnp.where(own, v_ref[...], jnp.zeros((), BF))
        band = spread_band(band_ref[side])
        near[...] = jnp.zeros_like(near)
        half = slice(side * HEAD_DIM, (side + 1) * HEAD_DIM)
        for block in range(TOK // QBLK):
            rows = slice(block * QBLK, (block + 1) * QBLK)
            slot = block % 2
            st[slot] = dot(keys, queries[rows], 1, 1)
            dp[slot] = dot(values, do_ref[rows, :], 1, 1)
            for part in range(QBLK // TILE):
                tile = block * (QBLK // TILE) + part
                first, last = near_rows(tile)
                at = (slot, slice(first * TILE, last * TILE), slice(part * TILE, (part + 1) * TILE))
                st[at] += band[(first - tile + 1) * TILE : (last - tile + 1) * TILE]
            lse = lse_ref[side, :, rows]
            spread = jnp.zeros((1, QBLK), F32)
            for chunk in range(TILES):
                at = slice(chunk * TILE, (chunk + 1) * TILE)
                weights = jnp.exp(st[slot, at] - lse)
                st[slot, at] = weights
                pb[slot, at] = weights.astype(BF)
                spread = spread + jnp.sum(weights * dp[slot, at], axis=0, keepdims=True)
            for chunk in range(TILES):
                at = slice(chunk * TILE, (chunk + 1) * TILE)
                sb[slot, at] = (st[slot, at] * (dp[slot, at] - spread)).astype(BF)
            for part in range(QBLK // TILE):
                tile = block * (QBLK // TILE) + part
                first, last = near_rows(tile)
                at = (slot, slice(first * TILE, last * TILE), slice(part * TILE, (part + 1) * TILE))
                near[(first - tile + 1) * TILE : (last - tile + 1) * TILE, :TILE] += sb[at].astype(F32)
            dv = dot(pb[slot], do_ref[rows, :])
            dk = dot(sb[slot], queries[rows])
            if block == 0:
                dvt[side] = dv
                dkt[side] = dk
            else:
                dvt[side] += dv
                dkt[side] += dk
            dqt[half, rows] = dot(k_t[half], sb[slot])
        for tile in range(TILES):
            tiles_ref[side, tile : tile + 1, :] = jnp.sum(
                dkt[side, tile * TILE : (tile + 1) * TILE], axis=0, keepdims=True
            )
        folded = near[0:8, :]
        for first in range(8, 3 * TILE, 8):
            folded = folded + pltpu.roll(near[first : first + 8, :], 4 * LANES - first, 1)
        diagonal = folded[0:1]
        for row in range(1, 8):
            diagonal = diagonal + pltpu.roll(folded[row : row + 1], 4 * LANES - row, 1)
        diag_ref[side] = diagonal
    found = (
        dqt[...].T.astype(BF),
        jnp.where(low, dkt[0], dkt[1]).astype(BF),
        jnp.where(low, dvt[0], dvt[1]).astype(BF),
    )
    for pair in range(SIDE_PAIRS):

        @pl.when(pl.program_id(0) == pair)
        def _():
            for kind in range(3):
                first = kind * SIDE + pair * LANES
                grad_ref[:, first : first + LANES] = found[kind]


def attend_back(half, qkv, grad_context, query_features, key_features, lse, band):
    first = half * SIDE_PAIRS
    column = pl.BlockSpec((TOK, LANES), lambda p: (0, first + p))
    return pl.pallas_call(
        attend_back_kernel,
        grid=(SIDE_PAIRS,),
        in_specs=[
            *(
                pl.BlockSpec(
                    (TOK, LANES), lambda p, kind=kind: (0, (3 * half + kind) * SIDE_PAIRS + p)
                )
                for kind in range(3)
            ),
            column,
            whole((TOK, LANES)),
            column,
            pl.BlockSpec((2, 1, TOK), lambda p: (first + p, 0, 0)),
            pl.BlockSpec((2, 1, 4 * LANES), lambda p: (first + p, 0, 0)),
        ],
        out_specs=[
            whole((TOK, SPLIT)),
            pl.BlockSpec((2, TILES, LANES), lambda p: (p, 0, 0)),
            pl.BlockSpec((2, 1, 4 * LANES), lambda p: (p, 0, 0)),
        ],
        out_shape=[
            jax.ShapeDtypeStruct((TOK, SPLIT), BF),
            jax.ShapeDtypeStruct((HEADS // 2, TILES, LANES), F32),
            jax.ShapeDtypeStruct((HEADS // 2, 1, 4 * LANES), F32),
        ],
        scratch_shapes=[
            pltpu.VMEM((2, TOK, QBLK), F32),
            pltpu.VMEM((2, TOK, QBLK), F32),
            pltpu.VMEM((2, TOK, QBLK), BF),
            pltpu.VMEM((2, TOK, QBLK), BF),
            pltpu.VMEM((LANES, TOK), F32),
            pltpu.VMEM((2, TOK, LANES), F32),
            pltpu.VMEM((2, TOK, LANES), F32),
            pltpu.VMEM((3 * TILE, 4 * LANES), F32),
        ],
        compiler_params=params(("arbitrary",)),
        cost_estimate=cost(5 * HEADS * TOK * TOK * 256, 8 * TOK * D, HEADS * TOK * TOK // 2, share=0.3),
        name="attend_back",
    )(qkv, qkv, qkv, grad_context, query_features, key_features, lse, band)


def table_gradient(tiles, diagonals):
    near = jnp.einsum(
        "hl,lb->bh", diagonals[:, 0, :], band_onehot(), precision=lax.Precision.HIGHEST
    )
    sums = jnp.concatenate(
        [tiles[h : h + 1, :, (HEAD_DIM if h % 2 == 0 else 0) + 4 :][:, :, :TILES] for h in range(HEADS)],
        axis=0,
    )
    apart = (
        jnp.arange(TILES, dtype=jnp.int32)[:, None] - jnp.arange(TILES, dtype=jnp.int32)[None, :]
    )[None]
    before = jnp.sum(jnp.where(apart <= -2, sums, 0.0), axis=(1, 2))
    after = jnp.sum(jnp.where(apart >= 2, sums, 0.0), axis=(1, 2))
    place = jnp.arange(BUCKETS, dtype=jnp.int32)[:, None]
    return (
        near
        + jnp.where(place == FAR_BEFORE, before[None, :], 0.0)
        + jnp.where(place == FAR_AFTER, after[None, :], 0.0)
    )


def middle_kernel(context, tokens, out_left, out_right, gain, router, route_col, slot_row, experts,
                  middle, sending_low, sending_high, gate, normed, w_out):
    w_out[:, :SIDE] = out_left[...]
    w_out[:, SIDE:] = out_right[...]
    for first in range(0, TOK, 256):
        at = slice(first, first + 256)
        mid = tokens[at, :].astype(F32) + dot(context[at, :], w_out[...])
        middle[at, :] = mid
        low = (mid * inverse_rms(mid) * gain[...]).astype(BF)
        normed[at, :] = low
        probs = router_softmax(low, router[...], experts)
        lane = lax.broadcasted_iota(jnp.int32, probs.shape, 1)
        gate[at, :] = jnp.sum(
            jnp.where(lane == route_col[at, :], probs, 0.0), axis=1, keepdims=True
        )
    dispatch(slot_row[...], normed[...], [sending_low, sending_high])


def router_softmax(rows, router, experts):
    logits = dot(rows, router)
    lane = lax.broadcasted_iota(jnp.int32, logits.shape, 1)
    logits = jnp.where(lane < experts, logits, UNPAIRED)
    raised = jnp.exp(logits - jnp.max(logits, axis=1, keepdims=True))
    return raised / jnp.sum(raised, axis=1, keepdims=True)


def make_middle(context, tokens, left, right, gain, router, routes, slot_row, experts, capacity):
    total = experts * capacity

    def kernel(*refs):
        middle_kernel(*refs[:8], experts, *refs[8:])

    out_half = pl.BlockSpec((D, SIDE), lambda r: (0, 3))
    return pl.pallas_call(
        kernel,
        grid=(1,),
        in_specs=[
            whole((TOK, D)),
            whole((TOK, D)),
            out_half,
            out_half,
            whole((1, D)),
            whole(router.shape),
            whole((TOK, 1)),
            whole((1, TOK)),
        ],
        out_specs=(
            whole((TOK, D)),
            whole((total // 2, D)),
            whole((total // 2, D)),
            whole((TOK, 1)),
        ),
        out_shape=(
            jax.ShapeDtypeStruct((TOK, D), F32),
            jax.ShapeDtypeStruct((total // 2, D), BF),
            jax.ShapeDtypeStruct((total // 2, D), BF),
            jax.ShapeDtypeStruct((TOK, 1), F32),
        ),
        scratch_shapes=[pltpu.VMEM((TOK, D), BF), pltpu.VMEM((D, D), BF)],
        compiler_params=params(),
        cost_estimate=cost(2 * total * TOK * D + 2 * TOK * D * D, 12 * TOK * D + 2 * total * D),
        name="middle",
    )(context, tokens, left, right, gain, router, routes, slot_row)


def gelu_parts(v):
    size = jnp.abs(v)
    t = 1.0 / (1.0 + (0.3275911 * 0.7071067811865476) * size)
    bell = jnp.exp(-0.5 * (v * v))
    series = t * (
        0.5 * 0.254829592
        + t * (0.5 * -0.284496736 + t * (0.5 * 1.421413741 + t * (0.5 * -1.453152027 + t * (0.5 * 1.061405429))))
    )
    tail = series * bell
    phi = jnp.where(v < 0, tail, 1.0 - tail)
    return v * phi, phi + v * (bell * 0.3989422804014327)


def expert_kernel(experts, x, c3, w_first, w_second, router, router_t, mine, *refs):
    act_ref, dh_ref, result, grad_x, gate_ref, grad_router, acc_r, acc_x = refs[-8:]
    step = pl.program_id(0)
    rows = x.shape[0]
    chunk = EXPERT_ROWS
    share = c3.shape[1]
    per = chunk // share

    @pl.when(step == 0)
    def _():
        acc_r[...] = jnp.zeros_like(acc_r)
        acc_x[...] = jnp.zeros_like(acc_x)

    for first in range(0, rows, chunk):
        at = slice(first, first + chunk)
        sources = slice(first // share, first // share + per)
        hidden = dot(x[at, :], w_first[...])
        grad_act = dot(c3[sources].reshape(chunk, D), w_second[...], 1, 1)
        act, slope = gelu_parts(hidden)
        act = act.astype(BF)
        grad_hidden = (grad_act * slope).astype(BF)
        act_ref[at, :] = act
        dh_ref[at, :] = grad_hidden
        acc_r[at, :] += dot(act, w_second[...])
        acc_x[at, :] += dot(grad_hidden, w_first[...], 1, 1)

    @pl.when(step == pl.num_programs(0) - 1)
    def _():
        total_router = jnp.zeros(grad_router.shape, F32)
        for first in range(0, rows, chunk):
            at = slice(first, first + chunk)
            sources = slice(first // share, first // share + per)
            rounded = acc_r[at, :].astype(BF)
            result[at, :] = rounded
            probs = router_softmax(x[at, :], router[...], experts)
            lane = lax.broadcasted_iota(jnp.int32, probs.shape, 1)
            here = lane == mine[0, 0]
            gate = jnp.sum(jnp.where(here, probs, 0.0), axis=1, keepdims=True)
            grad_gate = jnp.sum(
                c3[sources].reshape(chunk, D).astype(F32) * rounded.astype(F32), axis=1, keepdims=True
            )
            grad_logits = (
                probs * (jnp.where(here, grad_gate, 0.0) - gate * grad_gate)
            ).astype(BF)
            gate_ref[at, :] = gate
            grad_x[at, :] = (acc_x[at, :] * gate + dot(grad_logits, router_t[...])).astype(BF)
            total_router = total_router + dot(x[at, :], grad_logits, 0, 0)
        grad_router[...] = total_router


def run_expert(part, x, c, w_first, w_second, router, router_t, mine, experts):
    rows = x.shape[0]
    hidden_size = w_first.shape[1]
    lanes = router.shape[1]
    sources, capacity = c.shape[:2]
    half = pl.BlockSpec((sources, capacity // HALVES, D), lambda f: (0, part, 0))
    return pl.pallas_call(
        functools.partial(expert_kernel, experts),
        grid=(hidden_size // EXPERT_TILE,),
        in_specs=[
            whole((rows, D)),
            half,
            pl.BlockSpec((D, EXPERT_TILE), lambda f: (0, f)),
            pl.BlockSpec((EXPERT_TILE, D), lambda f: (f, 0)),
            whole((D, lanes)),
            whole((lanes, D)),
            pl.BlockSpec(memory_space=pltpu.SMEM),
        ],
        out_specs=[
            pl.BlockSpec((rows, EXPERT_TILE), lambda f: (0, f)),
            pl.BlockSpec((rows, EXPERT_TILE), lambda f: (0, f)),
            whole((rows, D)),
            whole((rows, D)),
            whole((rows, 1)),
            whole((D, lanes)),
        ],
        out_shape=[
            jax.ShapeDtypeStruct((rows, hidden_size), BF),
            jax.ShapeDtypeStruct((rows, hidden_size), BF),
            jax.ShapeDtypeStruct((rows, D), BF),
            jax.ShapeDtypeStruct((rows, D), BF),
            jax.ShapeDtypeStruct((rows, 1), F32),
            jax.ShapeDtypeStruct((D, lanes), F32),
        ],
        scratch_shapes=[pltpu.VMEM((rows, D), F32), pltpu.VMEM((rows, D), F32)],
        compiler_params=params(("arbitrary",)),
        cost_estimate=cost(
            8 * rows * D * hidden_size, 4 * rows * hidden_size + 4 * D * hidden_size
        ),
        name="expert",
    )(x, c, w_first, w_second, router, router_t, mine)


def expert_weights_kernel(parts, side, *refs):
    if side is not None:
        side, refs = refs[0], refs[1:]
    xs, gates = refs[:parts], refs[parts : 2 * parts]
    acts, dhs = refs[2 * parts : 3 * parts], refs[3 * parts : 4 * parts]
    cots = refs[4 * parts]
    if side is None:
        grad_first, grad_second, x_t, c_t = refs[4 * parts + 1 :]
    else:
        kept_first, sent_first, kept_second, sent_second, x_t, c_t, whole_first = refs[4 * parts + 1 :]
    rows = xs[0].shape[0]
    share = cots.shape[1] // parts
    chunk = 256
    per = chunk // share

    @pl.when(pl.program_id(0) == 0)
    def _():
        for part in range(parts):
            for first in range(0, rows, chunk):
                at = slice(first, first + chunk)
                to = slice(part * rows + first, part * rows + first + chunk)
                gate = gates[part][at, :]
                x_t[:, to] = (xs[part][at, :].astype(F32) * gate).T.astype(BF)
                cot = cots[
                    first // chunk * per : (first // chunk + 1) * per,
                    part * share : (part + 1) * share,
                ].reshape(chunk, D)
                c_t[:, to] = (cot.astype(F32) * gate).T.astype(BF)

    first_sum, second_sum = None, None
    for part in range(parts):
        at = slice(part * rows, (part + 1) * rows)
        one = dot(x_t[:, at], dhs[part][...])
        two = dot(c_t[:, at], acts[part][...])
        first_sum = one if first_sum is None else first_sum + one
        second_sum = two if second_sum is None else second_sum + two
    if side is None:
        grad_first[...] = first_sum.astype(BF)
        grad_second[...] = second_sum.T.astype(BF)
        return
    mine = side[0]
    half = D // 2
    whole_first[...] = first_sum.astype(BF)
    kept_first[...] = whole_first[pl.ds(pl.multiple_of(mine * half, half), half), :]
    sent_first[...] = whole_first[pl.ds(pl.multiple_of((1 - mine) * half, half), half), :]
    here = pl.program_id(0) // (pl.num_programs(0) // 2) == mine

    @pl.when(here)
    def _():
        kept_second[...] = second_sum.T.astype(BF)

    @pl.when(jnp.logical_not(here))
    def _():
        sent_second[...] = second_sum.T.astype(BF)


def expert_weights(xs, cots, gates, acts, dhs, side):
    parts = len(xs)
    rows = xs[0].shape[0]
    hidden_size = acts[0].shape[1]
    steps = hidden_size // FF_TILE
    in_specs = (
        [whole((rows, D))] * parts
        + [whole((rows, 1))] * parts
        + [pl.BlockSpec((rows, FF_TILE), lambda f, *_: (0, f))] * (2 * parts)
        + [whole(cots.shape)]
    )
    scratch = [pltpu.VMEM((D, parts * rows), BF), pltpu.VMEM((D, parts * rows), BF)]
    if side is None:
        out_specs = [
            pl.BlockSpec((D, FF_TILE), lambda f: (0, f)),
            pl.BlockSpec((FF_TILE, D), lambda f: (f, 0)),
        ]
        shapes = [(D, hidden_size), (hidden_size, D)]
    else:
        columns = pl.BlockSpec((D // 2, FF_TILE), lambda f, s: (0, f))

        def rows_of(place):
            def index(f, s):
                start = jnp.where(s[0] == 1, place, 1 - place) * (steps // 2)
                return (jnp.clip(f - start, 0, steps // 2 - 1), 0)

            return pl.BlockSpec((FF_TILE, D), index)

        out_specs = [columns, columns, rows_of(1), rows_of(0)]
        shapes = [(D // 2, hidden_size)] * 2 + [(hidden_size // 2, D)] * 2
        scratch = scratch + [pltpu.VMEM((D, FF_TILE), BF)]
    prefetched = () if side is None else (side,)
    return pl.pallas_call(
        functools.partial(expert_weights_kernel, parts, side is not None or None),
        grid_spec=pltpu.PrefetchScalarGridSpec(
            num_scalar_prefetch=len(prefetched),
            grid=(steps,),
            in_specs=in_specs,
            out_specs=out_specs,
            scratch_shapes=scratch,
        ),
        out_shape=[jax.ShapeDtypeStruct(shape, BF) for shape in shapes],
        compiler_params=params(("arbitrary",)),
        cost_estimate=cost(
            4 * parts * rows * D * hidden_size, 4 * (parts * rows + D) * hidden_size
        ),
        name="expert_weights",
    )(*prefetched, *xs, *gates, *acts, *dhs, cots)


def rms_back(values, factor, grad):
    inverse = inverse_rms(values)
    scaled = grad * factor
    mean = jnp.mean(scaled * values, axis=-1, keepdims=True)
    return (
        inverse * scaled - values * (inverse * inverse * inverse * mean),
        jnp.sum(grad * values * inverse, axis=0, keepdims=True),
    )


def undispatch(slot_col, parts):
    out = None
    offset = 0
    for part in parts:
        total = part.shape[0]
        place = lax.broadcasted_iota(jnp.int32, (slot_col.shape[0], total), 1) + offset
        found = dot((place == slot_col).astype(BF), part[...])
        out = found if out is None else out + found
        offset += total
    return out


def middle_back_kernel(parts, *refs):
    backs = refs[:parts]
    (
        slot_col, middle, cot, gain, out_left, out_right,
        grad_middle, grad_attn, grad_context, grad_gain, w_out,
    ) = refs[parts:]

    @pl.when(pl.program_id(0) == 0)
    def _():
        w_out[:, :SIDE] = out_left[...]
        w_out[:, SIDE:] = out_right[...]

    grad_normed = undispatch(slot_col[...], backs)
    part, gain_part = rms_back(middle[...], gain[...], grad_normed)
    grad = cot[...].astype(F32) + part
    grad_middle[...] = grad
    low = grad.astype(BF)
    grad_attn[...] = low
    grad_context[...] = dot(low, w_out[...], 1, 1).astype(BF)

    @pl.when(pl.program_id(0) == 0)
    def _():
        grad_gain[...] = gain_part

    @pl.when(pl.program_id(0) > 0)
    def _():
        grad_gain[...] += gain_part


def middle_back(backs, slot_col, middle, cot, gain, left, right):
    parts = len(backs)
    block = 256
    rows = pl.BlockSpec((block, D), lambda r: (r, 0))
    return pl.pallas_call(
        functools.partial(middle_back_kernel, parts),
        grid=(TOK // block,),
        in_specs=[whole(back.shape) for back in backs]
        + [
            pl.BlockSpec((block, 1), lambda r: (r, 0)),
            rows,
            rows,
            whole((1, D)),
            pl.BlockSpec((D, SIDE), lambda r: (0, 3)),
            pl.BlockSpec((D, SIDE), lambda r: (0, 3)),
        ],
        out_specs=[rows, rows, rows, whole((1, D))],
        scratch_shapes=[pltpu.VMEM((D, D), BF)],
        out_shape=[
            jax.ShapeDtypeStruct((TOK, D), F32),
            jax.ShapeDtypeStruct((TOK, D), BF),
            jax.ShapeDtypeStruct((TOK, D), BF),
            jax.ShapeDtypeStruct((1, D), F32),
        ],
        compiler_params=params(("arbitrary",)),
        cost_estimate=cost(2 * 2 * TOK * TOK * D + 2 * TOK * D * D, 16 * TOK * D),
        name="middle_back",
    )(*backs, slot_col, middle, cot, gain, left, right)


def mix_kernel(parts, *refs):
    backs = refs[:parts]
    slot_col, middle, gate, mixed = refs[parts:]
    mixed[...] = middle[...] + gate[...] * undispatch(slot_col[...], backs)


def mix(backs, slot_col, middle, gate):
    parts = len(backs)
    block = 256
    rows = pl.BlockSpec((block, D), lambda r: (r, 0))
    column = pl.BlockSpec((block, 1), lambda r: (r, 0))
    return pl.pallas_call(
        functools.partial(mix_kernel, parts),
        grid=(TOK // block,),
        in_specs=[whole(back.shape) for back in backs] + [column, rows, column],
        out_specs=rows,
        out_shape=jax.ShapeDtypeStruct((TOK, D), F32),
        compiler_params=params(("arbitrary",)),
        cost_estimate=cost(2 * 2 * TOK * TOK * D, 12 * TOK * D),
        name="mix",
    )(*backs, slot_col, middle, gate)


def tokens_back_kernel(g_left, g_right, left, right, tokens, gain, grad_middle, grad_tokens):
    grad_normed = dot(g_left[...], left[...], 1, 1) + dot(g_right[...], right[...], 1, 1)
    grad_tokens[...] = grad_middle[...] + rms_back(
        tokens[...].astype(F32), gain[...], grad_normed
    )[0]


def tokens_back(g_left, g_right, left, right, tokens, gain, grad_middle):
    block = 256
    rows = pl.BlockSpec((block, D), lambda r: (r, 0))
    return pl.pallas_call(
        tokens_back_kernel,
        grid=(TOK // block,),
        in_specs=[
            pl.BlockSpec((block, SPLIT), lambda r: (r, 0)),
            pl.BlockSpec((block, SPLIT), lambda r: (r, 0)),
            whole((D, SPLIT)),
            whole((D, SPLIT)),
            rows,
            whole((1, D)),
            rows,
        ],
        out_specs=rows,
        out_shape=jax.ShapeDtypeStruct((TOK, D), F32),
        compiler_params=params(("arbitrary",)),
        cost_estimate=cost(6 * TOK * D * D, 16 * TOK * D),
        name="tokens_back",
    )(g_left, g_right, left, right, tokens, gain, grad_middle)


def weights_back_kernel(turned, grads, context, grad_attn, out):
    last = pl.num_programs(0) - 1

    @pl.when(pl.program_id(0) < last)
    def _():
        out[...] = dot(turned[...], grads[...])

    @pl.when(pl.program_id(0) == last)
    def _():
        out[...] = dot(context[...], grad_attn[...], 0, 0)


def weights_back(half, turned, grads, context, grad_attn):
    steps = grads.shape[1] // SIDE
    columns = (steps + 1) * SIDE
    return pl.pallas_call(
        weights_back_kernel,
        grid=(steps + 1,),
        in_specs=[
            whole(turned.shape),
            pl.BlockSpec((TOK, SIDE), lambda c: (0, jnp.minimum(c, steps - 1))),
            whole((TOK, D)),
            pl.BlockSpec((TOK, SIDE), lambda c: (0, half)),
        ],
        out_specs=pl.BlockSpec((D, SIDE), lambda c: (0, c)),
        out_shape=jax.ShapeDtypeStruct((D, columns), F32),
        compiler_params=params(("arbitrary",)),
        cost_estimate=cost(2 * TOK * D * columns, 2 * TOK * (D + columns) + 4 * D * columns),
        name="weights_back",
    )(turned, grads, context, grad_attn)


def swap(block, axis, bit):
    size = lax.axis_size(axis)
    return lax.ppermute(block, axis, [(place, place ^ bit) for place in range(size)])


def on_upper(axis, bit):
    return (lax.axis_index(axis) // bit) % 2 == 1


def axis_bits(*axes):
    found = []
    for axis in axes:
        bit = lax.axis_size(axis) // 2
        while bit >= 1:
            found.append((axis, bit))
            bit //= 2
    return found


def orders():
    bits = axis_bits("dp", "expert")
    dp = [at for at, (axis, _) in enumerate(bits) if axis == "dp"]
    core = len(bits) - 1
    along = [at for at, (axis, bit) in enumerate(bits) if axis == "expert" and bit == 2]
    rest = [at for at in range(core) if at not in dp and at not in along]
    return (rest + along + dp + [core], rest + dp + along + [core])


def gather_start(shard):
    return shard.reshape((1,) * len(axis_bits("dp", "expert")) + shard.shape)


def gather_step(block, place):
    axis, bit = axis_bits("dp", "expert")[place]
    other = swap(block, axis, bit)
    upper = on_upper(axis, bit)
    return jnp.concatenate(
        [jnp.where(upper, other, block), jnp.where(upper, block, other)], axis=place
    )


def gather_end(block):
    return block.reshape((-1, block.shape[-1]))


def scatter_start(total):
    bits = axis_bits("dp", "expert")
    rows = total.shape[0] >> len(bits)
    return total.reshape((2,) * len(bits) + (rows,) + total.shape[1:])


def scatter_step(block, place, *others):
    axis, bit = axis_bits("dp", "expert")[place]
    lower = lax.slice_in_dim(block, 0, 1, axis=place)
    higher = lax.slice_in_dim(block, 1, 2, axis=place)
    upper = on_upper(axis, bit)
    sent = jnp.where(upper, lower, higher).astype(BF)
    kept = after(jnp.where(upper, higher, lower), *others)
    return kept + swap(sent, axis, bit).astype(F32)


def scatter_rest(block, order):
    for place in order:
        block = scatter_step(block, place)
    return block.reshape(block.shape[len(axis_bits("dp", "expert")) :])


def sum_all(total, beside):
    for number, (axis, bit) in enumerate(axis_bits("dp", "expert")):
        kept = after(total, beside[number]) if number < len(beside) else total
        total = kept + swap(total, axis, bit)
    return total


def gather_dp(block, axis, other=None):
    if lax.axis_size("dp") != 2:
        return lax.all_gather(block, "dp", axis=axis, tiled=True)
    if other is None:
        other = swap(block, "dp", 1)
    upper = on_upper("dp", 1)
    return jnp.concatenate(
        [jnp.where(upper, other, block), jnp.where(upper, block, other)], axis=axis
    )


def receive_dp(halves):
    if len(halves) == 1:
        return (lax.psum_scatter(halves[0], "dp", scatter_dimension=0, tiled=True),)
    kept, sent = halves
    return (kept, swap(sent, "dp", 1))


def add_dp(parts, *others):
    kept, *received = parts
    total = after(kept, *others).astype(F32)
    for part in received:
        total = total + part.astype(F32)
    return total[None]


def after(value, *others):
    return lax.optimization_barrier((value, *others))[0]


def body(
    tokens, seq_ids, routes, cotangent, w_query, w_key, w_value, w_out,
    rel_table, gain_attn, gain_ffn, router, expert_in, expert_out,
):
    experts = lax.axis_size("expert")
    capacity = 2 * TOK // experts
    shard = w_query.shape[0]
    lanes = -(-(experts + 2) // LANES) * LANES

    small = jnp.concatenate(
        [
            router,
            gain_attn[:, None],
            gain_ffn[:, None],
            jnp.zeros((shard, lanes - experts - 2), BF),
        ],
        axis=1,
    )
    first, second = orders()
    kinds = (w_query, w_key, w_value, w_out)
    paired = lax.axis_size("dp") == 2
    own_first, own_second = expert_in[0], expert_out[0]
    second_cut = own_second.shape[0] // 2
    table = gather_dp(rel_table, 0)
    early = [swap(own_second[:second_cut], "dp", 1)] if paired else []
    left = gather_start(jnp.concatenate([w[:, :SIDE] for w in kinds], axis=1))
    right = gather_start(jnp.concatenate([w[:, SIDE:] for w in kinds] + [small], axis=1))
    dp_bits = len(axis_bits("dp"))
    rest = len(first) - dp_bits - 2
    left, right = gather_step(left, first[0]), gather_step(right, second[0])
    slot_col, slot_row, sending_cot = make_slots(
        after(routes, left), cotangent, experts, capacity
    )
    for at in range(1, rest):
        left, right = gather_step(left, first[at]), gather_step(right, second[at])
    wide_table = table.astype(F32)
    query_features, key_features = lane_features(seq_ids.reshape(TOK, 1), wide_table)
    band = jnp.sum(band_onehot()[None, :, :] * wide_table.T[:, None, :], axis=2)[:, None, :]
    left = gather_step(left, first[rest])
    right = after(right, query_features, key_features, band, *early)
    for place in second[rest : rest + dp_bits]:
        right = gather_step(right, place)
    left = after(left, sending_cot)
    for place in first[rest + 1 :]:
        left = gather_step(left, place)
    for place in second[rest + dp_bits :]:
        right = gather_step(right, place)
    left, right = gather_end(left), gather_end(right)

    def exchange(rows):
        return lax.all_to_all(
            rows.reshape(experts, -1, D), "expert", split_axis=0, concat_axis=0, tiled=True
        )

    cots = exchange(after(sending_cot, left, right))
    if paired:
        other_first = swap(after(own_first, left, right), "dp", 1)
        late = swap(after(own_second[second_cut:], other_first), "dp", 1)
        other_second = jnp.concatenate([*early, late], axis=0)
        early.append(other_first)
    else:
        other_first = other_second = None
    w_first = gather_dp(own_first, 0, other_first)
    w_second = gather_dp(own_second, 0, other_second)

    extra = right[:, SPLIT + SIDE :]
    full_router = jnp.where(jnp.arange(lanes)[None, :] < experts, extra, jnp.zeros((), BF))
    router_t = full_router.T
    attn_gain = extra[:, experts].astype(F32).reshape(1, D)
    ffn_gain = extra[:, experts + 1].astype(F32).reshape(1, D)

    turned, qkv = project(tokens, attn_gain, left, right)
    context, lse = attend(qkv, query_features, key_features, band)

    middle, *sending, gate = make_middle(
        context, tokens, left, right, ffn_gain, full_router, routes, slot_row, experts, capacity
    )
    sending[0] = after(sending[0], cots, *early)
    sending[1] = after(sending[1], w_first, w_second)
    rows_in = [exchange(part).reshape(-1, D) for part in sending]
    mine = lax.axis_index("expert").astype(jnp.int32).reshape(1, 1)
    acts, dhs, results, grads, gates, router_parts = zip(
        *(
            run_expert(
                part, rows, cots, w_first, w_second, full_router, router_t, mine, experts
            )
            for part, rows in enumerate(rows_in)
        )
    )
    grads_home = [exchange(part).reshape(-1, D) for part in grads]
    weight_parts = expert_weights(
        rows_in,
        cots,
        (after(gates[0], grads_home[0]), *gates[1:]),
        acts,
        dhs,
        lax.axis_index("dp").astype(jnp.int32).reshape(1) if paired else None,
    )
    half = len(weight_parts) // 2
    grad_first, grad_second = weight_parts[:half], weight_parts[half:]
    results_home = []
    for part in results:
        part = after(part, *grads_home, *weight_parts, *results_home)
        results_home.append(exchange(part).reshape(-1, D))
    grads_home[0] = after(grads_home[0], *weight_parts)
    grad_middle, grad_attn, grad_context, grad_gain_f = middle_back(
        grads_home, slot_col, middle, cotangent, ffn_gain, left, right
    )
    down, down_other = second[::-1], first[::-1]

    def back(half, *others):
        return attend_back(
            half, qkv, after(grad_context, *others), query_features, key_features, lse, band
        )

    g_left, tiles_left, diagonals_left = back(0)
    left_block = scatter_start(weights_back(0, turned, g_left, context, grad_attn))
    g_right, tiles_right, diagonals_right = back(1, left_block, results_home[0])
    left_block = after(left_block, results_home[0])
    first_halves, second_halves = receive_dp(grad_first), receive_dp(grad_second)
    grad_right = weights_back(
        1, turned, after(g_right, results_home[1]), context, grad_attn
    )
    left_block = scatter_step(left_block, down[0], grad_right)
    right_block = scatter_step(scatter_start(grad_right), down_other[0], second_halves[-1])
    grad_tokens = tokens_back(
        g_left, after(g_right, right_block), left, right, tokens, attn_gain, grad_middle
    )
    mixed = mix(results_home, slot_col, middle, after(gate, grad_tokens))
    beside = [left_block]
    left_block = scatter_step(left_block, down[1], mixed)
    beside.append(left_block)
    right_block = scatter_step(right_block, down_other[1], mixed, first_halves[-1])
    near = 2 + len(axis_bits("dp"))
    for place in down[2:near]:
        left_block = scatter_step(left_block, place)
    beside.append(left_block)
    for place in down_other[2:near]:
        right_block = scatter_step(right_block, place)
    joined = jnp.concatenate([left_block, right_block], axis=-1)
    grad_expert_in = add_dp(first_halves, joined)
    grad_expert_out = add_dp(second_halves, joined)
    joined = scatter_step(joined, down[near])
    beside.append(joined)
    dense = scatter_rest(joined, down[near + 1 :])
    grad_left, grad_right = dense[:, : SPLIT + SIDE], dense[:, SPLIT + SIDE :]
    tiles = jnp.concatenate([tiles_left, tiles_right], axis=0)
    diagonals = jnp.concatenate([diagonals_left, diagonals_right], axis=0)
    grad_router = sum(router_parts)[:, :experts]
    grad_table = table_gradient(tiles, diagonals)

    own_weights = jnp.concatenate(
        [w[:, :SIDE] for w in kinds[:3]] + [w[:, SIDE:] for w in kinds[:3]], axis=1
    ).astype(F32)
    own_grads = jnp.concatenate([grad_left[:, :SPLIT], grad_right[:, :SPLIT]], axis=1)
    grad_gain_a = jnp.sum(own_weights * own_grads, axis=1) / gain_attn.astype(F32)

    sizes = (D * experts, D, BUCKETS * HEADS)
    sums = sum_all(
        jnp.concatenate(
            [part.reshape(-1, LANES) for part in (grad_router, grad_gain_f, grad_table)], axis=0
        ),
        beside,
    ).reshape(-1)
    ends = [sum(sizes[: at + 1]) for at in range(len(sizes))]
    grad_router, grad_gain_f, grad_table = (
        sums[end - size : end] for end, size in zip(ends, sizes)
    )
    number = lax.axis_index("dp") * experts + lax.axis_index("expert")
    table_height = BUCKETS // lax.axis_size("dp")

    def own(rows, height, place):
        return lax.dynamic_slice_in_dim(rows, place * height, height, 0)

    return (
        mixed,
        grad_tokens,
        *(
            jnp.concatenate(
                [side[:, kind * SIDE : (kind + 1) * SIDE] for side in (grad_left, grad_right)],
                axis=1,
            )
            for kind in range(4)
        ),
        own(grad_table.reshape(BUCKETS, HEADS), table_height, lax.axis_index("dp")),
        grad_gain_a,
        own(grad_gain_f, shard, number),
        own(grad_router.reshape(D, experts), shard, number),
        grad_expert_in,
        grad_expert_out,
    )


def solution(mesh):
    rows = P(("dp", "expert"), None)
    flat = P(("dp", "expert"))
    expert = P("expert", "dp", None)
    return jax.shard_map(
        body,
        mesh=mesh,
        in_specs=(
            rows, flat, rows, rows, rows, rows, rows, rows,
            P("dp", None), flat, flat, rows, expert, expert,
        ),
        out_specs=(
            rows, rows, rows, rows, rows, rows,
            P("dp", None), flat, flat, rows, expert, expert,
        ),
        check_vma=False,
    )
```

```python
import functools

import jax
import jax.numpy as jnp
from jax import lax
from jax.experimental import pallas as pl
from jax.experimental.pallas import tpu as pltpu
from jax.sharding import PartitionSpec as P

D = 768
HEADS = 12
HEAD_DIM = 64
BUCKETS = 32
TOK = 1024
TILE = 128
TILES = TOK // TILE
QBLK = 256
FF_TILE = 512
EXPERT_TILE = 512
EXPERT_ROWS = 1024
HALVES = 2
SIDE = D // 2
SPLIT = 3 * SIDE
PAIRS = HEADS // 2
SIDE_PAIRS = PAIRS // 2
COST_SHARE = 0.05
LANES = 128

EPSILON = 1e-06
DISTANCE_EDGES = (12, 16, 23, 32, 46, 64, 91)
FAR_BEFORE = 15
FAR_AFTER = 31
UNPAIRED = -1e30
BF = jnp.bfloat16
F32 = jnp.float32
VMEM_LIMIT = 56 * 1024 * 1024


def dot(left, right, left_dim=1, right_dim=0):
    return lax.dot_general(
        left, right, (((left_dim,), (right_dim,)), ((), ())), preferred_element_type=F32
    )


def params(semantics=None):
    return pltpu.CompilerParams(vmem_limit_bytes=VMEM_LIMIT, dimension_semantics=semantics)


def cost(flops, bytes_accessed, transcendentals=0, share=COST_SHARE):
    return pl.CostEstimate(
        flops=int(flops * share),
        bytes_accessed=int(bytes_accessed * share),
        transcendentals=int(transcendentals * share),
    )


def whole(shape):
    return pl.BlockSpec(shape, lambda *_: (0,) * len(shape))


def inverse_rms(values):
    return lax.rsqrt(jnp.mean(values * values, axis=-1, keepdims=True) + EPSILON)


def bucket_of(offset):
    distance = jnp.abs(offset)
    distant = 8 + sum(((distance >= boundary).astype(jnp.int32) for boundary in DISTANCE_EDGES))
    return jnp.where(distance < 8, distance, distant) + jnp.where(offset > 0, 16, 0)


def place_in_buffers(route, rank, experts, capacity):
    share = capacity // HALVES
    part = (rank >= share).astype(jnp.int32)
    return part * (experts * share) + route * share + (rank - part * share)


def slots_kernel(experts, capacity, route_col, route_row, cot, slot_col, slot_row, sending):
    padded = -(-experts // LANES) * LANES
    picked = (
        lax.broadcasted_iota(jnp.int32, (TOK, padded), 1) == route_col[...]
    ).astype(BF)
    picked_t = (
        lax.broadcasted_iota(jnp.int32, (padded, TOK), 0) == route_row[...]
    ).astype(BF)
    upto = (
        lax.broadcasted_iota(jnp.int32, (TOK, TOK), 0)
        <= lax.broadcasted_iota(jnp.int32, (TOK, TOK), 1)
    ).astype(BF)
    from_t = (
        lax.broadcasted_iota(jnp.int32, (TOK, TOK), 0)
        >= lax.broadcasted_iota(jnp.int32, (TOK, TOK), 1)
    ).astype(BF)
    counts = dot(from_t, picked) * picked.astype(F32)
    rank = jnp.sum(counts, axis=1, keepdims=True).astype(jnp.int32) - 1
    slot_col[...] = place_in_buffers(route_col[...], rank, experts, capacity)
    counts_t = dot(picked_t, upto) * picked_t.astype(F32)
    rank_row = jnp.sum(counts_t, axis=0, keepdims=True).astype(jnp.int32) - 1
    slot_row[...] = place_in_buffers(route_row[...], rank_row, experts, capacity)
    dispatch(route_row[...] * capacity + rank_row, cot[...], [sending])


def dispatch(row, rows, parts):
    step = 512
    offset = 0
    for sending in parts:
        for first in range(0, sending.shape[0], step):
            chosen = (
                lax.broadcasted_iota(jnp.int32, (step, TOK), 0) + (first + offset) == row
            ).astype(BF)
            sending[first : first + step, :] = dot(chosen, rows).astype(BF)
        offset += sending.shape[0]


def make_slots(routes, cotangent, experts, capacity):
    total = experts * capacity
    return pl.pallas_call(
        functools.partial(slots_kernel, experts, capacity),
        out_shape=(
            jax.ShapeDtypeStruct((TOK, 1), jnp.int32),
            jax.ShapeDtypeStruct((1, TOK), jnp.int32),
            jax.ShapeDtypeStruct((total, D), BF),
        ),
        compiler_params=params(),
        cost_estimate=cost(2 * total * TOK * D, 6 * total * D),
        name="slots",
    )(routes, routes.reshape(1, TOK), cotangent)


def project_kernel(tokens, gain, left, right, turned, qkv):
    x = tokens[...].astype(F32)
    wide = x * inverse_rms(x) * gain[...]
    low = wide.astype(BF)
    turned[...] = wide.T.astype(BF)
    qkv[:, :SPLIT] = dot(low, left[...]).astype(BF)
    qkv[:, SPLIT:] = dot(low, right[...]).astype(BF)


def project(tokens, gain, left, right):
    block = 256
    rows = pl.BlockSpec((block, D), lambda r: (r, 0))
    return pl.pallas_call(
        project_kernel,
        grid=(TOK // block,),
        in_specs=[rows, whole((1, D)), whole((D, SPLIT)), whole((D, SPLIT))],
        out_specs=[
            pl.BlockSpec((D, block), lambda r: (0, r)),
            pl.BlockSpec((block, 3 * D), lambda r: (r, 0)),
        ],
        out_shape=[
            jax.ShapeDtypeStruct((D, TOK), BF),
            jax.ShapeDtypeStruct((TOK, 3 * D), BF),
        ],
        compiler_params=params(("arbitrary",)),
        cost_estimate=cost(6 * TOK * D * D, 12 * TOK * D),
        name="project",
    )(tokens, gain, left, right)


def lane_features(seq_col, rel_table):
    lane = jnp.arange(LANES, dtype=jnp.int32)[None, :]
    feature = lane % HEAD_DIM
    tile = jnp.arange(TOK, dtype=jnp.int32)[:, None] // TILE
    on_tile = feature - 4
    query_features = jnp.where(
        feature < 4,
        jnp.where(feature == seq_col, 0.0, UNPAIRED),
        jnp.where(on_tile == tile, 1.0, 0.0),
    ).astype(BF)
    wide = jnp.arange(D, dtype=jnp.int32)[None, :]
    feature = wide % HEAD_DIM
    on_tile = feature - 4
    swapped = jnp.arange(HEADS, dtype=jnp.int32) ^ 1
    before = jnp.repeat(rel_table[FAR_BEFORE][swapped], HEAD_DIM)[None, :]
    after = jnp.repeat(rel_table[FAR_AFTER][swapped], HEAD_DIM)[None, :]
    apart = tile - on_tile
    far = jnp.where(apart >= 2, after, jnp.where(apart <= -2, before, 0.0))
    key_features = jnp.where(
        feature < 4,
        jnp.where(feature == seq_col, 1.0, 0.0),
        jnp.where(on_tile < TILES, far, 0.0),
    ).astype(BF)
    return query_features, key_features


def band_offsets():
    place = jnp.arange(4 * LANES, dtype=jnp.int32)
    return 255 - (place + 383) % 512


def band_onehot():
    return (
        bucket_of(band_offsets())[:, None] == jnp.arange(BUCKETS, dtype=jnp.int32)[None, :]
    ).astype(F32)


def near_rows(tile):
    first = max(tile - 1, 0)
    last = min(tile + 2, TILES)
    return first, last


def spread_band(values):
    wide = jnp.broadcast_to(values, (3 * TILE, 4 * LANES))
    return pltpu.roll(wide, 0, 1, stride=1, stride_axis=0)[:, :TILE]


def add_band(st, slot, block, band):
    for part in range(QBLK // TILE):
        tile = block * (QBLK // TILE) + part
        first, last = near_rows(tile)
        at = (slot, slice(first * TILE, last * TILE), slice(part * TILE, (part + 1) * TILE))
        st[at] += band[(first - tile + 1) * TILE : (last - tile + 1) * TILE]


def attend_kernel(q_ref, k_ref, v_ref, qx_ref, kx_ref, band_ref, out_ref, lse_ref, st, pb, ot):
    low = lax.broadcasted_iota(jnp.int32, (TOK, LANES), 1) < HEAD_DIM
    v_t = v_ref[...].astype(F32).T.astype(BF)
    sides = []
    for side in range(2):
        own = low if side == 0 else ~low
        sides.append(
            (
                jnp.where(own, q_ref[...], qx_ref[...]),
                jnp.where(own, k_ref[...], kx_ref[...]),
                spread_band(band_ref[side]),
            )
        )
    work = [(side, block) for side in range(2) for block in range(TOK // QBLK)]

    def score(number):
        side, block = work[number]
        queries, keys, band = sides[side]
        st[number % 2] = dot(keys, queries[block * QBLK : (block + 1) * QBLK], 1, 1)

    def finish(number):
        side, block = work[number]
        slot = number % 2
        rows = slice(block * QBLK, (block + 1) * QBLK)
        add_band(st, slot, block, sides[side][2])
        top = jnp.max(st[slot, 0:TILE], axis=0, keepdims=True)
        for chunk in range(1, TILES):
            top = jnp.maximum(
                top,
                jnp.max(st[slot, chunk * TILE : (chunk + 1) * TILE], axis=0, keepdims=True),
            )
        total = jnp.zeros((1, QBLK), F32)
        for chunk in range(TILES):
            at = slice(chunk * TILE, (chunk + 1) * TILE)
            raised = jnp.exp(st[slot, at] - top)
            total = total + jnp.sum(raised, axis=0, keepdims=True)
            pb[slot, at] = raised.astype(BF)
        lse_ref[side, :, rows] = top + jnp.log(total)
        return total

    def mix_values(number, total):
        side, block = work[number]
        half = slice(side * HEAD_DIM, (side + 1) * HEAD_DIM)
        rows = slice(block * QBLK, (block + 1) * QBLK)
        ot[half, rows] = dot(v_t[half], pb[number % 2]) * (1.0 / total)

    score(0)
    waiting = None
    for number in range(len(work)):
        if number + 1 < len(work):
            score(number + 1)
        if waiting is not None:
            mix_values(number - 1, waiting)
        waiting = finish(number)
    mix_values(len(work) - 1, waiting)
    out_ref[...] = ot[...].T.astype(BF)


def attend(qkv, query_features, key_features, band):
    return pl.pallas_call(
        attend_kernel,
        grid=(PAIRS,),
        in_specs=[
            *(
                pl.BlockSpec(
                    (TOK, LANES),
                    lambda p, kind=kind: (
                        0,
                        p // SIDE_PAIRS * (3 * SIDE_PAIRS) + kind * SIDE_PAIRS + p % SIDE_PAIRS,
                    ),
                )
                for kind in range(3)
            ),
            whole((TOK, LANES)),
            pl.BlockSpec((TOK, LANES), lambda p: (0, p)),
            pl.BlockSpec((2, 1, 4 * LANES), lambda p: (p, 0, 0)),
        ],
        out_specs=[
            pl.BlockSpec((TOK, LANES), lambda p: (0, p)),
            pl.BlockSpec((2, 1, TOK), lambda p: (p, 0, 0)),
        ],
        out_shape=[
            jax.ShapeDtypeStruct((TOK, D), BF),
            jax.ShapeDtypeStruct((HEADS, 1, TOK), F32),
        ],
        scratch_shapes=[
            pltpu.VMEM((2, TOK, QBLK), F32),
            pltpu.VMEM((2, TOK, QBLK), BF),
            pltpu.VMEM((LANES, TOK), F32),
        ],
        compiler_params=params(("arbitrary",)),
        cost_estimate=cost(2 * 3 * HEADS * TOK * TOK * 256, 10 * TOK * D, HEADS * TOK * TOK),
        name="attend",
    )(qkv, qkv, qkv, query_features, key_features, band)


def attend_back_kernel(
    q_ref, k_ref, v_ref, do_ref, qx_ref, kx_ref, lse_ref, band_ref,
    grad_ref, tiles_ref, diag_ref,
    st, dp, pb, sb, dqt, dkt, dvt, near,
):
    low = lax.broadcasted_iota(jnp.int32, (TOK, LANES), 1) < HEAD_DIM
    k_t = k_ref[...].astype(F32).T.astype(BF)
    sides = []
    for side in range(2):
        own = low if side == 0 else ~low
        sides.append(
            (
                jnp.where(own, q_ref[...], qx_ref[...]),
                jnp.where(own, k_ref[...], kx_ref[...]),
                jnp.where(own, v_ref[...], jnp.zeros((), BF)),
                spread_band(band_ref[side]),
            )
        )
    near[...] = jnp.zeros_like(near)
    work = [(side, block) for side in range(2) for block in range(TOK // QBLK)]

    def rows_of(block):
        return slice(block * QBLK, (block + 1) * QBLK)

    def score(number):
        side, block = work[number]
        queries, keys, values, _ = sides[side]
        st[number % 2] = dot(keys, queries[rows_of(block)], 1, 1)
        dp[number % 2] = dot(values, do_ref[rows_of(block), :], 1, 1)

    def finish(number):
        side, block = work[number]
        slot = number % 2
        add_band(st, slot, block, sides[side][3])
        lse = lse_ref[side, :, rows_of(block)]
        spread = jnp.zeros((1, QBLK), F32)
        for chunk in range(TILES):
            at = slice(chunk * TILE, (chunk + 1) * TILE)
            weights = jnp.exp(st[slot, at] - lse)
            st[slot, at] = weights
            pb[slot, at] = weights.astype(BF)
            spread = spread + jnp.sum(weights * dp[slot, at], axis=0, keepdims=True)
        for chunk in range(TILES):
            at = slice(chunk * TILE, (chunk + 1) * TILE)
            sb[slot, at] = (st[slot, at] * (dp[slot, at] - spread)).astype(BF)
        for part in range(QBLK // TILE):
            tile = block * (QBLK // TILE) + part
            first, last = near_rows(tile)
            at = (slot, slice(first * TILE, last * TILE), slice(part * TILE, (part + 1) * TILE))
            near[side, (first - tile + 1) * TILE : (last - tile + 1) * TILE, :TILE] += sb[
                at
            ].astype(F32)

    def multiply(number):
        side, block = work[number]
        slot = number % 2
        rows = rows_of(block)
        half = slice(side * HEAD_DIM, (side + 1) * HEAD_DIM)
        dv = dot(pb[slot], do_ref[rows, :])
        dk = dot(sb[slot], sides[side][0][rows])
        if block == 0:
            dvt[side] = dv
            dkt[side] = dk
        else:
            dvt[side] += dv
            dkt[side] += dk
        dqt[half, rows] = dot(k_t[half], sb[slot])

    score(0)
    for number in range(len(work)):
        if number + 1 < len(work):
            score(number + 1)
        if number > 0:
            multiply(number - 1)
        finish(number)
    multiply(len(work) - 1)
    for side in range(2):
        for tile in range(TILES):
            tiles_ref[side, tile : tile + 1, :] = jnp.sum(
                dkt[side, tile * TILE : (tile + 1) * TILE], axis=0, keepdims=True
            )
        folded = near[side, 0:8, :]
        for first in range(8, 3 * TILE, 8):
            folded = folded + pltpu.roll(near[side, first : first + 8, :], 4 * LANES - first, 1)
        diagonal = folded[0:1]
        for row in range(1, 8):
            diagonal = diagonal + pltpu.roll(folded[row : row + 1], 4 * LANES - row, 1)
        diag_ref[side] = diagonal
    found = (
        dqt[...].T.astype(BF),
        jnp.where(low, dkt[0], dkt[1]).astype(BF),
        jnp.where(low, dvt[0], dvt[1]).astype(BF),
    )
    for pair in range(SIDE_PAIRS):

        @pl.when(pl.program_id(0) == pair)
        def _():
            for kind in range(3):
                first = kind * SIDE + pair * LANES
                grad_ref[:, first : first + LANES] = found[kind]


def attend_back(half, qkv, grad_context, query_features, key_features, lse, band):
    first = half * SIDE_PAIRS
    column = pl.BlockSpec((TOK, LANES), lambda p: (0, first + p))
    return pl.pallas_call(
        attend_back_kernel,
        grid=(SIDE_PAIRS,),
        in_specs=[
            *(
                pl.BlockSpec(
                    (TOK, LANES), lambda p, kind=kind: (0, (3 * half + kind) * SIDE_PAIRS + p)
                )
                for kind in range(3)
            ),
            column,
            whole((TOK, LANES)),
            column,
            pl.BlockSpec((2, 1, TOK), lambda p: (first + p, 0, 0)),
            pl.BlockSpec((2, 1, 4 * LANES), lambda p: (first + p, 0, 0)),
        ],
        out_specs=[
            whole((TOK, SPLIT)),
            pl.BlockSpec((2, TILES, LANES), lambda p: (p, 0, 0)),
            pl.BlockSpec((2, 1, 4 * LANES), lambda p: (p, 0, 0)),
        ],
        out_shape=[
            jax.ShapeDtypeStruct((TOK, SPLIT), BF),
            jax.ShapeDtypeStruct((HEADS // 2, TILES, LANES), F32),
            jax.ShapeDtypeStruct((HEADS // 2, 1, 4 * LANES), F32),
        ],
        scratch_shapes=[
            pltpu.VMEM((2, TOK, QBLK), F32),
            pltpu.VMEM((2, TOK, QBLK), F32),
            pltpu.VMEM((2, TOK, QBLK), BF),
            pltpu.VMEM((2, TOK, QBLK), BF),
            pltpu.VMEM((LANES, TOK), F32),
            pltpu.VMEM((2, TOK, LANES), F32),
            pltpu.VMEM((2, TOK, LANES), F32),
            pltpu.VMEM((2, 3 * TILE, 4 * LANES), F32),
        ],
        compiler_params=params(("arbitrary",)),
        cost_estimate=cost(5 * HEADS * TOK * TOK * 256, 8 * TOK * D, HEADS * TOK * TOK // 2, share=0.3),
        name="attend_back",
    )(qkv, qkv, qkv, grad_context, query_features, key_features, lse, band)


def table_gradient(tiles, diagonals):
    near = jnp.einsum(
        "hl,lb->bh", diagonals[:, 0, :], band_onehot(), precision=lax.Precision.HIGHEST
    )
    sums = jnp.concatenate(
        [tiles[h : h + 1, :, (HEAD_DIM if h % 2 == 0 else 0) + 4 :][:, :, :TILES] for h in range(HEADS)],
        axis=0,
    )
    apart = (
        jnp.arange(TILES, dtype=jnp.int32)[:, None] - jnp.arange(TILES, dtype=jnp.int32)[None, :]
    )[None]
    before = jnp.sum(jnp.where(apart <= -2, sums, 0.0), axis=(1, 2))
    after = jnp.sum(jnp.where(apart >= 2, sums, 0.0), axis=(1, 2))
    place = jnp.arange(BUCKETS, dtype=jnp.int32)[:, None]
    return (
        near
        + jnp.where(place == FAR_BEFORE, before[None, :], 0.0)
        + jnp.where(place == FAR_AFTER, after[None, :], 0.0)
    )


def middle_kernel(context, tokens, out_left, out_right, gain, router, route_col, slot_row, experts,
                  middle, sending_low, sending_high, gate, normed, w_out):
    w_out[:, :SIDE] = out_left[...]
    w_out[:, SIDE:] = out_right[...]
    for first in range(0, TOK, 256):
        at = slice(first, first + 256)
        mid = tokens[at, :].astype(F32) + dot(context[at, :], w_out[...])
        middle[at, :] = mid
        low = (mid * inverse_rms(mid) * gain[...]).astype(BF)
        normed[at, :] = low
        probs = router_softmax(low, router[...], experts)
        lane = lax.broadcasted_iota(jnp.int32, probs.shape, 1)
        gate[at, :] = jnp.sum(
            jnp.where(lane == route_col[at, :], probs, 0.0), axis=1, keepdims=True
        )
    dispatch(slot_row[...], normed[...], [sending_low, sending_high])


def router_softmax(rows, router, experts):
    logits = dot(rows, router)
    lane = lax.broadcasted_iota(jnp.int32, logits.shape, 1)
    logits = jnp.where(lane < experts, logits, UNPAIRED)
    raised = jnp.exp(logits - jnp.max(logits, axis=1, keepdims=True))
    return raised / jnp.sum(raised, axis=1, keepdims=True)


def make_middle(context, tokens, left, right, gain, router, routes, slot_row, experts, capacity):
    total = experts * capacity

    def kernel(*refs):
        middle_kernel(*refs[:8], experts, *refs[8:])

    out_half = pl.BlockSpec((D, SIDE), lambda r: (0, 3))
    return pl.pallas_call(
        kernel,
        grid=(1,),
        in_specs=[
            whole((TOK, D)),
            whole((TOK, D)),
            out_half,
            out_half,
            whole((1, D)),
            whole(router.shape),
            whole((TOK, 1)),
            whole((1, TOK)),
        ],
        out_specs=(
            whole((TOK, D)),
            whole((total // 2, D)),
            whole((total // 2, D)),
            whole((TOK, 1)),
        ),
        out_shape=(
            jax.ShapeDtypeStruct((TOK, D), F32),
            jax.ShapeDtypeStruct((total // 2, D), BF),
            jax.ShapeDtypeStruct((total // 2, D), BF),
            jax.ShapeDtypeStruct((TOK, 1), F32),
        ),
        scratch_shapes=[pltpu.VMEM((TOK, D), BF), pltpu.VMEM((D, D), BF)],
        compiler_params=params(),
        cost_estimate=cost(2 * total * TOK * D + 2 * TOK * D * D, 12 * TOK * D + 2 * total * D),
        name="middle",
    )(context, tokens, left, right, gain, router, routes, slot_row)


def gelu_parts(v):
    size = jnp.abs(v)
    t = 1.0 / (1.0 + (0.3275911 * 0.7071067811865476) * size)
    bell = jnp.exp(-0.5 * (v * v))
    series = t * (
        0.5 * 0.254829592
        + t * (0.5 * -0.284496736 + t * (0.5 * 1.421413741 + t * (0.5 * -1.453152027 + t * (0.5 * 1.061405429))))
    )
    tail = series * bell
    phi = jnp.where(v < 0, tail, 1.0 - tail)
    return v * phi, phi + v * (bell * 0.3989422804014327)


def expert_kernel(experts, x, c3, w_first, w_second, router, router_t, mine, *refs):
    act_ref, dh_ref, result, grad_x, gate_ref, grad_router, acc_r, acc_x = refs[-8:]
    step = pl.program_id(0)
    rows = x.shape[0]
    chunk = EXPERT_ROWS
    share = c3.shape[1]
    per = chunk // share

    @pl.when(step == 0)
    def _():
        acc_r[...] = jnp.zeros_like(acc_r)
        acc_x[...] = jnp.zeros_like(acc_x)

    for first in range(0, rows, chunk):
        at = slice(first, first + chunk)
        sources = slice(first // share, first // share + per)
        hidden = dot(x[at, :], w_first[...])
        grad_act = dot(c3[sources].reshape(chunk, D), w_second[...], 1, 1)
        act, slope = gelu_parts(hidden)
        act = act.astype(BF)
        grad_hidden = (grad_act * slope).astype(BF)
        act_ref[at, :] = act
        dh_ref[at, :] = grad_hidden
        acc_r[at, :] += dot(act, w_second[...])
        acc_x[at, :] += dot(grad_hidden, w_first[...], 1, 1)

    @pl.when(step == pl.num_programs(0) - 1)
    def _():
        total_router = jnp.zeros(grad_router.shape, F32)
        for first in range(0, rows, chunk):
            at = slice(first, first + chunk)
            sources = slice(first // share, first // share + per)
            rounded = acc_r[at, :].astype(BF)
            result[at, :] = rounded
            probs = router_softmax(x[at, :], router[...], experts)
            lane = lax.broadcasted_iota(jnp.int32, probs.shape, 1)
            here = lane == mine[0, 0]
            gate = jnp.sum(jnp.where(here, probs, 0.0), axis=1, keepdims=True)
            grad_gate = jnp.sum(
                c3[sources].reshape(chunk, D).astype(F32) * rounded.astype(F32), axis=1, keepdims=True
            )
            grad_logits = (
                probs * (jnp.where(here, grad_gate, 0.0) - gate * grad_gate)
            ).astype(BF)
            gate_ref[at, :] = gate
            grad_x[at, :] = (acc_x[at, :] * gate + dot(grad_logits, router_t[...])).astype(BF)
            total_router = total_router + dot(x[at, :], grad_logits, 0, 0)
        grad_router[...] = total_router


def run_expert(part, x, c, w_first, w_second, router, router_t, mine, experts):
    rows = x.shape[0]
    hidden_size = w_first.shape[1]
    lanes = router.shape[1]
    sources, capacity = c.shape[:2]
    half = pl.BlockSpec((sources, capacity // HALVES, D), lambda f: (0, part, 0))
    return pl.pallas_call(
        functools.partial(expert_kernel, experts),
        grid=(hidden_size // EXPERT_TILE,),
        in_specs=[
            whole((rows, D)),
            half,
            pl.BlockSpec((D, EXPERT_TILE), lambda f: (0, f)),
            pl.BlockSpec((EXPERT_TILE, D), lambda f: (f, 0)),
            whole((D, lanes)),
            whole((lanes, D)),
            pl.BlockSpec(memory_space=pltpu.SMEM),
        ],
        out_specs=[
            pl.BlockSpec((rows, EXPERT_TILE), lambda f: (0, f)),
            pl.BlockSpec((rows, EXPERT_TILE), lambda f: (0, f)),
            whole((rows, D)),
            whole((rows, D)),
            whole((rows, 1)),
            whole((D, lanes)),
        ],
        out_shape=[
            jax.ShapeDtypeStruct((rows, hidden_size), BF),
            jax.ShapeDtypeStruct((rows, hidden_size), BF),
            jax.ShapeDtypeStruct((rows, D), BF),
            jax.ShapeDtypeStruct((rows, D), BF),
            jax.ShapeDtypeStruct((rows, 1), F32),
            jax.ShapeDtypeStruct((D, lanes), F32),
        ],
        scratch_shapes=[pltpu.VMEM((rows, D), F32), pltpu.VMEM((rows, D), F32)],
        compiler_params=params(("arbitrary",)),
        cost_estimate=cost(
            8 * rows * D * hidden_size, 4 * rows * hidden_size + 4 * D * hidden_size
        ),
        name="expert",
    )(x, c, w_first, w_second, router, router_t, mine)


def expert_weights_kernel(parts, side, *refs):
    if side is not None:
        side, refs = refs[0], refs[1:]
    xs, gates = refs[:parts], refs[parts : 2 * parts]
    acts, dhs = refs[2 * parts : 3 * parts], refs[3 * parts : 4 * parts]
    cots = refs[4 * parts]
    if side is None:
        grad_first, grad_second, x_t, c_t = refs[4 * parts + 1 :]
    else:
        kept_first, sent_first, kept_second, sent_second, x_t, c_t, whole_first = refs[4 * parts + 1 :]
    rows = xs[0].shape[0]
    share = cots.shape[1] // parts
    chunk = 256
    per = chunk // share

    @pl.when(pl.program_id(0) == 0)
    def _():
        for part in range(parts):
            for first in range(0, rows, chunk):
                at = slice(first, first + chunk)
                to = slice(part * rows + first, part * rows + first + chunk)
                gate = gates[part][at, :]
                x_t[:, to] = (xs[part][at, :].astype(F32) * gate).T.astype(BF)
                cot = cots[
                    first // chunk * per : (first // chunk + 1) * per,
                    part * share : (part + 1) * share,
                ].reshape(chunk, D)
                c_t[:, to] = (cot.astype(F32) * gate).T.astype(BF)

    first_sum, second_sum = None, None
    for part in range(parts):
        at = slice(part * rows, (part + 1) * rows)
        one = dot(x_t[:, at], dhs[part][...])
        two = dot(c_t[:, at], acts[part][...])
        first_sum = one if first_sum is None else first_sum + one
        second_sum = two if second_sum is None else second_sum + two
    if side is None:
        grad_first[...] = first_sum.astype(BF)
        grad_second[...] = second_sum.T.astype(BF)
        return
    mine = side[0]
    half = D // 2
    whole_first[...] = first_sum.astype(BF)
    kept_first[...] = whole_first[pl.ds(pl.multiple_of(mine * half, half), half), :]
    sent_first[...] = whole_first[pl.ds(pl.multiple_of((1 - mine) * half, half), half), :]
    here = pl.program_id(0) // (pl.num_programs(0) // 2) == mine

    @pl.when(here)
    def _():
        kept_second[...] = second_sum.T.astype(BF)

    @pl.when(jnp.logical_not(here))
    def _():
        sent_second[...] = second_sum.T.astype(BF)


def expert_weights(xs, cots, gates, acts, dhs, side):
    parts = len(xs)
    rows = xs[0].shape[0]
    hidden_size = acts[0].shape[1]
    steps = hidden_size // FF_TILE
    in_specs = (
        [whole((rows, D))] * parts
        + [whole((rows, 1))] * parts
        + [pl.BlockSpec((rows, FF_TILE), lambda f, *_: (0, f))] * (2 * parts)
        + [whole(cots.shape)]
    )
    scratch = [pltpu.VMEM((D, parts * rows), BF), pltpu.VMEM((D, parts * rows), BF)]
    if side is None:
        out_specs = [
            pl.BlockSpec((D, FF_TILE), lambda f: (0, f)),
            pl.BlockSpec((FF_TILE, D), lambda f: (f, 0)),
        ]
        shapes = [(D, hidden_size), (hidden_size, D)]
    else:
        columns = pl.BlockSpec((D // 2, FF_TILE), lambda f, s: (0, f))

        def rows_of(place):
            def index(f, s):
                start = jnp.where(s[0] == 1, place, 1 - place) * (steps // 2)
                return (jnp.clip(f - start, 0, steps // 2 - 1), 0)

            return pl.BlockSpec((FF_TILE, D), index)

        out_specs = [columns, columns, rows_of(1), rows_of(0)]
        shapes = [(D // 2, hidden_size)] * 2 + [(hidden_size // 2, D)] * 2
        scratch = scratch + [pltpu.VMEM((D, FF_TILE), BF)]
    prefetched = () if side is None else (side,)
    return pl.pallas_call(
        functools.partial(expert_weights_kernel, parts, side is not None or None),
        grid_spec=pltpu.PrefetchScalarGridSpec(
            num_scalar_prefetch=len(prefetched),
            grid=(steps,),
            in_specs=in_specs,
            out_specs=out_specs,
            scratch_shapes=scratch,
        ),
        out_shape=[jax.ShapeDtypeStruct(shape, BF) for shape in shapes],
        compiler_params=params(("arbitrary",)),
        cost_estimate=cost(
            4 * parts * rows * D * hidden_size, 4 * (parts * rows + D) * hidden_size
        ),
        name="expert_weights",
    )(*prefetched, *xs, *gates, *acts, *dhs, cots)


def rms_back(values, factor, grad):
    inverse = inverse_rms(values)
    scaled = grad * factor
    mean = jnp.mean(scaled * values, axis=-1, keepdims=True)
    return (
        inverse * scaled - values * (inverse * inverse * inverse * mean),
        jnp.sum(grad * values * inverse, axis=0, keepdims=True),
    )


def undispatch(slot_col, parts):
    out = None
    offset = 0
    for part in parts:
        total = part.shape[0]
        place = lax.broadcasted_iota(jnp.int32, (slot_col.shape[0], total), 1) + offset
        found = dot((place == slot_col).astype(BF), part[...])
        out = found if out is None else out + found
        offset += total
    return out


def middle_back_kernel(parts, *refs):
    backs = refs[:parts]
    (
        slot_col, middle, cot, gain, out_left, out_right,
        grad_middle, grad_attn, grad_context, grad_gain, w_out,
    ) = refs[parts:]

    @pl.when(pl.program_id(0) == 0)
    def _():
        w_out[:, :SIDE] = out_left[...]
        w_out[:, SIDE:] = out_right[...]

    grad_normed = undispatch(slot_col[...], backs)
    part, gain_part = rms_back(middle[...], gain[...], grad_normed)
    grad = cot[...].astype(F32) + part
    grad_middle[...] = grad
    low = grad.astype(BF)
    grad_attn[...] = low
    grad_context[...] = dot(low, w_out[...], 1, 1).astype(BF)

    @pl.when(pl.program_id(0) == 0)
    def _():
        grad_gain[...] = gain_part

    @pl.when(pl.program_id(0) > 0)
    def _():
        grad_gain[...] += gain_part


def middle_back(backs, slot_col, middle, cot, gain, left, right):
    parts = len(backs)
    block = 256
    rows = pl.BlockSpec((block, D), lambda r: (r, 0))
    return pl.pallas_call(
        functools.partial(middle_back_kernel, parts),
        grid=(TOK // block,),
        in_specs=[whole(back.shape) for back in backs]
        + [
            pl.BlockSpec((block, 1), lambda r: (r, 0)),
            rows,
            rows,
            whole((1, D)),
            pl.BlockSpec((D, SIDE), lambda r: (0, 3)),
            pl.BlockSpec((D, SIDE), lambda r: (0, 3)),
        ],
        out_specs=[rows, rows, rows, whole((1, D))],
        scratch_shapes=[pltpu.VMEM((D, D), BF)],
        out_shape=[
            jax.ShapeDtypeStruct((TOK, D), F32),
            jax.ShapeDtypeStruct((TOK, D), BF),
            jax.ShapeDtypeStruct((TOK, D), BF),
            jax.ShapeDtypeStruct((1, D), F32),
        ],
        compiler_params=params(("arbitrary",)),
        cost_estimate=cost(2 * 2 * TOK * TOK * D + 2 * TOK * D * D, 16 * TOK * D),
        name="middle_back",
    )(*backs, slot_col, middle, cot, gain, left, right)


def mix_kernel(parts, *refs):
    backs = refs[:parts]
    slot_col, middle, gate, mixed = refs[parts:]
    mixed[...] = middle[...] + gate[...] * undispatch(slot_col[...], backs)


def mix(backs, slot_col, middle, gate):
    parts = len(backs)
    block = 256
    rows = pl.BlockSpec((block, D), lambda r: (r, 0))
    column = pl.BlockSpec((block, 1), lambda r: (r, 0))
    return pl.pallas_call(
        functools.partial(mix_kernel, parts),
        grid=(TOK // block,),
        in_specs=[whole(back.shape) for back in backs] + [column, rows, column],
        out_specs=rows,
        out_shape=jax.ShapeDtypeStruct((TOK, D), F32),
        compiler_params=params(("arbitrary",)),
        cost_estimate=cost(2 * 2 * TOK * TOK * D, 12 * TOK * D, share=1),
        name="mix",
    )(*backs, slot_col, middle, gate)


def tokens_back_kernel(g_left, g_right, left, right, tokens, gain, grad_middle, grad_tokens):
    grad_normed = dot(g_left[...], left[...], 1, 1) + dot(g_right[...], right[...], 1, 1)
    grad_tokens[...] = grad_middle[...] + rms_back(
        tokens[...].astype(F32), gain[...], grad_normed
    )[0]


def tokens_back(g_left, g_right, left, right, tokens, gain, grad_middle):
    block = 256
    rows = pl.BlockSpec((block, D), lambda r: (r, 0))
    return pl.pallas_call(
        tokens_back_kernel,
        grid=(TOK // block,),
        in_specs=[
            pl.BlockSpec((block, SPLIT), lambda r: (r, 0)),
            pl.BlockSpec((block, SPLIT), lambda r: (r, 0)),
            whole((D, SPLIT)),
            whole((D, SPLIT)),
            rows,
            whole((1, D)),
            rows,
        ],
        out_specs=rows,
        out_shape=jax.ShapeDtypeStruct((TOK, D), F32),
        compiler_params=params(("arbitrary",)),
        cost_estimate=cost(6 * TOK * D * D, 16 * TOK * D, share=1),
        name="tokens_back",
    )(g_left, g_right, left, right, tokens, gain, grad_middle)


def weights_back_kernel(turned, grads, context, grad_attn, out):
    last = pl.num_programs(0) - 1

    @pl.when(pl.program_id(0) < last)
    def _():
        out[...] = dot(turned[...], grads[...])

    @pl.when(pl.program_id(0) == last)
    def _():
        out[...] = dot(context[...], grad_attn[...], 0, 0)


def weights_back(half, turned, grads, context, grad_attn):
    steps = grads.shape[1] // SIDE
    columns = (steps + 1) * SIDE
    return pl.pallas_call(
        weights_back_kernel,
        grid=(steps + 1,),
        in_specs=[
            whole(turned.shape),
            pl.BlockSpec((TOK, SIDE), lambda c: (0, jnp.minimum(c, steps - 1))),
            whole((TOK, D)),
            pl.BlockSpec((TOK, SIDE), lambda c: (0, half)),
        ],
        out_specs=pl.BlockSpec((D, SIDE), lambda c: (0, c)),
        out_shape=jax.ShapeDtypeStruct((D, columns), F32),
        compiler_params=params(("arbitrary",)),
        cost_estimate=cost(2 * TOK * D * columns, 2 * TOK * (D + columns) + 4 * D * columns),
        name="weights_back",
    )(turned, grads, context, grad_attn)


def swap(block, axis, bit):
    size = lax.axis_size(axis)
    return lax.ppermute(block, axis, [(place, place ^ bit) for place in range(size)])


def on_upper(axis, bit):
    return (lax.axis_index(axis) // bit) % 2 == 1


def axis_bits(*axes):
    found = []
    for axis in axes:
        bit = lax.axis_size(axis) // 2
        while bit >= 1:
            found.append((axis, bit))
            bit //= 2
    return found


def orders():
    bits = axis_bits("dp", "expert")
    dp = [at for at, (axis, _) in enumerate(bits) if axis == "dp"]
    core = len(bits) - 1
    along = [at for at, (axis, bit) in enumerate(bits) if axis == "expert" and bit == 2]
    rest = [at for at in range(core) if at not in dp and at not in along]
    return (rest + along + dp + [core], rest + dp + along + [core])


def gather_start(shard):
    return shard.reshape((1,) * len(axis_bits("dp", "expert")) + shard.shape)


def gather_step(block, place):
    axis, bit = axis_bits("dp", "expert")[place]
    other = swap(block, axis, bit)
    upper = on_upper(axis, bit)
    return jnp.concatenate(
        [jnp.where(upper, other, block), jnp.where(upper, block, other)], axis=place
    )


def gather_end(block):
    return block.reshape((-1, block.shape[-1]))


def scatter_start(total):
    bits = axis_bits("dp", "expert")
    rows = total.shape[0] >> len(bits)
    return total.reshape((2,) * len(bits) + (rows,) + total.shape[1:])


def scatter_step(block, place, *others):
    axis, bit = axis_bits("dp", "expert")[place]
    lower = lax.slice_in_dim(block, 0, 1, axis=place)
    higher = lax.slice_in_dim(block, 1, 2, axis=place)
    upper = on_upper(axis, bit)
    sent = jnp.where(upper, lower, higher).astype(BF)
    kept = after(jnp.where(upper, higher, lower), *others)
    return kept + swap(sent, axis, bit).astype(F32)


def scatter_rest(block, order):
    for place in order:
        block = scatter_step(block, place)
    return block.reshape(block.shape[len(axis_bits("dp", "expert")) :])


def sum_all(total, beside):
    for number, (axis, bit) in enumerate(axis_bits("dp", "expert")):
        kept = after(total, beside[number]) if number < len(beside) else total
        total = kept + swap(total, axis, bit)
    return total


def gather_dp(block, axis, other=None):
    if lax.axis_size("dp") != 2:
        return lax.all_gather(block, "dp", axis=axis, tiled=True)
    if other is None:
        other = swap(block, "dp", 1)
    upper = on_upper("dp", 1)
    return jnp.concatenate(
        [jnp.where(upper, other, block), jnp.where(upper, block, other)], axis=axis
    )


def receive_dp(halves):
    if len(halves) == 1:
        return (lax.psum_scatter(halves[0], "dp", scatter_dimension=0, tiled=True),)
    kept, sent = halves
    return (kept, swap(sent, "dp", 1))


def add_dp(parts, *others):
    kept, *received = parts
    total = after(kept, *others).astype(F32)
    for part in received:
        total = total + part.astype(F32)
    return total[None]


def after(value, *others):
    return lax.optimization_barrier((value, *others))[0]


def body(
    tokens, seq_ids, routes, cotangent, w_query, w_key, w_value, w_out,
    rel_table, gain_attn, gain_ffn, router, expert_in, expert_out,
):
    experts = lax.axis_size("expert")
    capacity = 2 * TOK // experts
    shard = w_query.shape[0]
    lanes = -(-(experts + 2) // LANES) * LANES

    small = jnp.concatenate(
        [
            router,
            gain_attn[:, None],
            gain_ffn[:, None],
            jnp.zeros((shard, lanes - experts - 2), BF),
        ],
        axis=1,
    )
    first, second = orders()
    kinds = (w_query, w_key, w_value, w_out)
    paired = lax.axis_size("dp") == 2
    own_first, own_second = expert_in[0], expert_out[0]
    second_cut = own_second.shape[0] // 2
    early = [swap(own_second[:second_cut], "dp", 1)] if paired else []
    ahead = [own_second[:second_cut]] if paired else []
    left = gather_start(
        jnp.concatenate([after(w_query[:, :SIDE], *ahead)] + [w[:, :SIDE] for w in kinds[1:]], axis=1)
    )
    right = gather_start(
        jnp.concatenate(
            [after(w_query[:, SIDE:], *ahead)] + [w[:, SIDE:] for w in kinds[1:]] + [small], axis=1
        )
    )
    table = gather_dp(rel_table, 0)
    dp_bits = len(axis_bits("dp"))
    rest = len(first) - dp_bits - 2
    for at in range(rest):
        left, right = gather_step(left, first[at]), gather_step(right, second[at])
    left, right = lax.optimization_barrier((left, right, *early))[:2]
    slot_col, slot_row, sending_cot = make_slots(
        after(routes, left), cotangent, experts, capacity
    )
    left = gather_step(left, first[rest])
    for place in second[rest : rest + dp_bits]:
        right = gather_step(right, place)
    wide_table = after(table, right).astype(F32)
    query_features, key_features = lane_features(
        after(seq_ids, right).reshape(TOK, 1), wide_table
    )
    band = jnp.sum(band_onehot()[None, :, :] * wide_table.T[:, None, :], axis=2)[:, None, :]
    for place in first[rest + 1 : -1]:
        left = gather_step(left, place)
    for place in second[rest + dp_bits : -1]:
        right = gather_step(right, place)
    left = after(left, sending_cot)
    right = after(right, query_features, key_features, band)
    left = gather_end(gather_step(left, first[-1]))
    right = gather_end(gather_step(right, second[-1]))

    def exchange(rows):
        return lax.all_to_all(
            rows.reshape(experts, -1, D), "expert", split_axis=0, concat_axis=0, tiled=True
        )

    cots = exchange(after(sending_cot, left, right))
    if paired:
        other_first = swap(after(own_first, left, right), "dp", 1)
        late = swap(after(own_second[second_cut:], other_first), "dp", 1)
        other_second = jnp.concatenate([*early, late], axis=0)
        early.append(other_first)
    else:
        other_first = other_second = None
    w_first = gather_dp(own_first, 0, other_first)
    w_second = gather_dp(own_second, 0, other_second)

    extra = right[:, SPLIT + SIDE :]
    full_router = jnp.where(jnp.arange(lanes)[None, :] < experts, extra, jnp.zeros((), BF))
    router_t = full_router.T
    attn_gain = extra[:, experts].astype(F32).reshape(1, D)
    ffn_gain = extra[:, experts + 1].astype(F32).reshape(1, D)

    turned, qkv = project(tokens, attn_gain, left, right)
    context, lse = attend(qkv, query_features, key_features, band)

    middle, *sending, gate = make_middle(
        context, tokens, left, right, ffn_gain, full_router, routes, slot_row, experts, capacity
    )
    sending[0] = after(sending[0], cots, *early)
    sending[1] = after(sending[1], w_first, w_second)
    rows_in = [exchange(part).reshape(-1, D) for part in sending]
    mine = lax.axis_index("expert").astype(jnp.int32).reshape(1, 1)
    acts, dhs, results, grads, gates, router_parts = zip(
        *(
            run_expert(
                part, rows, cots, w_first, w_second, full_router, router_t, mine, experts
            )
            for part, rows in enumerate(rows_in)
        )
    )
    grads_home = [exchange(part).reshape(-1, D) for part in grads]
    weight_parts = expert_weights(
        rows_in,
        cots,
        (after(gates[0], grads_home[0]), *gates[1:]),
        acts,
        dhs,
        lax.axis_index("dp").astype(jnp.int32).reshape(1) if paired else None,
    )
    half = len(weight_parts) // 2
    grad_first, grad_second = weight_parts[:half], weight_parts[half:]
    results_home = []
    for part in results:
        part = after(part, *grads_home, *weight_parts, *results_home)
        results_home.append(exchange(part).reshape(-1, D))
    grads_home[0] = after(grads_home[0], *weight_parts)
    grad_middle, grad_attn, grad_context, grad_gain_f = middle_back(
        grads_home, slot_col, middle, cotangent, ffn_gain, left, right
    )
    down, down_other = second[::-1], first[::-1]

    def back(half, *others):
        return attend_back(
            half, qkv, after(grad_context, *others), query_features, key_features, lse, band
        )

    g_left, tiles_left, diagonals_left = back(0)
    left_block = scatter_start(weights_back(0, turned, g_left, context, grad_attn))
    g_right, tiles_right, diagonals_right = back(1, left_block, results_home[0])
    left_block = after(left_block, results_home[0])
    first_halves, second_halves = receive_dp(grad_first), receive_dp(grad_second)
    grad_right = weights_back(
        1, turned, after(g_right, results_home[1]), context, grad_attn
    )
    left_block = scatter_step(left_block, down[0], grad_right)
    right_block = scatter_step(scatter_start(grad_right), down_other[0], second_halves[-1])
    grad_tokens = tokens_back(
        g_left, after(g_right, right_block), left, right, tokens, attn_gain, grad_middle
    )
    beside = [left_block]
    left_block = scatter_step(left_block, down[1], grad_tokens)
    right_block = scatter_step(right_block, down_other[1], grad_tokens)
    beside.append(left_block)
    mixed = mix(results_home, slot_col, middle, after(gate, left_block, right_block))
    near = 2 + len(axis_bits("dp"))
    for place in down[2:near]:
        left_block = scatter_step(left_block, place, mixed, first_halves[-1])
    beside.append(left_block)
    for place in down_other[2:near]:
        right_block = scatter_step(right_block, place, mixed)
    joined = jnp.concatenate([left_block, right_block], axis=-1)
    grad_expert_in = add_dp(first_halves, joined)
    grad_expert_out = add_dp(second_halves, joined)
    joined = scatter_step(joined, down[near])
    beside.append(joined)
    dense = scatter_rest(joined, down[near + 1 :])
    grad_left, grad_right = dense[:, : SPLIT + SIDE], dense[:, SPLIT + SIDE :]
    tiles = jnp.concatenate([tiles_left, tiles_right], axis=0)
    diagonals = jnp.concatenate([diagonals_left, diagonals_right], axis=0)
    grad_router = sum(router_parts)[:, :experts]
    grad_table = table_gradient(tiles, diagonals)

    grad_weights = [
        jnp.concatenate(
            [side[:, kind * SIDE : (kind + 1) * SIDE] for side in (grad_left, grad_right)], axis=1
        )
        for kind in range(4)
    ]
    products = sum(w.astype(F32) * grad for w, grad in zip(kinds[:3], grad_weights[:3]))
    grad_gain_a = jnp.sum(products, axis=1) / gain_attn.astype(F32)

    sizes = (D * experts, D, BUCKETS * HEADS)
    sums = sum_all(
        jnp.concatenate(
            [part.reshape(-1, LANES) for part in (grad_router, grad_gain_f, grad_table)], axis=0
        ),
        beside,
    ).reshape(-1)
    ends = [sum(sizes[: at + 1]) for at in range(len(sizes))]
    grad_router, grad_gain_f, grad_table = (
        sums[end - size : end] for end, size in zip(ends, sizes)
    )
    number = lax.axis_index("dp") * experts + lax.axis_index("expert")
    table_height = BUCKETS // lax.axis_size("dp")

    def own(rows, height, place):
        return lax.dynamic_slice_in_dim(rows, place * height, height, 0)

    return (
        mixed,
        grad_tokens,
        *grad_weights,
        own(grad_table.reshape(BUCKETS, HEADS), table_height, lax.axis_index("dp")),
        grad_gain_a,
        own(grad_gain_f, shard, number),
        own(grad_router.reshape(D, experts), shard, number),
        grad_expert_in,
        grad_expert_out,
    )


def solution(mesh):
    rows = P(("dp", "expert"), None)
    flat = P(("dp", "expert"))
    expert = P("expert", "dp", None)
    return jax.shard_map(
        body,
        mesh=mesh,
        in_specs=(
            rows, flat, rows, rows, rows, rows, rows, rows,
            P("dp", None), flat, flat, rows, expert, expert,
        ),
        out_specs=(
            rows, rows, rows, rows, rows, rows,
            P("dp", None), flat, flat, rows, expert, expert,
        ),
        check_vma=False,
    )
```

```python
import functools

import jax
import jax.numpy as jnp
from jax import lax
from jax.experimental import pallas as pl
from jax.experimental.pallas import tpu as pltpu
from jax.sharding import PartitionSpec as P

D = 768
HEADS = 12
HEAD_DIM = 64
BUCKETS = 32
TOK = 1024
TILE = 128
TILES = TOK // TILE
QBLK = 256
FF_TILE = 512
EXPERT_TILE = 512
EXPERT_ROWS = 1024
HALVES = 2
SIDE = D // 2
SPLIT = 3 * SIDE
PAIRS = HEADS // 2
SIDE_PAIRS = PAIRS // 2
COST_SHARE = 0.05
LANES = 128

EPSILON = 1e-06
DISTANCE_EDGES = (12, 16, 23, 32, 46, 64, 91)
FAR_BEFORE = 15
FAR_AFTER = 31
UNPAIRED = -1e30
BF = jnp.bfloat16
F32 = jnp.float32
VMEM_LIMIT = 56 * 1024 * 1024


def dot(left, right, left_dim=1, right_dim=0):
    return lax.dot_general(
        left, right, (((left_dim,), (right_dim,)), ((), ())), preferred_element_type=F32
    )


def params(semantics=None):
    return pltpu.CompilerParams(vmem_limit_bytes=VMEM_LIMIT, dimension_semantics=semantics)


def cost(flops, bytes_accessed, transcendentals=0, share=COST_SHARE):
    return pl.CostEstimate(
        flops=int(flops * share),
        bytes_accessed=int(bytes_accessed * share),
        transcendentals=int(transcendentals * share),
    )


def whole(shape):
    return pl.BlockSpec(shape, lambda *_: (0,) * len(shape))


def inverse_rms(values):
    return lax.rsqrt(jnp.mean(values * values, axis=-1, keepdims=True) + EPSILON)


def bucket_of(offset):
    distance = jnp.abs(offset)
    distant = 8 + sum(((distance >= boundary).astype(jnp.int32) for boundary in DISTANCE_EDGES))
    return jnp.where(distance < 8, distance, distant) + jnp.where(offset > 0, 16, 0)


def place_in_buffers(route, rank, experts, capacity):
    share = capacity // HALVES
    part = (rank >= share).astype(jnp.int32)
    return part * (experts * share) + route * share + (rank - part * share)


def slots_kernel(experts, capacity, route_col, route_row, cot, slot_col, flat_col, slot_row, sending):
    padded = -(-experts // LANES) * LANES
    picked = (
        lax.broadcasted_iota(jnp.int32, (TOK, padded), 1) == route_col[...]
    ).astype(BF)
    picked_t = (
        lax.broadcasted_iota(jnp.int32, (padded, TOK), 0) == route_row[...]
    ).astype(BF)
    upto = (
        lax.broadcasted_iota(jnp.int32, (TOK, TOK), 0)
        <= lax.broadcasted_iota(jnp.int32, (TOK, TOK), 1)
    ).astype(BF)
    from_t = (
        lax.broadcasted_iota(jnp.int32, (TOK, TOK), 0)
        >= lax.broadcasted_iota(jnp.int32, (TOK, TOK), 1)
    ).astype(BF)
    counts = dot(from_t, picked) * picked.astype(F32)
    rank = jnp.sum(counts, axis=1, keepdims=True).astype(jnp.int32) - 1
    slot_col[...] = place_in_buffers(route_col[...], rank, experts, capacity)
    flat_col[...] = route_col[...] * capacity + rank
    counts_t = dot(picked_t, upto) * picked_t.astype(F32)
    rank_row = jnp.sum(counts_t, axis=0, keepdims=True).astype(jnp.int32) - 1
    slot_row[...] = place_in_buffers(route_row[...], rank_row, experts, capacity)
    dispatch(route_row[...] * capacity + rank_row, cot[...], [sending])


def dispatch(row, rows, parts):
    step = 512
    offset = 0
    for sending in parts:
        for first in range(0, sending.shape[0], step):
            chosen = (
                lax.broadcasted_iota(jnp.int32, (step, TOK), 0) + (first + offset) == row
            ).astype(BF)
            sending[first : first + step, :] = dot(chosen, rows).astype(BF)
        offset += sending.shape[0]


def make_slots(routes, cotangent, experts, capacity):
    total = experts * capacity
    return pl.pallas_call(
        functools.partial(slots_kernel, experts, capacity),
        out_shape=(
            jax.ShapeDtypeStruct((TOK, 1), jnp.int32),
            jax.ShapeDtypeStruct((TOK, 1), jnp.int32),
            jax.ShapeDtypeStruct((1, TOK), jnp.int32),
            jax.ShapeDtypeStruct((total, D), BF),
        ),
        compiler_params=params(),
        cost_estimate=cost(2 * total * TOK * D, 6 * total * D),
        name="slots",
    )(routes, routes.reshape(1, TOK), cotangent)


def project_kernel(tokens, gain, left, right, turned, qkv):
    x = tokens[...].astype(F32)
    wide = x * inverse_rms(x) * gain[...]
    low = wide.astype(BF)
    turned[...] = wide.T.astype(BF)
    qkv[:, :SPLIT] = dot(low, left[...]).astype(BF)
    qkv[:, SPLIT:] = dot(low, right[...]).astype(BF)


def project(tokens, gain, left, right):
    block = 256
    rows = pl.BlockSpec((block, D), lambda r: (r, 0))
    return pl.pallas_call(
        project_kernel,
        grid=(TOK // block,),
        in_specs=[rows, whole((1, D)), whole((D, SPLIT)), whole((D, SPLIT))],
        out_specs=[
            pl.BlockSpec((D, block), lambda r: (0, r)),
            pl.BlockSpec((block, 3 * D), lambda r: (r, 0)),
        ],
        out_shape=[
            jax.ShapeDtypeStruct((D, TOK), BF),
            jax.ShapeDtypeStruct((TOK, 3 * D), BF),
        ],
        compiler_params=params(("arbitrary",)),
        cost_estimate=cost(6 * TOK * D * D, 12 * TOK * D),
        name="project",
    )(tokens, gain, left, right)


def lane_features(seq_col, rel_table):
    lane = jnp.arange(LANES, dtype=jnp.int32)[None, :]
    feature = lane % HEAD_DIM
    tile = jnp.arange(TOK, dtype=jnp.int32)[:, None] // TILE
    on_tile = feature - 4
    query_features = jnp.where(
        feature < 4,
        jnp.where(feature == seq_col, 0.0, UNPAIRED),
        jnp.where(on_tile == tile, 1.0, 0.0),
    ).astype(BF)
    wide = jnp.arange(D, dtype=jnp.int32)[None, :]
    feature = wide % HEAD_DIM
    on_tile = feature - 4
    swapped = jnp.arange(HEADS, dtype=jnp.int32) ^ 1
    before = jnp.repeat(rel_table[FAR_BEFORE][swapped], HEAD_DIM)[None, :]
    after = jnp.repeat(rel_table[FAR_AFTER][swapped], HEAD_DIM)[None, :]
    apart = tile - on_tile
    far = jnp.where(apart >= 2, after, jnp.where(apart <= -2, before, 0.0))
    key_features = jnp.where(
        feature < 4,
        jnp.where(feature == seq_col, 1.0, 0.0),
        jnp.where(on_tile < TILES, far, 0.0),
    ).astype(BF)
    return query_features, key_features


def band_offsets():
    place = jnp.arange(4 * LANES, dtype=jnp.int32)
    return 255 - (place + 383) % 512


def band_onehot():
    return (
        bucket_of(band_offsets())[:, None] == jnp.arange(BUCKETS, dtype=jnp.int32)[None, :]
    ).astype(F32)


def near_rows(tile):
    first = max(tile - 1, 0)
    last = min(tile + 2, TILES)
    return first, last


def spread_band(values):
    wide = jnp.broadcast_to(values, (3 * TILE, 4 * LANES))
    return pltpu.roll(wide, 0, 1, stride=1, stride_axis=0)[:, :TILE]


def add_band(st, slot, block, band):
    for part in range(QBLK // TILE):
        tile = block * (QBLK // TILE) + part
        first, last = near_rows(tile)
        at = (slot, slice(first * TILE, last * TILE), slice(part * TILE, (part + 1) * TILE))
        st[at] += band[(first - tile + 1) * TILE : (last - tile + 1) * TILE]


def attend_kernel(q_ref, k_ref, v_ref, qx_ref, kx_ref, band_ref, out_ref, lse_ref, st, pb, ot):
    low = lax.broadcasted_iota(jnp.int32, (TOK, LANES), 1) < HEAD_DIM
    v_t = v_ref[...].astype(F32).T.astype(BF)
    sides = []
    for side in range(2):
        own = low if side == 0 else ~low
        sides.append(
            (
                jnp.where(own, q_ref[...], qx_ref[...]),
                jnp.where(own, k_ref[...], kx_ref[...]),
                spread_band(band_ref[side]),
            )
        )
    work = [(side, block) for side in range(2) for block in range(TOK // QBLK)]

    def score(number):
        side, block = work[number]
        queries, keys, band = sides[side]
        st[number % 2] = dot(keys, queries[block * QBLK : (block + 1) * QBLK], 1, 1)

    def finish(number):
        side, block = work[number]
        slot = number % 2
        rows = slice(block * QBLK, (block + 1) * QBLK)
        add_band(st, slot, block, sides[side][2])
        top = jnp.max(st[slot, 0:TILE], axis=0, keepdims=True)
        for chunk in range(1, TILES):
            top = jnp.maximum(
                top,
                jnp.max(st[slot, chunk * TILE : (chunk + 1) * TILE], axis=0, keepdims=True),
            )
        total = jnp.zeros((1, QBLK), F32)
        for chunk in range(TILES):
            at = slice(chunk * TILE, (chunk + 1) * TILE)
            raised = jnp.exp(st[slot, at] - top)
            total = total + jnp.sum(raised, axis=0, keepdims=True)
            pb[slot, at] = raised.astype(BF)
        lse_ref[side, :, rows] = top + jnp.log(total)
        return total

    def mix_values(number, total):
        side, block = work[number]
        half = slice(side * HEAD_DIM, (side + 1) * HEAD_DIM)
        rows = slice(block * QBLK, (block + 1) * QBLK)
        ot[half, rows] = dot(v_t[half], pb[number % 2]) * (1.0 / total)

    score(0)
    waiting = None
    for number in range(len(work)):
        if number + 1 < len(work):
            score(number + 1)
        if waiting is not None:
            mix_values(number - 1, waiting)
        waiting = finish(number)
    mix_values(len(work) - 1, waiting)
    out_ref[...] = ot[...].T.astype(BF)


def attend(qkv, query_features, key_features, band):
    return pl.pallas_call(
        attend_kernel,
        grid=(PAIRS,),
        in_specs=[
            *(
                pl.BlockSpec(
                    (TOK, LANES),
                    lambda p, kind=kind: (
                        0,
                        p // SIDE_PAIRS * (3 * SIDE_PAIRS) + kind * SIDE_PAIRS + p % SIDE_PAIRS,
                    ),
                )
                for kind in range(3)
            ),
            whole((TOK, LANES)),
            pl.BlockSpec((TOK, LANES), lambda p: (0, p)),
            pl.BlockSpec((2, 1, 4 * LANES), lambda p: (p, 0, 0)),
        ],
        out_specs=[
            pl.BlockSpec((TOK, LANES), lambda p: (0, p)),
            pl.BlockSpec((2, 1, TOK), lambda p: (p, 0, 0)),
        ],
        out_shape=[
            jax.ShapeDtypeStruct((TOK, D), BF),
            jax.ShapeDtypeStruct((HEADS, 1, TOK), F32),
        ],
        scratch_shapes=[
            pltpu.VMEM((2, TOK, QBLK), F32),
            pltpu.VMEM((2, TOK, QBLK), BF),
            pltpu.VMEM((LANES, TOK), F32),
        ],
        compiler_params=params(("arbitrary",)),
        cost_estimate=cost(2 * 3 * HEADS * TOK * TOK * 256, 10 * TOK * D, HEADS * TOK * TOK),
        name="attend",
    )(qkv, qkv, qkv, query_features, key_features, band)


def attend_back_kernel(
    q_ref, k_ref, v_ref, do_ref, qx_ref, kx_ref, lse_ref, band_ref,
    grad_ref, tiles_ref, diag_ref,
    st, dp, pb, sb, dqt, dkt, dvt, near,
):
    low = lax.broadcasted_iota(jnp.int32, (TOK, LANES), 1) < HEAD_DIM
    k_t = k_ref[...].astype(F32).T.astype(BF)
    sides = []
    for side in range(2):
        own = low if side == 0 else ~low
        sides.append(
            (
                jnp.where(own, q_ref[...], qx_ref[...]),
                jnp.where(own, k_ref[...], kx_ref[...]),
                jnp.where(own, v_ref[...], jnp.zeros((), BF)),
                spread_band(band_ref[side]),
            )
        )
    near[...] = jnp.zeros_like(near)
    work = [(side, block) for side in range(2) for block in range(TOK // QBLK)]

    def rows_of(block):
        return slice(block * QBLK, (block + 1) * QBLK)

    def score(number):
        side, block = work[number]
        queries, keys, values, _ = sides[side]
        st[number % 2] = dot(keys, queries[rows_of(block)], 1, 1)
        dp[number % 2] = dot(values, do_ref[rows_of(block), :], 1, 1)

    def finish(number):
        side, block = work[number]
        slot = number % 2
        add_band(st, slot, block, sides[side][3])
        lse = lse_ref[side, :, rows_of(block)]
        spread = jnp.zeros((1, QBLK), F32)
        for chunk in range(TILES):
            at = slice(chunk * TILE, (chunk + 1) * TILE)
            weights = jnp.exp(st[slot, at] - lse)
            st[slot, at] = weights
            pb[slot, at] = weights.astype(BF)
            spread = spread + jnp.sum(weights * dp[slot, at], axis=0, keepdims=True)
        for chunk in range(TILES):
            at = slice(chunk * TILE, (chunk + 1) * TILE)
            sb[slot, at] = (st[slot, at] * (dp[slot, at] - spread)).astype(BF)
        for part in range(QBLK // TILE):
            tile = block * (QBLK // TILE) + part
            first, last = near_rows(tile)
            at = (slot, slice(first * TILE, last * TILE), slice(part * TILE, (part + 1) * TILE))
            near[side, (first - tile + 1) * TILE : (last - tile + 1) * TILE, :TILE] += sb[
                at
            ].astype(F32)

    def multiply(number):
        side, block = work[number]
        slot = number % 2
        rows = rows_of(block)
        half = slice(side * HEAD_DIM, (side + 1) * HEAD_DIM)
        dv = dot(pb[slot], do_ref[rows, :])
        dk = dot(sb[slot], sides[side][0][rows])
        if block == 0:
            dvt[side] = dv
            dkt[side] = dk
        else:
            dvt[side] += dv
            dkt[side] += dk
        dqt[half, rows] = dot(k_t[half], sb[slot])

    score(0)
    for number in range(len(work)):
        if number + 1 < len(work):
            score(number + 1)
        if number > 0:
            multiply(number - 1)
        finish(number)
    multiply(len(work) - 1)
    for side in range(2):
        for tile in range(TILES):
            tiles_ref[side, tile : tile + 1, :] = jnp.sum(
                dkt[side, tile * TILE : (tile + 1) * TILE], axis=0, keepdims=True
            )
        folded = near[side, 0:8, :]
        for first in range(8, 3 * TILE, 8):
            folded = folded + pltpu.roll(near[side, first : first + 8, :], 4 * LANES - first, 1)
        diagonal = folded[0:1]
        for row in range(1, 8):
            diagonal = diagonal + pltpu.roll(folded[row : row + 1], 4 * LANES - row, 1)
        diag_ref[side] = diagonal
    found = (
        dqt[...].T.astype(BF),
        jnp.where(low, dkt[0], dkt[1]).astype(BF),
        jnp.where(low, dvt[0], dvt[1]).astype(BF),
    )
    for pair in range(SIDE_PAIRS):

        @pl.when(pl.program_id(0) == pair)
        def _():
            for kind in range(3):
                first = kind * SIDE + pair * LANES
                grad_ref[:, first : first + LANES] = found[kind]


def attend_back(half, qkv, grad_context, query_features, key_features, lse, band):
    first = half * SIDE_PAIRS
    column = pl.BlockSpec((TOK, LANES), lambda p: (0, first + p))
    return pl.pallas_call(
        attend_back_kernel,
        grid=(SIDE_PAIRS,),
        in_specs=[
            *(
                pl.BlockSpec(
                    (TOK, LANES), lambda p, kind=kind: (0, (3 * half + kind) * SIDE_PAIRS + p)
                )
                for kind in range(3)
            ),
            column,
            whole((TOK, LANES)),
            column,
            pl.BlockSpec((2, 1, TOK), lambda p: (first + p, 0, 0)),
            pl.BlockSpec((2, 1, 4 * LANES), lambda p: (first + p, 0, 0)),
        ],
        out_specs=[
            whole((TOK, SPLIT)),
            pl.BlockSpec((2, TILES, LANES), lambda p: (p, 0, 0)),
            pl.BlockSpec((2, 1, 4 * LANES), lambda p: (p, 0, 0)),
        ],
        out_shape=[
            jax.ShapeDtypeStruct((TOK, SPLIT), BF),
            jax.ShapeDtypeStruct((HEADS // 2, TILES, LANES), F32),
            jax.ShapeDtypeStruct((HEADS // 2, 1, 4 * LANES), F32),
        ],
        scratch_shapes=[
            pltpu.VMEM((2, TOK, QBLK), F32),
            pltpu.VMEM((2, TOK, QBLK), F32),
            pltpu.VMEM((2, TOK, QBLK), BF),
            pltpu.VMEM((2, TOK, QBLK), BF),
            pltpu.VMEM((LANES, TOK), F32),
            pltpu.VMEM((2, TOK, LANES), F32),
            pltpu.VMEM((2, TOK, LANES), F32),
            pltpu.VMEM((2, 3 * TILE, 4 * LANES), F32),
        ],
        compiler_params=params(("arbitrary",)),
        cost_estimate=cost(5 * HEADS * TOK * TOK * 256, 8 * TOK * D, HEADS * TOK * TOK // 2, share=0.3),
        name="attend_back",
    )(qkv, qkv, qkv, grad_context, query_features, key_features, lse, band)


def table_gradient(tiles, diagonals):
    near = jnp.einsum(
        "hl,lb->bh", diagonals[:, 0, :], band_onehot(), precision=lax.Precision.HIGHEST
    )
    sums = jnp.concatenate(
        [tiles[h : h + 1, :, (HEAD_DIM if h % 2 == 0 else 0) + 4 :][:, :, :TILES] for h in range(HEADS)],
        axis=0,
    )
    apart = (
        jnp.arange(TILES, dtype=jnp.int32)[:, None] - jnp.arange(TILES, dtype=jnp.int32)[None, :]
    )[None]
    before = jnp.sum(jnp.where(apart <= -2, sums, 0.0), axis=(1, 2))
    after = jnp.sum(jnp.where(apart >= 2, sums, 0.0), axis=(1, 2))
    place = jnp.arange(BUCKETS, dtype=jnp.int32)[:, None]
    return (
        near
        + jnp.where(place == FAR_BEFORE, before[None, :], 0.0)
        + jnp.where(place == FAR_AFTER, after[None, :], 0.0)
    )


def middle_kernel(context, tokens, out_left, out_right, gain, router, route_col, slot_row, experts,
                  middle, sending_low, sending_high, gate, normed, w_out):
    w_out[:, :SIDE] = out_left[...]
    w_out[:, SIDE:] = out_right[...]
    for first in range(0, TOK, 256):
        at = slice(first, first + 256)
        mid = tokens[at, :].astype(F32) + dot(context[at, :], w_out[...])
        middle[at, :] = mid
        low = (mid * inverse_rms(mid) * gain[...]).astype(BF)
        normed[at, :] = low
        probs = router_softmax(low, router[...], experts)
        lane = lax.broadcasted_iota(jnp.int32, probs.shape, 1)
        gate[at, :] = jnp.sum(
            jnp.where(lane == route_col[at, :], probs, 0.0), axis=1, keepdims=True
        )
    dispatch(slot_row[...], normed[...], [sending_low, sending_high])


def router_softmax(rows, router, experts):
    logits = dot(rows, router)
    lane = lax.broadcasted_iota(jnp.int32, logits.shape, 1)
    logits = jnp.where(lane < experts, logits, UNPAIRED)
    raised = jnp.exp(logits - jnp.max(logits, axis=1, keepdims=True))
    return raised / jnp.sum(raised, axis=1, keepdims=True)


def make_middle(context, tokens, left, right, gain, router, routes, slot_row, experts, capacity):
    total = experts * capacity

    def kernel(*refs):
        middle_kernel(*refs[:8], experts, *refs[8:])

    out_half = pl.BlockSpec((D, SIDE), lambda r: (0, 3))
    return pl.pallas_call(
        kernel,
        grid=(1,),
        in_specs=[
            whole((TOK, D)),
            whole((TOK, D)),
            out_half,
            out_half,
            whole((1, D)),
            whole(router.shape),
            whole((TOK, 1)),
            whole((1, TOK)),
        ],
        out_specs=(
            whole((TOK, D)),
            whole((total // 2, D)),
            whole((total // 2, D)),
            whole((TOK, 1)),
        ),
        out_shape=(
            jax.ShapeDtypeStruct((TOK, D), F32),
            jax.ShapeDtypeStruct((total // 2, D), BF),
            jax.ShapeDtypeStruct((total // 2, D), BF),
            jax.ShapeDtypeStruct((TOK, 1), F32),
        ),
        scratch_shapes=[pltpu.VMEM((TOK, D), BF), pltpu.VMEM((D, D), BF)],
        compiler_params=params(),
        cost_estimate=cost(2 * total * TOK * D + 2 * TOK * D * D, 12 * TOK * D + 2 * total * D),
        name="middle",
    )(context, tokens, left, right, gain, router, routes, slot_row)


def gelu_parts(v):
    size = jnp.abs(v)
    t = 1.0 / (1.0 + (0.3275911 * 0.7071067811865476) * size)
    bell = jnp.exp(-0.5 * (v * v))
    series = t * (
        0.5 * 0.254829592
        + t * (0.5 * -0.284496736 + t * (0.5 * 1.421413741 + t * (0.5 * -1.453152027 + t * (0.5 * 1.061405429))))
    )
    tail = series * bell
    phi = jnp.where(v < 0, tail, 1.0 - tail)
    return v * phi, phi + v * (bell * 0.3989422804014327)


def expert_kernel(experts, x, c3, w_first, w_second, router, router_t, mine, *refs):
    act_ref, dh_ref, result, grad_x, gate_ref, grad_router, acc_r, acc_x = refs[-8:]
    step = pl.program_id(0)
    rows = x.shape[0]
    chunk = EXPERT_ROWS
    share = c3.shape[1]
    per = chunk // share

    @pl.when(step == 0)
    def _():
        acc_r[...] = jnp.zeros_like(acc_r)
        acc_x[...] = jnp.zeros_like(acc_x)

    for first in range(0, rows, chunk):
        at = slice(first, first + chunk)
        sources = slice(first // share, first // share + per)
        hidden = dot(x[at, :], w_first[...])
        grad_act = dot(c3[sources].reshape(chunk, D), w_second[...], 1, 1)
        act, slope = gelu_parts(hidden)
        act = act.astype(BF)
        grad_hidden = (grad_act * slope).astype(BF)
        act_ref[at, :] = act
        dh_ref[at, :] = grad_hidden
        acc_r[at, :] += dot(act, w_second[...])
        acc_x[at, :] += dot(grad_hidden, w_first[...], 1, 1)

    @pl.when(step == pl.num_programs(0) - 1)
    def _():
        total_router = jnp.zeros(grad_router.shape, F32)
        for first in range(0, rows, chunk):
            at = slice(first, first + chunk)
            sources = slice(first // share, first // share + per)
            rounded = acc_r[at, :].astype(BF)
            result[sources] = rounded.reshape(per, share, D)
            probs = router_softmax(x[at, :], router[...], experts)
            lane = lax.broadcasted_iota(jnp.int32, probs.shape, 1)
            here = lane == mine[0, 0]
            gate = jnp.sum(jnp.where(here, probs, 0.0), axis=1, keepdims=True)
            grad_gate = jnp.sum(
                c3[sources].reshape(chunk, D).astype(F32) * rounded.astype(F32), axis=1, keepdims=True
            )
            grad_logits = (
                probs * (jnp.where(here, grad_gate, 0.0) - gate * grad_gate)
            ).astype(BF)
            gate_ref[at, :] = gate
            grad_x[at, :] = (acc_x[at, :] * gate + dot(grad_logits, router_t[...])).astype(BF)
            total_router = total_router + dot(x[at, :], grad_logits, 0, 0)
        grad_router[...] = total_router


def run_expert(part, x, c, w_first, w_second, router, router_t, mine, experts, results=None):
    rows = x.shape[0]
    hidden_size = w_first.shape[1]
    lanes = router.shape[1]
    sources, capacity = c.shape[:2]
    half = pl.BlockSpec((sources, capacity // HALVES, D), lambda f: (0, part, 0))
    chained = () if results is None else (results,)
    return pl.pallas_call(
        functools.partial(expert_kernel, experts),
        grid=(hidden_size // EXPERT_TILE,),
        in_specs=[
            whole((rows, D)),
            half,
            pl.BlockSpec((D, EXPERT_TILE), lambda f: (0, f)),
            pl.BlockSpec((EXPERT_TILE, D), lambda f: (f, 0)),
            whole((D, lanes)),
            whole((lanes, D)),
            pl.BlockSpec(memory_space=pltpu.SMEM),
        ]
        + [pl.BlockSpec(memory_space=pl.ANY)] * len(chained),
        out_specs=[
            pl.BlockSpec((rows, EXPERT_TILE), lambda f: (0, f)),
            pl.BlockSpec((rows, EXPERT_TILE), lambda f: (0, f)),
            half,
            whole((rows, D)),
            whole((rows, 1)),
            whole((D, lanes)),
        ],
        out_shape=[
            jax.ShapeDtypeStruct((rows, hidden_size), BF),
            jax.ShapeDtypeStruct((rows, hidden_size), BF),
            jax.ShapeDtypeStruct(c.shape, BF),
            jax.ShapeDtypeStruct((rows, D), BF),
            jax.ShapeDtypeStruct((rows, 1), F32),
            jax.ShapeDtypeStruct((D, lanes), F32),
        ],
        scratch_shapes=[pltpu.VMEM((rows, D), F32), pltpu.VMEM((rows, D), F32)],
        input_output_aliases={7: 2} if chained else {},
        compiler_params=params(("arbitrary",)),
        cost_estimate=cost(
            8 * rows * D * hidden_size, 4 * rows * hidden_size + 4 * D * hidden_size
        ),
        name="expert",
    )(x, c, w_first, w_second, router, router_t, mine, *chained)


def expert_weights_kernel(parts, side, *refs):
    if side is not None:
        side, refs = refs[0], refs[1:]
    xs, gates = refs[:parts], refs[parts : 2 * parts]
    acts, dhs = refs[2 * parts : 3 * parts], refs[3 * parts : 4 * parts]
    cots = refs[4 * parts]
    if side is None:
        grad_first, grad_second, x_t, c_t = refs[4 * parts + 1 :]
    else:
        kept_first, sent_first, kept_second, sent_second, x_t, c_t, whole_first = refs[4 * parts + 1 :]
    rows = xs[0].shape[0]
    share = cots.shape[1] // parts
    chunk = 256
    per = chunk // share

    @pl.when(pl.program_id(0) == 0)
    def _():
        for part in range(parts):
            for first in range(0, rows, chunk):
                at = slice(first, first + chunk)
                to = slice(part * rows + first, part * rows + first + chunk)
                gate = gates[part][at, :]
                x_t[:, to] = (xs[part][at, :].astype(F32) * gate).T.astype(BF)
                cot = cots[
                    first // chunk * per : (first // chunk + 1) * per,
                    part * share : (part + 1) * share,
                ].reshape(chunk, D)
                c_t[:, to] = (cot.astype(F32) * gate).T.astype(BF)

    first_sum, second_sum = None, None
    for part in range(parts):
        at = slice(part * rows, (part + 1) * rows)
        one = dot(x_t[:, at], dhs[part][...])
        two = dot(c_t[:, at], acts[part][...])
        first_sum = one if first_sum is None else first_sum + one
        second_sum = two if second_sum is None else second_sum + two
    if side is None:
        grad_first[...] = first_sum.astype(BF)
        grad_second[...] = second_sum.T.astype(BF)
        return
    mine = side[0]
    half = D // 2
    whole_first[...] = first_sum.astype(BF)
    kept_first[...] = whole_first[pl.ds(pl.multiple_of(mine * half, half), half), :]
    sent_first[...] = whole_first[pl.ds(pl.multiple_of((1 - mine) * half, half), half), :]
    here = pl.program_id(0) // (pl.num_programs(0) // 2) == mine

    @pl.when(here)
    def _():
        kept_second[...] = second_sum.T.astype(BF)

    @pl.when(jnp.logical_not(here))
    def _():
        sent_second[...] = second_sum.T.astype(BF)


def expert_weights(xs, cots, gates, acts, dhs, side):
    parts = len(xs)
    rows = xs[0].shape[0]
    hidden_size = acts[0].shape[1]
    steps = hidden_size // FF_TILE
    in_specs = (
        [whole((rows, D))] * parts
        + [whole((rows, 1))] * parts
        + [pl.BlockSpec((rows, FF_TILE), lambda f, *_: (0, f))] * (2 * parts)
        + [whole(cots.shape)]
    )
    scratch = [pltpu.VMEM((D, parts * rows), BF), pltpu.VMEM((D, parts * rows), BF)]
    if side is None:
        out_specs = [
            pl.BlockSpec((D, FF_TILE), lambda f: (0, f)),
            pl.BlockSpec((FF_TILE, D), lambda f: (f, 0)),
        ]
        shapes = [(D, hidden_size), (hidden_size, D)]
    else:
        columns = pl.BlockSpec((D // 2, FF_TILE), lambda f, s: (0, f))

        def rows_of(place):
            def index(f, s):
                start = jnp.where(s[0] == 1, place, 1 - place) * (steps // 2)
                return (jnp.clip(f - start, 0, steps // 2 - 1), 0)

            return pl.BlockSpec((FF_TILE, D), index)

        out_specs = [columns, columns, rows_of(1), rows_of(0)]
        shapes = [(D // 2, hidden_size)] * 2 + [(hidden_size // 2, D)] * 2
        scratch = scratch + [pltpu.VMEM((D, FF_TILE), BF)]
    prefetched = () if side is None else (side,)
    return pl.pallas_call(
        functools.partial(expert_weights_kernel, parts, side is not None or None),
        grid_spec=pltpu.PrefetchScalarGridSpec(
            num_scalar_prefetch=len(prefetched),
            grid=(steps,),
            in_specs=in_specs,
            out_specs=out_specs,
            scratch_shapes=scratch,
        ),
        out_shape=[jax.ShapeDtypeStruct(shape, BF) for shape in shapes],
        compiler_params=params(("arbitrary",)),
        cost_estimate=cost(
            4 * parts * rows * D * hidden_size, 4 * (parts * rows + D) * hidden_size
        ),
        name="expert_weights",
    )(*prefetched, *xs, *gates, *acts, *dhs, cots)


def rms_back(values, factor, grad):
    inverse = inverse_rms(values)
    scaled = grad * factor
    mean = jnp.mean(scaled * values, axis=-1, keepdims=True)
    return (
        inverse * scaled - values * (inverse * inverse * inverse * mean),
        jnp.sum(grad * values * inverse, axis=0, keepdims=True),
    )


def undispatch(slot_col, parts):
    out = None
    offset = 0
    for part in parts:
        total = part.shape[0]
        place = lax.broadcasted_iota(jnp.int32, (slot_col.shape[0], total), 1) + offset
        found = dot((place == slot_col).astype(BF), part[...])
        out = found if out is None else out + found
        offset += total
    return out


def middle_back_kernel(parts, *refs):
    backs = refs[:parts]
    (
        slot_col, middle, cot, gain, out_left, out_right,
        grad_middle, grad_attn, grad_context, grad_gain, w_out,
    ) = refs[parts:]

    @pl.when(pl.program_id(0) == 0)
    def _():
        w_out[:, :SIDE] = out_left[...]
        w_out[:, SIDE:] = out_right[...]

    grad_normed = undispatch(slot_col[...], backs)
    part, gain_part = rms_back(middle[...], gain[...], grad_normed)
    grad = cot[...].astype(F32) + part
    grad_middle[...] = grad
    low = grad.astype(BF)
    grad_attn[...] = low
    grad_context[...] = dot(low, w_out[...], 1, 1).astype(BF)

    @pl.when(pl.program_id(0) == 0)
    def _():
        grad_gain[...] = gain_part

    @pl.when(pl.program_id(0) > 0)
    def _():
        grad_gain[...] += gain_part


def middle_back(backs, slot_col, middle, cot, gain, left, right):
    parts = len(backs)
    block = 256
    rows = pl.BlockSpec((block, D), lambda r: (r, 0))
    return pl.pallas_call(
        functools.partial(middle_back_kernel, parts),
        grid=(TOK // block,),
        in_specs=[whole(back.shape) for back in backs]
        + [
            pl.BlockSpec((block, 1), lambda r: (r, 0)),
            rows,
            rows,
            whole((1, D)),
            pl.BlockSpec((D, SIDE), lambda r: (0, 3)),
            pl.BlockSpec((D, SIDE), lambda r: (0, 3)),
        ],
        out_specs=[rows, rows, rows, whole((1, D))],
        scratch_shapes=[pltpu.VMEM((D, D), BF)],
        out_shape=[
            jax.ShapeDtypeStruct((TOK, D), F32),
            jax.ShapeDtypeStruct((TOK, D), BF),
            jax.ShapeDtypeStruct((TOK, D), BF),
            jax.ShapeDtypeStruct((1, D), F32),
        ],
        compiler_params=params(("arbitrary",)),
        cost_estimate=cost(2 * 2 * TOK * TOK * D + 2 * TOK * D * D, 16 * TOK * D),
        name="middle_back",
    )(*backs, slot_col, middle, cot, gain, left, right)


def mix_kernel(parts, *refs):
    backs = refs[:parts]
    slot_col, middle, gate, mixed = refs[parts:]
    mixed[...] = middle[...] + gate[...] * undispatch(slot_col[...], backs)


def mix(backs, slot_col, middle, gate):
    parts = len(backs)
    block = 256
    rows = pl.BlockSpec((block, D), lambda r: (r, 0))
    column = pl.BlockSpec((block, 1), lambda r: (r, 0))
    return pl.pallas_call(
        functools.partial(mix_kernel, parts),
        grid=(TOK // block,),
        in_specs=[whole(back.shape) for back in backs] + [column, rows, column],
        out_specs=rows,
        out_shape=jax.ShapeDtypeStruct((TOK, D), F32),
        compiler_params=params(("arbitrary",)),
        cost_estimate=cost(2 * 2 * TOK * TOK * D, 12 * TOK * D, share=1),
        name="mix",
    )(*backs, slot_col, middle, gate)


def tokens_back_kernel(g_left, g_right, left, right, tokens, gain, grad_middle, grad_tokens):
    grad_normed = dot(g_left[...], left[...], 1, 1) + dot(g_right[...], right[...], 1, 1)
    grad_tokens[...] = grad_middle[...] + rms_back(
        tokens[...].astype(F32), gain[...], grad_normed
    )[0]


def tokens_back(g_left, g_right, left, right, tokens, gain, grad_middle):
    block = 256
    rows = pl.BlockSpec((block, D), lambda r: (r, 0))
    return pl.pallas_call(
        tokens_back_kernel,
        grid=(TOK // block,),
        in_specs=[
            pl.BlockSpec((block, SPLIT), lambda r: (r, 0)),
            pl.BlockSpec((block, SPLIT), lambda r: (r, 0)),
            whole((D, SPLIT)),
            whole((D, SPLIT)),
            rows,
            whole((1, D)),
            rows,
        ],
        out_specs=rows,
        out_shape=jax.ShapeDtypeStruct((TOK, D), F32),
        compiler_params=params(("arbitrary",)),
        cost_estimate=cost(6 * TOK * D * D, 16 * TOK * D, share=1),
        name="tokens_back",
    )(g_left, g_right, left, right, tokens, gain, grad_middle)


def weights_back_kernel(steps, turned, grads, *refs):
    if len(refs) == 1:
        refs[0][...] = dot(turned[...], grads[...])
        return
    context, grad_attn, out = refs

    @pl.when(pl.program_id(0) < steps)
    def _():
        out[...] = dot(turned[...], grads[...])

    @pl.when(pl.program_id(0) >= steps)
    def _():
        out[...] = dot(context[...], grad_attn[...], 0, 0)


def weights_back(turned, grads, *others):
    steps = grads.shape[1] // SIDE
    more = others[1].shape[1] // SIDE if others else 0
    columns = (steps + more) * SIDE
    return pl.pallas_call(
        functools.partial(weights_back_kernel, steps),
        grid=(steps + more,),
        in_specs=[
            whole(turned.shape),
            pl.BlockSpec((TOK, SIDE), lambda c: (0, jnp.minimum(c, steps - 1))),
        ]
        + (
            [
                whole((TOK, D)),
                pl.BlockSpec((TOK, SIDE), lambda c: (0, jnp.maximum(c - steps, 0))),
            ]
            if others
            else []
        ),
        out_specs=pl.BlockSpec((D, SIDE), lambda c: (0, c)),
        out_shape=jax.ShapeDtypeStruct((D, columns), F32),
        compiler_params=params(("arbitrary",)),
        cost_estimate=cost(2 * TOK * D * columns, 2 * TOK * (D + columns) + 4 * D * columns),
        name="weights_back",
    )(turned, grads, *others)


def swap(block, axis, bit):
    size = lax.axis_size(axis)
    return lax.ppermute(block, axis, [(place, place ^ bit) for place in range(size)])


def on_upper(axis, bit):
    return (lax.axis_index(axis) // bit) % 2 == 1


def axis_bits(*axes):
    found = []
    for axis in axes:
        bit = lax.axis_size(axis) // 2
        while bit >= 1:
            found.append((axis, bit))
            bit //= 2
    return found


def orders():
    bits = axis_bits("dp", "expert")
    dp = [at for at, (axis, _) in enumerate(bits) if axis == "dp"]
    core = len(bits) - 1
    along = [at for at, (axis, bit) in enumerate(bits) if axis == "expert" and bit == 2]
    rest = [at for at in range(core) if at not in dp and at not in along]
    return (rest + along + dp + [core], rest + dp + along + [core])


def gather_start(shard):
    return shard.reshape((1,) * len(axis_bits("dp", "expert")) + shard.shape)


def gather_step(block, place):
    axis, bit = axis_bits("dp", "expert")[place]
    other = swap(block, axis, bit)
    upper = on_upper(axis, bit)
    return jnp.concatenate(
        [jnp.where(upper, other, block), jnp.where(upper, block, other)], axis=place
    )


def gather_end(block):
    return block.reshape((-1, block.shape[-1]))


def scatter_start(total):
    bits = axis_bits("dp", "expert")
    rows = total.shape[0] >> len(bits)
    return total.reshape((2,) * len(bits) + (rows,) + total.shape[1:])


def scatter_step(block, place, *others):
    axis, bit = axis_bits("dp", "expert")[place]
    lower = lax.slice_in_dim(block, 0, 1, axis=place)
    higher = lax.slice_in_dim(block, 1, 2, axis=place)
    upper = on_upper(axis, bit)
    sent = jnp.where(upper, lower, higher).astype(BF)
    kept = after(jnp.where(upper, higher, lower), *others)
    return kept + swap(sent, axis, bit).astype(F32)


def scatter_rest(block, order):
    for place in order:
        block = scatter_step(block, place)
    return block.reshape(block.shape[len(axis_bits("dp", "expert")) :])


def sum_all(total, beside):
    for number, (axis, bit) in enumerate(axis_bits("dp", "expert")):
        kept = after(total, beside[number]) if number < len(beside) else total
        total = kept + swap(total, axis, bit)
    return total


def gather_dp(block, axis, other=None):
    if lax.axis_size("dp") != 2:
        return lax.all_gather(block, "dp", axis=axis, tiled=True)
    if other is None:
        other = swap(block, "dp", 1)
    upper = on_upper("dp", 1)
    return jnp.concatenate(
        [jnp.where(upper, other, block), jnp.where(upper, block, other)], axis=axis
    )


def receive_dp(halves):
    if len(halves) == 1:
        return (lax.psum_scatter(halves[0], "dp", scatter_dimension=0, tiled=True),)
    kept, sent = halves
    return (kept, swap(sent, "dp", 1))


def add_dp(parts, *others):
    kept, *received = parts
    total = after(kept, *others).astype(F32)
    for part in received:
        total = total + part.astype(F32)
    return total[None]


def after(value, *others):
    return lax.optimization_barrier((value, *others))[0]


def body(
    tokens, seq_ids, routes, cotangent, w_query, w_key, w_value, w_out,
    rel_table, gain_attn, gain_ffn, router, expert_in, expert_out,
):
    experts = lax.axis_size("expert")
    capacity = 2 * TOK // experts
    shard = w_query.shape[0]
    lanes = -(-(experts + 2) // LANES) * LANES

    small = jnp.concatenate(
        [
            router,
            gain_attn[:, None],
            gain_ffn[:, None],
            jnp.zeros((shard, lanes - experts - 2), BF),
        ],
        axis=1,
    )
    first, second = orders()
    kinds = (w_query, w_key, w_value, w_out)
    paired = lax.axis_size("dp") == 2
    own_first, own_second = expert_in[0], expert_out[0]
    second_cut = own_second.shape[0] // 2
    early = [swap(own_second[:second_cut], "dp", 1)] if paired else []
    ahead = [own_second[:second_cut]] if paired else []
    left = gather_start(
        jnp.concatenate([after(w_query[:, :SIDE], *ahead)] + [w[:, :SIDE] for w in kinds[1:]], axis=1)
    )
    right = gather_start(
        jnp.concatenate(
            [after(w_query[:, SIDE:], *ahead)] + [w[:, SIDE:] for w in kinds[1:]] + [small], axis=1
        )
    )
    table = gather_dp(rel_table, 0)
    dp_bits = len(axis_bits("dp"))
    rest = len(first) - dp_bits - 2
    for at in range(rest):
        left, right = gather_step(left, first[at]), gather_step(right, second[at])
    left, right = lax.optimization_barrier((left, right, *early))[:2]
    slot_col, flat_col, slot_row, sending_cot = make_slots(
        after(routes, left), cotangent, experts, capacity
    )
    left = gather_step(left, first[rest])
    for place in second[rest : rest + dp_bits]:
        right = gather_step(right, place)
    wide_table = after(table, right).astype(F32)
    query_features, key_features = lane_features(
        after(seq_ids, right).reshape(TOK, 1), wide_table
    )
    band = jnp.sum(band_onehot()[None, :, :] * wide_table.T[:, None, :], axis=2)[:, None, :]
    for place in first[rest + 1 : -1]:
        left = gather_step(left, place)
    for place in second[rest + dp_bits : -1]:
        right = gather_step(right, place)
    left = after(left, sending_cot)
    right = after(right, query_features, key_features, band)
    left = gather_end(gather_step(left, first[-1]))
    right = gather_end(gather_step(right, second[-1]))

    def exchange(rows):
        return lax.all_to_all(
            rows.reshape(experts, -1, D), "expert", split_axis=0, concat_axis=0, tiled=True
        )

    cots = exchange(after(sending_cot, left, right))
    if paired:
        third_cut = second_cut + second_cut // 3
        other_first = swap(after(own_first, left, right), "dp", 1)
        early.append(swap(after(own_second[second_cut:third_cut], left, right), "dp", 1))
        late = swap(after(own_second[third_cut:], other_first), "dp", 1)
        other_second = jnp.concatenate([*early, late], axis=0)
        early.append(other_first)
    else:
        other_first = other_second = None
    w_first = gather_dp(own_first, 0, other_first)
    w_second = gather_dp(own_second, 0, other_second)

    extra = right[:, SPLIT + SIDE :]
    full_router = jnp.where(jnp.arange(lanes)[None, :] < experts, extra, jnp.zeros((), BF))
    router_t = full_router.T
    attn_gain = extra[:, experts].astype(F32).reshape(1, D)
    ffn_gain = extra[:, experts + 1].astype(F32).reshape(1, D)

    turned, qkv = project(tokens, attn_gain, left, right)
    context, lse = attend(qkv, query_features, key_features, band)

    middle, *sending, gate = make_middle(
        context, tokens, left, right, ffn_gain, full_router, routes, slot_row, experts, capacity
    )
    sending[0] = after(sending[0], cots, *early)
    sending[1] = after(sending[1], w_first, w_second)
    rows_in = [exchange(part).reshape(-1, D) for part in sending]
    mine = lax.axis_index("expert").astype(jnp.int32).reshape(1, 1)
    runs, results = [], None
    for part, rows in enumerate(rows_in):
        act, dh, results, *others = run_expert(
            part, rows, cots, w_first, w_second, full_router, router_t, mine, experts, results
        )
        runs.append((act, dh, *others))
    acts, dhs, grads, gates, router_parts = zip(*runs)
    grads_home = [exchange(part).reshape(-1, D) for part in grads]
    weight_parts = expert_weights(
        rows_in,
        cots,
        (after(gates[0], grads_home[0]), *gates[1:]),
        acts,
        dhs,
        lax.axis_index("dp").astype(jnp.int32).reshape(1) if paired else None,
    )
    half = len(weight_parts) // 2
    grad_first, grad_second = weight_parts[:half], weight_parts[half:]
    results_home = exchange(after(results, *grads_home, *weight_parts)).reshape(-1, D)
    grads_home[0] = after(grads_home[0], *weight_parts)
    grad_middle, grad_attn, grad_context, grad_gain_f = middle_back(
        grads_home, slot_col, middle, cotangent, ffn_gain, left, right
    )
    down, down_other = second[::-1], first[::-1]

    def back(half, *others):
        return attend_back(
            half, qkv, after(grad_context, *others), query_features, key_features, lse, band
        )

    g_left, tiles_left, diagonals_left = back(0)
    left_block = scatter_start(weights_back(turned, g_left, context, grad_attn))
    g_right, tiles_right, diagonals_right = back(1, left_block)
    first_halves, second_halves = receive_dp(grad_first), receive_dp(grad_second)
    grad_right = weights_back(turned, after(g_right, results_home))
    left_block = scatter_step(left_block, down[0], grad_right)
    right_block = scatter_step(scatter_start(grad_right), down_other[0], second_halves[-1])
    grad_tokens = tokens_back(
        g_left, after(g_right, right_block), left, right, tokens, attn_gain, grad_middle
    )
    beside = [left_block]
    left_block = scatter_step(left_block, down[1], grad_tokens)
    right_block = scatter_step(right_block, down_other[1], grad_tokens)
    beside.append(left_block)
    mixed = mix([results_home], flat_col, middle, after(gate, left_block, right_block))
    near = 2 + len(axis_bits("dp"))
    for place in down[2:near]:
        left_block = scatter_step(left_block, place, mixed, first_halves[-1])
    beside.append(left_block)
    for place in down_other[2:near]:
        right_block = scatter_step(right_block, place, mixed)
    joined = jnp.concatenate([left_block, right_block], axis=-1)
    grad_expert_in = add_dp(first_halves, joined)
    grad_expert_out = add_dp(second_halves, joined)
    joined = scatter_step(joined, down[near])
    beside.append(joined)
    dense = scatter_rest(joined, down[near + 1 :])
    grad_left, grad_w_out, grad_right = jnp.split(dense, (SPLIT, SPLIT + D), axis=1)
    tiles = jnp.concatenate([tiles_left, tiles_right], axis=0)
    diagonals = jnp.concatenate([diagonals_left, diagonals_right], axis=0)
    grad_router = sum(router_parts)[:, :experts]
    grad_table = table_gradient(tiles, diagonals)

    grad_weights = [
        jnp.concatenate(
            [side[:, kind * SIDE : (kind + 1) * SIDE] for side in (grad_left, grad_right)], axis=1
        )
        for kind in range(3)
    ]
    products = sum(w.astype(F32) * grad for w, grad in zip(kinds[:3], grad_weights))
    grad_gain_a = jnp.sum(products, axis=1) / gain_attn.astype(F32)

    sizes = (D * experts, D, BUCKETS * HEADS)
    sums = sum_all(
        jnp.concatenate(
            [part.reshape(-1, LANES) for part in (grad_router, grad_gain_f, grad_table)], axis=0
        ),
        beside,
    ).reshape(-1)
    ends = [sum(sizes[: at + 1]) for at in range(len(sizes))]
    grad_router, grad_gain_f, grad_table = (
        sums[end - size : end] for end, size in zip(ends, sizes)
    )
    number = lax.axis_index("dp") * experts + lax.axis_index("expert")
    table_height = BUCKETS // lax.axis_size("dp")

    def own(rows, height, place):
        return lax.dynamic_slice_in_dim(rows, place * height, height, 0)

    return (
        mixed,
        grad_tokens,
        *grad_weights,
        grad_w_out,
        own(grad_table.reshape(BUCKETS, HEADS), table_height, lax.axis_index("dp")),
        grad_gain_a,
        own(grad_gain_f, shard, number),
        own(grad_router.reshape(D, experts), shard, number),
        grad_expert_in,
        grad_expert_out,
    )


def solution(mesh):
    rows = P(("dp", "expert"), None)
    flat = P(("dp", "expert"))
    expert = P("expert", "dp", None)
    return jax.shard_map(
        body,
        mesh=mesh,
        in_specs=(
            rows, flat, rows, rows, rows, rows, rows, rows,
            P("dp", None), flat, flat, rows, expert, expert,
        ),
        out_specs=(
            rows, rows, rows, rows, rows, rows,
            P("dp", None), flat, flat, rows, expert, expert,
        ),
        check_vma=False,
    )
```

```python
import functools

import jax
import jax.numpy as jnp
from jax import lax
from jax.experimental import pallas as pl
from jax.experimental.pallas import tpu as pltpu
from jax.sharding import PartitionSpec as P

D = 768
HEADS = 12
HEAD_DIM = 64
BUCKETS = 32
TOK = 1024
TILE = 128
TILES = TOK // TILE
QBLK = 256
FF_TILE = 512
EXPERT_TILE = 512
EXPERT_ROWS = 1024
HALVES = 2
SIDE = D // 2
SPLIT = 3 * SIDE
PAIRS = HEADS // 2
SIDE_PAIRS = PAIRS // 2
COST_SHARE = 0.05
LANES = 128

EPSILON = 1e-06
DISTANCE_EDGES = (12, 16, 23, 32, 46, 64, 91)
FAR_BEFORE = 15
FAR_AFTER = 31
UNPAIRED = -1e30
BF = jnp.bfloat16
F32 = jnp.float32
VMEM_LIMIT = 56 * 1024 * 1024


def dot(left, right, left_dim=1, right_dim=0):
    return lax.dot_general(
        left, right, (((left_dim,), (right_dim,)), ((), ())), preferred_element_type=F32
    )


def params(semantics=None):
    return pltpu.CompilerParams(vmem_limit_bytes=VMEM_LIMIT, dimension_semantics=semantics)


def cost(flops, bytes_accessed, transcendentals=0, share=COST_SHARE):
    return pl.CostEstimate(
        flops=int(flops * share),
        bytes_accessed=int(bytes_accessed * share),
        transcendentals=int(transcendentals * share),
    )


def whole(shape):
    return pl.BlockSpec(shape, lambda *_: (0,) * len(shape))


def inverse_rms(values):
    return lax.rsqrt(jnp.mean(values * values, axis=-1, keepdims=True) + EPSILON)


def bucket_of(offset):
    distance = jnp.abs(offset)
    distant = 8 + sum(((distance >= boundary).astype(jnp.int32) for boundary in DISTANCE_EDGES))
    return jnp.where(distance < 8, distance, distant) + jnp.where(offset > 0, 16, 0)


def place_in_buffers(route, rank, experts, capacity):
    share = capacity // HALVES
    part = (rank >= share).astype(jnp.int32)
    return part * (experts * share) + route * share + (rank - part * share)


def slots_kernel(experts, capacity, route_col, route_row, cot, slot_col, slot_row, sending):
    padded = -(-experts // LANES) * LANES
    picked = (
        lax.broadcasted_iota(jnp.int32, (TOK, padded), 1) == route_col[...]
    ).astype(BF)
    picked_t = (
        lax.broadcasted_iota(jnp.int32, (padded, TOK), 0) == route_row[...]
    ).astype(BF)
    upto = (
        lax.broadcasted_iota(jnp.int32, (TOK, TOK), 0)
        <= lax.broadcasted_iota(jnp.int32, (TOK, TOK), 1)
    ).astype(BF)
    from_t = (
        lax.broadcasted_iota(jnp.int32, (TOK, TOK), 0)
        >= lax.broadcasted_iota(jnp.int32, (TOK, TOK), 1)
    ).astype(BF)
    counts = dot(from_t, picked) * picked.astype(F32)
    rank = jnp.sum(counts, axis=1, keepdims=True).astype(jnp.int32) - 1
    slot_col[...] = place_in_buffers(route_col[...], rank, experts, capacity)
    counts_t = dot(picked_t, upto) * picked_t.astype(F32)
    rank_row = jnp.sum(counts_t, axis=0, keepdims=True).astype(jnp.int32) - 1
    slot_row[...] = place_in_buffers(route_row[...], rank_row, experts, capacity)
    dispatch(route_row[...] * capacity + rank_row, cot[...], [sending])


def dispatch(row, rows, parts):
    step = 512
    offset = 0
    for sending in parts:
        for first in range(0, sending.shape[0], step):
            chosen = (
                lax.broadcasted_iota(jnp.int32, (step, TOK), 0) + (first + offset) == row
            ).astype(BF)
            sending[first : first + step, :] = dot(chosen, rows).astype(BF)
        offset += sending.shape[0]


def make_slots(routes, cotangent, experts, capacity):
    total = experts * capacity
    return pl.pallas_call(
        functools.partial(slots_kernel, experts, capacity),
        out_shape=(
            jax.ShapeDtypeStruct((TOK, 1), jnp.int32),
            jax.ShapeDtypeStruct((1, TOK), jnp.int32),
            jax.ShapeDtypeStruct((total, D), BF),
        ),
        compiler_params=params(),
        cost_estimate=cost(2 * total * TOK * D, 6 * total * D),
        name="slots",
    )(routes, routes.reshape(1, TOK), cotangent)


def project_kernel(tokens, gain, left, right, turned, qkv):
    x = tokens[...].astype(F32)
    wide = x * inverse_rms(x) * gain[...]
    low = wide.astype(BF)
    turned[...] = wide.T.astype(BF)
    qkv[:, :SPLIT] = dot(low, left[...]).astype(BF)
    qkv[:, SPLIT:] = dot(low, right[...]).astype(BF)


def project(tokens, gain, left, right):
    block = 256
    rows = pl.BlockSpec((block, D), lambda r: (r, 0))
    return pl.pallas_call(
        project_kernel,
        grid=(TOK // block,),
        in_specs=[rows, whole((1, D)), whole((D, SPLIT)), whole((D, SPLIT))],
        out_specs=[
            pl.BlockSpec((D, block), lambda r: (0, r)),
            pl.BlockSpec((block, 3 * D), lambda r: (r, 0)),
        ],
        out_shape=[
            jax.ShapeDtypeStruct((D, TOK), BF),
            jax.ShapeDtypeStruct((TOK, 3 * D), BF),
        ],
        compiler_params=params(("arbitrary",)),
        cost_estimate=cost(6 * TOK * D * D, 12 * TOK * D),
        name="project",
    )(tokens, gain, left, right)


def lane_features(seq_col, rel_table):
    lane = jnp.arange(LANES, dtype=jnp.int32)[None, :]
    feature = lane % HEAD_DIM
    tile = jnp.arange(TOK, dtype=jnp.int32)[:, None] // TILE
    on_tile = feature - 4
    query_features = jnp.where(
        feature < 4,
        jnp.where(feature == seq_col, 0.0, UNPAIRED),
        jnp.where(on_tile == tile, 1.0, 0.0),
    ).astype(BF)
    wide = jnp.arange(D, dtype=jnp.int32)[None, :]
    feature = wide % HEAD_DIM
    on_tile = feature - 4
    swapped = jnp.arange(HEADS, dtype=jnp.int32) ^ 1
    before = jnp.repeat(rel_table[FAR_BEFORE][swapped], HEAD_DIM)[None, :]
    after = jnp.repeat(rel_table[FAR_AFTER][swapped], HEAD_DIM)[None, :]
    apart = tile - on_tile
    far = jnp.where(apart >= 2, after, jnp.where(apart <= -2, before, 0.0))
    key_features = jnp.where(
        feature < 4,
        jnp.where(feature == seq_col, 1.0, 0.0),
        jnp.where(on_tile < TILES, far, 0.0),
    ).astype(BF)
    return query_features, key_features


def band_offsets():
    place = jnp.arange(4 * LANES, dtype=jnp.int32)
    return 255 - (place + 383) % 512


def band_onehot():
    return (
        bucket_of(band_offsets())[:, None] == jnp.arange(BUCKETS, dtype=jnp.int32)[None, :]
    ).astype(F32)


def near_rows(tile):
    first = max(tile - 1, 0)
    last = min(tile + 2, TILES)
    return first, last


def spread_band(values):
    wide = jnp.broadcast_to(values, (3 * TILE, 4 * LANES))
    return pltpu.roll(wide, 0, 1, stride=1, stride_axis=0)[:, :TILE]


def add_band(st, slot, block, band):
    for part in range(QBLK // TILE):
        tile = block * (QBLK // TILE) + part
        first, last = near_rows(tile)
        at = (slot, slice(first * TILE, last * TILE), slice(part * TILE, (part + 1) * TILE))
        st[at] += band[(first - tile + 1) * TILE : (last - tile + 1) * TILE]


def attend_kernel(q_ref, k_ref, v_ref, qx_ref, kx_ref, band_ref, out_ref, lse_ref, st, pb, ot):
    low = lax.broadcasted_iota(jnp.int32, (TOK, LANES), 1) < HEAD_DIM
    v_t = v_ref[...].astype(F32).T.astype(BF)
    sides = []
    for side in range(2):
        own = low if side == 0 else ~low
        sides.append(
            (
                jnp.where(own, q_ref[...], qx_ref[...]),
                jnp.where(own, k_ref[...], kx_ref[...]),
                spread_band(band_ref[side]),
            )
        )
    work = [(side, block) for side in range(2) for block in range(TOK // QBLK)]

    def score(number):
        side, block = work[number]
        queries, keys, band = sides[side]
        st[number % 2] = dot(keys, queries[block * QBLK : (block + 1) * QBLK], 1, 1)

    def finish(number):
        side, block = work[number]
        slot = number % 2
        rows = slice(block * QBLK, (block + 1) * QBLK)
        add_band(st, slot, block, sides[side][2])
        top = jnp.max(st[slot, 0:TILE], axis=0, keepdims=True)
        for chunk in range(1, TILES):
            top = jnp.maximum(
                top,
                jnp.max(st[slot, chunk * TILE : (chunk + 1) * TILE], axis=0, keepdims=True),
            )
        total = jnp.zeros((1, QBLK), F32)
        for chunk in range(TILES):
            at = slice(chunk * TILE, (chunk + 1) * TILE)
            raised = jnp.exp(st[slot, at] - top)
            total = total + jnp.sum(raised, axis=0, keepdims=True)
            pb[slot, at] = raised.astype(BF)
        lse_ref[side, :, rows] = top + jnp.log(total)
        return total

    def mix_values(number, total):
        side, block = work[number]
        half = slice(side * HEAD_DIM, (side + 1) * HEAD_DIM)
        rows = slice(block * QBLK, (block + 1) * QBLK)
        ot[half, rows] = dot(v_t[half], pb[number % 2]) * (1.0 / total)

    score(0)
    waiting = None
    for number in range(len(work)):
        if number + 1 < len(work):
            score(number + 1)
        if waiting is not None:
            mix_values(number - 1, waiting)
        waiting = finish(number)
    mix_values(len(work) - 1, waiting)
    out_ref[...] = ot[...].T.astype(BF)


def attend(qkv, query_features, key_features, band):
    return pl.pallas_call(
        attend_kernel,
        grid=(PAIRS,),
        in_specs=[
            *(
                pl.BlockSpec(
                    (TOK, LANES),
                    lambda p, kind=kind: (
                        0,
                        p // SIDE_PAIRS * (3 * SIDE_PAIRS) + kind * SIDE_PAIRS + p % SIDE_PAIRS,
                    ),
                )
                for kind in range(3)
            ),
            whole((TOK, LANES)),
            pl.BlockSpec((TOK, LANES), lambda p: (0, p)),
            pl.BlockSpec((2, 1, 4 * LANES), lambda p: (p, 0, 0)),
        ],
        out_specs=[
            pl.BlockSpec((TOK, LANES), lambda p: (0, p)),
            pl.BlockSpec((2, 1, TOK), lambda p: (p, 0, 0)),
        ],
        out_shape=[
            jax.ShapeDtypeStruct((TOK, D), BF),
            jax.ShapeDtypeStruct((HEADS, 1, TOK), F32),
        ],
        scratch_shapes=[
            pltpu.VMEM((2, TOK, QBLK), F32),
            pltpu.VMEM((2, TOK, QBLK), BF),
            pltpu.VMEM((LANES, TOK), F32),
        ],
        compiler_params=params(("arbitrary",)),
        cost_estimate=cost(2 * 3 * HEADS * TOK * TOK * 256, 10 * TOK * D, HEADS * TOK * TOK),
        name="attend",
    )(qkv, qkv, qkv, query_features, key_features, band)


def attend_back_kernel(
    q_ref, k_ref, v_ref, do_ref, qx_ref, kx_ref, lse_ref, band_ref,
    grad_ref, tiles_ref, diag_ref,
    st, dp, pb, sb, dqt, dkt, dvt, near,
):
    low = lax.broadcasted_iota(jnp.int32, (TOK, LANES), 1) < HEAD_DIM
    k_t = k_ref[...].astype(F32).T.astype(BF)
    sides = []
    for side in range(2):
        own = low if side == 0 else ~low
        sides.append(
            (
                jnp.where(own, q_ref[...], qx_ref[...]),
                jnp.where(own, k_ref[...], kx_ref[...]),
                jnp.where(own, v_ref[...], jnp.zeros((), BF)),
                spread_band(band_ref[side]),
            )
        )
    near[...] = jnp.zeros_like(near)
    work = [(side, block) for side in range(2) for block in range(TOK // QBLK)]

    def rows_of(block):
        return slice(block * QBLK, (block + 1) * QBLK)

    def score(number):
        side, block = work[number]
        queries, keys, values, _ = sides[side]
        st[number % 2] = dot(keys, queries[rows_of(block)], 1, 1)
        dp[number % 2] = dot(values, do_ref[rows_of(block), :], 1, 1)

    def finish(number):
        side, block = work[number]
        slot = number % 2
        add_band(st, slot, block, sides[side][3])
        lse = lse_ref[side, :, rows_of(block)]
        spread = jnp.zeros((1, QBLK), F32)
        for chunk in range(TILES):
            at = slice(chunk * TILE, (chunk + 1) * TILE)
            weights = jnp.exp(st[slot, at] - lse)
            st[slot, at] = weights
            pb[slot, at] = weights.astype(BF)
            spread = spread + jnp.sum(weights * dp[slot, at], axis=0, keepdims=True)
        for chunk in range(TILES):
            at = slice(chunk * TILE, (chunk + 1) * TILE)
            sb[slot, at] = (st[slot, at] * (dp[slot, at] - spread)).astype(BF)
        for part in range(QBLK // TILE):
            tile = block * (QBLK // TILE) + part
            first, last = near_rows(tile)
            at = (slot, slice(first * TILE, last * TILE), slice(part * TILE, (part + 1) * TILE))
            near[side, (first - tile + 1) * TILE : (last - tile + 1) * TILE, :TILE] += sb[
                at
            ].astype(F32)

    def multiply(number):
        side, block = work[number]
        slot = number % 2
        rows = rows_of(block)
        half = slice(side * HEAD_DIM, (side + 1) * HEAD_DIM)
        dv = dot(pb[slot], do_ref[rows, :])
        dk = dot(sb[slot], sides[side][0][rows])
        if block == 0:
            dvt[side] = dv
            dkt[side] = dk
        else:
            dvt[side] += dv
            dkt[side] += dk
        dqt[half, rows] = dot(k_t[half], sb[slot])

    score(0)
    for number in range(len(work)):
        if number + 1 < len(work):
            score(number + 1)
        if number > 0:
            multiply(number - 1)
        finish(number)
    multiply(len(work) - 1)
    for side in range(2):
        for tile in range(TILES):
            tiles_ref[side, tile : tile + 1, :] = jnp.sum(
                dkt[side, tile * TILE : (tile + 1) * TILE], axis=0, keepdims=True
            )
        folded = near[side, 0:8, :]
        for first in range(8, 3 * TILE, 8):
            folded = folded + pltpu.roll(near[side, first : first + 8, :], 4 * LANES - first, 1)
        diagonal = folded[0:1]
        for row in range(1, 8):
            diagonal = diagonal + pltpu.roll(folded[row : row + 1], 4 * LANES - row, 1)
        diag_ref[side] = diagonal
    found = (
        dqt[...].T.astype(BF),
        jnp.where(low, dkt[0], dkt[1]).astype(BF),
        jnp.where(low, dvt[0], dvt[1]).astype(BF),
    )
    for pair in range(SIDE_PAIRS):

        @pl.when(pl.program_id(0) == pair)
        def _():
            for kind in range(3):
                first = kind * SIDE + pair * LANES
                grad_ref[:, first : first + LANES] = found[kind]


def attend_back(half, qkv, grad_context, query_features, key_features, lse, band):
    first = half * SIDE_PAIRS
    column = pl.BlockSpec((TOK, LANES), lambda p: (0, first + p))
    return pl.pallas_call(
        attend_back_kernel,
        grid=(SIDE_PAIRS,),
        in_specs=[
            *(
                pl.BlockSpec(
                    (TOK, LANES), lambda p, kind=kind: (0, (3 * half + kind) * SIDE_PAIRS + p)
                )
                for kind in range(3)
            ),
            column,
            whole((TOK, LANES)),
            column,
            pl.BlockSpec((2, 1, TOK), lambda p: (first + p, 0, 0)),
            pl.BlockSpec((2, 1, 4 * LANES), lambda p: (first + p, 0, 0)),
        ],
        out_specs=[
            whole((TOK, SPLIT)),
            pl.BlockSpec((2, TILES, LANES), lambda p: (p, 0, 0)),
            pl.BlockSpec((2, 1, 4 * LANES), lambda p: (p, 0, 0)),
        ],
        out_shape=[
            jax.ShapeDtypeStruct((TOK, SPLIT), BF),
            jax.ShapeDtypeStruct((HEADS // 2, TILES, LANES), F32),
            jax.ShapeDtypeStruct((HEADS // 2, 1, 4 * LANES), F32),
        ],
        scratch_shapes=[
            pltpu.VMEM((2, TOK, QBLK), F32),
            pltpu.VMEM((2, TOK, QBLK), F32),
            pltpu.VMEM((2, TOK, QBLK), BF),
            pltpu.VMEM((2, TOK, QBLK), BF),
            pltpu.VMEM((LANES, TOK), F32),
            pltpu.VMEM((2, TOK, LANES), F32),
            pltpu.VMEM((2, TOK, LANES), F32),
            pltpu.VMEM((2, 3 * TILE, 4 * LANES), F32),
        ],
        compiler_params=params(("arbitrary",)),
        cost_estimate=cost(5 * HEADS * TOK * TOK * 256, 8 * TOK * D, HEADS * TOK * TOK // 2, share=0.3),
        name="attend_back",
    )(qkv, qkv, qkv, grad_context, query_features, key_features, lse, band)


def table_gradient(tiles, diagonals):
    near = jnp.einsum(
        "hl,lb->bh", diagonals[:, 0, :], band_onehot(), precision=lax.Precision.HIGHEST
    )
    sums = jnp.concatenate(
        [tiles[h : h + 1, :, (HEAD_DIM if h % 2 == 0 else 0) + 4 :][:, :, :TILES] for h in range(HEADS)],
        axis=0,
    )
    apart = (
        jnp.arange(TILES, dtype=jnp.int32)[:, None] - jnp.arange(TILES, dtype=jnp.int32)[None, :]
    )[None]
    before = jnp.sum(jnp.where(apart <= -2, sums, 0.0), axis=(1, 2))
    after = jnp.sum(jnp.where(apart >= 2, sums, 0.0), axis=(1, 2))
    place = jnp.arange(BUCKETS, dtype=jnp.int32)[:, None]
    return (
        near
        + jnp.where(place == FAR_BEFORE, before[None, :], 0.0)
        + jnp.where(place == FAR_AFTER, after[None, :], 0.0)
    )


def middle_kernel(context, tokens, out_left, out_right, gain, router, route_col, slot_row, experts,
                  middle, sending_low, sending_high, gate, normed, w_out):
    w_out[:, :SIDE] = out_left[...]
    w_out[:, SIDE:] = out_right[...]
    for first in range(0, TOK, 256):
        at = slice(first, first + 256)
        mid = tokens[at, :].astype(F32) + dot(context[at, :], w_out[...])
        middle[at, :] = mid
        low = (mid * inverse_rms(mid) * gain[...]).astype(BF)
        normed[at, :] = low
        probs = router_softmax(low, router[...], experts)
        lane = lax.broadcasted_iota(jnp.int32, probs.shape, 1)
        gate[at, :] = jnp.sum(
            jnp.where(lane == route_col[at, :], probs, 0.0), axis=1, keepdims=True
        )
    dispatch(slot_row[...], normed[...], [sending_low, sending_high])


def router_softmax(rows, router, experts):
    logits = dot(rows, router)
    lane = lax.broadcasted_iota(jnp.int32, logits.shape, 1)
    logits = jnp.where(lane < experts, logits, UNPAIRED)
    raised = jnp.exp(logits - jnp.max(logits, axis=1, keepdims=True))
    return raised / jnp.sum(raised, axis=1, keepdims=True)


def make_middle(context, tokens, left, right, gain, router, routes, slot_row, experts, capacity):
    total = experts * capacity

    def kernel(*refs):
        middle_kernel(*refs[:8], experts, *refs[8:])

    out_half = pl.BlockSpec((D, SIDE), lambda r: (0, 3))
    return pl.pallas_call(
        kernel,
        grid=(1,),
        in_specs=[
            whole((TOK, D)),
            whole((TOK, D)),
            out_half,
            out_half,
            whole((1, D)),
            whole(router.shape),
            whole((TOK, 1)),
            whole((1, TOK)),
        ],
        out_specs=(
            whole((TOK, D)),
            whole((total // 2, D)),
            whole((total // 2, D)),
            whole((TOK, 1)),
        ),
        out_shape=(
            jax.ShapeDtypeStruct((TOK, D), F32),
            jax.ShapeDtypeStruct((total // 2, D), BF),
            jax.ShapeDtypeStruct((total // 2, D), BF),
            jax.ShapeDtypeStruct((TOK, 1), F32),
        ),
        scratch_shapes=[pltpu.VMEM((TOK, D), BF), pltpu.VMEM((D, D), BF)],
        compiler_params=params(),
        cost_estimate=cost(2 * total * TOK * D + 2 * TOK * D * D, 12 * TOK * D + 2 * total * D),
        name="middle",
    )(context, tokens, left, right, gain, router, routes, slot_row)


def gelu_parts(v):
    size = jnp.abs(v)
    t = 1.0 / (1.0 + (0.3275911 * 0.7071067811865476) * size)
    bell = jnp.exp(-0.5 * (v * v))
    series = t * (
        0.5 * 0.254829592
        + t * (0.5 * -0.284496736 + t * (0.5 * 1.421413741 + t * (0.5 * -1.453152027 + t * (0.5 * 1.061405429))))
    )
    tail = series * bell
    phi = jnp.where(v < 0, tail, 1.0 - tail)
    return v * phi, phi + v * (bell * 0.3989422804014327)


def expert_kernel(experts, x, c3, w_first, w_second, router, router_t, mine, *refs):
    act_ref, dh_ref, result, grad_x, gate_ref, grad_router, acc_r, acc_x = refs[-8:]
    step = pl.program_id(0)
    rows = x.shape[0]
    chunk = EXPERT_ROWS
    share = c3.shape[1]
    per = chunk // share

    @pl.when(step == 0)
    def _():
        acc_r[...] = jnp.zeros_like(acc_r)
        acc_x[...] = jnp.zeros_like(acc_x)

    for first in range(0, rows, chunk):
        at = slice(first, first + chunk)
        sources = slice(first // share, first // share + per)
        hidden = dot(x[at, :], w_first[...])
        grad_act = dot(c3[sources].reshape(chunk, D), w_second[...], 1, 1)
        act, slope = gelu_parts(hidden)
        act = act.astype(BF)
        grad_hidden = (grad_act * slope).astype(BF)
        act_ref[at, :] = act
        dh_ref[at, :] = grad_hidden
        acc_r[at, :] += dot(act, w_second[...])
        acc_x[at, :] += dot(grad_hidden, w_first[...], 1, 1)

    @pl.when(step == pl.num_programs(0) - 1)
    def _():
        total_router = jnp.zeros(grad_router.shape, F32)
        for first in range(0, rows, chunk):
            at = slice(first, first + chunk)
            sources = slice(first // share, first // share + per)
            rounded = acc_r[at, :].astype(BF)
            result[at, :] = rounded
            probs = router_softmax(x[at, :], router[...], experts)
            lane = lax.broadcasted_iota(jnp.int32, probs.shape, 1)
            here = lane == mine[0, 0]
            gate = jnp.sum(jnp.where(here, probs, 0.0), axis=1, keepdims=True)
            grad_gate = jnp.sum(
                c3[sources].reshape(chunk, D).astype(F32) * rounded.astype(F32), axis=1, keepdims=True
            )
            grad_logits = (
                probs * (jnp.where(here, grad_gate, 0.0) - gate * grad_gate)
            ).astype(BF)
            gate_ref[at, :] = gate
            grad_x[at, :] = (acc_x[at, :] * gate + dot(grad_logits, router_t[...])).astype(BF)
            total_router = total_router + dot(x[at, :], grad_logits, 0, 0)
        grad_router[...] = total_router


def run_expert(part, x, c, w_first, w_second, router, router_t, mine, experts):
    rows = x.shape[0]
    hidden_size = w_first.shape[1]
    lanes = router.shape[1]
    sources, capacity = c.shape[:2]
    half = pl.BlockSpec((sources, capacity // HALVES, D), lambda f: (0, part, 0))
    return pl.pallas_call(
        functools.partial(expert_kernel, experts),
        grid=(hidden_size // EXPERT_TILE,),
        in_specs=[
            whole((rows, D)),
            half,
            pl.BlockSpec((D, EXPERT_TILE), lambda f: (0, f)),
            pl.BlockSpec((EXPERT_TILE, D), lambda f: (f, 0)),
            whole((D, lanes)),
            whole((lanes, D)),
            pl.BlockSpec(memory_space=pltpu.SMEM),
        ],
        out_specs=[
            pl.BlockSpec((rows, EXPERT_TILE), lambda f: (0, f)),
            pl.BlockSpec((rows, EXPERT_TILE), lambda f: (0, f)),
            whole((rows, D)),
            whole((rows, D)),
            whole((rows, 1)),
            whole((D, lanes)),
        ],
        out_shape=[
            jax.ShapeDtypeStruct((rows, hidden_size), BF),
            jax.ShapeDtypeStruct((rows, hidden_size), BF),
            jax.ShapeDtypeStruct((rows, D), BF),
            jax.ShapeDtypeStruct((rows, D), BF),
            jax.ShapeDtypeStruct((rows, 1), F32),
            jax.ShapeDtypeStruct((D, lanes), F32),
        ],
        scratch_shapes=[pltpu.VMEM((rows, D), F32), pltpu.VMEM((rows, D), F32)],
        compiler_params=params(("arbitrary",)),
        cost_estimate=cost(
            8 * rows * D * hidden_size, 4 * rows * hidden_size + 4 * D * hidden_size
        ),
        name="expert",
    )(x, c, w_first, w_second, router, router_t, mine)


def expert_weights_kernel(parts, side, *refs):
    if side is not None:
        side, refs = refs[0], refs[1:]
    xs, gates = refs[:parts], refs[parts : 2 * parts]
    acts, dhs = refs[2 * parts : 3 * parts], refs[3 * parts : 4 * parts]
    cots = refs[4 * parts]
    if side is None:
        grad_first, grad_second, x_t, c_t = refs[4 * parts + 1 :]
    else:
        kept_first, sent_first, kept_second, sent_second, x_t, c_t, whole_first = refs[4 * parts + 1 :]
    rows = xs[0].shape[0]
    share = cots.shape[1] // parts
    chunk = 256
    per = chunk // share

    @pl.when(pl.program_id(0) == 0)
    def _():
        for part in range(parts):
            for first in range(0, rows, chunk):
                at = slice(first, first + chunk)
                to = slice(part * rows + first, part * rows + first + chunk)
                gate = gates[part][at, :]
                x_t[:, to] = (xs[part][at, :].astype(F32) * gate).T.astype(BF)
                cot = cots[
                    first // chunk * per : (first // chunk + 1) * per,
                    part * share : (part + 1) * share,
                ].reshape(chunk, D)
                c_t[:, to] = (cot.astype(F32) * gate).T.astype(BF)

    first_sum, second_sum = None, None
    for part in range(parts):
        at = slice(part * rows, (part + 1) * rows)
        one = dot(x_t[:, at], dhs[part][...])
        two = dot(c_t[:, at], acts[part][...])
        first_sum = one if first_sum is None else first_sum + one
        second_sum = two if second_sum is None else second_sum + two
    if side is None:
        grad_first[...] = first_sum.astype(BF)
        grad_second[...] = second_sum.T.astype(BF)
        return
    mine = side[0]
    half = D // 2
    whole_first[...] = first_sum.astype(BF)
    kept_first[...] = whole_first[pl.ds(pl.multiple_of(mine * half, half), half), :]
    sent_first[...] = whole_first[pl.ds(pl.multiple_of((1 - mine) * half, half), half), :]
    here = pl.program_id(0) // (pl.num_programs(0) // 2) == mine

    @pl.when(here)
    def _():
        kept_second[...] = second_sum.T.astype(BF)

    @pl.when(jnp.logical_not(here))
    def _():
        sent_second[...] = second_sum.T.astype(BF)


def expert_weights(xs, cots, gates, acts, dhs, side):
    parts = len(xs)
    rows = xs[0].shape[0]
    hidden_size = acts[0].shape[1]
    steps = hidden_size // FF_TILE
    in_specs = (
        [whole((rows, D))] * parts
        + [whole((rows, 1))] * parts
        + [pl.BlockSpec((rows, FF_TILE), lambda f, *_: (0, f))] * (2 * parts)
        + [whole(cots.shape)]
    )
    scratch = [pltpu.VMEM((D, parts * rows), BF), pltpu.VMEM((D, parts * rows), BF)]
    if side is None:
        out_specs = [
            pl.BlockSpec((D, FF_TILE), lambda f: (0, f)),
            pl.BlockSpec((FF_TILE, D), lambda f: (f, 0)),
        ]
        shapes = [(D, hidden_size), (hidden_size, D)]
    else:
        columns = pl.BlockSpec((D // 2, FF_TILE), lambda f, s: (0, f))

        def rows_of(place):
            def index(f, s):
                start = jnp.where(s[0] == 1, place, 1 - place) * (steps // 2)
                return (jnp.clip(f - start, 0, steps // 2 - 1), 0)

            return pl.BlockSpec((FF_TILE, D), index)

        out_specs = [columns, columns, rows_of(1), rows_of(0)]
        shapes = [(D // 2, hidden_size)] * 2 + [(hidden_size // 2, D)] * 2
        scratch = scratch + [pltpu.VMEM((D, FF_TILE), BF)]
    prefetched = () if side is None else (side,)
    return pl.pallas_call(
        functools.partial(expert_weights_kernel, parts, side is not None or None),
        grid_spec=pltpu.PrefetchScalarGridSpec(
            num_scalar_prefetch=len(prefetched),
            grid=(steps,),
            in_specs=in_specs,
            out_specs=out_specs,
            scratch_shapes=scratch,
        ),
        out_shape=[jax.ShapeDtypeStruct(shape, BF) for shape in shapes],
        compiler_params=params(("arbitrary",)),
        cost_estimate=cost(
            4 * parts * rows * D * hidden_size, 4 * (parts * rows + D) * hidden_size
        ),
        name="expert_weights",
    )(*prefetched, *xs, *gates, *acts, *dhs, cots)


def rms_back(values, factor, grad):
    inverse = inverse_rms(values)
    scaled = grad * factor
    mean = jnp.mean(scaled * values, axis=-1, keepdims=True)
    return (
        inverse * scaled - values * (inverse * inverse * inverse * mean),
        jnp.sum(grad * values * inverse, axis=0, keepdims=True),
    )


def undispatch(slot_col, parts):
    out = None
    offset = 0
    for part in parts:
        total = part.shape[0]
        place = lax.broadcasted_iota(jnp.int32, (slot_col.shape[0], total), 1) + offset
        found = dot((place == slot_col).astype(BF), part[...])
        out = found if out is None else out + found
        offset += total
    return out


def middle_back_kernel(parts, *refs):
    backs = refs[:parts]
    (
        slot_col, middle, cot, gain, out_left, out_right,
        grad_middle, grad_attn, grad_context, grad_gain, w_out,
    ) = refs[parts:]

    @pl.when(pl.program_id(0) == 0)
    def _():
        w_out[:, :SIDE] = out_left[...]
        w_out[:, SIDE:] = out_right[...]

    grad_normed = undispatch(slot_col[...], backs)
    part, gain_part = rms_back(middle[...], gain[...], grad_normed)
    grad = cot[...].astype(F32) + part
    grad_middle[...] = grad
    low = grad.astype(BF)
    grad_attn[...] = low
    grad_context[...] = dot(low, w_out[...], 1, 1).astype(BF)

    @pl.when(pl.program_id(0) == 0)
    def _():
        grad_gain[...] = gain_part

    @pl.when(pl.program_id(0) > 0)
    def _():
        grad_gain[...] += gain_part


def middle_back(backs, slot_col, middle, cot, gain, left, right):
    parts = len(backs)
    block = 256
    rows = pl.BlockSpec((block, D), lambda r: (r, 0))
    return pl.pallas_call(
        functools.partial(middle_back_kernel, parts),
        grid=(TOK // block,),
        in_specs=[whole(back.shape) for back in backs]
        + [
            pl.BlockSpec((block, 1), lambda r: (r, 0)),
            rows,
            rows,
            whole((1, D)),
            pl.BlockSpec((D, SIDE), lambda r: (0, 3)),
            pl.BlockSpec((D, SIDE), lambda r: (0, 3)),
        ],
        out_specs=[rows, rows, rows, whole((1, D))],
        scratch_shapes=[pltpu.VMEM((D, D), BF)],
        out_shape=[
            jax.ShapeDtypeStruct((TOK, D), F32),
            jax.ShapeDtypeStruct((TOK, D), BF),
            jax.ShapeDtypeStruct((TOK, D), BF),
            jax.ShapeDtypeStruct((1, D), F32),
        ],
        compiler_params=params(("arbitrary",)),
        cost_estimate=cost(2 * 2 * TOK * TOK * D + 2 * TOK * D * D, 16 * TOK * D),
        name="middle_back",
    )(*backs, slot_col, middle, cot, gain, left, right)


def mix_kernel(parts, *refs):
    backs = refs[:parts]
    slot_col, middle, gate, mixed = refs[parts:]
    mixed[...] = middle[...] + gate[...] * undispatch(slot_col[...], backs)


def mix(backs, slot_col, middle, gate):
    parts = len(backs)
    block = 256
    rows = pl.BlockSpec((block, D), lambda r: (r, 0))
    column = pl.BlockSpec((block, 1), lambda r: (r, 0))
    return pl.pallas_call(
        functools.partial(mix_kernel, parts),
        grid=(TOK // block,),
        in_specs=[whole(back.shape) for back in backs] + [column, rows, column],
        out_specs=rows,
        out_shape=jax.ShapeDtypeStruct((TOK, D), F32),
        compiler_params=params(("arbitrary",)),
        cost_estimate=cost(2 * 2 * TOK * TOK * D, 12 * TOK * D, share=1),
        name="mix",
    )(*backs, slot_col, middle, gate)


def tokens_back_kernel(g_left, g_right, left, right, tokens, gain, grad_middle, grad_tokens):
    grad_normed = dot(g_left[...], left[...], 1, 1) + dot(g_right[...], right[...], 1, 1)
    grad_tokens[...] = grad_middle[...] + rms_back(
        tokens[...].astype(F32), gain[...], grad_normed
    )[0]


def tokens_back(g_left, g_right, left, right, tokens, gain, grad_middle):
    block = 256
    rows = pl.BlockSpec((block, D), lambda r: (r, 0))
    return pl.pallas_call(
        tokens_back_kernel,
        grid=(TOK // block,),
        in_specs=[
            pl.BlockSpec((block, SPLIT), lambda r: (r, 0)),
            pl.BlockSpec((block, SPLIT), lambda r: (r, 0)),
            whole((D, SPLIT)),
            whole((D, SPLIT)),
            rows,
            whole((1, D)),
            rows,
        ],
        out_specs=rows,
        out_shape=jax.ShapeDtypeStruct((TOK, D), F32),
        compiler_params=params(("arbitrary",)),
        cost_estimate=cost(6 * TOK * D * D, 16 * TOK * D, share=1),
        name="tokens_back",
    )(g_left, g_right, left, right, tokens, gain, grad_middle)


def weights_back_kernel(turned, grads, context, grad_attn, out):
    last = pl.num_programs(0) - 1

    @pl.when(pl.program_id(0) < last)
    def _():
        out[...] = dot(turned[...], grads[...])

    @pl.when(pl.program_id(0) == last)
    def _():
        out[...] = dot(context[...], grad_attn[...], 0, 0)


def weights_back(half, turned, grads, context, grad_attn):
    steps = grads.shape[1] // SIDE
    columns = (steps + 1) * SIDE
    return pl.pallas_call(
        weights_back_kernel,
        grid=(steps + 1,),
        in_specs=[
            whole(turned.shape),
            pl.BlockSpec((TOK, SIDE), lambda c: (0, jnp.minimum(c, steps - 1))),
            whole((TOK, D)),
            pl.BlockSpec((TOK, SIDE), lambda c: (0, half)),
        ],
        out_specs=pl.BlockSpec((D, SIDE), lambda c: (0, c)),
        out_shape=jax.ShapeDtypeStruct((D, columns), F32),
        compiler_params=params(("arbitrary",)),
        cost_estimate=cost(2 * TOK * D * columns, 2 * TOK * (D + columns) + 4 * D * columns),
        name="weights_back",
    )(turned, grads, context, grad_attn)


def swap(block, axis, bit):
    size = lax.axis_size(axis)
    return lax.ppermute(block, axis, [(place, place ^ bit) for place in range(size)])


def on_upper(axis, bit):
    return (lax.axis_index(axis) // bit) % 2 == 1


def axis_bits(*axes):
    found = []
    for axis in axes:
        bit = lax.axis_size(axis) // 2
        while bit >= 1:
            found.append((axis, bit))
            bit //= 2
    return found


def orders():
    bits = axis_bits("dp", "expert")
    dp = [at for at, (axis, _) in enumerate(bits) if axis == "dp"]
    core = len(bits) - 1
    along = [at for at, (axis, bit) in enumerate(bits) if axis == "expert" and bit == 2]
    rest = [at for at in range(core) if at not in dp and at not in along]
    return (rest + along + dp + [core], rest + dp + along + [core])


def gather_start(shard):
    return shard.reshape((1,) * len(axis_bits("dp", "expert")) + shard.shape)


def gather_step(block, place):
    axis, bit = axis_bits("dp", "expert")[place]
    other = swap(block, axis, bit)
    upper = on_upper(axis, bit)
    return jnp.concatenate(
        [jnp.where(upper, other, block), jnp.where(upper, block, other)], axis=place
    )


def gather_end(block):
    return block.reshape((-1, block.shape[-1]))


def scatter_start(total):
    bits = axis_bits("dp", "expert")
    rows = total.shape[0] >> len(bits)
    return total.reshape((2,) * len(bits) + (rows,) + total.shape[1:])


def scatter_step(block, place, *others):
    axis, bit = axis_bits("dp", "expert")[place]
    lower = lax.slice_in_dim(block, 0, 1, axis=place)
    higher = lax.slice_in_dim(block, 1, 2, axis=place)
    upper = on_upper(axis, bit)
    sent = jnp.where(upper, lower, higher).astype(BF)
    kept = after(jnp.where(upper, higher, lower), *others)
    return kept + swap(sent, axis, bit).astype(F32)


def scatter_rest(block, order):
    for place in order:
        block = scatter_step(block, place)
    return block.reshape(block.shape[len(axis_bits("dp", "expert")) :])


def sum_all(total, beside):
    for number, (axis, bit) in enumerate(axis_bits("dp", "expert")):
        kept = after(total, beside[number]) if number < len(beside) else total
        total = kept + swap(total, axis, bit)
    return total


def gather_dp(block, axis, other=None):
    if lax.axis_size("dp") != 2:
        return lax.all_gather(block, "dp", axis=axis, tiled=True)
    if other is None:
        other = swap(block, "dp", 1)
    upper = on_upper("dp", 1)
    return jnp.concatenate(
        [jnp.where(upper, other, block), jnp.where(upper, block, other)], axis=axis
    )


def receive_dp(halves):
    if len(halves) == 1:
        return (lax.psum_scatter(halves[0], "dp", scatter_dimension=0, tiled=True),)
    kept, sent = halves
    return (kept, swap(sent, "dp", 1))


def add_dp(parts, *others):
    kept, *received = parts
    total = after(kept, *others).astype(F32)
    for part in received:
        total = total + part.astype(F32)
    return total[None]


def after(value, *others):
    return lax.optimization_barrier((value, *others))[0]


def body(
    tokens, seq_ids, routes, cotangent, w_query, w_key, w_value, w_out,
    rel_table, gain_attn, gain_ffn, router, expert_in, expert_out,
):
    experts = lax.axis_size("expert")
    capacity = 2 * TOK // experts
    shard = w_query.shape[0]
    lanes = -(-(experts + 2) // LANES) * LANES

    small = jnp.concatenate(
        [
            router,
            gain_attn[:, None],
            gain_ffn[:, None],
            jnp.zeros((shard, lanes - experts - 2), BF),
        ],
        axis=1,
    )
    first, second = orders()
    kinds = (w_query, w_key, w_value, w_out)
    paired = lax.axis_size("dp") == 2
    own_first, own_second = expert_in[0], expert_out[0]
    second_cut = own_second.shape[0] // 2
    early = [swap(own_second[:second_cut], "dp", 1)] if paired else []
    ahead = [own_second[:second_cut]] if paired else []
    left = gather_start(
        jnp.concatenate([after(w_query[:, :SIDE], *ahead)] + [w[:, :SIDE] for w in kinds[1:]], axis=1)
    )
    right = gather_start(
        jnp.concatenate(
            [after(w_query[:, SIDE:], *ahead)] + [w[:, SIDE:] for w in kinds[1:]] + [small], axis=1
        )
    )
    table = gather_dp(rel_table, 0)
    dp_bits = len(axis_bits("dp"))
    rest = len(first) - dp_bits - 2
    for at in range(rest):
        left, right = gather_step(left, first[at]), gather_step(right, second[at])
    left, right = lax.optimization_barrier((left, right, *early))[:2]
    slot_col, slot_row, sending_cot = make_slots(
        after(routes, left), cotangent, experts, capacity
    )
    left = gather_step(left, first[rest])
    for place in second[rest : rest + dp_bits]:
        right = gather_step(right, place)
    wide_table = after(table, right).astype(F32)
    query_features, key_features = lane_features(
        after(seq_ids, right).reshape(TOK, 1), wide_table
    )
    band = jnp.sum(band_onehot()[None, :, :] * wide_table.T[:, None, :], axis=2)[:, None, :]
    for place in first[rest + 1 : -1]:
        left = gather_step(left, place)
    for place in second[rest + dp_bits : -1]:
        right = gather_step(right, place)
    left = after(left, sending_cot)
    right = after(right, query_features, key_features, band)
    left = gather_end(gather_step(left, first[-1]))
    right = gather_end(gather_step(right, second[-1]))

    def exchange(rows):
        return lax.all_to_all(
            rows.reshape(experts, -1, D), "expert", split_axis=0, concat_axis=0, tiled=True
        )

    cots = exchange(after(sending_cot, left, right))
    if paired:
        other_first = swap(after(own_first, left, right), "dp", 1)
        late = swap(after(own_second[second_cut:], other_first), "dp", 1)
        other_second = jnp.concatenate([*early, late], axis=0)
        early.append(other_first)
    else:
        other_first = other_second = None
    w_first = gather_dp(own_first, 0, other_first)
    w_second = gather_dp(own_second, 0, other_second)

    extra = right[:, SPLIT + SIDE :]
    full_router = jnp.where(jnp.arange(lanes)[None, :] < experts, extra, jnp.zeros((), BF))
    router_t = full_router.T
    attn_gain = extra[:, experts].astype(F32).reshape(1, D)
    ffn_gain = extra[:, experts + 1].astype(F32).reshape(1, D)

    turned, qkv = project(tokens, attn_gain, left, right)
    context, lse = attend(qkv, query_features, key_features, band)

    middle, *sending, gate = make_middle(
        context, tokens, left, right, ffn_gain, full_router, routes, slot_row, experts, capacity
    )
    sending[0] = after(sending[0], cots, *early)
    sending[1] = after(sending[1], w_first, w_second)
    rows_in = [exchange(part).reshape(-1, D) for part in sending]
    mine = lax.axis_index("expert").astype(jnp.int32).reshape(1, 1)
    acts, dhs, results, grads, gates, router_parts = zip(
        *(
            run_expert(
                part, rows, cots, w_first, w_second, full_router, router_t, mine, experts
            )
            for part, rows in enumerate(rows_in)
        )
    )
    grads_home = [exchange(part).reshape(-1, D) for part in grads]
    weight_parts = expert_weights(
        rows_in,
        cots,
        (after(gates[0], grads_home[0]), *gates[1:]),
        acts,
        dhs,
        lax.axis_index("dp").astype(jnp.int32).reshape(1) if paired else None,
    )
    half = len(weight_parts) // 2
    grad_first, grad_second = weight_parts[:half], weight_parts[half:]
    results_home = []
    for part in results:
        part = after(part, *grads_home, *weight_parts, *results_home)
        results_home.append(exchange(part).reshape(-1, D))
    grads_home[0] = after(grads_home[0], *weight_parts)
    grad_middle, grad_attn, grad_context, grad_gain_f = middle_back(
        grads_home, slot_col, middle, cotangent, ffn_gain, left, right
    )
    down, down_other = second[::-1], first[::-1]

    def back(half, *others):
        return attend_back(
            half, qkv, after(grad_context, *others), query_features, key_features, lse, band
        )

    g_left, tiles_left, diagonals_left = back(0)
    left_block = scatter_start(weights_back(0, turned, g_left, context, grad_attn))
    g_right, tiles_right, diagonals_right = back(1, left_block, results_home[0])
    left_block = after(left_block, results_home[0])
    first_halves, second_halves = receive_dp(grad_first), receive_dp(grad_second)
    grad_right = weights_back(
        1, turned, after(g_right, results_home[1]), context, grad_attn
    )
    left_block = scatter_step(left_block, down[0], grad_right)
    right_block = scatter_step(scatter_start(grad_right), down_other[0], second_halves[-1])
    beside = [left_block]
    left_block = scatter_step(left_block, down[1])
    grad_tokens = tokens_back(
        g_left, after(g_right, right_block, left_block), left, right, tokens, attn_gain, grad_middle
    )
    right_block = scatter_step(right_block, down_other[1], grad_tokens)
    beside.append(right_block)
    near = 2 + len(axis_bits("dp"))
    for place in down[2:near]:
        left_block = scatter_step(left_block, place, right_block, first_halves[-1])
    beside.append(left_block)
    for place in down_other[2:near]:
        right_block = scatter_step(right_block, place)
    joined = jnp.concatenate([left_block, right_block], axis=-1)
    grad_expert_in = add_dp(first_halves, joined)
    grad_expert_out = add_dp(second_halves, joined)
    mixed = mix(results_home, slot_col, middle, after(gate, joined))
    joined = scatter_step(joined, down[near])
    beside.append(joined)
    dense = scatter_rest(joined, down[near + 1 :])
    grad_left, grad_right = dense[:, : SPLIT + SIDE], dense[:, SPLIT + SIDE :]
    tiles = jnp.concatenate([tiles_left, tiles_right], axis=0)
    diagonals = jnp.concatenate([diagonals_left, diagonals_right], axis=0)
    grad_router = sum(router_parts)[:, :experts]
    grad_table = table_gradient(tiles, diagonals)

    grad_weights = [
        jnp.concatenate(
            [side[:, kind * SIDE : (kind + 1) * SIDE] for side in (grad_left, grad_right)], axis=1
        )
        for kind in range(4)
    ]
    products = sum(w.astype(F32) * grad for w, grad in zip(kinds[:3], grad_weights[:3]))
    grad_gain_a = jnp.sum(products, axis=1) / gain_attn.astype(F32)

    sizes = (D * experts, D, BUCKETS * HEADS)
    sums = sum_all(
        jnp.concatenate(
            [part.reshape(-1, LANES) for part in (grad_router, grad_gain_f, grad_table)], axis=0
        ),
        beside,
    ).reshape(-1)
    ends = [sum(sizes[: at + 1]) for at in range(len(sizes))]
    grad_router, grad_gain_f, grad_table = (
        sums[end - size : end] for end, size in zip(ends, sizes)
    )
    number = lax.axis_index("dp") * experts + lax.axis_index("expert")
    table_height = BUCKETS // lax.axis_size("dp")

    def own(rows, height, place):
        return lax.dynamic_slice_in_dim(rows, place * height, height, 0)

    return (
        mixed,
        grad_tokens,
        *grad_weights,
        own(grad_table.reshape(BUCKETS, HEADS), table_height, lax.axis_index("dp")),
        grad_gain_a,
        own(grad_gain_f, shard, number),
        own(grad_router.reshape(D, experts), shard, number),
        grad_expert_in,
        grad_expert_out,
    )


def solution(mesh):
    rows = P(("dp", "expert"), None)
    flat = P(("dp", "expert"))
    expert = P("expert", "dp", None)
    return jax.shard_map(
        body,
        mesh=mesh,
        in_specs=(
            rows, flat, rows, rows, rows, rows, rows, rows,
            P("dp", None), flat, flat, rows, expert, expert,
        ),
        out_specs=(
            rows, rows, rows, rows, rows, rows,
            P("dp", None), flat, flat, rows, expert, expert,
        ),
        check_vma=False,
    )
```

```python
import functools

import jax
import jax.numpy as jnp
from jax import lax
from jax.experimental import pallas as pl
from jax.experimental.pallas import tpu as pltpu
from jax.sharding import PartitionSpec as P

D = 768
HEADS = 12
HEAD_DIM = 64
BUCKETS = 32
TOK = 1024
TILE = 128
TILES = TOK // TILE
QBLK = 256
FF_TILE = 512
EXPERT_TILE = 512
EXPERT_ROWS = 1024
HALVES = 2
SIDE = D // 2
SPLIT = 3 * SIDE
PAIRS = HEADS // 2
SIDE_PAIRS = PAIRS // 2
COST_SHARE = 0.05
LANES = 128

EPSILON = 1e-06
DISTANCE_EDGES = (12, 16, 23, 32, 46, 64, 91)
FAR_BEFORE = 15
FAR_AFTER = 31
UNPAIRED = -1e30
BF = jnp.bfloat16
F32 = jnp.float32
VMEM_LIMIT = 56 * 1024 * 1024


def dot(left, right, left_dim=1, right_dim=0):
    return lax.dot_general(
        left, right, (((left_dim,), (right_dim,)), ((), ())), preferred_element_type=F32
    )


def params(semantics=None):
    return pltpu.CompilerParams(vmem_limit_bytes=VMEM_LIMIT, dimension_semantics=semantics)


def cost(flops, bytes_accessed, transcendentals=0, share=COST_SHARE):
    return pl.CostEstimate(
        flops=int(flops * share),
        bytes_accessed=int(bytes_accessed * share),
        transcendentals=int(transcendentals * share),
    )


def whole(shape):
    return pl.BlockSpec(shape, lambda *_: (0,) * len(shape))


def inverse_rms(values):
    return lax.rsqrt(jnp.mean(values * values, axis=-1, keepdims=True) + EPSILON)


def bucket_of(offset):
    distance = jnp.abs(offset)
    distant = 8 + sum(((distance >= boundary).astype(jnp.int32) for boundary in DISTANCE_EDGES))
    return jnp.where(distance < 8, distance, distant) + jnp.where(offset > 0, 16, 0)


def place_in_buffers(route, rank, experts, capacity):
    share = capacity // HALVES
    part = (rank >= share).astype(jnp.int32)
    return part * (experts * share) + route * share + (rank - part * share)


def slots_kernel(experts, capacity, route_col, route_row, cot, slot_col, slot_row, sending):
    padded = -(-experts // LANES) * LANES
    picked = (
        lax.broadcasted_iota(jnp.int32, (TOK, padded), 1) == route_col[...]
    ).astype(BF)
    picked_t = (
        lax.broadcasted_iota(jnp.int32, (padded, TOK), 0) == route_row[...]
    ).astype(BF)
    upto = (
        lax.broadcasted_iota(jnp.int32, (TOK, TOK), 0)
        <= lax.broadcasted_iota(jnp.int32, (TOK, TOK), 1)
    ).astype(BF)
    from_t = (
        lax.broadcasted_iota(jnp.int32, (TOK, TOK), 0)
        >= lax.broadcasted_iota(jnp.int32, (TOK, TOK), 1)
    ).astype(BF)
    counts = dot(from_t, picked) * picked.astype(F32)
    rank = jnp.sum(counts, axis=1, keepdims=True).astype(jnp.int32) - 1
    slot_col[...] = place_in_buffers(route_col[...], rank, experts, capacity)
    counts_t = dot(picked_t, upto) * picked_t.astype(F32)
    rank_row = jnp.sum(counts_t, axis=0, keepdims=True).astype(jnp.int32) - 1
    slot_row[...] = place_in_buffers(route_row[...], rank_row, experts, capacity)
    dispatch(route_row[...] * capacity + rank_row, cot[...], [sending])


def dispatch(row, rows, parts):
    step = 512
    offset = 0
    for sending in parts:
        for first in range(0, sending.shape[0], step):
            chosen = (
                lax.broadcasted_iota(jnp.int32, (step, TOK), 0) + (first + offset) == row
            ).astype(BF)
            sending[first : first + step, :] = dot(chosen, rows).astype(BF)
        offset += sending.shape[0]


def make_slots(routes, cotangent, experts, capacity):
    total = experts * capacity
    return pl.pallas_call(
        functools.partial(slots_kernel, experts, capacity),
        out_shape=(
            jax.ShapeDtypeStruct((TOK, 1), jnp.int32),
            jax.ShapeDtypeStruct((1, TOK), jnp.int32),
            jax.ShapeDtypeStruct((total, D), BF),
        ),
        compiler_params=params(),
        cost_estimate=cost(2 * total * TOK * D, 6 * total * D),
        name="slots",
    )(routes, routes.reshape(1, TOK), cotangent)


def project_kernel(tokens, gain, left, right, turned, qkv):
    x = tokens[...].astype(F32)
    wide = x * inverse_rms(x) * gain[...]
    low = wide.astype(BF)
    turned[...] = wide.T.astype(BF)
    qkv[:, :SPLIT] = dot(low, left[...]).astype(BF)
    qkv[:, SPLIT:] = dot(low, right[...]).astype(BF)


def project(tokens, gain, left, right):
    block = 256
    rows = pl.BlockSpec((block, D), lambda r: (r, 0))
    return pl.pallas_call(
        project_kernel,
        grid=(TOK // block,),
        in_specs=[rows, whole((1, D)), whole((D, SPLIT)), whole((D, SPLIT))],
        out_specs=[
            pl.BlockSpec((D, block), lambda r: (0, r)),
            pl.BlockSpec((block, 3 * D), lambda r: (r, 0)),
        ],
        out_shape=[
            jax.ShapeDtypeStruct((D, TOK), BF),
            jax.ShapeDtypeStruct((TOK, 3 * D), BF),
        ],
        compiler_params=params(("arbitrary",)),
        cost_estimate=cost(6 * TOK * D * D, 12 * TOK * D),
        name="project",
    )(tokens, gain, left, right)


def lane_features(seq_col, rel_table):
    lane = jnp.arange(LANES, dtype=jnp.int32)[None, :]
    feature = lane % HEAD_DIM
    tile = jnp.arange(TOK, dtype=jnp.int32)[:, None] // TILE
    on_tile = feature - 4
    query_features = jnp.where(
        feature < 4,
        jnp.where(feature == seq_col, 0.0, UNPAIRED),
        jnp.where(on_tile == tile, 1.0, 0.0),
    ).astype(BF)
    wide = jnp.arange(D, dtype=jnp.int32)[None, :]
    feature = wide % HEAD_DIM
    on_tile = feature - 4
    swapped = jnp.arange(HEADS, dtype=jnp.int32) ^ 1
    before = jnp.repeat(rel_table[FAR_BEFORE][swapped], HEAD_DIM)[None, :]
    after = jnp.repeat(rel_table[FAR_AFTER][swapped], HEAD_DIM)[None, :]
    apart = tile - on_tile
    far = jnp.where(apart >= 2, after, jnp.where(apart <= -2, before, 0.0))
    key_features = jnp.where(
        feature < 4,
        jnp.where(feature == seq_col, 1.0, 0.0),
        jnp.where(on_tile < TILES, far, 0.0),
    ).astype(BF)
    return query_features, key_features


def band_offsets():
    place = jnp.arange(4 * LANES, dtype=jnp.int32)
    return 255 - (place + 383) % 512


def band_onehot():
    return (
        bucket_of(band_offsets())[:, None] == jnp.arange(BUCKETS, dtype=jnp.int32)[None, :]
    ).astype(F32)


def near_rows(tile):
    first = max(tile - 1, 0)
    last = min(tile + 2, TILES)
    return first, last


def spread_band(values):
    wide = jnp.broadcast_to(values, (3 * TILE, 4 * LANES))
    return pltpu.roll(wide, 0, 1, stride=1, stride_axis=0)[:, :TILE]


def add_band(st, slot, block, band):
    for part in range(QBLK // TILE):
        tile = block * (QBLK // TILE) + part
        first, last = near_rows(tile)
        at = (slot, slice(first * TILE, last * TILE), slice(part * TILE, (part + 1) * TILE))
        st[at] += band[(first - tile + 1) * TILE : (last - tile + 1) * TILE]


def attend_kernel(q_ref, k_ref, v_ref, qx_ref, kx_ref, band_ref, out_ref, lse_ref, st, pb, ot):
    low = lax.broadcasted_iota(jnp.int32, (TOK, LANES), 1) < HEAD_DIM
    v_t = v_ref[...].astype(F32).T.astype(BF)
    sides = []
    for side in range(2):
        own = low if side == 0 else ~low
        sides.append(
            (
                jnp.where(own, q_ref[...], qx_ref[...]),
                jnp.where(own, k_ref[...], kx_ref[...]),
                spread_band(band_ref[side]),
            )
        )
    work = [(side, block) for side in range(2) for block in range(TOK // QBLK)]

    def score(number):
        side, block = work[number]
        queries, keys, band = sides[side]
        st[number % 2] = dot(keys, queries[block * QBLK : (block + 1) * QBLK], 1, 1)

    def finish(number):
        side, block = work[number]
        slot = number % 2
        rows = slice(block * QBLK, (block + 1) * QBLK)
        add_band(st, slot, block, sides[side][2])
        top = jnp.max(st[slot, 0:TILE], axis=0, keepdims=True)
        for chunk in range(1, TILES):
            top = jnp.maximum(
                top,
                jnp.max(st[slot, chunk * TILE : (chunk + 1) * TILE], axis=0, keepdims=True),
            )
        total = jnp.zeros((1, QBLK), F32)
        for chunk in range(TILES):
            at = slice(chunk * TILE, (chunk + 1) * TILE)
            raised = jnp.exp(st[slot, at] - top)
            total = total + jnp.sum(raised, axis=0, keepdims=True)
            pb[slot, at] = raised.astype(BF)
        lse_ref[side, :, rows] = top + jnp.log(total)
        return total

    def mix_values(number, total):
        side, block = work[number]
        half = slice(side * HEAD_DIM, (side + 1) * HEAD_DIM)
        rows = slice(block * QBLK, (block + 1) * QBLK)
        ot[half, rows] = dot(v_t[half], pb[number % 2]) * (1.0 / total)

    score(0)
    waiting = None
    for number in range(len(work)):
        if number + 1 < len(work):
            score(number + 1)
        if waiting is not None:
            mix_values(number - 1, waiting)
        waiting = finish(number)
    mix_values(len(work) - 1, waiting)
    out_ref[...] = ot[...].T.astype(BF)


def attend(qkv, query_features, key_features, band):
    return pl.pallas_call(
        attend_kernel,
        grid=(PAIRS,),
        in_specs=[
            *(
                pl.BlockSpec(
                    (TOK, LANES),
                    lambda p, kind=kind: (
                        0,
                        p // SIDE_PAIRS * (3 * SIDE_PAIRS) + kind * SIDE_PAIRS + p % SIDE_PAIRS,
                    ),
                )
                for kind in range(3)
            ),
            whole((TOK, LANES)),
            pl.BlockSpec((TOK, LANES), lambda p: (0, p)),
            pl.BlockSpec((2, 1, 4 * LANES), lambda p: (p, 0, 0)),
        ],
        out_specs=[
            pl.BlockSpec((TOK, LANES), lambda p: (0, p)),
            pl.BlockSpec((2, 1, TOK), lambda p: (p, 0, 0)),
        ],
        out_shape=[
            jax.ShapeDtypeStruct((TOK, D), BF),
            jax.ShapeDtypeStruct((HEADS, 1, TOK), F32),
        ],
        scratch_shapes=[
            pltpu.VMEM((2, TOK, QBLK), F32),
            pltpu.VMEM((2, TOK, QBLK), BF),
            pltpu.VMEM((LANES, TOK), F32),
        ],
        compiler_params=params(("arbitrary",)),
        cost_estimate=cost(2 * 3 * HEADS * TOK * TOK * 256, 10 * TOK * D, HEADS * TOK * TOK),
        name="attend",
    )(qkv, qkv, qkv, query_features, key_features, band)


def attend_back_kernel(
    q_ref, k_ref, v_ref, do_ref, qx_ref, kx_ref, lse_ref, band_ref,
    grad_ref, tiles_ref, diag_ref,
    st, dp, pb, sb, dqt, dkt, dvt, near,
):
    low = lax.broadcasted_iota(jnp.int32, (TOK, LANES), 1) < HEAD_DIM
    k_t = k_ref[...].astype(F32).T.astype(BF)
    sides = []
    for side in range(2):
        own = low if side == 0 else ~low
        sides.append(
            (
                jnp.where(own, q_ref[...], qx_ref[...]),
                jnp.where(own, k_ref[...], kx_ref[...]),
                jnp.where(own, v_ref[...], jnp.zeros((), BF)),
                spread_band(band_ref[side]),
            )
        )
    near[...] = jnp.zeros_like(near)
    work = [(side, block) for side in range(2) for block in range(TOK // QBLK)]

    def rows_of(block):
        return slice(block * QBLK, (block + 1) * QBLK)

    def score(number):
        side, block = work[number]
        queries, keys, values, _ = sides[side]
        st[number % 2] = dot(keys, queries[rows_of(block)], 1, 1)
        dp[number % 2] = dot(values, do_ref[rows_of(block), :], 1, 1)

    def finish(number):
        side, block = work[number]
        slot = number % 2
        add_band(st, slot, block, sides[side][3])
        lse = lse_ref[side, :, rows_of(block)]
        spread = jnp.zeros((1, QBLK), F32)
        for chunk in range(TILES):
            at = slice(chunk * TILE, (chunk + 1) * TILE)
            weights = jnp.exp(st[slot, at] - lse)
            st[slot, at] = weights
            pb[slot, at] = weights.astype(BF)
            spread = spread + jnp.sum(weights * dp[slot, at], axis=0, keepdims=True)
        for chunk in range(TILES):
            at = slice(chunk * TILE, (chunk + 1) * TILE)
            sb[slot, at] = (st[slot, at] * (dp[slot, at] - spread)).astype(BF)
        for part in range(QBLK // TILE):
            tile = block * (QBLK // TILE) + part
            first, last = near_rows(tile)
            at = (slot, slice(first * TILE, last * TILE), slice(part * TILE, (part + 1) * TILE))
            near[side, (first - tile + 1) * TILE : (last - tile + 1) * TILE, :TILE] += sb[
                at
            ].astype(F32)

    def multiply(number):
        side, block = work[number]
        slot = number % 2
        rows = rows_of(block)
        half = slice(side * HEAD_DIM, (side + 1) * HEAD_DIM)
        dv = dot(pb[slot], do_ref[rows, :])
        dk = dot(sb[slot], sides[side][0][rows])
        if block == 0:
            dvt[side] = dv
            dkt[side] = dk
        else:
            dvt[side] += dv
            dkt[side] += dk
        dqt[half, rows] = dot(k_t[half], sb[slot])

    score(0)
    for number in range(len(work)):
        if number + 1 < len(work):
            score(number + 1)
        if number > 0:
            multiply(number - 1)
        finish(number)
    multiply(len(work) - 1)
    for side in range(2):
        for tile in range(TILES):
            tiles_ref[side, tile : tile + 1, :] = jnp.sum(
                dkt[side, tile * TILE : (tile + 1) * TILE], axis=0, keepdims=True
            )
        folded = near[side, 0:8, :]
        for first in range(8, 3 * TILE, 8):
            folded = folded + pltpu.roll(near[side, first : first + 8, :], 4 * LANES - first, 1)
        diagonal = folded[0:1]
        for row in range(1, 8):
            diagonal = diagonal + pltpu.roll(folded[row : row + 1], 4 * LANES - row, 1)
        diag_ref[side] = diagonal
    found = (
        dqt[...].T.astype(BF),
        jnp.where(low, dkt[0], dkt[1]).astype(BF),
        jnp.where(low, dvt[0], dvt[1]).astype(BF),
    )
    for pair in range(SIDE_PAIRS):

        @pl.when(pl.program_id(0) == pair)
        def _():
            for kind in range(3):
                first = kind * SIDE + pair * LANES
                grad_ref[:, first : first + LANES] = found[kind]


def attend_back(half, qkv, grad_context, query_features, key_features, lse, band):
    first = half * SIDE_PAIRS
    column = pl.BlockSpec((TOK, LANES), lambda p: (0, first + p))
    return pl.pallas_call(
        attend_back_kernel,
        grid=(SIDE_PAIRS,),
        in_specs=[
            *(
                pl.BlockSpec(
                    (TOK, LANES), lambda p, kind=kind: (0, (3 * half + kind) * SIDE_PAIRS + p)
                )
                for kind in range(3)
            ),
            column,
            whole((TOK, LANES)),
            column,
            pl.BlockSpec((2, 1, TOK), lambda p: (first + p, 0, 0)),
            pl.BlockSpec((2, 1, 4 * LANES), lambda p: (first + p, 0, 0)),
        ],
        out_specs=[
            whole((TOK, SPLIT)),
            pl.BlockSpec((2, TILES, LANES), lambda p: (p, 0, 0)),
            pl.BlockSpec((2, 1, 4 * LANES), lambda p: (p, 0, 0)),
        ],
        out_shape=[
            jax.ShapeDtypeStruct((TOK, SPLIT), BF),
            jax.ShapeDtypeStruct((HEADS // 2, TILES, LANES), F32),
            jax.ShapeDtypeStruct((HEADS // 2, 1, 4 * LANES), F32),
        ],
        scratch_shapes=[
            pltpu.VMEM((2, TOK, QBLK), F32),
            pltpu.VMEM((2, TOK, QBLK), F32),
            pltpu.VMEM((2, TOK, QBLK), BF),
            pltpu.VMEM((2, TOK, QBLK), BF),
            pltpu.VMEM((LANES, TOK), F32),
            pltpu.VMEM((2, TOK, LANES), F32),
            pltpu.VMEM((2, TOK, LANES), F32),
            pltpu.VMEM((2, 3 * TILE, 4 * LANES), F32),
        ],
        compiler_params=params(("arbitrary",)),
        cost_estimate=cost(5 * HEADS * TOK * TOK * 256, 8 * TOK * D, HEADS * TOK * TOK // 2, share=0.3),
        name="attend_back",
    )(qkv, qkv, qkv, grad_context, query_features, key_features, lse, band)


def table_gradient(tiles, diagonals):
    near = jnp.einsum(
        "hl,lb->bh", diagonals[:, 0, :], band_onehot(), precision=lax.Precision.HIGHEST
    )
    sums = jnp.concatenate(
        [tiles[h : h + 1, :, (HEAD_DIM if h % 2 == 0 else 0) + 4 :][:, :, :TILES] for h in range(HEADS)],
        axis=0,
    )
    apart = (
        jnp.arange(TILES, dtype=jnp.int32)[:, None] - jnp.arange(TILES, dtype=jnp.int32)[None, :]
    )[None]
    before = jnp.sum(jnp.where(apart <= -2, sums, 0.0), axis=(1, 2))
    after = jnp.sum(jnp.where(apart >= 2, sums, 0.0), axis=(1, 2))
    place = jnp.arange(BUCKETS, dtype=jnp.int32)[:, None]
    return (
        near
        + jnp.where(place == FAR_BEFORE, before[None, :], 0.0)
        + jnp.where(place == FAR_AFTER, after[None, :], 0.0)
    )


def middle_kernel(context, tokens, out_left, out_right, gain, router, route_col, slot_row, experts,
                  middle, sending_low, sending_high, gate, normed, w_out):
    w_out[:, :SIDE] = out_left[...]
    w_out[:, SIDE:] = out_right[...]
    for first in range(0, TOK, 256):
        at = slice(first, first + 256)
        mid = tokens[at, :].astype(F32) + dot(context[at, :], w_out[...])
        middle[at, :] = mid
        low = (mid * inverse_rms(mid) * gain[...]).astype(BF)
        normed[at, :] = low
        probs = router_softmax(low, router[...], experts)
        lane = lax.broadcasted_iota(jnp.int32, probs.shape, 1)
        gate[at, :] = jnp.sum(
            jnp.where(lane == route_col[at, :], probs, 0.0), axis=1, keepdims=True
        )
    dispatch(slot_row[...], normed[...], [sending_low, sending_high])


def router_softmax(rows, router, experts):
    logits = dot(rows, router)
    lane = lax.broadcasted_iota(jnp.int32, logits.shape, 1)
    logits = jnp.where(lane < experts, logits, UNPAIRED)
    raised = jnp.exp(logits - jnp.max(logits, axis=1, keepdims=True))
    return raised / jnp.sum(raised, axis=1, keepdims=True)


def make_middle(context, tokens, left, right, gain, router, routes, slot_row, experts, capacity):
    total = experts * capacity

    def kernel(*refs):
        middle_kernel(*refs[:8], experts, *refs[8:])

    out_half = pl.BlockSpec((D, SIDE), lambda r: (0, 3))
    return pl.pallas_call(
        kernel,
        grid=(1,),
        in_specs=[
            whole((TOK, D)),
            whole((TOK, D)),
            out_half,
            out_half,
            whole((1, D)),
            whole(router.shape),
            whole((TOK, 1)),
            whole((1, TOK)),
        ],
        out_specs=(
            whole((TOK, D)),
            whole((total // 2, D)),
            whole((total // 2, D)),
            whole((TOK, 1)),
        ),
        out_shape=(
            jax.ShapeDtypeStruct((TOK, D), F32),
            jax.ShapeDtypeStruct((total // 2, D), BF),
            jax.ShapeDtypeStruct((total // 2, D), BF),
            jax.ShapeDtypeStruct((TOK, 1), F32),
        ),
        scratch_shapes=[pltpu.VMEM((TOK, D), BF), pltpu.VMEM((D, D), BF)],
        compiler_params=params(),
        cost_estimate=cost(2 * total * TOK * D + 2 * TOK * D * D, 12 * TOK * D + 2 * total * D),
        name="middle",
    )(context, tokens, left, right, gain, router, routes, slot_row)


def gelu_parts(v):
    size = jnp.abs(v)
    t = 1.0 / (1.0 + (0.3275911 * 0.7071067811865476) * size)
    bell = jnp.exp(-0.5 * (v * v))
    series = t * (
        0.5 * 0.254829592
        + t * (0.5 * -0.284496736 + t * (0.5 * 1.421413741 + t * (0.5 * -1.453152027 + t * (0.5 * 1.061405429))))
    )
    tail = series * bell
    phi = jnp.where(v < 0, tail, 1.0 - tail)
    return v * phi, phi + v * (bell * 0.3989422804014327)


def expert_kernel(experts, x, c3, w_first, w_second, router, router_t, mine, *refs):
    act_ref, dh_ref, result, grad_x, gate_ref, grad_router, acc_r, acc_x = refs[-8:]
    step = pl.program_id(0)
    rows = x.shape[0]
    chunk = EXPERT_ROWS
    share = c3.shape[1]
    per = chunk // share

    @pl.when(step == 0)
    def _():
        acc_r[...] = jnp.zeros_like(acc_r)
        acc_x[...] = jnp.zeros_like(acc_x)

    for first in range(0, rows, chunk):
        at = slice(first, first + chunk)
        sources = slice(first // share, first // share + per)
        hidden = dot(x[at, :], w_first[...])
        grad_act = dot(c3[sources].reshape(chunk, D), w_second[...], 1, 1)
        act, slope = gelu_parts(hidden)
        act = act.astype(BF)
        grad_hidden = (grad_act * slope).astype(BF)
        act_ref[at, :] = act
        dh_ref[at, :] = grad_hidden
        acc_r[at, :] += dot(act, w_second[...])
        acc_x[at, :] += dot(grad_hidden, w_first[...], 1, 1)

    @pl.when(step == pl.num_programs(0) - 1)
    def _():
        total_router = jnp.zeros(grad_router.shape, F32)
        for first in range(0, rows, chunk):
            at = slice(first, first + chunk)
            sources = slice(first // share, first // share + per)
            rounded = acc_r[at, :].astype(BF)
            result[at, :] = rounded
            probs = router_softmax(x[at, :], router[...], experts)
            lane = lax.broadcasted_iota(jnp.int32, probs.shape, 1)
            here = lane == mine[0, 0]
            gate = jnp.sum(jnp.where(here, probs, 0.0), axis=1, keepdims=True)
            grad_gate = jnp.sum(
                c3[sources].reshape(chunk, D).astype(F32) * rounded.astype(F32), axis=1, keepdims=True
            )
            grad_logits = (
                probs * (jnp.where(here, grad_gate, 0.0) - gate * grad_gate)
            ).astype(BF)
            gate_ref[at, :] = gate
            grad_x[at, :] = (acc_x[at, :] * gate + dot(grad_logits, router_t[...])).astype(BF)
            total_router = total_router + dot(x[at, :], grad_logits, 0, 0)
        grad_router[...] = total_router


def run_expert(part, x, c, w_first, w_second, router, router_t, mine, experts):
    rows = x.shape[0]
    hidden_size = w_first.shape[1]
    lanes = router.shape[1]
    sources, capacity = c.shape[:2]
    half = pl.BlockSpec((sources, capacity // HALVES, D), lambda f: (0, part, 0))
    return pl.pallas_call(
        functools.partial(expert_kernel, experts),
        grid=(hidden_size // EXPERT_TILE,),
        in_specs=[
            whole((rows, D)),
            half,
            pl.BlockSpec((D, EXPERT_TILE), lambda f: (0, f)),
            pl.BlockSpec((EXPERT_TILE, D), lambda f: (f, 0)),
            whole((D, lanes)),
            whole((lanes, D)),
            pl.BlockSpec(memory_space=pltpu.SMEM),
        ],
        out_specs=[
            pl.BlockSpec((rows, EXPERT_TILE), lambda f: (0, f)),
            pl.BlockSpec((rows, EXPERT_TILE), lambda f: (0, f)),
            whole((rows, D)),
            whole((rows, D)),
            whole((rows, 1)),
            whole((D, lanes)),
        ],
        out_shape=[
            jax.ShapeDtypeStruct((rows, hidden_size), BF),
            jax.ShapeDtypeStruct((rows, hidden_size), BF),
            jax.ShapeDtypeStruct((rows, D), BF),
            jax.ShapeDtypeStruct((rows, D), BF),
            jax.ShapeDtypeStruct((rows, 1), F32),
            jax.ShapeDtypeStruct((D, lanes), F32),
        ],
        scratch_shapes=[pltpu.VMEM((rows, D), F32), pltpu.VMEM((rows, D), F32)],
        compiler_params=params(("arbitrary",)),
        cost_estimate=cost(
            8 * rows * D * hidden_size, 4 * rows * hidden_size + 4 * D * hidden_size
        ),
        name="expert",
    )(x, c, w_first, w_second, router, router_t, mine)


def expert_weights_kernel(parts, side, *refs):
    if side is not None:
        side, refs = refs[0], refs[1:]
    xs, gates = refs[:parts], refs[parts : 2 * parts]
    acts, dhs = refs[2 * parts : 3 * parts], refs[3 * parts : 4 * parts]
    cots = refs[4 * parts]
    if side is None:
        grad_first, grad_second, x_t, c_t = refs[4 * parts + 1 :]
    else:
        kept_first, sent_first, kept_second, sent_second, x_t, c_t, whole_first = refs[4 * parts + 1 :]
    rows = xs[0].shape[0]
    share = cots.shape[1] // parts
    chunk = 256
    per = chunk // share

    @pl.when(pl.program_id(0) == 0)
    def _():
        for part in range(parts):
            for first in range(0, rows, chunk):
                at = slice(first, first + chunk)
                to = slice(part * rows + first, part * rows + first + chunk)
                gate = gates[part][at, :]
                x_t[:, to] = (xs[part][at, :].astype(F32) * gate).T.astype(BF)
                cot = cots[
                    first // chunk * per : (first // chunk + 1) * per,
                    part * share : (part + 1) * share,
                ].reshape(chunk, D)
                c_t[:, to] = (cot.astype(F32) * gate).T.astype(BF)

    first_sum, second_sum = None, None
    for part in range(parts):
        at = slice(part * rows, (part + 1) * rows)
        one = dot(x_t[:, at], dhs[part][...])
        two = dot(c_t[:, at], acts[part][...])
        first_sum = one if first_sum is None else first_sum + one
        second_sum = two if second_sum is None else second_sum + two
    if side is None:
        grad_first[...] = first_sum.astype(BF)
        grad_second[...] = second_sum.T.astype(BF)
        return
    mine = side[0]
    half = D // 2
    whole_first[...] = first_sum.astype(BF)
    kept_first[...] = whole_first[pl.ds(pl.multiple_of(mine * half, half), half), :]
    sent_first[...] = whole_first[pl.ds(pl.multiple_of((1 - mine) * half, half), half), :]
    here = pl.program_id(0) // (pl.num_programs(0) // 2) == mine

    @pl.when(here)
    def _():
        kept_second[...] = second_sum.T.astype(BF)

    @pl.when(jnp.logical_not(here))
    def _():
        sent_second[...] = second_sum.T.astype(BF)


def expert_weights(xs, cots, gates, acts, dhs, side):
    parts = len(xs)
    rows = xs[0].shape[0]
    hidden_size = acts[0].shape[1]
    steps = hidden_size // FF_TILE
    in_specs = (
        [whole((rows, D))] * parts
        + [whole((rows, 1))] * parts
        + [pl.BlockSpec((rows, FF_TILE), lambda f, *_: (0, f))] * (2 * parts)
        + [whole(cots.shape)]
    )
    scratch = [pltpu.VMEM((D, parts * rows), BF), pltpu.VMEM((D, parts * rows), BF)]
    if side is None:
        out_specs = [
            pl.BlockSpec((D, FF_TILE), lambda f: (0, f)),
            pl.BlockSpec((FF_TILE, D), lambda f: (f, 0)),
        ]
        shapes = [(D, hidden_size), (hidden_size, D)]
    else:
        columns = pl.BlockSpec((D // 2, FF_TILE), lambda f, s: (0, f))

        def rows_of(place):
            def index(f, s):
                start = jnp.where(s[0] == 1, place, 1 - place) * (steps // 2)
                return (jnp.clip(f - start, 0, steps // 2 - 1), 0)

            return pl.BlockSpec((FF_TILE, D), index)

        out_specs = [columns, columns, rows_of(1), rows_of(0)]
        shapes = [(D // 2, hidden_size)] * 2 + [(hidden_size // 2, D)] * 2
        scratch = scratch + [pltpu.VMEM((D, FF_TILE), BF)]
    prefetched = () if side is None else (side,)
    return pl.pallas_call(
        functools.partial(expert_weights_kernel, parts, side is not None or None),
        grid_spec=pltpu.PrefetchScalarGridSpec(
            num_scalar_prefetch=len(prefetched),
            grid=(steps,),
            in_specs=in_specs,
            out_specs=out_specs,
            scratch_shapes=scratch,
        ),
        out_shape=[jax.ShapeDtypeStruct(shape, BF) for shape in shapes],
        compiler_params=params(("arbitrary",)),
        cost_estimate=cost(
            4 * parts * rows * D * hidden_size, 4 * (parts * rows + D) * hidden_size
        ),
        name="expert_weights",
    )(*prefetched, *xs, *gates, *acts, *dhs, cots)


def rms_back(values, factor, grad):
    inverse = inverse_rms(values)
    scaled = grad * factor
    mean = jnp.mean(scaled * values, axis=-1, keepdims=True)
    return (
        inverse * scaled - values * (inverse * inverse * inverse * mean),
        jnp.sum(grad * values * inverse, axis=0, keepdims=True),
    )


def undispatch(slot_col, parts):
    out = None
    offset = 0
    for part in parts:
        total = part.shape[0]
        place = lax.broadcasted_iota(jnp.int32, (slot_col.shape[0], total), 1) + offset
        found = dot((place == slot_col).astype(BF), part[...])
        out = found if out is None else out + found
        offset += total
    return out


def middle_back_kernel(parts, *refs):
    backs = refs[:parts]
    (
        slot_col, middle, cot, gain, out_left, out_right,
        grad_middle, grad_attn, grad_context, grad_gain, w_out,
    ) = refs[parts:]

    @pl.when(pl.program_id(0) == 0)
    def _():
        w_out[:, :SIDE] = out_left[...]
        w_out[:, SIDE:] = out_right[...]

    grad_normed = undispatch(slot_col[...], backs)
    part, gain_part = rms_back(middle[...], gain[...], grad_normed)
    grad = cot[...].astype(F32) + part
    grad_middle[...] = grad
    low = grad.astype(BF)
    grad_attn[...] = low
    grad_context[...] = dot(low, w_out[...], 1, 1).astype(BF)

    @pl.when(pl.program_id(0) == 0)
    def _():
        grad_gain[...] = gain_part

    @pl.when(pl.program_id(0) > 0)
    def _():
        grad_gain[...] += gain_part


def middle_back(backs, slot_col, middle, cot, gain, left, right):
    parts = len(backs)
    block = 256
    rows = pl.BlockSpec((block, D), lambda r: (r, 0))
    return pl.pallas_call(
        functools.partial(middle_back_kernel, parts),
        grid=(TOK // block,),
        in_specs=[whole(back.shape) for back in backs]
        + [
            pl.BlockSpec((block, 1), lambda r: (r, 0)),
            rows,
            rows,
            whole((1, D)),
            pl.BlockSpec((D, SIDE), lambda r: (0, 3)),
            pl.BlockSpec((D, SIDE), lambda r: (0, 3)),
        ],
        out_specs=[rows, rows, rows, whole((1, D))],
        scratch_shapes=[pltpu.VMEM((D, D), BF)],
        out_shape=[
            jax.ShapeDtypeStruct((TOK, D), F32),
            jax.ShapeDtypeStruct((TOK, D), BF),
            jax.ShapeDtypeStruct((TOK, D), BF),
            jax.ShapeDtypeStruct((1, D), F32),
        ],
        compiler_params=params(("arbitrary",)),
        cost_estimate=cost(2 * 2 * TOK * TOK * D + 2 * TOK * D * D, 16 * TOK * D),
        name="middle_back",
    )(*backs, slot_col, middle, cot, gain, left, right)


def mix_kernel(parts, *refs):
    backs = refs[:parts]
    slot_col, middle, gate, mixed = refs[parts:]
    mixed[...] = middle[...] + gate[...] * undispatch(slot_col[...], backs)


def mix(backs, slot_col, middle, gate):
    parts = len(backs)
    block = 256
    rows = pl.BlockSpec((block, D), lambda r: (r, 0))
    column = pl.BlockSpec((block, 1), lambda r: (r, 0))
    return pl.pallas_call(
        functools.partial(mix_kernel, parts),
        grid=(TOK // block,),
        in_specs=[whole(back.shape) for back in backs] + [column, rows, column],
        out_specs=rows,
        out_shape=jax.ShapeDtypeStruct((TOK, D), F32),
        compiler_params=params(("arbitrary",)),
        cost_estimate=cost(2 * 2 * TOK * TOK * D, 12 * TOK * D, share=1),
        name="mix",
    )(*backs, slot_col, middle, gate)


def tokens_back_kernel(g_left, g_right, left, right, tokens, gain, grad_middle, grad_tokens):
    grad_normed = dot(g_left[...], left[...], 1, 1) + dot(g_right[...], right[...], 1, 1)
    grad_tokens[...] = grad_middle[...] + rms_back(
        tokens[...].astype(F32), gain[...], grad_normed
    )[0]


def tokens_back(g_left, g_right, left, right, tokens, gain, grad_middle):
    block = 256
    rows = pl.BlockSpec((block, D), lambda r: (r, 0))
    return pl.pallas_call(
        tokens_back_kernel,
        grid=(TOK // block,),
        in_specs=[
            pl.BlockSpec((block, SPLIT), lambda r: (r, 0)),
            pl.BlockSpec((block, SPLIT), lambda r: (r, 0)),
            whole((D, SPLIT)),
            whole((D, SPLIT)),
            rows,
            whole((1, D)),
            rows,
        ],
        out_specs=rows,
        out_shape=jax.ShapeDtypeStruct((TOK, D), F32),
        compiler_params=params(("arbitrary",)),
        cost_estimate=cost(6 * TOK * D * D, 16 * TOK * D, share=1),
        name="tokens_back",
    )(g_left, g_right, left, right, tokens, gain, grad_middle)


def weights_back_kernel(turned, grads, context, grad_attn, out):
    last = pl.num_programs(0) - 1

    @pl.when(pl.program_id(0) < last)
    def _():
        out[...] = dot(turned[...], grads[...])

    @pl.when(pl.program_id(0) == last)
    def _():
        out[...] = dot(context[...], grad_attn[...], 0, 0)


def weights_back(half, turned, grads, context, grad_attn):
    steps = grads.shape[1] // SIDE
    columns = (steps + 1) * SIDE
    return pl.pallas_call(
        weights_back_kernel,
        grid=(steps + 1,),
        in_specs=[
            whole(turned.shape),
            pl.BlockSpec((TOK, SIDE), lambda c: (0, jnp.minimum(c, steps - 1))),
            whole((TOK, D)),
            pl.BlockSpec((TOK, SIDE), lambda c: (0, half)),
        ],
        out_specs=pl.BlockSpec((D, SIDE), lambda c: (0, c)),
        out_shape=jax.ShapeDtypeStruct((D, columns), F32),
        compiler_params=params(("arbitrary",)),
        cost_estimate=cost(2 * TOK * D * columns, 2 * TOK * (D + columns) + 4 * D * columns),
        name="weights_back",
    )(turned, grads, context, grad_attn)


def swap(block, axis, bit):
    size = lax.axis_size(axis)
    return lax.ppermute(block, axis, [(place, place ^ bit) for place in range(size)])


def on_upper(axis, bit):
    return (lax.axis_index(axis) // bit) % 2 == 1


def axis_bits(*axes):
    found = []
    for axis in axes:
        bit = lax.axis_size(axis) // 2
        while bit >= 1:
            found.append((axis, bit))
            bit //= 2
    return found


def orders():
    bits = axis_bits("dp", "expert")
    dp = [at for at, (axis, _) in enumerate(bits) if axis == "dp"]
    core = len(bits) - 1
    along = [at for at, (axis, bit) in enumerate(bits) if axis == "expert" and bit == 2]
    rest = [at for at in range(core) if at not in dp and at not in along]
    return (rest + along + dp + [core], rest + dp + along + [core])


def gather_start(shard):
    return shard.reshape((1,) * len(axis_bits("dp", "expert")) + shard.shape)


def gather_step(block, place):
    axis, bit = axis_bits("dp", "expert")[place]
    other = swap(block, axis, bit)
    upper = on_upper(axis, bit)
    return jnp.concatenate(
        [jnp.where(upper, other, block), jnp.where(upper, block, other)], axis=place
    )


def gather_end(block):
    return block.reshape((-1, block.shape[-1]))


def scatter_start(total):
    bits = axis_bits("dp", "expert")
    rows = total.shape[0] >> len(bits)
    return total.reshape((2,) * len(bits) + (rows,) + total.shape[1:])


def scatter_step(block, place, *others):
    axis, bit = axis_bits("dp", "expert")[place]
    lower = lax.slice_in_dim(block, 0, 1, axis=place)
    higher = lax.slice_in_dim(block, 1, 2, axis=place)
    upper = on_upper(axis, bit)
    sent = jnp.where(upper, lower, higher).astype(BF)
    kept = after(jnp.where(upper, higher, lower), *others)
    return kept + swap(sent, axis, bit).astype(F32)


def scatter_rest(block, order):
    for place in order:
        block = scatter_step(block, place)
    return block.reshape(block.shape[len(axis_bits("dp", "expert")) :])


def sum_all(total, beside):
    for number, (axis, bit) in enumerate(axis_bits("dp", "expert")):
        kept = after(total, beside[number]) if number < len(beside) else total
        total = kept + swap(total, axis, bit)
    return total


def gather_dp(block, axis, other=None):
    if lax.axis_size("dp") != 2:
        return lax.all_gather(block, "dp", axis=axis, tiled=True)
    if other is None:
        other = swap(block, "dp", 1)
    upper = on_upper("dp", 1)
    return jnp.concatenate(
        [jnp.where(upper, other, block), jnp.where(upper, block, other)], axis=axis
    )


def receive_dp(halves):
    if len(halves) == 1:
        return (lax.psum_scatter(halves[0], "dp", scatter_dimension=0, tiled=True),)
    kept, sent = halves
    return (kept, swap(sent, "dp", 1))


def add_dp(parts, *others):
    kept, *received = parts
    total = after(kept, *others).astype(F32)
    for part in received:
        total = total + part.astype(F32)
    return total[None]


def after(value, *others):
    return lax.optimization_barrier((value, *others))[0]


def body(
    tokens, seq_ids, routes, cotangent, w_query, w_key, w_value, w_out,
    rel_table, gain_attn, gain_ffn, router, expert_in, expert_out,
):
    experts = lax.axis_size("expert")
    capacity = 2 * TOK // experts
    shard = w_query.shape[0]
    lanes = -(-(experts + 2) // LANES) * LANES

    small = jnp.concatenate(
        [
            router,
            gain_attn[:, None],
            gain_ffn[:, None],
            jnp.zeros((shard, lanes - experts - 2), BF),
        ],
        axis=1,
    )
    first, second = orders()
    kinds = (w_query, w_key, w_value, w_out)
    paired = lax.axis_size("dp") == 2
    own_first, own_second = expert_in[0], expert_out[0]
    second_cut = own_second.shape[0] // 2
    early = [swap(own_second[:second_cut], "dp", 1)] if paired else []
    ahead = [own_second[:second_cut]] if paired else []
    left = gather_start(
        jnp.concatenate([after(w_query[:, :SIDE], *ahead)] + [w[:, :SIDE] for w in kinds[1:]], axis=1)
    )
    right = gather_start(
        jnp.concatenate(
            [after(w_query[:, SIDE:], *ahead)] + [w[:, SIDE:] for w in kinds[1:]] + [small], axis=1
        )
    )
    table = gather_dp(rel_table, 0)
    dp_bits = len(axis_bits("dp"))
    rest = len(first) - dp_bits - 2
    for at in range(rest):
        left, right = gather_step(left, first[at]), gather_step(right, second[at])
    left, right = lax.optimization_barrier((left, right, table, *early))[:2]
    slot_col, slot_row, sending_cot = make_slots(
        after(routes, left), cotangent, experts, capacity
    )
    left = gather_step(left, first[rest])
    for place in second[rest : rest + dp_bits]:
        right = gather_step(right, place)
    wide_table = after(table, right).astype(F32)
    query_features, key_features = lane_features(
        after(seq_ids, right).reshape(TOK, 1), wide_table
    )
    band = jnp.sum(band_onehot()[None, :, :] * wide_table.T[:, None, :], axis=2)[:, None, :]
    for place in first[rest + 1 : -1]:
        left = gather_step(left, place)
    for place in second[rest + dp_bits : -1]:
        right = gather_step(right, place)
    ready = (left, right)
    left = after(left, sending_cot)
    right = after(right, query_features, key_features, band)
    left = gather_end(gather_step(left, first[-1]))
    right = gather_end(gather_step(right, second[-1]))

    def exchange(rows):
        return lax.all_to_all(
            rows.reshape(experts, -1, D), "expert", split_axis=0, concat_axis=0, tiled=True
        )

    cots = exchange(after(sending_cot, *ready))
    if paired:
        other_first = swap(after(own_first, *ready), "dp", 1)
        late = swap(after(own_second[second_cut:], other_first), "dp", 1)
        other_second = jnp.concatenate([*early, late], axis=0)
        early.append(other_first)
    else:
        other_first = other_second = None
    w_first = gather_dp(own_first, 0, other_first)
    w_second = gather_dp(own_second, 0, other_second)

    extra = right[:, SPLIT + SIDE :]
    full_router = jnp.where(jnp.arange(lanes)[None, :] < experts, extra, jnp.zeros((), BF))
    router_t = full_router.T
    attn_gain = extra[:, experts].astype(F32).reshape(1, D)
    ffn_gain = extra[:, experts + 1].astype(F32).reshape(1, D)

    turned, qkv = project(tokens, attn_gain, left, right)
    context, lse = attend(qkv, query_features, key_features, band)

    middle, *sending, gate = make_middle(
        context, tokens, left, right, ffn_gain, full_router, routes, slot_row, experts, capacity
    )
    sending[0] = after(sending[0], cots, *early)
    sending[1] = after(sending[1], w_first, w_second)
    rows_in = [exchange(part).reshape(-1, D) for part in sending]
    mine = lax.axis_index("expert").astype(jnp.int32).reshape(1, 1)
    acts, dhs, results, grads, gates, router_parts = zip(
        *(
            run_expert(
                part, rows, cots, w_first, w_second, full_router, router_t, mine, experts
            )
            for part, rows in enumerate(rows_in)
        )
    )
    grads_home = [exchange(part).reshape(-1, D) for part in grads]
    weight_parts = expert_weights(
        rows_in,
        cots,
        (after(gates[0], grads_home[0]), *gates[1:]),
        acts,
        dhs,
        lax.axis_index("dp").astype(jnp.int32).reshape(1) if paired else None,
    )
    half = len(weight_parts) // 2
    grad_first, grad_second = weight_parts[:half], weight_parts[half:]
    results_home = []
    for part in results:
        part = after(part, *grads_home, *weight_parts, *results_home)
        results_home.append(exchange(part).reshape(-1, D))
    grads_home[0] = after(grads_home[0], *weight_parts)
    grad_middle, grad_attn, grad_context, grad_gain_f = middle_back(
        grads_home, slot_col, middle, cotangent, ffn_gain, left, right
    )
    down, down_other = second[::-1], first[::-1]

    def back(half, *others):
        return attend_back(
            half, qkv, after(grad_context, *others), query_features, key_features, lse, band
        )

    g_left, tiles_left, diagonals_left = back(0)
    left_block = scatter_start(weights_back(0, turned, g_left, context, grad_attn))
    g_right, tiles_right, diagonals_right = back(1, left_block, results_home[0])
    left_block = after(left_block, results_home[0])
    first_halves, second_halves = receive_dp(grad_first), receive_dp(grad_second)
    grad_right = weights_back(
        1, turned, after(g_right, results_home[1]), context, grad_attn
    )
    left_block = scatter_step(left_block, down[0], grad_right)
    right_block = scatter_step(scatter_start(grad_right), down_other[0], second_halves[-1])
    grad_tokens = tokens_back(
        g_left, after(g_right, right_block), left, right, tokens, attn_gain, grad_middle
    )
    beside = [left_block]
    left_block = scatter_step(left_block, down[1], grad_tokens)
    right_block = scatter_step(right_block, down_other[1], grad_tokens)
    beside.append(left_block)
    mixed = mix(results_home, slot_col, middle, after(gate, left_block, right_block))
    near = 2 + len(axis_bits("dp"))
    for place in down[2:near]:
        left_block = scatter_step(left_block, place, mixed, first_halves[-1])
    beside.append(left_block)
    for place in down_other[2:near]:
        right_block = scatter_step(right_block, place, mixed)
    joined = jnp.concatenate([left_block, right_block], axis=-1)
    grad_expert_in = add_dp(first_halves, joined)
    grad_expert_out = add_dp(second_halves, joined)
    joined = scatter_step(joined, down[near])
    beside.append(joined)
    dense = scatter_rest(joined, down[near + 1 :])
    grad_left, grad_right = dense[:, : SPLIT + SIDE], dense[:, SPLIT + SIDE :]
    tiles = jnp.concatenate([tiles_left, tiles_right], axis=0)
    diagonals = jnp.concatenate([diagonals_left, diagonals_right], axis=0)
    grad_router = sum(router_parts)[:, :experts]
    grad_table = table_gradient(tiles, diagonals)

    grad_weights = [
        jnp.concatenate(
            [side[:, kind * SIDE : (kind + 1) * SIDE] for side in (grad_left, grad_right)], axis=1
        )
        for kind in range(4)
    ]
    products = sum(w.astype(F32) * grad for w, grad in zip(kinds[:3], grad_weights[:3]))
    grad_gain_a = jnp.sum(products, axis=1) / gain_attn.astype(F32)

    sizes = (D * experts, D, BUCKETS * HEADS)
    sums = sum_all(
        jnp.concatenate(
            [part.reshape(-1, LANES) for part in (grad_router, grad_gain_f, grad_table)], axis=0
        ),
        beside,
    ).reshape(-1)
    ends = [sum(sizes[: at + 1]) for at in range(len(sizes))]
    grad_router, grad_gain_f, grad_table = (
        sums[end - size : end] for end, size in zip(ends, sizes)
    )
    number = lax.axis_index("dp") * experts + lax.axis_index("expert")
    table_height = BUCKETS // lax.axis_size("dp")

    def own(rows, height, place):
        return lax.dynamic_slice_in_dim(rows, place * height, height, 0)

    return (
        mixed,
        grad_tokens,
        *grad_weights,
        own(grad_table.reshape(BUCKETS, HEADS), table_height, lax.axis_index("dp")),
        grad_gain_a,
        own(grad_gain_f, shard, number),
        own(grad_router.reshape(D, experts), shard, number),
        grad_expert_in,
        grad_expert_out,
    )


def solution(mesh):
    rows = P(("dp", "expert"), None)
    flat = P(("dp", "expert"))
    expert = P("expert", "dp", None)
    return jax.shard_map(
        body,
        mesh=mesh,
        in_specs=(
            rows, flat, rows, rows, rows, rows, rows, rows,
            P("dp", None), flat, flat, rows, expert, expert,
        ),
        out_specs=(
            rows, rows, rows, rows, rows, rows,
            P("dp", None), flat, flat, rows, expert, expert,
        ),
        check_vma=False,
    )
```
